32 devices in a mesh: dp: 8 (over y, x, core), mp: 4 (over z).
Axes of the slice: x: 2, y: 2, z: 4, core: 2. Of those that a mesh axis runs over, the one named last changes fastest.
Arguments:
- tokens: bfloat16 [16384, 1024], P(('dp', 'mp')), may hold values from -6 to 6
- kept_index: int32 [16384], P(('dp', 'mp')), may hold values from 0 to 1567
- lengths: int32 [8, 5], P('dp'), may hold values from 1 to 549, 2048 in all within a row
- first_gain: bfloat16 [1024], P(('dp', 'mp')), may hold values from 0.099609375 to 1.8984375
- first_shift: bfloat16 [1024], P(('dp', 'mp')), may hold values from -1.75 to 1.75
- query_weight: bfloat16 [1024, 1024], P(None, 'mp'), may hold values from -0.1875 to 0.1875
- key_weight: bfloat16 [1024, 1024], P(None, 'mp'), may hold values from -0.1875 to 0.1875
- value_weight: bfloat16 [1024, 1024], P(None, 'mp'), may hold values from -0.1875 to 0.1875
- query_bias: bfloat16 [1024], P(('dp', 'mp')), may hold values from -1.75 to 1.75
- value_bias: bfloat16 [1024], P(('dp', 'mp')), may hold values from -1.75 to 1.75
- output_weight: bfloat16 [1024, 1024], P('mp'), may hold values from -1.75 to 1.75
- output_bias: bfloat16 [1024], P(('dp', 'mp')), may hold values from -1.75 to 1.75
- second_gain: bfloat16 [1024], P(('dp', 'mp')), may hold values from 0.099609375 to 1.8984375
- second_shift: bfloat16 [1024], P(('dp', 'mp')), may hold values from -1.75 to 1.75
- expand_weight: bfloat16 [1024, 4096], P(None, 'mp'), may hold values from -0.1875 to 0.1875
- expand_bias: bfloat16 [4096], P(('dp', 'mp')), may hold values from -1.75 to 1.75
- reduce_weight: bfloat16 [4096, 1024], P('mp'), may hold values from -0.09375 to 0.09375
- reduce_bias: bfloat16 [1024], P(('dp', 'mp')), may hold values from -1.75 to 1.75
- cotangent: bfloat16 [16384, 1024], P(('dp', 'mp')), may hold values from -6 to 6
Outputs:
- activations: bfloat16 [16384, 1024], P(('dp', 'mp'))
- grad_tokens: bfloat16 [16384, 1024], P(('dp', 'mp'))
- grad_query_weight: float32 [1024, 1024], P('dp', 'mp')
- grad_key_weight: float32 [1024, 1024], P('dp', 'mp')
- grad_value_weight: float32 [1024, 1024], P('dp', 'mp')
- grad_output_weight: float32 [1024, 1024], P('mp', 'dp')
- grad_expand_weight: float32 [1024, 4096], P('dp', 'mp')
- grad_reduce_weight: float32 [4096, 1024], P('mp', 'dp')
- grad_first_gain: float32 [1024], P(('dp', 'mp'))
- grad_first_shift: float32 [1024], P(('dp', 'mp'))
- grad_query_bias: float32 [1024], P(('dp', 'mp'))
- grad_value_bias: float32 [1024], P(('dp', 'mp'))
- grad_output_bias: float32 [1024], P(('dp', 'mp'))
- grad_second_gain: float32 [1024], P(('dp', 'mp'))
- grad_second_shift: float32 [1024], P(('dp', 'mp'))
- grad_expand_bias: float32 [4096], P(('dp', 'mp'))
- grad_reduce_bias: float32 [1024], P(('dp', 'mp'))
The draws below stay inside these ranges and needn't reach their ends.
Inputs may be any that keep to these rules, and one draw needn't show every extreme that they name: `lengths`: each row lists, in order, the visible tokens of the 5 clips laid end to end in the 2048 tokens of one group; a row sums to 2048. `kept_index`: the patch position of a token in its clip, drawn for each token independently; positions are in no order and may repeat within a clip.
All inputs are finite; a program needn't handle non-finite values.
Results may differ from the reference program's by a relative error of at most 0.02.
Values may be sent and summed in bfloat16 or wider, within the bound.
A program may use at most 192 MiB of HBM per device.

```python
import math
import jax
import jax.numpy as jnp
import numpy as np
from jax import lax

D = 1024
HEADS = 16
HEAD_SIZE = 64
FF = 4096
PATCHES = 1568
CLIP_MEAN = 352
GROUP_ROWS = 2048
CLIPS = 5
LONGEST = 549
GROUPS = 8
TOKENS = 16384


def with_ends(values, key, low, largest):
    place = [jax.random.randint(jax.random.fold_in(key, axis), (), 0, length) for axis, length in enumerate(values.shape)]
    main_axis = values.shape.index(max(values.shape))
    neighbour = place[:main_axis] + [(place[main_axis] + 1) % values.shape[main_axis]] + place[main_axis + 1:]
    return values.at[tuple(place)].set(low).at[tuple(neighbour)].set(largest)


def strengthened(drawn, key, source, target, shards_of, factor):
    owner, partner = [(jnp.arange(drawn.shape[position]) // (drawn.shape[position] // shards_of)).reshape([-1 if axis == position else 1 for axis in range(drawn.ndim)]) for position in (source, target)]
    chosen = jax.random.permutation(key, shards_of)[partner]
    strong = (owner == chosen) | (owner == (partner + shards_of // 2) % shards_of)
    return jnp.where(strong, factor * drawn, drawn)


def level_of(key, shape, split, low, high):
    def one(axis_at, blocks):
        heights = jax.random.uniform(jax.random.fold_in(jax.random.fold_in(key, 6), axis_at), (blocks,), jnp.float32, low / len(split), high / len(split))
        return jnp.repeat(jnp.exp(heights), shape[axis_at] // blocks).reshape((-1,) + (1,) * (len(shape) - axis_at - 1))

    factor_of = one(*split[0])
    for cut in split[1:]:
        factor_of = factor_of * one(*cut)
    return factor_of


def length_profile(amount, total, most, skew):
    weights = [(1 << 20) // math.isqrt(rank ** skew) + 1 for rank in range(2, amount + 1)]
    rest, given = total - most - (amount - 1), [1] * (amount - 1)
    while rest > 0:
        movable = [i for i in range(amount - 1) if given[i] < most]
        mass, left = sum([weights[i] for i in movable]), rest
        for i in movable:
            extra = min(most - given[i], max(1, left * weights[i] // mass), rest)
            given[i] = given[i] + extra
            rest = rest - extra
    return np.array([most] + given)


def uneven_parts(own_key, count, total, most, skew):
    if count == 2:
        one = jax.random.randint(own_key, (), max(1, total - most), min(most, total - 1) + 1)
        return jnp.stack([one, total - one])
    sizes = jnp.asarray(length_profile(count, total, most, skew), jnp.int32)
    couples = (count - 1) // 2
    source_of, receiver = sizes[1:1 + 2 * couples:2], sizes[2:2 + 2 * couples:2]
    margin = jnp.minimum(source_of - 1, most - receiver)
    shifted = jax.random.randint(jax.random.fold_in(own_key, 1), (couples,), 0, 1 << 20) % (margin + 1)
    sizes = sizes.at[1:1 + 2 * couples:2].set(source_of - shifted).at[2:2 + 2 * couples:2].set(receiver + shifted)
    return sizes[jax.random.permutation(jax.random.fold_in(own_key, 2), count)]


def normal_values(rng, shape, deviation, most, cuts=(), kind=jnp.bfloat16):
    values = jax.random.normal(rng, shape, jnp.float32) * deviation
    if len(cuts) > 0:
        values = level_of(rng, shape, cuts, -0.22, 0.18) * values
    return jnp.clip(values, min=-most, max=most).astype(kind)


def heavy_noise(key, shape, width, bound, cuts, heavy, kind=jnp.bfloat16):
    values = width * jax.random.normal(key, shape, jnp.float32)
    if cuts:
        values = values * level_of(key, shape, cuts, -0.22, 0.18)
    return jnp.clip(strengthened(values, jax.random.fold_in(key, 3), *heavy), -bound, bound).astype(kind)


def setup_inputs(seed: int = 0) -> dict:
    arg_keys = jax.random.split(jax.random.key(seed), 20)
    tokens = heavy_noise(arg_keys[0], (TOKENS, D), 1.0, 6.0, ((0, 32),), (0, 1, 32, 2.75))
    kept_index = with_ends(jax.random.randint(arg_keys[1], (TOKENS,), 0, PATCHES), jax.random.fold_in(arg_keys[1], 1), 0, PATCHES - 1).astype(jnp.int32)
    lengths = jax.vmap(lambda own: uneven_parts(own, CLIPS, GROUP_ROWS, LONGEST, 2))(jax.random.split(arg_keys[2], GROUPS)).reshape((GROUPS, CLIPS)).astype(jnp.int32)
    first_gain = jnp.clip(1.0 + 0.18 * jax.random.normal(arg_keys[3], (D,), jnp.float32), 0.099609375, 1.8984375).astype(jnp.bfloat16)
    first_shift = normal_values(arg_keys[4], (D,), 0.3, 1.75, ((0, 32),))
    query_weight = normal_values(arg_keys[5], (D, D), D ** -0.5, 0.1875, ((1, 4),))
    key_weight = normal_values(arg_keys[6], (D, D), D ** -0.5, 0.1875, ((1, 4),))
    value_weight = normal_values(arg_keys[7], (D, D), D ** -0.5, 0.1875, ((1, 4),))
    query_bias = normal_values(arg_keys[8], (D,), 0.3, 1.75, ((0, 32),))
    value_bias = normal_values(arg_keys[9], (D,), 0.3, 1.75, ((0, 32),))
    output_weight = normal_values(arg_keys[10], (D, D), (max(1, D * 4 // CLIP_MEAN)) ** -0.5, 1.75, ((0, 4),))
    output_bias = normal_values(arg_keys[11], (D,), 0.3, 1.75, ((0, 32),))
    second_gain = jnp.clip(1.0 + 0.18 * jax.random.normal(arg_keys[12], (D,), jnp.float32), 0.099609375, 1.8984375).astype(jnp.bfloat16)
    second_shift = normal_values(arg_keys[13], (D,), 0.3, 1.75, ((0, 32),))
    expand_weight = normal_values(arg_keys[14], (D, FF), D ** -0.5, 0.1875, ((1, 4),))
    expand_bias = normal_values(arg_keys[15], (FF,), 0.3, 1.75, ((0, 32),))
    reduce_weight = normal_values(arg_keys[16], (FF, D), FF ** -0.5, 0.09375, ((0, 4),))
    reduce_bias = normal_values(arg_keys[17], (D,), 0.3, 1.75, ((0, 32),))
    cotangent = heavy_noise(arg_keys[18], (TOKENS, D), 1.0, 6.0, ((0, 32),), (0, 1, 32, 2.75))
    return dict(tokens=tokens, kept_index=kept_index, lengths=lengths, first_gain=first_gain, first_shift=first_shift, query_weight=query_weight, key_weight=key_weight, value_weight=value_weight, query_bias=query_bias, value_bias=value_bias, output_weight=output_weight, output_bias=output_bias, second_gain=second_gain, second_shift=second_shift, expand_weight=expand_weight, expand_bias=expand_bias, reduce_weight=reduce_weight, reduce_bias=reduce_bias, cotangent=cotangent)


EPSILON = 1e-06

@jax.custom_vjp
def low(v):
    return lax.optimization_barrier(v.astype(jnp.bfloat16)).astype(jnp.float32)

@jax.custom_vjp
def low_back(v):
    return v

def low_keep(v):
    return (low(v), None)

def low_pass(kept, grad):
    return (grad,)

def back_keep(v):
    return (v, None)

def back_low(kept, grad):
    return (low(grad),)
low.defvjp(low_keep, low_pass)
low_back.defvjp(back_keep, back_low)

def matmul(left, right):
    return jnp.dot(left, right, precision=lax.Precision.HIGHEST, preferred_element_type=jnp.float32)

def layer_norm(values, gain_vec, offset):
    center = values - lax.optimization_barrier(jnp.mean(values, axis=-1, keepdims=True))
    spread = lax.optimization_barrier(jnp.mean(center * center, axis=-1, keepdims=True))
    return center * lax.rsqrt(spread + EPSILON) * gain_vec + offset

def gelu(values):
    return 0.5 * values * (1.0 + lax.erf(values * 0.7071067811865476))

def sines(coords, extent):
    halfway = extent // 2
    inverse = jnp.exp(jnp.arange(halfway, dtype=jnp.float32) * (-math.log(10000.0) / halfway))
    angles = coords[:, None] * inverse[None, :]
    return [jnp.sin(angles), jnp.cos(angles)]

def position_table(kept_index, extent):
    frames = (kept_index // 196).astype(jnp.float32)
    across = (kept_index // 14 % 14).astype(jnp.float32)
    column = (kept_index % 14).astype(jnp.float32)
    quarter = extent // 4
    spatial = (extent - quarter) // 2
    pieces = sines(frames, quarter) + sines(across, spatial) + sines(column, spatial)
    return jnp.concatenate(pieces, axis=1)

def clip_labels(lengths, extent):
    bounds = jnp.cumsum(lengths, axis=-1).astype(jnp.int32)
    places = jnp.arange(extent, dtype=jnp.int32)
    return lax.optimization_barrier(jnp.sum((places[None, :, None] >= bounds[:, None, :]).astype(jnp.int32), axis=-1))

def one_head(inputs):
    queries, keys, values, labels = inputs
    scores = low_back(matmul(queries, keys.T) * (1.0 / math.sqrt(HEAD_SIZE)))
    same_clip = labels[:, None] == labels[None, :]
    scores = jnp.where(same_clip, scores, -1e+30)
    maxima = lax.optimization_barrier(jnp.max(scores, axis=1, keepdims=True))
    powers = jnp.exp(scores - maxima)
    weights = low(powers / lax.optimization_barrier(jnp.sum(powers, axis=1, keepdims=True)))
    return low_back(low(matmul(weights, values)))

def attention(queries, keys, values, labels):
    groups = labels.shape[0]
    extent = labels.shape[1]

    def by_head(array):
        return array.reshape(groups, extent, HEADS, HEAD_SIZE).transpose(0, 2, 1, 3).reshape(groups * HEADS, extent, HEAD_SIZE)
    labels_all = jnp.broadcast_to(labels[:, None, :], (groups, HEADS, extent)).reshape(groups * HEADS, extent)
    blended = lax.map(jax.checkpoint(one_head), (by_head(queries), by_head(keys), by_head(values), labels_all))
    return blended.reshape(groups, HEADS, extent, HEAD_SIZE).transpose(0, 2, 1, 3).reshape(groups * extent, HEADS * HEAD_SIZE)

def reference(tokens, kept_index, lengths, first_gain, first_shift, query_weight, key_weight, value_weight, query_bias, value_bias, output_weight, output_bias, second_gain, second_shift, expand_weight, expand_bias, reduce_weight, reduce_bias, cotangent):
    positions = position_table(kept_index, D)
    labels = clip_labels(lengths, GROUP_ROWS)
    params = tuple((item.astype(jnp.float32) for item in (first_gain, first_shift, query_weight, key_weight, value_weight, query_bias, value_bias, output_weight, output_bias, second_gain, second_shift, expand_weight, expand_bias, reduce_weight, reduce_bias)))

    def forward(stream_in, weights_all):
        gain_one, shift_one, weight_query, weight_key, weight_value, bias_query, bias_value, weight_output, bias_output, gain_two, shift_two, weight_expand, bias_expand, weight_reduce, bias_reduce = weights_all
        stream = stream_in + positions
        normed_one = low(layer_norm(stream, gain_one, shift_one))
        queries = low_back(low(matmul(normed_one, weight_query) + bias_query))
        keys = low_back(low(matmul(normed_one, weight_key)))
        values = low_back(low(matmul(normed_one, weight_value) + bias_value))
        attended = attention(queries, keys, values, labels)
        middle = stream + low_back(matmul(attended, weight_output)) + bias_output
        normed_two = low(layer_norm(middle, gain_two, shift_two))
        pre = low_back(matmul(normed_two, weight_expand) + bias_expand)
        hidden = low(gelu(pre))
        return middle + low_back(matmul(hidden, weight_reduce)) + bias_reduce
    result, pullback = jax.vjp(forward, tokens.astype(jnp.float32), params)
    grad_stream, grad_params = pullback(cotangent.astype(jnp.float32))
    g_gain_one, g_shift_one, g_query, g_key, g_value, g_bias_query, g_bias_value, g_output, g_bias_output, g_gain_two, g_shift_two, g_expand, g_bias_expand, g_reduce, g_bias_reduce = grad_params
    return (result.astype(jnp.bfloat16), grad_stream.astype(jnp.bfloat16), g_query, g_key, g_value, g_output, g_expand, g_reduce, g_gain_one, g_shift_one, g_bias_query, g_bias_value, g_bias_output, g_gain_two, g_shift_two, g_bias_expand, g_bias_reduce)
```

```python
import functools
import math

import jax
import jax.numpy as jnp
from jax import lax
from jax.experimental import pallas as pl
from jax.experimental.pallas import tpu as pltpu
from jax.sharding import PartitionSpec as P

HEAD_SIZE = 64
LONGEST = 549
EPSILON = 1e-06
TILE = 256
MIB = 1024 * 1024
F32 = jnp.float32
BF16 = jnp.bfloat16

NN = (((1,), (0,)), ((), ()))
NT = (((1,), (1,)), ((), ()))
TN = (((0,), (0,)), ((), ()))


def dot(left, right, dims=NN):
    return lax.dot_general(left, right, dims, preferred_element_type=F32)


def sines(coords, extent):
    halfway = extent // 2
    inverse = jnp.exp(jnp.arange(halfway, dtype=F32) * (-math.log(10000.0) / halfway))
    angles = coords[:, None] * inverse[None, :]
    return [jnp.sin(angles), jnp.cos(angles)]


def position_table(kept_index, extent):
    frames = (kept_index // 196).astype(F32)
    across = (kept_index // 14 % 14).astype(F32)
    column = (kept_index % 14).astype(F32)
    quarter = extent // 4
    spatial = (extent - quarter) // 2
    pieces = sines(frames, quarter) + sines(across, spatial) + sines(column, spatial)
    return jnp.concatenate(pieces, axis=1)


def norm_parts(values):
    center = values - jnp.mean(values, axis=-1, keepdims=True)
    spread = jnp.mean(center * center, axis=-1, keepdims=True)
    factor = lax.rsqrt(spread + EPSILON)
    return center * factor, factor


def norm_back(upstream, hat, factor, gain):
    scaled = upstream * gain
    first = jnp.mean(scaled, axis=-1, keepdims=True)
    second = jnp.mean(scaled * hat, axis=-1, keepdims=True)
    return factor * (scaled - first - hat * second)


def forward_kernel(bounds_ref, q_ref, k_ref, v_ref, lq_ref, lk_ref, o_ref, lse_ref, s_ref):
    rows = q_ref.shape[0]
    lane = lax.broadcasted_iota(jnp.int32, (TILE, 2 * HEAD_SIZE), 1)
    for block in range(rows // TILE):
        low = bounds_ref[2 * block]
        high = bounds_ref[2 * block + 1]
        span = slice(block * TILE, (block + 1) * TILE)
        query = q_ref[span, :]
        heads = [
            jnp.where(lane < HEAD_SIZE, query, jnp.zeros_like(query)),
            jnp.where(lane < HEAD_SIZE, jnp.zeros_like(query), query),
        ]
        label = lq_ref[span, :]
        label = jnp.concatenate([label, label], axis=1)

        def scores(t, carry):
            at = pl.multiple_of(t * TILE, TILE)
            key = k_ref[pl.ds(at, TILE), :]
            same = label == lk_ref[0:1, pl.ds(at, TILE)]
            out = []
            for h in range(2):
                s = jnp.where(same, dot(heads[h], key, NT), -1e30)
                s_ref[h, :, pl.ds(at, TILE)] = s
                out.append(jnp.maximum(carry[h], jnp.maximum(s[:, :128], s[:, 128:])))
            return tuple(out)

        least = jnp.full((TILE, 128), -1e30, F32)
        peaks = lax.fori_loop(low, high, scores, (least, least))
        peaks = [jnp.max(item, axis=1, keepdims=True) for item in peaks]

        def blend(t, carry):
            at = pl.multiple_of(t * TILE, TILE)
            value = v_ref[pl.ds(at, TILE), :]
            out = []
            for h in range(2):
                total, acc = carry[h]
                p = jnp.exp(s_ref[h, :, pl.ds(at, TILE)] - peaks[h])
                out.append((total + (p[:, :128] + p[:, 128:]), acc + dot(p.astype(BF16), value)))
            return tuple(out)

        zero = jnp.zeros((TILE, 128), F32)
        done = lax.fori_loop(low, high, blend, ((zero, zero), (zero, zero)))
        pieces = []
        for h in range(2):
            total = jnp.sum(done[h][0], axis=1, keepdims=True)
            pieces.append(done[h][1] / total)
            lse = jnp.broadcast_to(peaks[h] + jnp.log(total), (TILE, 128))
            lse_ref[0, h : h + 1, span] = lse.T[0:1, :]
        o_ref[span, :] = jnp.where(lane < HEAD_SIZE, pieces[0], pieces[1]).astype(BF16)


def backward_kernel(
    bounds_ref,
    q_ref,
    k_ref,
    v_ref,
    do_ref,
    o_ref,
    lse_ref,
    lq_ref,
    lk_ref,
    dq_ref,
    dk_ref,
    dv_ref,
    dk_acc,
    dv_acc,
):
    rows = q_ref.shape[0]
    lane = lax.broadcasted_iota(jnp.int32, (TILE, 2 * HEAD_SIZE), 1)
    row = lax.broadcasted_iota(jnp.int32, (2 * HEAD_SIZE, TILE), 0)
    dk_acc[...] = jnp.zeros_like(dk_acc)
    dv_acc[...] = jnp.zeros_like(dv_acc)

    def halves(array, where):
        zero = jnp.zeros_like(array)
        return [jnp.where(where < HEAD_SIZE, array, zero), jnp.where(where < HEAD_SIZE, zero, array)]

    for block in range(rows // TILE):
        low = bounds_ref[2 * block]
        high = bounds_ref[2 * block + 1]
        span = slice(block * TILE, (block + 1) * TILE)
        query, grad = q_ref[span, :], do_ref[span, :]
        query_t, grad_t = query.T, grad.T
        product = grad_t.astype(F32) * o_ref[span, :].T.astype(F32)
        deltas = [
            jnp.sum(product[h * HEAD_SIZE : (h + 1) * HEAD_SIZE], axis=0, keepdims=True)
            for h in range(2)
        ]
        lses = [lse_ref[0, h : h + 1, span] for h in range(2)]
        query_h, grad_h = halves(query, lane), halves(grad, lane)
        query_th, grad_th = halves(query_t, row), halves(grad_t, row)
        label = lq_ref[0:1, span]

        def step(t, carry):
            at = pl.multiple_of(t * TILE, TILE)
            key, value = k_ref[pl.ds(at, TILE), :], v_ref[pl.ds(at, TILE), :]
            key_t = key.T
            same = lk_ref[pl.ds(at, TILE), :]
            same = jnp.concatenate([same, same], axis=1) == label
            out, grad_k, grad_v = [], None, None
            for h in range(2):
                s = dot(key, query_th[h])
                p = jnp.where(same, jnp.exp(s - lses[h]), 0.0)
                dp = dot(value, grad_th[h])
                ds = (p * (dp - deltas[h])).astype(BF16)
                part_v = dot(p.astype(BF16), grad_h[h])
                part_k = dot(ds, query_h[h])
                grad_v = part_v if grad_v is None else grad_v + part_v
                grad_k = part_k if grad_k is None else grad_k + part_k
                out.append(carry[h] + dot(key_t[h * HEAD_SIZE : (h + 1) * HEAD_SIZE], ds))
            dk_acc[pl.ds(at, TILE), :] += grad_k
            dv_acc[pl.ds(at, TILE), :] += grad_v
            return tuple(out)

        zero = jnp.zeros((HEAD_SIZE, TILE), F32)
        parts = lax.fori_loop(low, high, step, (zero, zero))
        total = jnp.concatenate(parts, axis=0) * (1.0 / math.sqrt(HEAD_SIZE))
        dq_ref[span, :] = total.T.astype(BF16)
    dk_ref[...] = dk_acc[...].astype(BF16)
    dv_ref[...] = dv_acc[...].astype(BF16)


def attention_forward(bounds, queries, keys, values, label_q, label_k):
    rows, width = queries.shape
    window = keys.shape[0]
    pairs = width // (2 * HEAD_SIZE)
    column = lambda extent: pl.BlockSpec((extent, 2 * HEAD_SIZE), lambda p, b: (0, p))
    fixed = lambda shape: pl.BlockSpec(shape, lambda p, b: (0, 0))
    return pl.pallas_call(
        forward_kernel,
        grid_spec=pltpu.PrefetchScalarGridSpec(
            num_scalar_prefetch=1,
            grid=(pairs,),
            in_specs=[
                column(rows),
                column(window),
                column(window),
                fixed((rows, 128)),
                fixed((8, window)),
            ],
            out_specs=[column(rows), pl.BlockSpec((1, 2, rows), lambda p, b: (p, 0, 0))],
            scratch_shapes=[pltpu.VMEM((2, TILE, window), F32)],
        ),
        out_shape=[
            jax.ShapeDtypeStruct((rows, width), BF16),
            jax.ShapeDtypeStruct((pairs, 2, rows), F32),
        ],
        compiler_params=pltpu.CompilerParams(vmem_limit_bytes=32 * MIB),
        cost_estimate=pl.CostEstimate(
            flops=4 * rows * window * width, bytes_accessed=4 * window * width, transcendentals=0
        ),
        name="attention_forward",
    )(bounds, queries, keys, values, label_q, label_k)


def attention_backward(bounds, queries, keys, values, grads, attended, lse, label_q, label_k):
    rows, width = queries.shape
    window = keys.shape[0]
    pairs = width // (2 * HEAD_SIZE)
    column = lambda extent: pl.BlockSpec((extent, 2 * HEAD_SIZE), lambda p, b: (0, p))
    fixed = lambda shape: pl.BlockSpec(shape, lambda p, b: (0, 0))
    return pl.pallas_call(
        backward_kernel,
        grid_spec=pltpu.PrefetchScalarGridSpec(
            num_scalar_prefetch=1,
            grid=(pairs,),
            in_specs=[
                column(rows),
                column(window),
                column(window),
                column(rows),
                column(rows),
                pl.BlockSpec((1, 2, rows), lambda p, b: (p, 0, 0)),
                fixed((8, rows)),
                fixed((window, 128)),
            ],
            out_specs=[column(rows), column(window), column(window)],
            scratch_shapes=[
                pltpu.VMEM((window, 2 * HEAD_SIZE), F32),
                pltpu.VMEM((window, 2 * HEAD_SIZE), F32),
            ],
        ),
        out_shape=[
            jax.ShapeDtypeStruct((rows, width), BF16),
            jax.ShapeDtypeStruct((window, width), BF16),
            jax.ShapeDtypeStruct((window, width), BF16),
        ],
        compiler_params=pltpu.CompilerParams(vmem_limit_bytes=32 * MIB),
        cost_estimate=pl.CostEstimate(
            flops=10 * rows * window * width, bytes_accessed=8 * window * width, transcendentals=0
        ),
        name="attention_backward",
    )(bounds, queries, keys, values, grads, attended, lse, label_q, label_k)


def feed_kernel(
    x_ref,
    g_ref,
    xt_ref,
    gt_ref,
    we_ref,
    wr_ref,
    be_ref,
    out_ref,
    dx_ref,
    de_keep,
    de_send,
    dr_keep,
    dr_send,
    db_ref,
):
    step = pl.program_id(0)
    pre = dot(x_ref[...], we_ref[...]) + be_ref[0:1, :]
    cumulative = 0.5 * (1.0 + lax.erf(pre * 0.7071067811865476))
    hidden = (pre * cumulative).astype(BF16)
    slope = cumulative + pre * jnp.exp(-0.5 * pre * pre) * (1.0 / math.sqrt(2.0 * math.pi))
    grad_pre = (dot(g_ref[...], wr_ref[...]) * slope).astype(BF16)
    db_ref[...] = jnp.broadcast_to(
        jnp.sum(grad_pre.astype(F32), axis=0, keepdims=True), db_ref.shape
    )
    half = xt_ref.shape[0] // 2
    dr_keep[...] = dot(gt_ref[:half, :], hidden).astype(BF16)
    dr_send[...] = dot(gt_ref[half:, :], hidden).astype(BF16)
    de_keep[...] = dot(xt_ref[:half, :], grad_pre).astype(BF16)
    de_send[...] = dot(xt_ref[half:, :], grad_pre).astype(BF16)
    out = dot(hidden, wr_ref[...], NT)
    back = dot(grad_pre, we_ref[...], NT)

    @pl.when(step == 0)
    def _():
        out_ref[...] = out
        dx_ref[...] = back

    @pl.when(step > 0)
    def _():
        out_ref[...] += out
        dx_ref[...] += back


def feed_forward(x, g, x_t, g_t, expand, reduce_t, bias):
    rows, width = x.shape
    hidden = expand.shape[1]
    tile = 512
    whole = lambda shape: pl.BlockSpec(shape, lambda i: (0, 0))
    cut = lambda extent: pl.BlockSpec((extent, tile), lambda i: (0, i))
    half = width // 2
    return pl.pallas_call(
        feed_kernel,
        grid=(hidden // tile,),
        in_specs=[
            whole((rows, width)),
            whole((rows, width)),
            whole((width, rows)),
            whole((width, rows)),
            cut(width),
            cut(width),
            cut(8),
        ],
        out_specs=[
            whole((rows, width)),
            whole((rows, width)),
            cut(half),
            cut(half),
            cut(half),
            cut(half),
            cut(8),
        ],
        out_shape=[
            jax.ShapeDtypeStruct((rows, width), F32),
            jax.ShapeDtypeStruct((rows, width), F32),
            jax.ShapeDtypeStruct((half, hidden), BF16),
            jax.ShapeDtypeStruct((half, hidden), BF16),
            jax.ShapeDtypeStruct((half, hidden), BF16),
            jax.ShapeDtypeStruct((half, hidden), BF16),
            jax.ShapeDtypeStruct((8, hidden), F32),
        ],
        compiler_params=pltpu.CompilerParams(vmem_limit_bytes=48 * MIB),
        cost_estimate=pl.CostEstimate(
            flops=12 * rows * width * hidden, bytes_accessed=8 * width * hidden, transcendentals=0
        ),
        name="feed_forward",
    )(x, g, x_t, g_t, expand, reduce_t, bias)


class Plane:
    def __init__(self, size):
        self.size = size
        bits = list(range(1, size.bit_length() - 1))
        turn = len(bits) // 2
        self.orders = [bits, bits[turn:] + bits[:turn]]
        held = []
        for order in self.orders:
            masks = [0]
            for bit in order:
                masks = masks + [m ^ (1 << bit) for m in masks]
            held.append(masks)
        self.masks = [held[c] + [1 ^ m for m in held[1 - c]] for c in range(2)]
        self.steps = len(bits)

    def pairs(self, step):
        return [(i, i ^ (1 << self.orders[i % 2][step])) for i in range(self.size)]

    def siblings(self):
        return [(i, i ^ 1) for i in range(self.size)]

    def order(self, d):
        return jnp.bitwise_xor(jnp.array(self.masks, jnp.int32)[d % 2], d)

    def inverse(self, d):
        table = [[masks.index(m) for m in range(self.size)] for masks in self.masks]
        return jnp.array(table, jnp.int32)[d % 2][
            jnp.bitwise_xor(jnp.arange(self.size, dtype=jnp.int32), d)
        ]


def reorder(array, order, axis):
    count = order.shape[0]
    extent = array.shape[axis] // count
    return jnp.concatenate(
        [lax.dynamic_slice_in_dim(array, order[j] * extent, extent, axis) for j in range(count)],
        axis=axis,
    )


def cut_columns(array, widths):
    out, at = [], 0
    for width in widths:
        out.append(array[:, at : at + width])
        at += width
    return out


def gather_group(pieces, plane, mp):
    widths = [piece.shape[1] for piece in pieces]
    payload = jnp.concatenate(pieces, axis=1)
    got = [
        cut_columns(lax.ppermute(payload, "mp", [(i, (i + r) % mp) for i in range(mp)]), widths)
        for r in range(1, mp)
    ]
    held = jnp.concatenate([part[w] for w in range(len(widths)) for part in got], axis=1)
    for step in range(plane.steps):
        held = jnp.concatenate([held, lax.ppermute(held, "dp", plane.pairs(step))], axis=0)
    other = lax.ppermute(held, "dp", plane.siblings())
    whole = jnp.concatenate([held, other], axis=0)
    return cut_columns(whole, [width * (mp - 1) for width in widths])


def scatter_group(keeps, sends, plane, mp):
    sums = []
    for keep, send in zip(keeps, sends):
        got = lax.ppermute(send, "dp", plane.siblings())
        sums.append((keep.astype(F32) + got.astype(F32)).astype(BF16))
    widths = [item.shape[1] // mp for item in sums]
    held = jnp.concatenate(sums, axis=1) if len(sums) > 1 else sums[0]
    for step in reversed(range(plane.steps)):
        half = held.shape[0] // 2
        got = lax.ppermute(held[half:], "dp", plane.pairs(step))
        held = (held[:half].astype(F32) + got.astype(F32)).astype(BF16)
    at, columns = 0, []
    for width in widths:
        columns.append(held[:, at : at + mp * width])
        at += mp * width
    block = lambda r: jnp.concatenate(
        [item[:, r * width : (r + 1) * width] for item, width in zip(columns, widths)], axis=1
    )
    total = block(0).astype(F32)
    for r in range(1, mp):
        total = total + lax.ppermute(
            block(r), "mp", [(i, (i - r) % mp) for i in range(mp)]
        ).astype(F32)
    return cut_columns(total, widths)


def spread_kernel(count, mp, per_target, source_ref, *refs):
    *outs, slots, send_sem, recv_sem = refs
    me = lax.axis_index("dp") * mp + lax.axis_index("mp")
    devices = lambda i: (lax.div(i, mp), lax.rem(i, mp))
    barrier = pltpu.get_barrier_semaphore()

    def signal(step, carry):
        pl.semaphore_signal(
            barrier,
            inc=1,
            device_id=devices(lax.rem(me + step, count)),
            device_id_type=pl.DeviceIdType.MESH,
        )
        return carry

    lax.fori_loop(1, count, signal, 0)
    pl.semaphore_wait(barrier, count - 1)

    def copy(source, slot, target):
        return pltpu.make_async_remote_copy(
            src_ref=source_ref.at[source],
            dst_ref=slots.at[slot],
            send_sem=send_sem.at[target],
            recv_sem=recv_sem.at[slot],
            device_id=devices(target),
            device_id_type=pl.DeviceIdType.MESH,
        )

    def start(step, carry):
        target = lax.rem(me + step, count)
        copy(target if per_target else 0, me, target).start()
        return carry

    lax.fori_loop(1, count, start, 0)
    slots[me] = source_ref[me if per_target else 0]

    def finish(step, carry):
        target = lax.rem(me + step, count)
        copy(target if per_target else 0, me, target).wait_send()
        sender = lax.rem(me + count - step, count)
        copy(0, sender, sender).wait_recv()
        return carry

    lax.fori_loop(1, count, finish, 0)
    if per_target:
        outs[0][...] = jnp.sum(slots[...], axis=0)
        return
    for out, rows in zip(outs, (slice(0, 8), slice(8, 16))):
        share = count // out.shape[0]
        for c in range(out.shape[0]):
            out[c] = jnp.sum(slots[c * share : (c + 1) * share, rows, :], axis=0)


def spread(source, shapes, per_target, dp, mp, number):
    count = dp * mp
    vmem = pl.BlockSpec(memory_space=pltpu.VMEM)
    return pl.pallas_call(
        functools.partial(spread_kernel, count, mp, per_target),
        out_shape=[jax.ShapeDtypeStruct(shape, F32) for shape in shapes],
        in_specs=[vmem],
        out_specs=[vmem] * len(shapes),
        scratch_shapes=[
            pltpu.VMEM((count,) + source.shape[1:], F32),
            pltpu.SemaphoreType.DMA((count,)),
            pltpu.SemaphoreType.DMA((count,)),
        ],
        compiler_params=pltpu.CompilerParams(
            collective_id=number, has_side_effects=True, vmem_limit_bytes=16 * MIB
        ),
        name="spread_sum" if per_target else "spread_all",
    )(source)


def local(
    tokens,
    kept_index,
    lengths,
    first_gain,
    first_shift,
    query_weight,
    key_weight,
    value_weight,
    query_bias,
    value_bias,
    output_weight,
    output_bias,
    second_gain,
    second_shift,
    expand_weight,
    expand_bias,
    reduce_weight,
    reduce_bias,
    cotangent,
):
    dp, mp = lax.axis_size("dp"), lax.axis_size("mp")
    d, z = lax.axis_index("dp"), lax.axis_index("mp")
    plane = Plane(dp)
    order, inverse = plane.order(d), plane.inverse(d)
    turned = jnp.mod(z - jnp.arange(mp, dtype=jnp.int32), mp)
    rows, width = tokens.shape
    group_rows = rows * mp
    block = width // dp
    full_hidden = expand_weight.shape[1] * mp

    singles = (
        first_gain,
        first_shift,
        output_bias,
        second_gain,
        second_shift,
        reduce_bias,
        query_bias,
        value_bias,
    )
    single, wide = first_gain.shape[0], expand_bias.shape[0]
    me = d * mp + z
    lane = jnp.arange(128, dtype=jnp.int32)

    def placed(stack):
        count = 128 // stack.shape[1]
        return jnp.where(lane // stack.shape[1] == me % count, jnp.tile(stack, (1, count)), 0.0)

    sheet = jnp.concatenate(
        [
            placed(jnp.stack(singles).astype(F32)),
            placed(expand_bias[None].astype(F32)),
            jnp.zeros((7, 128), F32),
        ]
    )
    narrow, broad = spread(
        sheet[None], ((width // 128, 8, 128), (full_hidden // 128, 8, 128)), False, dp, mp, 1
    )
    vectors = [narrow[:, i].reshape(width) for i in range(len(singles))]
    by_order = lambda v: jnp.take(v.reshape(dp, -1), order, axis=0).reshape(-1)
    by_turn = lambda v: jnp.take(v.reshape(mp, -1), turned, axis=0).reshape(-1)
    gain_one, shift_one, bias_output, gain_two, shift_two, bias_reduce = map(by_order, vectors[:6])
    bias_query, bias_value = map(by_turn, vectors[6:])
    bias_expand = by_turn(broad[:, 0].reshape(full_hidden))

    own_rows = lambda w: lax.dynamic_slice_in_dim(w, d * block, block, 0)
    own_columns = lambda w: lax.dynamic_slice_in_dim(w, d * block, block, 1).T
    first_set = gather_group(
        [own_rows(query_weight), own_rows(key_weight), own_rows(value_weight)], plane, mp
    )
    own_set = cut_columns(
        reorder(jnp.concatenate([query_weight, key_weight, value_weight], axis=1), order, 0),
        [query_weight.shape[1]] * 3,
    )
    weight_q, weight_k, weight_v = [
        jnp.concatenate([own, rest], axis=1) for own, rest in zip(own_set, first_set)
    ]
    second_set = gather_group(
        [own_columns(output_weight), own_rows(expand_weight), own_columns(reduce_weight)], plane, mp
    )
    own_set = [
        reorder(output_weight, order, 1).T,
        reorder(expand_weight, order, 0),
        reorder(reduce_weight, order, 1).T,
    ]
    weight_o, weight_e, weight_r = [
        jnp.concatenate([own, rest], axis=1) for own, rest in zip(own_set, second_set)
    ]

    length = lengths[0]
    clips = length.shape[0]
    index = jnp.arange(clips, dtype=jnp.int32)
    ends = jnp.sum(jnp.where(index[None, :] <= index[:, None], length[None, :], 0), axis=1)
    starts = ends - length
    reach, hops, left = LONGEST - 1, [], 0
    while reach > 0:
        extent = min(rows, -(-reach // 64) * 64)
        hops.append(extent)
        left, reach = left + extent, reach - extent
    margin = -(-left // 128) * 128
    while (2 * margin + rows) % TILE:
        margin += 128
    window = 2 * margin + rows
    base = z * rows - margin
    places = base + jnp.arange(window, dtype=jnp.int32)
    labels = jnp.sum((places[:, None] >= ends[None, :]).astype(jnp.int32), axis=1)
    labels = jnp.where((places >= 0) & (places < group_rows), labels, -1)
    label_own = labels[margin : margin + rows]
    limits = []
    for i in range(rows // TILE):
        first = z * rows + i * TILE
        last = first + TILE - 1
        start = jnp.sum(jnp.where(ends <= first, length, 0))
        end = jnp.sum(jnp.where(starts <= last, length, 0))
        limits.append(lax.div(start - base, TILE))
        limits.append(lax.div(end - base + TILE - 1, TILE))
    bounds = jnp.stack(limits).astype(jnp.int32)

    stream = reorder(tokens.astype(F32) + position_table(kept_index, width), order, 1)
    hat_one, factor_one = norm_parts(stream)
    normed_one = (hat_one * gain_one + shift_one).astype(BF16)
    lefts, rights = [], []
    for hop, extent in enumerate(hops, 1):
        lefts.append(
            lax.ppermute(
                normed_one[rows - extent :], "mp", [(i, i + hop) for i in range(mp - hop)]
            )
        )
        rights.append(
            lax.ppermute(normed_one[:extent], "mp", [(i + hop, i) for i in range(mp - hop)])
        )
    padding = jnp.zeros((margin - left, width), BF16)
    around = jnp.concatenate([padding] + lefts[::-1] + [normed_one] + rights + [padding], axis=0)
    scale = 1.0 / math.sqrt(HEAD_SIZE)
    queries = (dot(normed_one, weight_q) + bias_query).astype(BF16) * jnp.asarray(scale, BF16)
    keys = dot(around, weight_k).astype(BF16)
    values = (dot(around, weight_v) + bias_value).astype(BF16)
    attended, lse = attention_forward(
        bounds,
        queries,
        keys,
        values,
        jnp.broadcast_to(label_own[:, None], (rows, 128)),
        jnp.broadcast_to(labels[None, :], (8, window)),
    )
    middle = stream + dot(attended, weight_o, NT) + bias_output

    hat_two, factor_two = norm_parts(middle)
    normed_two = (hat_two * gain_two + shift_two).astype(BF16)
    upstream = reorder(cotangent, order, 1)
    branch_two, grad_normed_two, de_keep, de_send, dr_keep, dr_send, grad_expand_bias = feed_forward(
        normed_two,
        upstream,
        normed_two.T,
        upstream.T,
        weight_e,
        weight_r,
        jnp.broadcast_to(bias_expand[None, :], (8, full_hidden)),
    )
    activations = reorder((middle + branch_two + bias_reduce).astype(BF16), inverse, 1)
    grad_output = upstream.astype(F32)
    grad_reduce_bias = jnp.sum(grad_output, axis=0)
    grad_second_gain = jnp.sum(grad_normed_two * hat_two, axis=0)
    grad_second_shift = jnp.sum(grad_normed_two, axis=0)
    grad_middle = grad_output + norm_back(grad_normed_two, hat_two, factor_two, gain_two)
    grad_output_bias = jnp.sum(grad_middle, axis=0)
    grad_branch = grad_middle.astype(BF16)
    half = width // 2
    do_keep = dot(grad_branch[:, :half], attended, TN).astype(BF16)
    do_send = dot(grad_branch[:, half:], attended, TN).astype(BF16)
    (grad_reduce,) = scatter_group([dr_keep], [dr_send], plane, mp)
    grad_expand, grad_out = scatter_group([de_keep, do_keep], [de_send, do_send], plane, mp)

    grad_attended = dot(grad_branch, weight_o).astype(BF16)
    grad_queries, grad_keys, grad_values = attention_backward(
        bounds,
        queries,
        keys,
        values,
        grad_attended,
        attended,
        lse,
        jnp.broadcast_to(label_own[None, :], (8, rows)),
        jnp.broadcast_to(labels[:, None], (window, 128)),
    )
    grad_query_bias = jnp.sum(grad_queries.astype(F32), axis=0)
    grad_value_bias = jnp.sum(grad_values.astype(F32), axis=0)
    grad_around = dot(grad_keys, weight_k, NT) + dot(grad_values, weight_v, NT)
    sent = grad_around.astype(BF16)
    grad_normed_one = grad_around[margin : margin + rows] + dot(grad_queries, weight_q, NT)
    at_left, at_right = margin, margin + rows
    for hop, extent in enumerate(hops, 1):
        from_right = lax.ppermute(
            sent[at_left - extent : at_left], "mp", [(i + hop, i) for i in range(mp - hop)]
        )
        from_left = lax.ppermute(
            sent[at_right : at_right + extent], "mp", [(i, i + hop) for i in range(mp - hop)]
        )
        at_left, at_right = at_left - extent, at_right + extent
        grad_normed_one = grad_normed_one + jnp.pad(
            from_right.astype(F32), ((rows - extent, 0), (0, 0))
        )
        grad_normed_one = grad_normed_one + jnp.pad(
            from_left.astype(F32), ((0, rows - extent), (0, 0))
        )
    keeps, sends = [], []
    for left_side, right_side in (
        (normed_one, grad_queries),
        (around, grad_keys),
        (around, grad_values),
    ):
        keeps.append(dot(left_side[:, :half], right_side, TN).astype(BF16))
        sends.append(dot(left_side[:, half:], right_side, TN).astype(BF16))
    grad_query, grad_key, grad_value = scatter_group(keeps, sends, plane, mp)
    grad_first_gain = jnp.sum(grad_normed_one * hat_one, axis=0)
    grad_first_shift = jnp.sum(grad_normed_one, axis=0)
    grad_stream = grad_middle + norm_back(grad_normed_one, hat_one, factor_one, gain_one)
    grad_tokens = reorder(grad_stream.astype(BF16), inverse, 1)

    in_order = lambda v: jnp.take(v.reshape(dp, -1), inverse, axis=0).reshape(-1)
    in_turn = lambda v: jnp.take(v.reshape(mp, -1), turned, axis=0).reshape(-1)
    vector_grads = [
        in_order(v)
        for v in (
            grad_first_gain,
            grad_first_shift,
            grad_output_bias,
            grad_second_gain,
            grad_second_shift,
            grad_reduce_bias,
        )
    ] + [in_turn(grad_query_bias), in_turn(grad_value_bias), in_turn(grad_expand_bias[0])]
    narrow = jnp.stack(vector_grads[:8]).reshape(8, width // 128, 128).transpose(1, 0, 2)
    broad = vector_grads[8].reshape(full_hidden // 128, 1, 128)
    repeat = lambda a: jnp.broadcast_to(
        a[:, None], (a.shape[0], dp * mp // a.shape[0]) + a.shape[1:]
    ).reshape((dp * mp,) + a.shape[1:])
    sheets = jnp.concatenate(
        [repeat(narrow), repeat(broad), jnp.zeros((dp * mp, 7, 128), F32)], axis=1
    )
    (summed,) = spread(sheets, ((16, 128),), True, dp, mp, 2)
    taken = lambda stack, extent: lax.dynamic_slice_in_dim(
        stack, me % (128 // extent) * extent, extent, 1
    )
    small = taken(summed[:8], single)
    outs = [small[i] for i in range(8)]
    return (
        activations,
        grad_tokens,
        grad_query,
        grad_key,
        grad_value,
        grad_out.T,
        grad_expand,
        grad_reduce.T,
        outs[0],
        outs[1],
        outs[6],
        outs[7],
        outs[2],
        outs[3],
        outs[4],
        taken(summed[8:9], wide)[0],
        outs[5],
    )


def solution(mesh):
    vector = P(("dp", "mp"))
    tall = P(("dp", "mp"), None)
    in_specs = (
        tall,
        vector,
        P("dp", None),
        vector,
        vector,
        P(None, "mp"),
        P(None, "mp"),
        P(None, "mp"),
        vector,
        vector,
        P("mp", None),
        vector,
        vector,
        vector,
        P(None, "mp"),
        vector,
        P("mp", None),
        vector,
        tall,
    )
    out_specs = (
        tall,
        tall,
        P("dp", "mp"),
        P("dp", "mp"),
        P("dp", "mp"),
        P("mp", "dp"),
        P("dp", "mp"),
        P("mp", "dp"),
    ) + (vector,) * 9
    return jax.shard_map(local, mesh=mesh, in_specs=in_specs, out_specs=out_specs, check_vma=False)
```

```python
import functools
import math

import jax
import jax.numpy as jnp
import numpy as np
from jax import lax
from jax.experimental import pallas as pl
from jax.experimental.pallas import tpu as pltpu
from jax.sharding import PartitionSpec as P

HEAD_SIZE = 64
LONGEST = 549
EPSILON = 1e-06
TILE = 256
MIB = 1024 * 1024
F32 = jnp.float32
BF16 = jnp.bfloat16

NN = (((1,), (0,)), ((), ()))
NT = (((1,), (1,)), ((), ()))
TN = (((0,), (0,)), ((), ()))


def dot(left, right, dims=NN):
    return lax.dot_general(left, right, dims, preferred_element_type=F32)


def position_lines(extent):
    quarter = extent // 4
    spatial = (extent - quarter) // 2
    table = np.zeros((128, extent), np.float32)
    at, first = 0, 0
    for count, part in ((8, quarter), (14, spatial), (14, spatial)):
        half = part // 2
        inverse = np.exp(np.arange(half, dtype=np.float32) * np.float32(-math.log(10000.0) / half))
        angles = np.arange(count, dtype=np.float32)[:, None] * inverse[None, :]
        table[first : first + count, at : at + half] = np.sin(angles)
        table[first : first + count, at + half : at + part] = np.cos(angles)
        at, first = at + part, first + count
    return table


def norm_parts(values):
    center = values - jnp.mean(values, axis=-1, keepdims=True)
    spread = jnp.mean(center * center, axis=-1, keepdims=True)
    factor = lax.rsqrt(spread + EPSILON)
    return center * factor, factor


def norm_back(upstream, hat, factor, gain):
    scaled = upstream * gain
    first = jnp.mean(scaled, axis=-1, keepdims=True)
    second = jnp.mean(scaled * hat, axis=-1, keepdims=True)
    return factor * (scaled - first - hat * second)


def forward_kernel(bounds_ref, q_ref, k_ref, v_ref, lq_ref, lk_ref, o_ref, lse_ref, s_ref):
    rows = q_ref.shape[0]
    lane = lax.broadcasted_iota(jnp.int32, (TILE, 2 * HEAD_SIZE), 1)
    for block in range(rows // TILE):
        low = bounds_ref[2 * block]
        high = bounds_ref[2 * block + 1]
        span = slice(block * TILE, (block + 1) * TILE)
        query = q_ref[span, :]
        heads = [
            jnp.where(lane < HEAD_SIZE, query, jnp.zeros_like(query)),
            jnp.where(lane < HEAD_SIZE, jnp.zeros_like(query), query),
        ]
        label = lq_ref[span, :]
        label = jnp.concatenate([label, label], axis=1)

        def scores(t, carry):
            at = pl.multiple_of(t * TILE, TILE)
            key = k_ref[pl.ds(at, TILE), :]
            same = label == lk_ref[0:1, pl.ds(at, TILE)]
            out = []
            for h in range(2):
                s = jnp.where(same, dot(heads[h], key, NT), -1e30)
                s_ref[h, :, pl.ds(at, TILE)] = s
                out.append(jnp.maximum(carry[h], jnp.maximum(s[:, :128], s[:, 128:])))
            return tuple(out)

        least = jnp.full((TILE, 128), -1e30, F32)
        peaks = lax.fori_loop(low, high, scores, (least, least))
        peaks = [jnp.max(item, axis=1, keepdims=True) for item in peaks]

        def blend(t, carry):
            at = pl.multiple_of(t * TILE, TILE)
            value = v_ref[pl.ds(at, TILE), :]
            out = []
            for h in range(2):
                total, acc = carry[h]
                p = jnp.exp(s_ref[h, :, pl.ds(at, TILE)] - peaks[h])
                out.append((total + (p[:, :128] + p[:, 128:]), acc + dot(p.astype(BF16), value)))
            return tuple(out)

        zero = jnp.zeros((TILE, 128), F32)
        done = lax.fori_loop(low, high, blend, ((zero, zero), (zero, zero)))
        pieces = []
        for h in range(2):
            total = jnp.sum(done[h][0], axis=1, keepdims=True)
            pieces.append(done[h][1] / total)
            lse = jnp.broadcast_to(peaks[h] + jnp.log(total), (TILE, 128))
            lse_ref[0, h : h + 1, span] = lse.T[0:1, :]
        o_ref[span, :] = jnp.where(lane < HEAD_SIZE, pieces[0], pieces[1]).astype(BF16)


def backward_kernel(
    bounds_ref,
    q_ref,
    k_ref,
    v_ref,
    do_ref,
    o_ref,
    lse_ref,
    lq_ref,
    lk_ref,
    dq_ref,
    dk_ref,
    dv_ref,
    dk_acc,
    dv_acc,
):
    rows = q_ref.shape[0]
    lane = lax.broadcasted_iota(jnp.int32, (TILE, 2 * HEAD_SIZE), 1)
    row = lax.broadcasted_iota(jnp.int32, (2 * HEAD_SIZE, TILE), 0)
    dk_acc[...] = jnp.zeros_like(dk_acc)
    dv_acc[...] = jnp.zeros_like(dv_acc)

    def halves(array, where):
        zero = jnp.zeros_like(array)
        return [jnp.where(where < HEAD_SIZE, array, zero), jnp.where(where < HEAD_SIZE, zero, array)]

    for block in range(rows // TILE):
        low = bounds_ref[2 * block]
        high = bounds_ref[2 * block + 1]
        span = slice(block * TILE, (block + 1) * TILE)
        query, grad = q_ref[span, :], do_ref[span, :]
        query_t, grad_t = query.T, grad.T
        product = grad_t.astype(F32) * o_ref[span, :].T.astype(F32)
        deltas = [
            jnp.sum(product[h * HEAD_SIZE : (h + 1) * HEAD_SIZE], axis=0, keepdims=True)
            for h in range(2)
        ]
        lses = [lse_ref[0, h : h + 1, span] for h in range(2)]
        query_h, grad_h = halves(query, lane), halves(grad, lane)
        query_th, grad_th = halves(query_t, row), halves(grad_t, row)
        label = lq_ref[0:1, span]

        def step(t, carry):
            at = pl.multiple_of(t * TILE, TILE)
            key, value = k_ref[pl.ds(at, TILE), :], v_ref[pl.ds(at, TILE), :]
            key_t = key.T
            same = lk_ref[pl.ds(at, TILE), :]
            same = jnp.concatenate([same, same], axis=1) == label
            out, grad_k, grad_v = [], None, None
            for h in range(2):
                s = dot(key, query_th[h])
                p = jnp.where(same, jnp.exp(s - lses[h]), 0.0)
                dp = dot(value, grad_th[h])
                ds = (p * (dp - deltas[h])).astype(BF16)
                part_v = dot(p.astype(BF16), grad_h[h])
                part_k = dot(ds, query_h[h])
                grad_v = part_v if grad_v is None else grad_v + part_v
                grad_k = part_k if grad_k is None else grad_k + part_k
                out.append(carry[h] + dot(key_t[h * HEAD_SIZE : (h + 1) * HEAD_SIZE], ds))
            dk_acc[pl.ds(at, TILE), :] += grad_k
            dv_acc[pl.ds(at, TILE), :] += grad_v
            return tuple(out)

        zero = jnp.zeros((HEAD_SIZE, TILE), F32)
        parts = lax.fori_loop(low, high, step, (zero, zero))
        total = jnp.concatenate(parts, axis=0) * (1.0 / math.sqrt(HEAD_SIZE))
        dq_ref[span, :] = total.T.astype(BF16)
    dk_ref[...] = dk_acc[...].astype(BF16)
    dv_ref[...] = dv_acc[...].astype(BF16)


def attention_forward(bounds, queries, keys, values, label_q, label_k):
    rows, width = queries.shape
    window = keys.shape[0]
    pairs = width // (2 * HEAD_SIZE)
    column = lambda extent: pl.BlockSpec((extent, 2 * HEAD_SIZE), lambda p, b: (0, p))
    fixed = lambda shape: pl.BlockSpec(shape, lambda p, b: (0, 0))
    return pl.pallas_call(
        forward_kernel,
        grid_spec=pltpu.PrefetchScalarGridSpec(
            num_scalar_prefetch=1,
            grid=(pairs,),
            in_specs=[
                column(rows),
                column(window),
                column(window),
                fixed((rows, 128)),
                fixed((8, window)),
            ],
            out_specs=[column(rows), pl.BlockSpec((1, 2, rows), lambda p, b: (p, 0, 0))],
            scratch_shapes=[pltpu.VMEM((2, TILE, window), F32)],
        ),
        out_shape=[
            jax.ShapeDtypeStruct((rows, width), BF16),
            jax.ShapeDtypeStruct((pairs, 2, rows), F32),
        ],
        compiler_params=pltpu.CompilerParams(vmem_limit_bytes=32 * MIB),
        cost_estimate=pl.CostEstimate(
            flops=40 * rows * window * width, bytes_accessed=4 * window * width, transcendentals=0
        ),
        name="attention_forward",
    )(bounds, queries, keys, values, label_q, label_k)


def attention_backward(bounds, queries, keys, values, grads, attended, lse, label_q, label_k):
    rows, width = queries.shape
    window = keys.shape[0]
    pairs = width // (2 * HEAD_SIZE)
    column = lambda extent: pl.BlockSpec((extent, 2 * HEAD_SIZE), lambda p, b: (0, p))
    fixed = lambda shape: pl.BlockSpec(shape, lambda p, b: (0, 0))
    return pl.pallas_call(
        backward_kernel,
        grid_spec=pltpu.PrefetchScalarGridSpec(
            num_scalar_prefetch=1,
            grid=(pairs,),
            in_specs=[
                column(rows),
                column(window),
                column(window),
                column(rows),
                column(rows),
                pl.BlockSpec((1, 2, rows), lambda p, b: (p, 0, 0)),
                fixed((8, rows)),
                fixed((window, 128)),
            ],
            out_specs=[column(rows), column(window), column(window)],
            scratch_shapes=[
                pltpu.VMEM((window, 2 * HEAD_SIZE), F32),
                pltpu.VMEM((window, 2 * HEAD_SIZE), F32),
            ],
        ),
        out_shape=[
            jax.ShapeDtypeStruct((rows, width), BF16),
            jax.ShapeDtypeStruct((window, width), BF16),
            jax.ShapeDtypeStruct((window, width), BF16),
        ],
        compiler_params=pltpu.CompilerParams(vmem_limit_bytes=32 * MIB),
        cost_estimate=pl.CostEstimate(
            flops=48 * rows * window * width, bytes_accessed=8 * window * width, transcendentals=0
        ),
        name="attention_backward",
    )(bounds, queries, keys, values, grads, attended, lse, label_q, label_k)


def assemble(target, buffers, meta, block, first=0):
    each = buffers[0].shape[0] // block
    span = slice(first, first + buffers[0].shape[1])
    for i in range(len(buffers) * each):
        at = pl.multiple_of(meta[1 + i] * block, block)
        source = buffers[i // each]
        target[pl.ds(at, block), span] = source[i % each * block : (i % each + 1) * block, :]


def turn(target, source, meta, block, lead):
    lead[...] = source.T
    for i in range(target.shape[0] // block):
        at = pl.multiple_of(meta[1 + i] * block, block)
        target[i * block : (i + 1) * block, :] = lead[pl.ds(at, block), :]


def fixed(shape):
    return pl.BlockSpec(shape, lambda *_: (0,) * len(shape), pipeline_mode=pl.Buffered(1))


def call(kernel, name, grid, meta, ins, outs, scratch, vmem, flops, moved=0):
    return pl.pallas_call(
        kernel,
        grid_spec=pltpu.PrefetchScalarGridSpec(
            num_scalar_prefetch=1,
            grid=grid,
            in_specs=[spec for _, spec in ins],
            out_specs=[spec for _, _, spec in outs],
            scratch_shapes=scratch,
        ),
        out_shape=[jax.ShapeDtypeStruct(shape, kind) for shape, kind, _ in outs],
        compiler_params=pltpu.CompilerParams(vmem_limit_bytes=vmem * MIB),
        cost_estimate=pl.CostEstimate(flops=flops, bytes_accessed=moved, transcendentals=0),
        name=name,
    )(meta, *[array for array, _ in ins])


def turn_kernel(block, meta, source, target, lead):
    turn(target, source[...], meta, block, lead)


def turned_rows(source, meta, block):
    rows, width = source.shape
    return call(
        functools.partial(turn_kernel, block),
        "turn",
        (1,),
        meta,
        [(source, fixed(source.shape))],
        [((width, rows), BF16, fixed((width, rows)))],
        [pltpu.VMEM((width, rows), BF16)],
        24,
        4 * 10**9,
    )[0]


def project_kernel(block, scale, own, meta, x, around, bias, *refs):
    weights, (q, k, v), scratch = refs[:-6], refs[-6:-3], refs[-3:]
    if own:
        scratch = weights
    else:
        for w in range(3):
            assemble(scratch[w], weights[4 * w : 4 * w + 4], meta, block)
    q[...] = (dot(x[...], scratch[0][...]) + bias[6:7, :]).astype(BF16) * jnp.asarray(scale, BF16)
    k[...] = dot(around[...], scratch[1][...]).astype(BF16)
    v[...] = (dot(around[...], scratch[2][...]) + bias[7:8, :]).astype(BF16)


def gathered_specs(buffers, kinds, extent, stride):
    return [
        (item, pl.BlockSpec((item.shape[0], extent), lambda i, m, kind=kind: (0, i * stride + kind)))
        for kind in kinds
        for item in buffers
    ]


def project(x, around, weights, narrow, meta, block, mp, own):
    rows, width = x.shape
    window = around.shape[0]
    extent = width // mp
    first, count = (0, 1) if own else (1, mp - 1)
    column = lambda n: pl.BlockSpec((n, extent), lambda i, m: (0, i))
    turned = lambda i, m: (0, lax.rem(m[0] - first - i + mp, mp))
    return call(
        functools.partial(project_kernel, block, 1.0 / math.sqrt(HEAD_SIZE), own),
        "project",
        (count,),
        meta,
        [
            (x, fixed(x.shape)),
            (around, fixed(around.shape)),
            (narrow, pl.BlockSpec((8, extent), turned)),
        ]
        + (
            [(w, fixed(w.shape)) for w in weights]
            if own
            else gathered_specs(weights, (0, 1, 2), extent, 4)
        ),
        [
            ((rows, count * extent), BF16, column(rows)),
            ((window, count * extent), BF16, column(window)),
            ((window, count * extent), BF16, column(window)),
        ],
        [pltpu.VMEM((width, extent), BF16)] * 3,
        40,
        count * 4 * 10**9,
    )


def output_weight_rows(target, own, got, meta, block, mp):
    extent = own.shape[0]
    target[:, :extent] = own[...].T
    for r in range(1, mp):
        assemble(target, got[4 * (r - 1) : 4 * r], meta, block, r * extent)


def enter_kernel(block, mp, meta, stream, near, far, vectors, own, *refs):
    got = refs[: 4 * (mp - 1)]
    middle, normed, normed_t, weight, lead = refs[4 * (mp - 1) :]
    output_weight_rows(weight, own, got, meta, block, mp)
    cut = near.shape[1]
    mixed = dot(near[...], weight[:, :cut], NT) + dot(far[...], weight[:, cut:], NT)
    mid = stream[...] + mixed + vectors[2:3, :]
    middle[...] = mid
    hat, _ = norm_parts(mid)
    out = (hat * vectors[3:4, :] + vectors[4:5, :]).astype(BF16)
    normed[...] = out
    turn(normed_t, out, meta, block, lead)


def output_specs(buffers, mp, extent):
    return [
        (
            item,
            pl.BlockSpec(
                (item.shape[0], extent),
                lambda i, m, r=r: (0, (r - 1) * 4 + 3),
                pipeline_mode=pl.Buffered(1),
            ),
        )
        for r in range(1, mp)
        for item in buffers
    ]


def enter(stream, attended, narrow, weight, buffers, meta, block, mp):
    rows, width = stream.shape
    extent = weight.shape[0]
    return call(
        functools.partial(enter_kernel, block, mp),
        "enter",
        (1,),
        meta,
        [
            (stream, fixed(stream.shape)),
            (attended[0], fixed(attended[0].shape)),
            (attended[1], fixed(attended[1].shape)),
            (narrow, fixed(narrow.shape)),
            (weight, fixed(weight.shape)),
        ]
        + output_specs(buffers, mp, extent),
        [
            ((rows, width), F32, fixed((rows, width))),
            ((rows, width), BF16, fixed((rows, width))),
            ((width, rows), BF16, fixed((width, rows))),
        ],
        [
            pltpu.VMEM((width, width), BF16),
            pltpu.VMEM((width, rows), BF16),
        ],
        40,
        8 * 10**9,
    )


def feed_kernel(block, per, has_own, meta, x, g, x_t, g_t, bias, *refs):
    if has_own:
        own_e, own_r, refs = refs[0], refs[1], refs[2:]
    else:
        before, refs = refs[:2], refs[2:]
    got_e, got_r = refs[:4], refs[4:8]
    out_ref, dx_ref, keep, send, db_ref, weight_e, weight_r = refs[8:]
    step = pl.program_id(0)

    def gathered():
        assemble(weight_e, got_e, meta, block)
        assemble(weight_r, got_r, meta, block)

    if has_own:

        @pl.when(step < per)
        def _():
            weight_e[...] = own_e[...]
            weight_r[...] = own_r[...].T

        pl.when(step >= per)(gathered)
    else:
        gathered()

    pre = dot(x[...], weight_e[...]) + bias[0:1, :]
    cumulative = 0.5 * (1.0 + lax.erf(pre * 0.7071067811865476))
    hidden = (pre * cumulative).astype(BF16)
    slope = cumulative + pre * jnp.exp(-0.5 * pre * pre) * (1.0 / math.sqrt(2.0 * math.pi))
    grad_pre = (dot(g[...], weight_r[...]) * slope).astype(BF16)
    db_ref[...] = jnp.broadcast_to(
        jnp.sum(grad_pre.astype(F32), axis=0, keepdims=True), db_ref.shape
    )
    half, tile = x_t.shape[0] // 2, pre.shape[1]
    keep[:, tile:] = dot(g_t[:half, :], hidden).astype(BF16)
    send[:, tile:] = dot(g_t[half:, :], hidden).astype(BF16)
    keep[:, :tile] = dot(x_t[:half, :], grad_pre).astype(BF16)
    send[:, :tile] = dot(x_t[half:, :], grad_pre).astype(BF16)
    out = dot(hidden, weight_r[...], NT)
    back = dot(grad_pre, weight_e[...], NT)

    @pl.when(step == 0)
    def _():
        out_ref[...] = out if has_own else before[0][...] + out
        dx_ref[...] = back if has_own else before[1][...] + back

    @pl.when(step > 0)
    def _():
        out_ref[...] += out
        dx_ref[...] += back


def feed(x, g, x_t, g_t, broad, own, before, buffers, meta, block, mp, first, count):
    rows, width = x.shape
    extent = broad.shape[1] // mp
    tile = min(512, extent)
    per = extent // tile
    half = width // 2
    skip = per if own else 0
    shard = lambda i: first + lax.div(i, per)

    def columns(kind):
        def at(i, m):
            j = jnp.maximum(i - skip, 0)
            return (0, lax.div(j, per) * 2 * per + kind * per + lax.rem(j, per))

        return at

    pieces = [
        (item, pl.BlockSpec((item.shape[0], tile), columns(kind)))
        for kind in range(2)
        for item in buffers
    ]
    if own:
        last = per - 1
        extra = [
            (own[0], pl.BlockSpec((width, tile), lambda i, m: (0, jnp.minimum(i, last)))),
            (own[1], pl.BlockSpec((tile, width), lambda i, m: (jnp.minimum(i, last), 0))),
        ]
    else:
        extra = [(item, fixed(item.shape)) for item in before]
    bias = lambda i, m: (0, lax.rem(m[0] - shard(i) + mp, mp) * per + lax.rem(i, per))
    total = count * extent
    return call(
        functools.partial(feed_kernel, block, per, bool(own)),
        "feed",
        (count * per,),
        meta,
        [
            (x, fixed(x.shape)),
            (g, fixed(g.shape)),
            (x_t, fixed(x_t.shape)),
            (g_t, fixed(g_t.shape)),
            (broad, pl.BlockSpec((8, tile), bias)),
        ]
        + extra
        + pieces,
        [
            ((rows, width), F32, fixed((rows, width))),
            ((rows, width), F32, fixed((rows, width))),
            ((half, 2 * total), BF16, pl.BlockSpec((half, 2 * tile), lambda i, m: (0, i))),
            ((half, 2 * total), BF16, pl.BlockSpec((half, 2 * tile), lambda i, m: (0, i))),
            ((8, total), F32, pl.BlockSpec((8, tile), lambda i, m: (0, i))),
        ],
        [pltpu.VMEM((width, tile), BF16)] * 2,
        48,
        20 * 10**9,
    )


def leave_kernel(block, mp, meta, middle, branch, upstream, g, vectors, own, *refs):
    got = refs[: 4 * (mp - 1)]
    act, grad_mid, branch_t, near, far, sums, weight, lead = refs[4 * (mp - 1) :]
    output_weight_rows(weight, own, got, meta, block, mp)
    mid, dy, grad = middle[...], upstream[...], g[...].astype(F32)
    act[...] = (mid + branch[...] + vectors[5:6, :]).astype(BF16)
    hat, factor = norm_parts(mid)
    back = grad + norm_back(dy, hat, factor, vectors[3:4, :])
    grad_mid[...] = back
    rounded = back.astype(BF16)
    turn(branch_t, rounded, meta, block, lead)
    cut = near.shape[1]
    near[...] = dot(rounded, weight[:, :cut]).astype(BF16)
    far[...] = dot(rounded, weight[:, cut:]).astype(BF16)
    add = lambda v: jnp.sum(v, axis=0, keepdims=True)
    zero = jnp.zeros((4, mid.shape[1]), F32)
    sums[...] = jnp.concatenate([add(back), add(dy * hat), add(dy), add(grad), zero], axis=0)


def leave(middle, branch, upstream, g, narrow, weight, buffers, meta, block, mp):
    rows, width = middle.shape
    extent = weight.shape[0]
    whole = lambda kind: ((rows, width), kind, fixed((rows, width)))
    return call(
        functools.partial(leave_kernel, block, mp),
        "leave",
        (1,),
        meta,
        [(item, fixed(item.shape)) for item in (middle, branch, upstream, g, narrow, weight)]
        + output_specs(buffers, mp, extent),
        [
            whole(BF16),
            whole(F32),
            ((width, rows), BF16, fixed((width, rows))),
            ((rows, extent), BF16, fixed((rows, extent))),
            ((rows, width - extent), BF16, fixed((rows, width - extent))),
            ((8, width), F32, fixed((8, width))),
        ],
        [pltpu.VMEM((width, width), BF16), pltpu.VMEM((width, rows), BF16)],
        48,
        10 * 10**9,
    )


def tail_kernel(block, margin, meta, around_t, branch_t, dq, dk, dv, att, *refs):
    got, (own_out, around_out, keep, send, bias), weights = refs[:12], refs[12:17], refs[17:]
    for w in range(3):
        assemble(weights[w], got[4 * w : 4 * w + 4], meta, block)
    step = pl.program_id(0)
    rows, half, extent = dq.shape[0], keep.shape[0], dq.shape[1]
    back = dot(dk[...], weights[1][...], NT) + dot(dv[...], weights[2][...], NT)
    more = dot(dq[...], weights[0][...], NT)

    @pl.when(step == 0)
    def _():
        around_out[...] = back
        own_out[...] = more

    @pl.when(step > 0)
    def _():
        around_out[...] += back
        own_out[...] += more

    middle, everything = slice(margin, margin + rows), slice(None)
    for at, (left, span, right) in enumerate(
        (
            (around_t, middle, dq),
            (around_t, everything, dk),
            (around_t, everything, dv),
            (branch_t, everything, att),
        )
    ):
        columns = slice(at * extent, (at + 1) * extent)
        keep[:, columns] = dot(left[:half, span], right[...]).astype(BF16)
        send[:, columns] = dot(left[half:, span], right[...]).astype(BF16)
    add = lambda v: jnp.sum(v[...].astype(F32), axis=0, keepdims=True)
    bias[...] = jnp.concatenate([add(dq), add(dv), jnp.zeros((6, extent), F32)], axis=0)


def tail(around_t, branch_t, grads, att, weights, meta, block, mp, margin):
    dq, dk, dv = grads
    rows, width = dq.shape[0], around_t.shape[0]
    window = around_t.shape[1]
    extent = width // mp
    half = width // 2
    count = mp - 1
    column = lambda n: pl.BlockSpec((n, extent), lambda i, m: (0, i))
    wide = pl.BlockSpec((half, 4 * extent), lambda i, m: (0, i))
    return call(
        functools.partial(tail_kernel, block, margin),
        "tail",
        (count,),
        meta,
        [(item, fixed(item.shape)) for item in (around_t, branch_t)]
        + [(dq, column(rows)), (dk, column(window)), (dv, column(window)), (att, column(rows))]
        + gathered_specs(weights, (0, 1, 2), extent, 4),
        [
            ((rows, width), F32, fixed((rows, width))),
            ((window, width), F32, fixed((window, width))),
            ((half, 4 * count * extent), BF16, wide),
            ((half, 4 * count * extent), BF16, wide),
            ((8, count * extent), F32, column(8)),
        ],
        [pltpu.VMEM((width, extent), BF16)] * 3,
        60,
        count * 8 * 10**9,
    )


def join(parts, axis):
    return jnp.concatenate(parts, axis=axis)


class Plane:
    def __init__(self, size):
        self.size = size
        bits = list(range(1, size.bit_length() - 1))
        turn = len(bits) // 2
        self.orders = [bits, bits[turn:] + bits[:turn]]
        held = []
        for order in self.orders:
            masks = [0]
            for bit in order:
                masks = masks + [m ^ (1 << bit) for m in masks]
            held.append(masks)
        self.masks = [held[c] + [1 ^ m for m in held[1 - c]] for c in range(2)]
        self.steps = len(bits)

    def pairs(self, step):
        return [(i, i ^ (1 << self.orders[i % 2][step])) for i in range(self.size)]

    def siblings(self):
        return [(i, i ^ 1) for i in range(self.size)]

    def order(self, d):
        return jnp.bitwise_xor(jnp.array(self.masks, jnp.int32)[d % 2], d)


def gather_group(payloads, shifts, plane, mp):
    got = [lax.ppermute(payloads, "mp", [(i, (i + r) % mp) for i in range(mp)]) for r in shifts]
    held = join(got, 1) if len(got) > 1 else got[0]
    for step in range(plane.steps - 1):
        held = join([held, lax.ppermute(held, "dp", plane.pairs(step))], 0)
    parts = [held, lax.ppermute(held, "dp", plane.pairs(plane.steps - 1))]
    return parts + [lax.ppermute(part, "dp", plane.siblings()) for part in parts]


def added(left, right):
    return (left.astype(F32) + right.astype(F32)).astype(BF16)


def after(value, *others):
    return lax.optimization_barrier((value,) + others)[0]


class Scatter:
    def __init__(self, keep, send, shifts, plane, mp):
        self.keep, self.shifts, self.plane, self.mp = keep, shifts, plane, mp
        self.step = plane.steps
        self.got = lax.ppermute(send, "dp", plane.siblings())

    def fold(self):
        half = self.keep.shape[0] // 2
        upper = added(self.keep[half:], self.got[half:])
        self.keep = added(self.keep[:half], self.got[:half])
        return upper

    def next(self):
        self.step -= 1
        self.got = lax.ppermute(self.fold(), "dp", self.plane.pairs(self.step))
        return self

    def last(self):
        while self.step > 0:
            self.next()
        extent = self.keep.shape[1] // len(self.shifts)
        self.own, self.moved = None, []
        for i, r in enumerate(self.shifts):
            span = slice(i * extent, (i + 1) * extent)
            keep, got = self.keep[:, span], self.got[:, span]
            if r == 0:
                self.own = keep.astype(F32) + got.astype(F32)
            else:
                pairs = [(j, (j - r) % self.mp) for j in range(self.mp)]
                self.moved.append(lax.ppermute(added(keep, got), "mp", pairs))
        return self


MESH = pl.DeviceIdType.MESH


def flipped(d, bit):
    return d + (1 - 2 * lax.rem(lax.div(d, 1 << bit), 2)) * (1 << bit)


def meet(d, z, dp, mp):
    barrier = pltpu.get_barrier_semaphore()
    for step in range(1, dp):
        there = (lax.rem(d + step, dp), z)
        pl.semaphore_signal(barrier, inc=1, device_id=there, device_id_type=MESH)
    for step in range(1, mp):
        there = (d, lax.rem(z + step, mp))
        pl.semaphore_signal(barrier, inc=1, device_id=there, device_id_type=MESH)
    pl.semaphore_wait(barrier, dp + mp - 2)


def remote(source, target, send_sem, recv_sem, device):
    return pltpu.make_async_remote_copy(
        src_ref=source,
        dst_ref=target,
        send_sem=send_sem,
        recv_sem=recv_sem,
        device_id=device,
        device_id_type=MESH,
    )


def peers_start(source, slots, send_sem, recv_sem, along, me, extent, each):
    copies = []
    for step in range(1, extent):
        place = lax.rem(me + step, extent)
        copies.append(
            remote(
                source.at[place if each else 0],
                slots.at[me],
                send_sem.at[step],
                recv_sem.at[me],
                along(step),
            )
        )
        copies[-1].start()
    slots[me] = source[me if each else 0]
    return copies


def peers_finish(copies, slots, recv_sem, me, extent):
    for step in range(1, extent):
        copies[step - 1].wait_send()
        sender = lax.rem(me + step, extent)
        pltpu.make_async_copy(slots.at[sender], slots.at[sender], recv_sem.at[sender]).wait()


def begin_kernel(plane, mp, hops, margin, *refs):
    (sheet, payload, tokens, index, table), refs = refs[:5], refs[5:]
    (narrow, broad, stream, around), buffers, refs = refs[:4], refs[4:8], refs[8:]
    (middle, first, second, normed, zeros), refs = refs[:5], refs[5:]
    send_one, recv_one, send_two, recv_two, refs = *refs[:4], refs[4:]
    z_send, z_recv, chip_send, chip_recv, core_send, core_recv, halo_send, halo_recv, local = refs
    dp = plane.size
    d, z = lax.axis_index("dp"), lax.axis_index("mp")
    core = lax.rem(d, 2)
    rows, width = tokens.shape
    block, columns = payload.shape
    along_dp = lambda step: (lax.rem(d + step, dp), z)
    along_mp = lambda step: (d, lax.rem(z + step, mp))
    zeros[...] = jnp.zeros_like(zeros)
    meet(d, z, dp, mp)
    vectors = peers_start(sheet, first, send_one, recv_one, along_mp, z, mp, False)

    each = dp // 4

    def place(j, r, other=False):
        return buffers[j // each + (2 if other else 0)].at[
            pl.ds(j % each * block, block), pl.ds((r - 1) * columns, columns)
        ]

    shards = [
        remote(payload, place(0, r), z_send.at[r], z_recv.at[r], along_mp(r)) for r in range(1, mp)
    ]
    for copy in shards:
        copy.start()

    count = lax.broadcasted_iota(jnp.int32, index.shape, 1)
    kept = index[...]
    coarse = lax.div(kept, 14)
    frame = lax.div(kept, 196)
    across = coarse - frame * 14
    line = kept - coarse * 14
    hot = ((count == frame) | (count == across + 8) | (count == line + 22)).astype(F32)
    hidden = tokens[...].astype(F32) + lax.dot_general(
        hot, table[...], NN, precision=lax.Precision.HIGHEST, preferred_element_type=F32
    )
    stream[...] = hidden

    peers_finish(vectors, first, recv_one, z, mp)
    middle[0] = jnp.sum(first[...], axis=0)
    vectors = peers_start(middle, second, send_two, recv_two, along_dp, d, dp, False)
    hat, _ = norm_parts(hidden)
    peers_finish(vectors, second, recv_two, d, dp)
    share = dp // (width // 128)
    for c in range(width // 128):
        narrow[:, c * 128 : (c + 1) * 128] = jnp.sum(
            second[c * share : (c + 1) * share, 0:8, :], axis=0
        )
    lines = broad.shape[1] // 128
    per = lines // dp
    for c in range(lines):
        row = second[c // per, 8 + c % per : 9 + c % per, :]
        broad[:, c * 128 : (c + 1) * 128] = jnp.broadcast_to(row, (8, 128))
    normed[...] = (hat * narrow[0:1, :] + narrow[1:2, :]).astype(BF16)

    waits, at_left, at_right = [], margin, margin + rows
    inside = pltpu.make_async_copy(
        normed, around.at[pl.ds(margin, rows), :], local.at[0]
    )
    inside.start()
    waits.append((None, inside.wait))
    for hop, extent in enumerate(hops, 1):
        left = around.at[pl.ds(at_left - extent, extent), :]
        right = around.at[pl.ds(at_right, extent), :]
        sides = (
            (left, normed.at[pl.ds(rows - extent, extent), :], z + hop, z - hop, 2 * hop - 2),
            (right, normed.at[pl.ds(0, extent), :], z - hop, z + hop, 2 * hop - 1),
        )
        for target, source, there, back, n in sides:
            goes = (there >= 0) & (there < mp)
            comes = (back >= 0) & (back < mp)
            copy = remote(source, target, halo_send.at[n], halo_recv.at[n], (d, there))
            blank = pltpu.make_async_copy(zeros.at[pl.ds(0, extent), :], target, local.at[1 + n])
            pl.when(goes)(copy.start)
            pl.when(jnp.logical_not(comes))(blank.start)
            waits.append((goes, copy.wait_send))
            waits.append((comes, copy.wait_recv))
            waits.append((jnp.logical_not(comes), blank.wait))
        at_left, at_right = at_left - extent, at_right + extent
    if at_left:
        for n, at in enumerate((0, at_right)):
            blank = pltpu.make_async_copy(
                zeros.at[pl.ds(0, at_left), :],
                around.at[pl.ds(at, at_left), :],
                local.at[1 + 2 * len(hops) + n],
            )
            blank.start()
            waits.append((None, blank.wait))

    sent = []

    def forward(j, r):
        for step in range(plane.steps):
            if j < 1 << step:
                there = (1 - core) * flipped(d, plane.orders[0][step]) + core * flipped(
                    d, plane.orders[1][step]
                )
                to = (1 << step) + j
                copy = remote(
                    place(j, r),
                    place(to, r),
                    chip_send.at[r, to],
                    chip_recv.at[r, to],
                    (there, z),
                )
                copy.start()
                sent.append(copy)
        copy = remote(
            place(j, r), place(j, r, True), core_send.at[r, j], core_recv.at[r, j], (flipped(d, 0), z)
        )
        copy.start()
        sent.append(copy)

    for r in range(1, mp):
        shards[r - 1].wait_recv()
        forward(0, r)
    for j in range(1, 1 << plane.steps):
        for r in range(1, mp):
            pltpu.make_async_copy(place(j, r), place(j, r), chip_recv.at[r, j]).wait()
            forward(j, r)
    for j in range(1 << plane.steps):
        for r in range(1, mp):
            pltpu.make_async_copy(place(j, r, True), place(j, r, True), core_recv.at[r, j]).wait()
    for copy in shards + sent:
        copy.wait_send()
    for when, wait in waits:
        wait() if when is None else pl.when(when)(wait)


def begin(sheet, payload, tokens, index, table, plane, mp, hops, margin, full_hidden):
    dp = plane.size
    rows, width = tokens.shape
    block, columns = payload.shape
    vmem, anywhere = pl.BlockSpec(memory_space=pltpu.VMEM), pl.BlockSpec(memory_space=pl.ANY)
    window = 2 * margin + rows
    dma = pltpu.SemaphoreType.DMA
    blocks = dp // 2
    return pl.pallas_call(
        functools.partial(begin_kernel, plane, mp, hops, margin),
        out_shape=[
            jax.ShapeDtypeStruct((8, width), F32),
            jax.ShapeDtypeStruct((8, full_hidden), F32),
            jax.ShapeDtypeStruct((rows, width), F32),
            jax.ShapeDtypeStruct((window, width), BF16),
        ]
        + [jax.ShapeDtypeStruct((width // 4, (mp - 1) * columns), BF16)] * 4,
        in_specs=[vmem] * 5,
        out_specs=[vmem] * 3 + [anywhere] * 5,
        scratch_shapes=[
            pltpu.VMEM((1, 16, 128), F32),
            pltpu.VMEM((mp, 16, 128), F32),
            pltpu.VMEM((dp, 16, 128), F32),
            pltpu.VMEM((rows, width), BF16),
            pltpu.VMEM((rows, width), BF16),
            dma((mp,)),
            dma((mp,)),
            dma((dp,)),
            dma((dp,)),
            dma((mp,)),
            dma((mp,)),
            dma((mp, blocks)),
            dma((mp, blocks)),
            dma((mp, blocks)),
            dma((mp, blocks)),
            dma((2 * len(hops),)),
            dma((2 * len(hops),)),
            dma((3 + 2 * len(hops),)),
        ],
        compiler_params=pltpu.CompilerParams(
            collective_id=1, has_side_effects=True, vmem_limit_bytes=40 * MIB
        ),
        cost_estimate=pl.CostEstimate(flops=4 * 10**10, bytes_accessed=0, transcendentals=0),
        name="begin",
    )(sheet, payload, tokens, index, table)


def finish_kernel(plane, mp, hops, margin, *refs):
    hbm, refs = refs[:17], refs[17:]
    upper, refs = refs[0], refs[1:]
    (grad_tokens, total, vectors), refs = refs[:3], refs[3:]
    loaded, refs = refs[:17], refs[17:]
    (halo_out, halo_in, keep, send, got, more_got, shards, table, sheets), refs = refs[:9], refs[9:]
    (middle, first, second), refs = refs[:3], refs[3:]
    load_sem, halo_send, halo_recv, core_sem, near_send, near_recv, far_send, far_recv = refs[:8]
    z_send, z_recv, send_one, recv_one, send_two, recv_two = refs[8:]
    (dq, dk, dv, att, wq, wk, wv, before_around, before_own) = loaded[:9]
    (around_t, branch_t, others, stream, grad_mid, narrow, early, broad) = loaded[9:]
    dp = plane.size
    d, z = lax.axis_index("dp"), lax.axis_index("mp")
    core = lax.rem(d, 2)
    rows, extent = dq.shape
    half = keep.shape[0]
    block = total.shape[0]
    columns = total.shape[1]
    left = sum(hops)

    loads = [
        pltpu.make_async_copy(source, target, load_sem.at[i])
        for i, (source, target) in enumerate(zip(hbm, loaded))
    ]
    for copy in loads:
        copy.start()
    halo_in[...] = jnp.zeros_like(halo_in)
    meet(d, z, dp, mp)

    def partner(step):
        there = (1 - core) * flipped(d, plane.orders[0][step]) + core * flipped(
            d, plane.orders[1][step]
        )
        return there, z

    top = half // 2
    far = remote(
        upper,
        more_got.at[pl.ds(0, top), :],
        far_send.at[plane.steps - 1],
        far_recv.at[plane.steps - 1],
        partner(plane.steps - 1),
    )
    far.start()
    sent = [far]

    for i in (1, 2, 5, 6, 7):
        loads[i].wait()
    waits, at_left, at_right, at = [], margin, margin + rows, 0
    copies = []
    for hop, reach in enumerate(hops, 1):
        sides = (
            (at_left - reach, z - hop, z + hop, 2 * hop - 2, rows - reach),
            (at_right, z + hop, z - hop, 2 * hop - 1, 0),
        )
        for start, there, back, n, place in sides:
            span = slice(start, start + reach)
            here = pl.ds(at, reach)
            part = dot(dk[span, :], wk[...], NT) + dot(dv[span, :], wv[...], NT)
            halo_out[here, :] = (before_around[span, :] + part).astype(BF16)
            goes = (there >= 0) & (there < mp)
            comes = (back >= 0) & (back < mp)
            copy = remote(
                halo_out.at[here, :],
                halo_in.at[here, :],
                halo_send.at[n],
                halo_recv.at[n],
                (d, there),
            )
            pl.when(goes)(copy.start)
            waits.append((goes, copy.wait_send))
            copies.append((comes, copy.wait_recv, place, at, reach))
            at += reach
        at_left, at_right = at_left - reach, at_right + reach

    for i in (0, 3, 9, 10):
        loads[i].wait()
    inner, everything = slice(margin, margin + rows), slice(None)

    def weight_grads(target, low):
        for n, (source, span, right) in enumerate(
            (
                (around_t, inner, dq),
                (around_t, everything, dk),
                (around_t, everything, dv),
                (branch_t, everything, att),
            )
        ):
            target[:, n * extent : (n + 1) * extent] = dot(
                source[low : low + half, span], right[...]
            ).astype(BF16)

    weight_grads(send, half)
    swap = remote(send, got.at[pl.ds(0, half), :], core_sem.at[0], core_sem.at[1], (flipped(d, 0), z))
    swap.start()
    sent.append(swap)
    weight_grads(keep, 0)

    def fold(target, source, at, count):
        target[:count, :] = added(target[:count, :], source[pl.ds(at, count), :])

    swap.wait_recv()
    fold(keep, got, 0, half)
    loads[4].wait()
    loads[8].wait()
    own = before_own[...] + before_around[inner, :] + dot(dq[...], wq[...], NT)
    own += dot(dk[inner, :], wk[...], NT) + dot(dv[inner, :], wv[...], NT)
    before_own[...] = own
    count, at_near, at_far = half, half, 0
    loads[11].wait()
    for step in reversed(range(plane.steps)):
        count //= 2
        near = remote(
            keep.at[pl.ds(count, count), :],
            got.at[pl.ds(at_near, count), :],
            near_send.at[step],
            near_recv.at[step],
            partner(step),
        )
        near.start()
        sent.append(near)
        far.wait_recv()
        fold(others, more_got, at_far, count)
        at_far += count
        if step:
            far = remote(
                others.at[pl.ds(count // 2, count // 2), :],
                more_got.at[pl.ds(at_far, count // 2), :],
                far_send.at[step - 1],
                far_recv.at[step - 1],
                partner(step - 1),
            )
            far.start()
            sent.append(far)
        near.wait_recv()
        fold(keep, got, at_near, count)
        at_near += count
    for r in range(1, mp):
        copy = remote(
            others.at[pl.ds(0, block), pl.ds((r - 1) * columns, columns)],
            shards.at[r],
            z_send.at[r],
            z_recv.at[r],
            (d, lax.rem(z - r + mp, mp)),
        )
        copy.start()
        sent.append(copy)

    for i in range(12, 17):
        loads[i].wait()
    for comes, wait, *_ in copies:
        pl.when(comes)(wait)
    for _, _, place, at, reach in copies:
        span = slice(place, place + reach)
        before_own[span, :] = before_own[span, :] + halo_in[at : at + reach, :].astype(F32)
    hat, factor = norm_parts(stream[...])
    upstream = before_own[...]
    add = lambda v: jnp.sum(v, axis=0, keepdims=True)
    back = grad_mid[...] + norm_back(upstream, hat, factor, narrow[0:1, :])
    grad_tokens[...] = back.astype(BF16)
    table[...] = early[...]
    table[0:1, :] = add(upstream * hat)
    table[1:2, :] = add(upstream)
    mine = pl.ds(pl.multiple_of(z * extent, extent), extent)
    table[6:7, mine] = add(dq[...].astype(F32))
    table[7:8, mine] = add(dv[...].astype(F32))
    each = dp // (early.shape[1] // 128)
    for i in range(dp):
        c = i // each
        sheets[i, 0:8, :] = table[:, c * 128 : (c + 1) * 128]
        sheets[i, 8:16, :] = broad[i]
    along_dp = lambda step: (lax.rem(d + step, dp), z)
    along_mp = lambda step: (d, lax.rem(z + step, mp))
    out = peers_start(sheets, second, send_two, recv_two, along_dp, d, dp, True)
    peers_finish(out, second, recv_two, d, dp)
    middle[0] = jnp.sum(second[...], axis=0)
    out = peers_start(middle, first, send_one, recv_one, along_mp, z, mp, False)

    full = keep[:block, :].astype(F32)
    for r in range(1, mp):
        pltpu.make_async_copy(shards.at[r], shards.at[r], z_recv.at[r]).wait()
        full += shards[r].astype(F32)
    total[...] = full
    peers_finish(out, first, recv_one, z, mp)
    vectors[...] = jnp.sum(first[...], axis=0)
    for copy in sent:
        copy.wait_send()
    for when, wait in waits:
        pl.when(when)(wait)


def finish(arrays, upper, plane, mp, hops, margin):
    dp = plane.size
    rows, extent = arrays[0].shape
    width = arrays[4].shape[0]
    block, half, columns = width // dp, width // 2, 4 * extent
    vmem, anywhere = pl.BlockSpec(memory_space=pltpu.VMEM), pl.BlockSpec(memory_space=pl.ANY)
    dma = pltpu.SemaphoreType.DMA
    left = sum(hops)
    return pl.pallas_call(
        functools.partial(finish_kernel, plane, mp, hops, margin),
        out_shape=[
            jax.ShapeDtypeStruct((rows, width), BF16),
            jax.ShapeDtypeStruct((block, columns), F32),
            jax.ShapeDtypeStruct((16, 128), F32),
        ],
        in_specs=[anywhere] * (len(arrays) + 1),
        out_specs=[vmem] * 3,
        scratch_shapes=[pltpu.VMEM(item.shape, item.dtype) for item in arrays]
        + [
            pltpu.VMEM((2 * left, width), BF16),
            pltpu.VMEM((2 * left, width), BF16),
            pltpu.VMEM((half, columns), BF16),
            pltpu.VMEM((half, columns), BF16),
            pltpu.VMEM((2 * half, columns), BF16),
            pltpu.VMEM((half, (mp - 1) * columns), BF16),
            pltpu.VMEM((mp, block, columns), BF16),
            pltpu.VMEM((8, width), F32),
            pltpu.VMEM((dp, 16, 128), F32),
            pltpu.VMEM((1, 16, 128), F32),
            pltpu.VMEM((mp, 16, 128), F32),
            pltpu.VMEM((dp, 16, 128), F32),
            dma((len(arrays),)),
            dma((2 * len(hops),)),
            dma((2 * len(hops),)),
            dma((2,)),
            dma((plane.steps,)),
            dma((plane.steps,)),
            dma((plane.steps,)),
            dma((plane.steps,)),
            dma((mp,)),
            dma((mp,)),
            dma((mp,)),
            dma((mp,)),
            dma((dp,)),
            dma((dp,)),
        ],
        compiler_params=pltpu.CompilerParams(
            collective_id=2, has_side_effects=True, vmem_limit_bytes=60 * MIB
        ),
        cost_estimate=pl.CostEstimate(flops=5 * 10**10, bytes_accessed=0, transcendentals=0),
        name="finish",
    )(*arrays, upper)


def local(
    tokens,
    kept_index,
    lengths,
    first_gain,
    first_shift,
    query_weight,
    key_weight,
    value_weight,
    query_bias,
    value_bias,
    output_weight,
    output_bias,
    second_gain,
    second_shift,
    expand_weight,
    expand_bias,
    reduce_weight,
    reduce_bias,
    cotangent,
):
    dp, mp = lax.axis_size("dp"), lax.axis_size("mp")
    d, z = lax.axis_index("dp"), lax.axis_index("mp")
    plane = Plane(dp)
    rows, width = tokens.shape
    group_rows = rows * mp
    block = width // dp
    full_hidden = expand_weight.shape[1] * mp
    meta = jnp.concatenate([z[None], plane.order(d)]).astype(jnp.int32)

    own_rows = lambda w: lax.dynamic_slice_in_dim(w, d * block, block, 0)
    own_columns = lambda w: lax.dynamic_slice_in_dim(w, d * block, block, 1).T
    first = jnp.concatenate(
        [
            own_rows(query_weight),
            own_rows(key_weight),
            own_rows(value_weight),
            own_columns(output_weight),
        ],
        axis=1,
    )
    second = jnp.concatenate([own_rows(expand_weight), own_columns(reduce_weight)], axis=1)
    singles = (
        first_gain,
        first_shift,
        output_bias,
        second_gain,
        second_shift,
        reduce_bias,
        query_bias,
        value_bias,
    )
    single, wide = first_gain.shape[0], expand_bias.shape[0]
    me = d * mp + z
    lane = jnp.arange(128, dtype=jnp.int32)
    lines = full_hidden // dp // 128

    def placed(stack):
        count = 128 // stack.shape[1]
        return jnp.where(lane // stack.shape[1] == me % count, jnp.tile(stack, (1, count)), 0.0)

    line = placed(expand_bias[None].astype(F32))
    at_line = (jnp.arange(8, dtype=jnp.int32) == me * wide // 128 % lines)[:, None]
    sheet = jnp.concatenate(
        [placed(jnp.stack(singles).astype(F32)), jnp.where(at_line, line, 0.0)], axis=0
    )
    length = lengths[0]
    clips = length.shape[0]
    index = jnp.arange(clips, dtype=jnp.int32)
    ends = jnp.sum(jnp.where(index[None, :] <= index[:, None], length[None, :], 0), axis=1)
    starts = ends - length
    reach, hops, left = LONGEST - 1, [], 0
    while reach > 0:
        extent = min(rows, -(-reach // 64) * 64)
        hops.append(extent)
        left, reach = left + extent, reach - extent
    margin = -(-left // 128) * 128
    while (2 * margin + rows) % TILE:
        margin += 128
    window = 2 * margin + rows
    base = z * rows - margin
    places = base + jnp.arange(window, dtype=jnp.int32)
    labels = jnp.sum((places[:, None] >= ends[None, :]).astype(jnp.int32), axis=1)
    labels = jnp.where((places >= 0) & (places < group_rows), labels, -1)
    label_own = labels[margin : margin + rows]
    limits = []
    for i in range(rows // TILE):
        low = z * rows + i * TILE
        last = low + TILE - 1
        start = jnp.sum(jnp.where(ends <= low, length, 0))
        end = jnp.sum(jnp.where(starts <= last, length, 0))
        limits.append(lax.div(start - base, TILE))
        limits.append(lax.div(end - base + TILE - 1, TILE))
    bounds = jnp.stack(limits).astype(jnp.int32)

    begun = begin(
        sheet[None],
        first,
        tokens,
        jnp.broadcast_to(kept_index[:, None], (rows, 128)),
        jnp.asarray(position_lines(width)),
        plane,
        mp,
        hops,
        margin,
        full_hidden,
    )
    narrow, broad, stream, around = begun[:4]
    buffers = begun[4:]
    normed_one = around[margin : margin + rows]
    scale = 1.0 / math.sqrt(HEAD_SIZE)
    middle_shift = mp // 2
    second = after(second, around)
    near = gather_group(second, list(range(1, middle_shift)), plane, mp)
    far = gather_group(second, list(range(middle_shift, mp)), plane, mp)
    around_t = turned_rows(around, meta, block)
    cotangent_t = turned_rows(cotangent, meta, block)
    projections = (query_weight, key_weight, value_weight)
    label_rows = jnp.broadcast_to(label_own[:, None], (rows, 128))
    label_line = jnp.broadcast_to(labels[None, :], (8, window))
    heads, attended, lses = [], [], []
    for own in (True, False):
        part = project(
            normed_one, around, projections if own else buffers, narrow, meta, block, mp, own
        )
        result, lse = attention_forward(bounds, *part, label_rows, label_line)
        heads.append(part)
        attended.append(result)
        lses.append(lse)

    middle, normed_two, normed_two_t = enter(
        stream, attended, narrow, output_weight, buffers, meta, block, mp
    )
    shared = (normed_two, cotangent, normed_two_t, cotangent_t, broad)
    out_one, back_one, keep, send, bias_one = feed(
        *shared, (expand_weight, reduce_weight), None, near, meta, block, mp, 0, middle_shift
    )
    sums_one = Scatter(keep, send, list(range(middle_shift)), plane, mp)
    branch_two, grad_normed_two, keep, send, bias_two = feed(
        *shared,
        None,
        (out_one, back_one),
        far,
        meta,
        block,
        mp,
        middle_shift,
        mp - middle_shift,
    )
    sums_two = Scatter(keep, send, list(range(middle_shift, mp)), plane, mp)
    branch_two = after(branch_two, sums_one.got)
    activations, grad_middle, branch_t, grad_near, grad_far, sums_mid = leave(
        middle, branch_two, grad_normed_two, cotangent, narrow, output_weight, buffers, meta, block, mp
    )

    label_line = jnp.broadcast_to(label_own[None, :], (8, rows))
    label_rows = jnp.broadcast_to(labels[:, None], (window, 128))
    sums_one.next()
    grad_far = after(grad_far, sums_two.got)
    grads_far = attention_backward(
        bounds, *heads[1], grad_far, attended[1], lses[1], label_line, label_rows
    )
    grads_far = lax.optimization_barrier((*grads_far, sums_one.got))[:3]
    sums_two.next()
    sums_one.next()
    partial = tail(around_t, branch_t, grads_far, attended[1], buffers, meta, block, mp, margin)
    sums_three = Scatter(partial[2], partial[3], list(range(1, mp)), plane, mp)
    grad_near = after(grad_near, sums_two.got, sums_one.got, partial[0])
    grads_near = attention_backward(
        bounds, *heads[0], grad_near, attended[0], lses[0], label_line, label_rows
    )
    sums_two.next()
    sums_one.last()
    sums_two.last()

    turned = jnp.mod(z - jnp.arange(mp, dtype=jnp.int32), mp)
    pick = turned[:, None] == jnp.arange(mp, dtype=jnp.int32)[None, :]

    def in_turn(v):
        parts = v.reshape(v.shape[0], 1, mp, v.shape[1] // mp)
        return jnp.sum(jnp.where(pick[None, :, :, None], parts, 0.0), axis=2).reshape(v.shape)

    bias_sums = in_turn(jnp.pad(partial[4][:2], ((0, 0), (width // mp, 0))))
    early = jnp.concatenate([jnp.zeros((2, width), F32), sums_mid[:4], bias_sums], axis=0)
    broad_sum = in_turn(jnp.concatenate([bias_one[:1], bias_two[:1]], axis=1))
    broad_part = jnp.pad(broad_sum.reshape(dp, lines, 128), ((0, 0), (0, 8 - lines), (0, 0)))
    upper = sums_three.fold()
    grad_tokens, total_one, summed = finish(
        (
            *grads_near,
            attended[0],
            *projections,
            partial[1],
            partial[0],
            around_t,
            branch_t,
            sums_three.keep,
            stream,
            grad_middle,
            narrow,
            early,
            broad_part,
        ),
        upper,
        plane,
        mp,
        hops,
        margin,
    )

    extent = width // mp
    grad_query, grad_key, grad_value, grad_out = [
        total_one[:, i * extent : (i + 1) * extent] for i in range(4)
    ]
    total_two = sums_one.own
    for item in sums_one.moved + sums_two.moved:
        total_two = total_two + item.astype(F32)
    extent = full_hidden // mp
    tile = min(512, extent)
    slabs = [total_two[:, i * tile : (i + 1) * tile] for i in range(2 * extent // tile)]
    grad_expand = jnp.concatenate(slabs[0::2], axis=1)
    grad_reduce = jnp.concatenate(slabs[1::2], axis=1)

    taken = lambda stack, extent: lax.dynamic_slice_in_dim(
        stack, me % (128 // extent) * extent, extent, 1
    )
    small = taken(summed[:8], single)
    broad_row = lax.dynamic_slice_in_dim(summed[8:], me * wide // 128 % lines, 1, 0)
    return (
        activations,
        grad_tokens,
        grad_query,
        grad_key,
        grad_value,
        grad_out.T,
        grad_expand,
        grad_reduce.T,
        small[0],
        small[1],
        small[6],
        small[7],
        small[2],
        small[3],
        small[4],
        taken(broad_row, wide)[0],
        small[5],
    )


def solution(mesh):
    vector = P(("dp", "mp"))
    tall = P(("dp", "mp"), None)
    in_specs = (
        tall,
        vector,
        P("dp", None),
        vector,
        vector,
        P(None, "mp"),
        P(None, "mp"),
        P(None, "mp"),
        vector,
        vector,
        P("mp", None),
        vector,
        vector,
        vector,
        P(None, "mp"),
        vector,
        P("mp", None),
        vector,
        tall,
    )
    out_specs = (
        tall,
        tall,
        P("dp", "mp"),
        P("dp", "mp"),
        P("dp", "mp"),
        P("mp", "dp"),
        P("dp", "mp"),
        P("mp", "dp"),
    ) + (vector,) * 9
    return jax.shard_map(local, mesh=mesh, in_specs=in_specs, out_specs=out_specs, check_vma=False)
```

```python
import functools
import math

import jax
import jax.numpy as jnp
import numpy as np
from jax import lax
from jax.experimental import pallas as pl
from jax.experimental.pallas import tpu as pltpu
from jax.sharding import PartitionSpec as P

HEAD_SIZE = 64
LONGEST = 549
EPSILON = 1e-06
TILE = 256
MIB = 1024 * 1024
F32 = jnp.float32
BF16 = jnp.bfloat16

NN = (((1,), (0,)), ((), ()))
NT = (((1,), (1,)), ((), ()))
TN = (((0,), (0,)), ((), ()))


def dot(left, right, dims=NN):
    return lax.dot_general(left, right, dims, preferred_element_type=F32)


def position_lines(extent):
    quarter = extent // 4
    spatial = (extent - quarter) // 2
    table = np.zeros((128, extent), np.float32)
    at, first = 0, 0
    for count, part in ((8, quarter), (14, spatial), (14, spatial)):
        half = part // 2
        inverse = np.exp(np.arange(half, dtype=np.float32) * np.float32(-math.log(10000.0) / half))
        angles = np.arange(count, dtype=np.float32)[:, None] * inverse[None, :]
        table[first : first + count, at : at + half] = np.sin(angles)
        table[first : first + count, at + half : at + part] = np.cos(angles)
        at, first = at + part, first + count
    return table


def norm_parts(values):
    center = values - jnp.mean(values, axis=-1, keepdims=True)
    spread = jnp.mean(center * center, axis=-1, keepdims=True)
    factor = lax.rsqrt(spread + EPSILON)
    return center * factor, factor


def norm_back(upstream, hat, factor, gain):
    scaled = upstream * gain
    first = jnp.mean(scaled, axis=-1, keepdims=True)
    second = jnp.mean(scaled * hat, axis=-1, keepdims=True)
    return factor * (scaled - first - hat * second)


def forward_kernel(bounds_ref, q_ref, k_ref, v_ref, lq_ref, lk_ref, o_ref, lse_ref, s_ref):
    rows = q_ref.shape[0]
    lane = lax.broadcasted_iota(jnp.int32, (TILE, 2 * HEAD_SIZE), 1)
    for block in range(rows // TILE):
        low = bounds_ref[2 * block]
        high = bounds_ref[2 * block + 1]
        span = slice(block * TILE, (block + 1) * TILE)
        query = q_ref[span, :]
        heads = [
            jnp.where(lane < HEAD_SIZE, query, jnp.zeros_like(query)),
            jnp.where(lane < HEAD_SIZE, jnp.zeros_like(query), query),
        ]
        label = lq_ref[span, :]
        label = jnp.concatenate([label, label], axis=1)

        def scores(t, carry):
            at = pl.multiple_of(t * TILE, TILE)
            key = k_ref[pl.ds(at, TILE), :]
            same = label == lk_ref[0:1, pl.ds(at, TILE)]
            out = []
            for h in range(2):
                s = jnp.where(same, dot(heads[h], key, NT), -1e30)
                s_ref[h, :, pl.ds(at, TILE)] = s
                out.append(jnp.maximum(carry[h], jnp.maximum(s[:, :128], s[:, 128:])))
            return tuple(out)

        least = jnp.full((TILE, 128), -1e30, F32)
        peaks = lax.fori_loop(low, high, scores, (least, least))
        peaks = [jnp.max(item, axis=1, keepdims=True) for item in peaks]

        def blend(t, carry):
            at = pl.multiple_of(t * TILE, TILE)
            value = v_ref[pl.ds(at, TILE), :]
            out = []
            for h in range(2):
                total, acc = carry[h]
                p = jnp.exp(s_ref[h, :, pl.ds(at, TILE)] - peaks[h])
                out.append((total + (p[:, :128] + p[:, 128:]), acc + dot(p.astype(BF16), value)))
            return tuple(out)

        zero = jnp.zeros((TILE, 128), F32)
        done = lax.fori_loop(low, high, blend, ((zero, zero), (zero, zero)))
        pieces = []
        for h in range(2):
            total = jnp.sum(done[h][0], axis=1, keepdims=True)
            pieces.append(done[h][1] / total)
            lse = jnp.broadcast_to(peaks[h] + jnp.log(total), (TILE, 128))
            lse_ref[0, h : h + 1, span] = lse.T[0:1, :]
        o_ref[span, :] = jnp.where(lane < HEAD_SIZE, pieces[0], pieces[1]).astype(BF16)


def backward_kernel(
    bounds_ref,
    q_ref,
    k_ref,
    v_ref,
    do_ref,
    o_ref,
    lse_ref,
    lq_ref,
    lk_ref,
    dq_ref,
    dk_ref,
    dv_ref,
    dk_acc,
    dv_acc,
):
    rows = q_ref.shape[0]
    lane = lax.broadcasted_iota(jnp.int32, (TILE, 2 * HEAD_SIZE), 1)
    row = lax.broadcasted_iota(jnp.int32, (2 * HEAD_SIZE, TILE), 0)
    dk_acc[...] = jnp.zeros_like(dk_acc)
    dv_acc[...] = jnp.zeros_like(dv_acc)

    def halves(array, where):
        zero = jnp.zeros_like(array)
        return [jnp.where(where < HEAD_SIZE, array, zero), jnp.where(where < HEAD_SIZE, zero, array)]

    for block in range(rows // TILE):
        low = bounds_ref[2 * block]
        high = bounds_ref[2 * block + 1]
        span = slice(block * TILE, (block + 1) * TILE)
        query, grad = q_ref[span, :], do_ref[span, :]
        query_t, grad_t = query.T, grad.T
        product = grad_t.astype(F32) * o_ref[span, :].T.astype(F32)
        deltas = [
            jnp.sum(product[h * HEAD_SIZE : (h + 1) * HEAD_SIZE], axis=0, keepdims=True)
            for h in range(2)
        ]
        lses = [lse_ref[0, h : h + 1, span] for h in range(2)]
        query_h, grad_h = halves(query, lane), halves(grad, lane)
        query_th, grad_th = halves(query_t, row), halves(grad_t, row)
        label = lq_ref[0:1, span]

        def step(t, carry):
            at = pl.multiple_of(t * TILE, TILE)
            key, value = k_ref[pl.ds(at, TILE), :], v_ref[pl.ds(at, TILE), :]
            key_t = key.T
            same = lk_ref[pl.ds(at, TILE), :]
            same = jnp.concatenate([same, same], axis=1) == label
            out, grad_k, grad_v = [], None, None
            for h in range(2):
                s = dot(key, query_th[h])
                p = jnp.where(same, jnp.exp(s - lses[h]), 0.0)
                dp = dot(value, grad_th[h])
                ds = (p * (dp - deltas[h])).astype(BF16)
                part_v = dot(p.astype(BF16), grad_h[h])
                part_k = dot(ds, query_h[h])
                grad_v = part_v if grad_v is None else grad_v + part_v
                grad_k = part_k if grad_k is None else grad_k + part_k
                out.append(carry[h] + dot(key_t[h * HEAD_SIZE : (h + 1) * HEAD_SIZE], ds))
            dk_acc[pl.ds(at, TILE), :] += grad_k
            dv_acc[pl.ds(at, TILE), :] += grad_v
            return tuple(out)

        zero = jnp.zeros((HEAD_SIZE, TILE), F32)
        parts = lax.fori_loop(low, high, step, (zero, zero))
        total = jnp.concatenate(parts, axis=0) * (1.0 / math.sqrt(HEAD_SIZE))
        dq_ref[span, :] = total.T.astype(BF16)
    dk_ref[...] = dk_acc[...].astype(BF16)
    dv_ref[...] = dv_acc[...].astype(BF16)


def attention_call(kernel, name, bounds, columns, others, outs, scratch, part, before, work):
    first, count, total = part
    pair = 2 * HEAD_SIZE
    anywhere = pl.BlockSpec(memory_space=pl.ANY)
    column = lambda item: pl.BlockSpec((item.shape[0], pair), lambda p, b: (0, first + p))
    result = pl.pallas_call(
        kernel,
        grid_spec=pltpu.PrefetchScalarGridSpec(
            num_scalar_prefetch=1,
            grid=(count,),
            in_specs=[column(item) for item in columns]
            + [
                pl.BlockSpec((1,) + item.shape[1:], lambda p, b: (first + p, 0, 0))
                if item.ndim == 3
                else pl.BlockSpec(item.shape, lambda p, b: (0, 0))
                for item in others
            ]
            + [anywhere] * len(before),
            out_specs=[
                pl.BlockSpec((1,) + shape[1:], lambda p, b: (first + p, 0, 0))
                if len(shape) == 3
                else pl.BlockSpec((shape[0], pair), lambda p, b: (0, first + p))
                for shape, _ in outs
            ],
            scratch_shapes=scratch,
        ),
        out_shape=[jax.ShapeDtypeStruct(shape, kind) for shape, kind in outs],
        input_output_aliases={
            1 + len(columns) + len(others) + i: i for i in range(len(before))
        },
        compiler_params=pltpu.CompilerParams(vmem_limit_bytes=32 * MIB),
        cost_estimate=pl.CostEstimate(flops=count * work, bytes_accessed=0, transcendentals=0),
        name=name,
    )(bounds, *columns, *others, *before)
    return result


def attention_forward(bounds, queries, keys, values, label_q, label_k, part, before=()):
    rows, width = queries.shape
    window = keys.shape[0]

    def kernel(*refs):
        forward_kernel(*refs[:6], *refs[6 + len(before) :])

    return attention_call(
        kernel,
        "attention_forward",
        bounds,
        (queries, keys, values),
        (label_q, label_k),
        [((rows, width), BF16), ((part[2], 2, rows), F32)],
        [pltpu.VMEM((2, TILE, window), F32)],
        part,
        before,
        5 * 10**9,
    )


def attention_backward(
    bounds, queries, keys, values, grads, attended, lse, label_q, label_k, part, before=()
):
    rows, width = queries.shape
    window = keys.shape[0]

    def kernel(*refs):
        backward_kernel(*refs[:9], *refs[9 + len(before) :])

    return attention_call(
        kernel,
        "attention_backward",
        bounds,
        (queries, keys, values, grads, attended),
        (lse, label_q, label_k),
        [((rows, width), BF16), ((window, width), BF16), ((window, width), BF16)],
        [pltpu.VMEM((window, 2 * HEAD_SIZE), F32)] * 2,
        part,
        before,
        6 * 10**9,
    )


def assemble(target, buffers, meta, block, first=0):
    each = buffers[0].shape[0] // block
    span = slice(first, first + buffers[0].shape[1])
    for i in range(len(buffers) * each):
        at = pl.multiple_of(meta[1 + i] * block, block)
        source = buffers[i // each]
        target[pl.ds(at, block), span] = source[i % each * block : (i % each + 1) * block, :]


def turn(target, source, meta, block, lead):
    lead[...] = source.T
    for i in range(target.shape[0] // block):
        at = pl.multiple_of(meta[1 + i] * block, block)
        target[i * block : (i + 1) * block, :] = lead[pl.ds(at, block), :]


def fixed(shape):
    return pl.BlockSpec(shape, lambda *_: (0,) * len(shape), pipeline_mode=pl.Buffered(1))


def call(kernel, name, grid, meta, ins, outs, scratch, vmem, flops, moved=0):
    return pl.pallas_call(
        kernel,
        grid_spec=pltpu.PrefetchScalarGridSpec(
            num_scalar_prefetch=1,
            grid=grid,
            in_specs=[spec for _, spec in ins],
            out_specs=[spec for _, _, spec in outs],
            scratch_shapes=scratch,
        ),
        out_shape=[jax.ShapeDtypeStruct(shape, kind) for shape, kind, _ in outs],
        compiler_params=pltpu.CompilerParams(vmem_limit_bytes=vmem * MIB),
        cost_estimate=pl.CostEstimate(flops=flops, bytes_accessed=moved, transcendentals=0),
        name=name,
    )(meta, *[array for array, _ in ins])


def turn_kernel(block, meta, source, target, lead):
    turn(target, source[...], meta, block, lead)


def turned_rows(source, meta, block):
    rows, width = source.shape
    return call(
        functools.partial(turn_kernel, block),
        "turn",
        (1,),
        meta,
        [(source, fixed(source.shape))],
        [((width, rows), BF16, fixed((width, rows)))],
        [pltpu.VMEM((width, rows), BF16)],
        24,
        4 * 10**9,
    )[0]


def project_kernel(block, scale, own, meta, x, around, bias, *refs):
    weights, (q, k, v), scratch = refs[:-6], refs[-6:-3], refs[-3:]
    if own:
        scratch = weights
    else:
        for w in range(3):
            assemble(scratch[w], weights[4 * w : 4 * w + 4], meta, block)
    q[...] = (dot(x[...], scratch[0][...]) + bias[6:7, :]).astype(BF16) * jnp.asarray(scale, BF16)
    k[...] = dot(around[...], scratch[1][...]).astype(BF16)
    v[...] = (dot(around[...], scratch[2][...]) + bias[7:8, :]).astype(BF16)


def gathered_specs(buffers, kinds, extent, stride):
    return [
        (item, pl.BlockSpec((item.shape[0], extent), lambda i, m, kind=kind: (0, i * stride + kind)))
        for kind in kinds
        for item in buffers
    ]


def project(x, around, weights, narrow, meta, block, mp, own):
    rows, width = x.shape
    window = around.shape[0]
    extent = width // mp
    first, count = (0, 1) if own else (1, mp - 1)
    column = lambda n: pl.BlockSpec((n, extent), lambda i, m: (0, i))
    turned = lambda i, m: (0, lax.rem(m[0] - first - i + mp, mp))
    return call(
        functools.partial(project_kernel, block, 1.0 / math.sqrt(HEAD_SIZE), own),
        "project",
        (count,),
        meta,
        [
            (x, fixed(x.shape)),
            (around, fixed(around.shape)),
            (narrow, pl.BlockSpec((8, extent), turned)),
        ]
        + (
            [(w, fixed(w.shape)) for w in weights]
            if own
            else gathered_specs(weights, (0, 1, 2), extent, 4)
        ),
        [
            ((rows, count * extent), BF16, column(rows)),
            ((window, count * extent), BF16, column(window)),
            ((window, count * extent), BF16, column(window)),
        ],
        [pltpu.VMEM((width, extent), BF16)] * 3,
        40,
        count * 4 * 10**9,
    )


def tail_kernel(block, margin, meta, around_t, branch_t, dq, dk, dv, att, *refs):
    got, (own_out, around_out, keep, send, bias), weights = refs[:12], refs[12:17], refs[17:]
    for w in range(3):
        assemble(weights[w], got[4 * w : 4 * w + 4], meta, block)
    step = pl.program_id(0)
    rows, half, extent = dq.shape[0], keep.shape[0], dq.shape[1]
    back = dot(dk[...], weights[1][...], NT) + dot(dv[...], weights[2][...], NT)
    more = dot(dq[...], weights[0][...], NT)

    @pl.when(step == 0)
    def _():
        around_out[...] = back
        own_out[...] = more

    @pl.when(step > 0)
    def _():
        around_out[...] += back
        own_out[...] += more

    middle, everything = slice(margin, margin + rows), slice(None)
    for at, (left, span, right) in enumerate(
        (
            (around_t, middle, dq),
            (around_t, everything, dk),
            (around_t, everything, dv),
            (branch_t, everything, att),
        )
    ):
        columns = slice(at * extent, (at + 1) * extent)
        keep[:, columns] = dot(left[:half, span], right[...]).astype(BF16)
        send[:, columns] = dot(left[half:, span], right[...]).astype(BF16)
    add = lambda v: jnp.sum(v[...].astype(F32), axis=0, keepdims=True)
    bias[...] = jnp.concatenate([add(dq), add(dv), jnp.zeros((6, extent), F32)], axis=0)


def tail(around_t, branch_t, grads, att, weights, meta, block, mp, margin):
    dq, dk, dv = grads
    rows, width = dq.shape[0], around_t.shape[0]
    window = around_t.shape[1]
    extent = width // mp
    half = width // 2
    count = mp - 1
    column = lambda n: pl.BlockSpec((n, extent), lambda i, m: (0, i))
    wide = pl.BlockSpec((half, 4 * extent), lambda i, m: (0, i))
    return call(
        functools.partial(tail_kernel, block, margin),
        "tail",
        (count,),
        meta,
        [(item, fixed(item.shape)) for item in (around_t, branch_t)]
        + [(dq, column(rows)), (dk, column(window)), (dv, column(window)), (att, column(rows))]
        + gathered_specs(weights, (0, 1, 2), extent, 4),
        [
            ((rows, width), F32, fixed((rows, width))),
            ((window, width), F32, fixed((window, width))),
            ((half, 4 * count * extent), BF16, wide),
            ((half, 4 * count * extent), BF16, wide),
            ((8, count * extent), F32, column(8)),
        ],
        [pltpu.VMEM((width, extent), BF16)] * 3,
        60,
        count * 8 * 10**9,
    )


def join(parts, axis):
    return jnp.concatenate(parts, axis=axis)


class Plane:
    def __init__(self, size):
        self.size = size
        bits = list(range(1, size.bit_length() - 1))
        turn = len(bits) // 2
        self.orders = [bits, bits[turn:] + bits[:turn]]
        held = []
        for order in self.orders:
            masks = [0]
            for bit in order:
                masks = masks + [m ^ (1 << bit) for m in masks]
            held.append(masks)
        self.masks = [held[c] + [1 ^ m for m in held[1 - c]] for c in range(2)]
        self.steps = len(bits)

    def pairs(self, step):
        return [(i, i ^ (1 << self.orders[i % 2][step])) for i in range(self.size)]

    def siblings(self):
        return [(i, i ^ 1) for i in range(self.size)]

    def order(self, d):
        return jnp.bitwise_xor(jnp.array(self.masks, jnp.int32)[d % 2], d)


def shifted(payload, r, mp):
    return lax.ppermute(payload, "mp", [(i, (i + r) % mp) for i in range(mp)])


def spread_chips(held, plane):
    for step in range(plane.steps - 2):
        held = join([held, lax.ppermute(held, "dp", plane.pairs(step))], 0)
    return held, lax.ppermute(held, "dp", plane.pairs(plane.steps - 2))


def added(left, right):
    return (left.astype(F32) + right.astype(F32)).astype(BF16)


def folded(keep, got):
    half = keep.shape[0] // 2
    return added(keep[:half], got[:half]), added(keep[half:], got[half:])


def after(value, *others):
    return lax.optimization_barrier((value,) + others)[0]


class Scatter:
    def __init__(self, keep, upper, shifts, plane, mp):
        self.keep, self.shifts, self.plane, self.mp = keep, shifts, plane, mp
        self.step = plane.steps - 1
        self.got = lax.ppermute(upper, "dp", plane.pairs(self.step))

    def next(self):
        self.step -= 1
        self.keep, upper = folded(self.keep, self.got)
        self.got = lax.ppermute(upper, "dp", self.plane.pairs(self.step))
        return self

    def last(self):
        while self.step > 0:
            self.next()
        extent = self.keep.shape[1] // len(self.shifts)
        self.moved = []
        for i, r in enumerate(self.shifts):
            span = slice(i * extent, (i + 1) * extent)
            pairs = [(j, (j - r) % self.mp) for j in range(self.mp)]
            part = added(self.keep[:, span], self.got[:, span])
            self.moved.append(lax.ppermute(part, "mp", pairs))
        return self


MESH = pl.DeviceIdType.MESH


def flipped(d, bit):
    return d + (1 - 2 * lax.rem(lax.div(d, 1 << bit), 2)) * (1 << bit)


def meet(d, z, dp, mp):
    barrier = pltpu.get_barrier_semaphore()
    for step in range(1, dp):
        there = (lax.rem(d + step, dp), z)
        pl.semaphore_signal(barrier, inc=1, device_id=there, device_id_type=MESH)
    for step in range(1, mp):
        there = (d, lax.rem(z + step, mp))
        pl.semaphore_signal(barrier, inc=1, device_id=there, device_id_type=MESH)
    pl.semaphore_wait(barrier, dp + mp - 2)


def remote(source, target, send_sem, recv_sem, device):
    return pltpu.make_async_remote_copy(
        src_ref=source,
        dst_ref=target,
        send_sem=send_sem,
        recv_sem=recv_sem,
        device_id=device,
        device_id_type=MESH,
    )


def peers_start(source, slots, send_sem, recv_sem, along, me, extent, each):
    copies = []
    for step in range(1, extent):
        place = lax.rem(me + step, extent)
        copies.append(
            remote(
                source.at[place if each else 0],
                slots.at[me],
                send_sem.at[step],
                recv_sem.at[me],
                along(step),
            )
        )
        copies[-1].start()
    slots[me] = source[me if each else 0]
    return copies


def peers_finish(copies, slots, recv_sem, me, extent):
    for step in range(1, extent):
        copies[step - 1].wait_send()
        sender = lax.rem(me + step, extent)
        pltpu.make_async_copy(slots.at[sender], slots.at[sender], recv_sem.at[sender]).wait()


def begin_kernel(plane, mp, hops, margin, *refs):
    (sheet, payload, tokens, index, table), refs = refs[:5], refs[5:]
    (narrow, broad, stream, around), buffers, refs = refs[:4], refs[4:8], refs[8:]
    (middle, first, second, normed, zeros), refs = refs[:5], refs[5:]
    send_one, recv_one, send_two, recv_two, refs = *refs[:4], refs[4:]
    z_send, z_recv, chip_send, chip_recv, core_send, core_recv, halo_send, halo_recv, local = refs
    dp = plane.size
    d, z = lax.axis_index("dp"), lax.axis_index("mp")
    core = lax.rem(d, 2)
    rows, width = tokens.shape
    block, columns = payload.shape
    along_dp = lambda step: (lax.rem(d + step, dp), z)
    along_mp = lambda step: (d, lax.rem(z + step, mp))
    zeros[...] = jnp.zeros_like(zeros)
    meet(d, z, dp, mp)
    vectors = peers_start(sheet, first, send_one, recv_one, along_mp, z, mp, False)

    each = dp // 4

    def place(j, r, other=False):
        return buffers[j // each + (2 if other else 0)].at[
            pl.ds(j % each * block, block), pl.ds((r - 1) * columns, columns)
        ]

    shards = [
        remote(payload, place(0, r), z_send.at[r], z_recv.at[r], along_mp(r)) for r in range(1, mp)
    ]
    for copy in shards:
        copy.start()

    count = lax.broadcasted_iota(jnp.int32, index.shape, 1)
    kept = index[...]
    coarse = lax.div(kept, 14)
    frame = lax.div(kept, 196)
    across = coarse - frame * 14
    line = kept - coarse * 14
    hot = ((count == frame) | (count == across + 8) | (count == line + 22)).astype(F32)
    hidden = tokens[...].astype(F32) + lax.dot_general(
        hot, table[...], NN, precision=lax.Precision.HIGHEST, preferred_element_type=F32
    )
    stream[...] = hidden

    peers_finish(vectors, first, recv_one, z, mp)
    middle[0] = jnp.sum(first[...], axis=0)
    vectors = peers_start(middle, second, send_two, recv_two, along_dp, d, dp, False)
    hat, _ = norm_parts(hidden)
    peers_finish(vectors, second, recv_two, d, dp)
    share = dp // (width // 128)
    for c in range(width // 128):
        narrow[:, c * 128 : (c + 1) * 128] = jnp.sum(
            second[c * share : (c + 1) * share, 0:8, :], axis=0
        )
    lines = broad.shape[1] // 128
    per = lines // dp
    for c in range(lines):
        row = second[c // per, 8 + c % per : 9 + c % per, :]
        broad[:, c * 128 : (c + 1) * 128] = jnp.broadcast_to(row, (8, 128))
    normed[...] = (hat * narrow[0:1, :] + narrow[1:2, :]).astype(BF16)

    waits, at_left, at_right = [], margin, margin + rows
    inside = pltpu.make_async_copy(
        normed, around.at[pl.ds(margin, rows), :], local.at[0]
    )
    inside.start()
    waits.append((None, inside.wait))
    for hop, extent in enumerate(hops, 1):
        left = around.at[pl.ds(at_left - extent, extent), :]
        right = around.at[pl.ds(at_right, extent), :]
        sides = (
            (left, normed.at[pl.ds(rows - extent, extent), :], z + hop, z - hop, 2 * hop - 2),
            (right, normed.at[pl.ds(0, extent), :], z - hop, z + hop, 2 * hop - 1),
        )
        for target, source, there, back, n in sides:
            goes = (there >= 0) & (there < mp)
            comes = (back >= 0) & (back < mp)
            copy = remote(source, target, halo_send.at[n], halo_recv.at[n], (d, there))
            blank = pltpu.make_async_copy(zeros.at[pl.ds(0, extent), :], target, local.at[1 + n])
            pl.when(goes)(copy.start)
            pl.when(jnp.logical_not(comes))(blank.start)
            waits.append((goes, copy.wait_send))
            waits.append((comes, copy.wait_recv))
            waits.append((jnp.logical_not(comes), blank.wait))
        at_left, at_right = at_left - extent, at_right + extent
    if at_left:
        for n, at in enumerate((0, at_right)):
            blank = pltpu.make_async_copy(
                zeros.at[pl.ds(0, at_left), :],
                around.at[pl.ds(at, at_left), :],
                local.at[1 + 2 * len(hops) + n],
            )
            blank.start()
            waits.append((None, blank.wait))

    sent = []

    def forward(j, r):
        for step in range(plane.steps):
            if j < 1 << step:
                there = (1 - core) * flipped(d, plane.orders[0][step]) + core * flipped(
                    d, plane.orders[1][step]
                )
                to = (1 << step) + j
                copy = remote(
                    place(j, r),
                    place(to, r),
                    chip_send.at[r, to],
                    chip_recv.at[r, to],
                    (there, z),
                )
                copy.start()
                sent.append(copy)
        copy = remote(
            place(j, r), place(j, r, True), core_send.at[r, j], core_recv.at[r, j], (flipped(d, 0), z)
        )
        copy.start()
        sent.append(copy)

    for r in range(1, mp):
        shards[r - 1].wait_recv()
        forward(0, r)
    for j in range(1, 1 << plane.steps):
        for r in range(1, mp):
            pltpu.make_async_copy(place(j, r), place(j, r), chip_recv.at[r, j]).wait()
            forward(j, r)
    for j in range(1 << plane.steps):
        for r in range(1, mp):
            pltpu.make_async_copy(place(j, r, True), place(j, r, True), core_recv.at[r, j]).wait()
    for copy in shards + sent:
        copy.wait_send()
    for when, wait in waits:
        wait() if when is None else pl.when(when)(wait)


def begin(sheet, payload, tokens, index, table, plane, mp, hops, margin, full_hidden):
    dp = plane.size
    rows, width = tokens.shape
    block, columns = payload.shape
    vmem, anywhere = pl.BlockSpec(memory_space=pltpu.VMEM), pl.BlockSpec(memory_space=pl.ANY)
    window = 2 * margin + rows
    dma = pltpu.SemaphoreType.DMA
    blocks = dp // 2
    return pl.pallas_call(
        functools.partial(begin_kernel, plane, mp, hops, margin),
        out_shape=[
            jax.ShapeDtypeStruct((8, width), F32),
            jax.ShapeDtypeStruct((8, full_hidden), F32),
            jax.ShapeDtypeStruct((rows, width), F32),
            jax.ShapeDtypeStruct((window, width), BF16),
        ]
        + [jax.ShapeDtypeStruct((width // 4, (mp - 1) * columns), BF16)] * 4,
        in_specs=[vmem] * 5,
        out_specs=[vmem] * 3 + [anywhere] * 5,
        scratch_shapes=[
            pltpu.VMEM((1, 16, 128), F32),
            pltpu.VMEM((mp, 16, 128), F32),
            pltpu.VMEM((dp, 16, 128), F32),
            pltpu.VMEM((rows, width), BF16),
            pltpu.VMEM((rows, width), BF16),
            dma((mp,)),
            dma((mp,)),
            dma((dp,)),
            dma((dp,)),
            dma((mp,)),
            dma((mp,)),
            dma((mp, blocks)),
            dma((mp, blocks)),
            dma((mp, blocks)),
            dma((mp, blocks)),
            dma((2 * len(hops),)),
            dma((2 * len(hops),)),
            dma((3 + 2 * len(hops),)),
        ],
        compiler_params=pltpu.CompilerParams(
            collective_id=1, has_side_effects=True, vmem_limit_bytes=60 * MIB
        ),
        cost_estimate=pl.CostEstimate(flops=4 * 10**10, bytes_accessed=0, transcendentals=0),
        name="begin",
    )(sheet, payload, tokens, index, table)


def xored(d, mask):
    for bit in range(mask.bit_length()):
        if mask >> bit & 1:
            d = flipped(d, bit)
    return d


def middle_kernel(plane, mp, tile, *refs):
    (stream_in, near_in, far_in, g_in, narrow_in, broad_in), refs = refs[:6], refs[6:]
    own_o, own_e, own_r, out_parts, refs = *refs[:3], refs[3:7], refs[7:]
    (early_a, early_b), late_a, refs = refs[:2], refs[2 : 2 * mp - 2], refs[2 * mp - 2 :]
    (sums, db, own_total, moved, act, grad_mid, branch_t, grad_near, grad_far), refs = refs[:9], refs[9:]
    (keep_out, upper_out, early_o, late_b, late_c, late_d), refs = refs[:6], refs[6:]
    (mid, near, far, g, narrow, broad, o_temp, weight_o, weights, r_temp), refs = refs[:10], refs[10:]
    (x, x_t, g_t, lead, out_acc, dx_acc, keep, send, got, more), refs = refs[:10], refs[10:]
    load, weight_sem, own_sem, core_send, core_recv, chip_send, chip_recv, refs = *refs[:7], refs[7:]
    sum_send, sum_recv, near_send, near_recv, store = refs
    dp, steps = plane.size, plane.steps
    d, z = lax.axis_index("dp"), lax.axis_index("mp")
    core = lax.rem(d, 2)
    rows, width = x.shape
    block, half, quarter = width // dp, width // 2, width // 4
    extent = own_e.shape[1]
    per = extent // tile
    tiles = mp * per
    wide = 2 * extent
    full = mp // 2
    orders = [
        (1 - core) * xored(d, plane.masks[0][i]) + core * xored(d, plane.masks[1][i])
        for i in range(dp)
    ]
    sibling = (flipped(d, 0), z)

    def partner(step):
        there = (1 - core) * flipped(d, plane.orders[0][step]) + core * flipped(
            d, plane.orders[1][step]
        )
        return there, z

    def home(i):
        return pl.ds(pl.multiple_of(orders[i] * block, block), block)

    def turned(target, source):
        lead[...] = source.T
        for i in range(dp):
            target[i * block : (i + 1) * block, :] = lead[home(i), :]

    loads = [
        pltpu.make_async_copy(source, target, load.at[i])
        for i, (source, target) in enumerate(
            (
                (stream_in, mid),
                (near_in, near),
                (far_in, far),
                (g_in, g),
                (narrow_in, narrow),
                (broad_in, broad),
                (own_o, o_temp),
            )
        )
    ]
    each = dp // 4
    part_o = own_o.shape[0]
    for i in range(dp):
        for r in range(1, mp):
            pltpu.make_async_copy(
                out_parts[i // each].at[
                    pl.ds(i % each * block, block), pl.ds((4 * r - 1) * part_o, part_o)
                ],
                weight_o.at[home(i), pl.ds(r * part_o, part_o)],
                load.at[7],
            ).start()
    rest_o = weight_o.at[:, pl.ds(part_o, width - part_o)]
    for copy in loads:
        copy.start()

    def fetch(i):
        slot, r, t = i % 2, i // per, i % per
        if r == 0:
            return [
                pltpu.make_async_copy(
                    own_e.at[:, pl.ds(t * tile, tile)], weights.at[slot, 0], own_sem.at[0]
                ),
                pltpu.make_async_copy(own_r.at[pl.ds(t * tile, tile), :], r_temp, own_sem.at[1]),
            ]
        if r == 1:
            parts = (early_a, early_b) + tuple(
                early_o.at[pl.ds(n * quarter, quarter), :] for n in range(2)
            )
            first = 0
        else:
            parts, first = (None, late_b, late_c, late_d), (r - 2) * wide

        def piece(n, kind):
            column = kind * extent + t * tile
            if r > 1 and n < each:
                few = each // 2
                return late_a[2 * (r - 2) + n // few].at[
                    pl.ds(n % few * block, block), pl.ds(column, tile)
                ]
            return parts[n // each].at[pl.ds(n % each * block, block), pl.ds(first + column, tile)]

        return [
            pltpu.make_async_copy(
                piece(n, kind),
                weights.at[slot, kind, home(n), :],
                weight_sem.at[slot],
            )
            for kind in range(2)
            for n in range(dp)
        ]

    for copy in fetch(0):
        copy.start()
    meet(d, z, dp, mp)

    def late(buffer, r):
        return buffer.at[:, pl.ds((r - 2) * wide, wide)]

    sent = []
    swaps, hops = {}, {}
    for n, part in enumerate((early_a, early_b)):
        swaps[1, n] = remote(
            part,
            early_o.at[pl.ds(n * quarter, quarter), :],
            core_send.at[1, n],
            core_recv.at[1, n],
            sibling,
        )
    for r in range(2, mp):
        for n in range(2):
            part = late_a[2 * (r - 2) + n]
            span = pl.ds(n * quarter // 2, quarter // 2)
            columns = pl.ds((r - 2) * wide, wide)
            hops[r, n] = remote(
                part,
                late_b.at[span, columns],
                chip_send.at[r, n],
                chip_recv.at[r, n],
                partner(steps - 1),
            )
            swaps[r, n] = remote(
                part, late_c.at[span, columns], core_send.at[r, n], core_recv.at[r, n], sibling
            )
        swaps[r, 2] = remote(
            late(late_b, r), late(late_d, r), core_send.at[r, 2], core_recv.at[r, 2], sibling
        )
    swaps[1, 0].start()
    swaps[1, 1].start()
    for r in range(2, mp):
        for n in range(2):
            hops[r, n].start()
        for n in range(2):
            swaps[r, n].start()

    for i in range(7):
        loads[i].wait()
    pltpu.make_async_copy(rest_o, rest_o, load.at[7]).wait()
    weight_o[:, :part_o] = o_temp[...].T
    cut = near.shape[1]
    mixed = dot(near[...], weight_o[:, :cut], NT) + dot(far[...], weight_o[:, cut:], NT)
    mid[...] = mid[...] + mixed + narrow[2:3, :]
    hat, _ = norm_parts(mid[...])
    x[...] = (hat * narrow[3:4, :] + narrow[4:5, :]).astype(BF16)
    turned(x_t, x[...])
    turned(g_t, g[...])
    out_acc[...] = jnp.zeros_like(out_acc)
    dx_acc[...] = jnp.zeros_like(dx_acc)

    def swap_of(c):
        return remote(
            send.at[c % 2], got.at[c], near_send.at[c], near_recv.at[c], sibling
        )

    def rows_of(step):
        count = half >> (steps - step)
        return count, half - 2 * count

    def sum_of(c, step):
        count, at = rows_of(step)
        return remote(
            keep.at[c, pl.ds(count, count), :],
            more.at[c, pl.ds(at, count), :],
            sum_send.at[c, step],
            sum_recv.at[c, step],
            partner(step),
        )

    def outs_of(c):
        span = pl.ds((c - full) * wide, wide)
        return [
            pltpu.make_async_copy(
                keep.at[c, pl.ds(n * quarter, quarter), :], target.at[:, span], store.at[c, n]
            )
            for n, target in enumerate((keep_out, upper_out))
        ]

    def core_done(c):
        swap_of(c).wait_recv()
        keep[c] = added(keep[c], got[c])
        if c < full:
            sum_of(c, steps - 1).start()
        else:
            for copy in outs_of(c):
                copy.start()

    def chips_done(c, step):
        sum_of(c, step).wait_recv()
        count, at = rows_of(step)
        keep[c, :count, :] = added(keep[c, :count, :], more[c, pl.ds(at, count), :])
        if step:
            sum_of(c, step - 1).start()

    events = {}
    for r in range(2, mp):

        def passed(r=r):
            hops[r, 0].wait_recv()
            hops[r, 1].wait_recv()
            swaps[r, 2].start()

        events.setdefault((r - 1) * per, []).append(passed)
    for r in range(1, mp):

        def arrived(r=r):
            for n in range(2 if r == 1 else 3):
                swaps[r, n].wait_recv()

        events.setdefault(r * per - 1, []).append(arrived)
    for i in range(1, tiles):

        def ahead(i=i):
            for copy in fetch(i):
                copy.start()

        if i >= per:
            events.setdefault(i - 1, []).append(ahead)
    for c in range(mp - 1):
        events.setdefault((c + 2) * per - 1, []).append(functools.partial(core_done, c))
    events.setdefault(tiles - per, []).append(functools.partial(chips_done, 0, steps - 1))

    def body(i, carry):
        slot, c, t = lax.rem(i, 2), lax.div(i, per), lax.rem(i, per)

        @pl.when(c == 0)
        def _():
            pltpu.make_async_copy(weights.at[0, 0], weights.at[0, 0], own_sem.at[0]).wait()
            pltpu.make_async_copy(r_temp, r_temp, own_sem.at[1]).wait()
            weights[slot, 1] = r_temp[...].T

        @pl.when(c > 0)
        def _():
            pltpu.make_async_copy(weights.at[slot], weights.at[slot], weight_sem.at[slot]).wait()

        for n in range(1, per):

            @pl.when(i == n - 1)
            def _():
                for copy in fetch(n):
                    copy.start()

        for n, actions in events.items():

            @pl.when(i == n)
            def _():
                for action in actions:
                    action()

        @pl.when((t == 0) & (c >= 2))
        def _():
            remote(
                send.at[lax.rem(c, 2)], got.at[c], near_send.at[c - 2], near_recv.at[c], sibling
            ).wait_send()

        weight_e, weight_r = weights[slot, 0], weights[slot, 1]
        at = pl.multiple_of(lax.rem(z - c + mp, mp) * extent + t * tile, tile)
        pre = dot(x[...], weight_e) + broad[0:1, pl.ds(at, tile)]
        cumulative = 0.5 * (1.0 + lax.erf(pre * 0.7071067811865476))
        hidden = (pre * cumulative).astype(BF16)
        slope = cumulative + pre * jnp.exp(-0.5 * pre * pre) * (1.0 / math.sqrt(2.0 * math.pi))
        grad_pre = (dot(g[...], weight_r) * slope).astype(BF16)
        line = jnp.sum(grad_pre.astype(F32), axis=0, keepdims=True)
        db[:, pl.ds(pl.multiple_of(i * tile, tile), tile)] = jnp.broadcast_to(line, (8, tile))
        first = pl.ds(pl.multiple_of(2 * t * tile, tile), tile)
        second = pl.ds(pl.multiple_of((2 * t + 1) * tile, tile), tile)
        out = lax.rem(c, 2)
        send[out, :, first] = dot(x_t[half:, :], grad_pre).astype(BF16)
        send[out, :, second] = dot(g_t[half:, :], hidden).astype(BF16)
        keep[c, :, first] = dot(x_t[:half, :], grad_pre).astype(BF16)
        keep[c, :, second] = dot(g_t[:half, :], hidden).astype(BF16)

        @pl.when(t == per - 1)
        def _():
            remote(send.at[out], got.at[c], near_send.at[c], near_recv.at[c], sibling).start()

        out_acc[...] += dot(hidden, weight_r, NT)
        dx_acc[...] += dot(grad_pre, weight_e, NT)
        return carry

    lax.fori_loop(0, tiles, body, 0)
    for c in range(1, full):
        if steps > 1:
            chips_done(c, steps - 1)
    if steps > 1 and full > 1:
        pass

    value, grad, dy = mid[...], g[...].astype(F32), dx_acc[...]
    x[...] = (value + out_acc[...] + narrow[5:6, :]).astype(BF16)
    hat, factor = norm_parts(value)
    back = grad + norm_back(dy, hat, factor, narrow[3:4, :])
    add = lambda v: jnp.sum(v, axis=0, keepdims=True)
    zero = jnp.zeros((4, width), F32)
    sums[...] = jnp.concatenate([add(back), add(dy * hat), add(dy), add(grad), zero], axis=0)
    mid[...] = back
    rounded = back.astype(BF16)
    turned(x_t, rounded)
    near[...] = dot(rounded, weight_o[:, :cut]).astype(BF16)
    far[...] = dot(rounded, weight_o[:, cut:]).astype(BF16)
    results = [
        pltpu.make_async_copy(source, target, load.at[i])
        for i, (source, target) in enumerate(
            ((x, act), (mid, grad_mid), (x_t, branch_t), (near, grad_near), (far, grad_far))
        )
    ]
    for copy in results:
        copy.start()

    core_done(mp - 1)
    for step in reversed(range(steps - 1)):
        for c in range(full):
            chips_done(c, step)
    own_total[...] = keep[0, :block, :].astype(F32)
    for c in range(1, full):
        moved[c - 1] = keep[c, :block, :]
    for c in range(max(0, mp - 2), mp):
        swap_of(c).wait_send()
    for c in range(full):
        for step in range(steps):
            sum_of(c, step).wait_send()
    for c in range(full, mp):
        for copy in outs_of(c):
            copy.wait()
    for copy in list(hops.values()) + list(swaps.values()):
        copy.wait_send()
    for copy in results:
        copy.wait()


def middle(arrays, weights, buffers, parts, plane, mp, hidden):
    dp = plane.size
    rows, width = arrays[0].shape
    extent = hidden // mp
    tile = min(512, extent)
    wide, half, quarter, full = 2 * extent, width // 2, width // 4, mp // 2
    vmem, anywhere = pl.BlockSpec(memory_space=pltpu.VMEM), pl.BlockSpec(memory_space=pl.ANY)
    dma = pltpu.SemaphoreType.DMA
    shape = jax.ShapeDtypeStruct
    near = arrays[1].shape[1]
    late = (quarter, (mp - 2) * wide)
    return pl.pallas_call(
        functools.partial(middle_kernel, plane, mp, tile),
        out_shape=[
            shape((8, width), F32),
            shape((8, hidden), F32),
            shape((width // dp, wide), F32),
            shape((max(full - 1, 1), width // dp, wide), BF16),
            shape((rows, width), BF16),
            shape((rows, width), F32),
            shape((width, rows), BF16),
            shape((rows, near), BF16),
            shape((rows, width - near), BF16),
            shape((quarter, (mp - full) * wide), BF16),
            shape((quarter, (mp - full) * wide), BF16),
            shape((half, wide), BF16),
            shape(late, BF16),
            shape(late, BF16),
            shape(late, BF16),
        ],
        in_specs=[anywhere] * (len(arrays) + len(weights) + len(buffers) + len(parts)),
        out_specs=[vmem] * 4 + [anywhere] * 11,
        scratch_shapes=[
            pltpu.VMEM((rows, width), F32),
            pltpu.VMEM(arrays[1].shape, BF16),
            pltpu.VMEM(arrays[2].shape, BF16),
            pltpu.VMEM((rows, width), BF16),
            pltpu.VMEM((8, width), F32),
            pltpu.VMEM((8, hidden), F32),
            pltpu.VMEM(weights[0].shape, BF16),
            pltpu.VMEM((width, width), BF16),
            pltpu.VMEM((2, 2, width, tile), BF16),
            pltpu.VMEM((tile, width), BF16),
            pltpu.VMEM((rows, width), BF16),
            pltpu.VMEM((width, rows), BF16),
            pltpu.VMEM((width, rows), BF16),
            pltpu.VMEM((width, rows), BF16),
            pltpu.VMEM((rows, width), F32),
            pltpu.VMEM((rows, width), F32),
            pltpu.VMEM((mp, half, wide), BF16),
            pltpu.VMEM((2, half, wide), BF16),
            pltpu.VMEM((mp, half, wide), BF16),
            pltpu.VMEM((full, half, wide), BF16),
            dma((8,)),
            dma((2,)),
            dma((2,)),
            dma((mp, 3)),
            dma((mp, 3)),
            dma((mp, 2)),
            dma((mp, 2)),
            dma((full, plane.steps)),
            dma((full, plane.steps)),
            dma((mp,)),
            dma((mp,)),
            dma((mp, 2)),
        ],
        compiler_params=pltpu.CompilerParams(
            collective_id=3, has_side_effects=True, vmem_limit_bytes=60 * MIB
        ),
        cost_estimate=pl.CostEstimate(flops=6 * 10**10, bytes_accessed=0, transcendentals=0),
        name="middle",
    )(*arrays, *weights, *buffers, *parts)


def finish_kernel(plane, mp, hops, margin, *refs):
    hbm, refs = refs[:17], refs[17:]
    upper, refs = refs[0], refs[1:]
    (grad_tokens, total, vectors), refs = refs[:3], refs[3:]
    loaded, refs = refs[:17], refs[17:]
    (halo_out, halo_in, keep, send, got, more_got, shards, table, sheets), refs = refs[:9], refs[9:]
    (middle, first, second), refs = refs[:3], refs[3:]
    load_sem, halo_send, halo_recv, core_sem, near_send, near_recv, far_send, far_recv = refs[:8]
    z_send, z_recv, send_one, recv_one, send_two, recv_two = refs[8:]
    (dq, dk, dv, att, wq, wk, wv, before_around, before_own) = loaded[:9]
    (around_t, branch_t, others, stream, grad_mid, narrow, early, broad) = loaded[9:]
    dp = plane.size
    d, z = lax.axis_index("dp"), lax.axis_index("mp")
    core = lax.rem(d, 2)
    rows, extent = dq.shape
    half = keep.shape[0]
    block = total.shape[0]
    columns = total.shape[1]
    left = sum(hops)

    loads = [
        pltpu.make_async_copy(source, target, load_sem.at[i])
        for i, (source, target) in enumerate(zip(hbm, loaded))
    ]
    for copy in loads:
        copy.start()
    halo_in[...] = jnp.zeros_like(halo_in)
    meet(d, z, dp, mp)

    def partner(step):
        there = (1 - core) * flipped(d, plane.orders[0][step]) + core * flipped(
            d, plane.orders[1][step]
        )
        return there, z

    top = half // 2
    far = remote(
        upper,
        more_got.at[pl.ds(0, top), :],
        far_send.at[plane.steps - 1],
        far_recv.at[plane.steps - 1],
        partner(plane.steps - 1),
    )
    far.start()
    sent = [far]

    for i in (1, 2, 5, 6, 7):
        loads[i].wait()
    waits, at_left, at_right, at = [], margin, margin + rows, 0
    copies = []
    for hop, reach in enumerate(hops, 1):
        sides = (
            (at_left - reach, z - hop, z + hop, 2 * hop - 2, rows - reach),
            (at_right, z + hop, z - hop, 2 * hop - 1, 0),
        )
        for start, there, back, n, place in sides:
            span = slice(start, start + reach)
            here = pl.ds(at, reach)
            part = dot(dk[span, :], wk[...], NT) + dot(dv[span, :], wv[...], NT)
            halo_out[here, :] = (before_around[span, :] + part).astype(BF16)
            goes = (there >= 0) & (there < mp)
            comes = (back >= 0) & (back < mp)
            copy = remote(
                halo_out.at[here, :],
                halo_in.at[here, :],
                halo_send.at[n],
                halo_recv.at[n],
                (d, there),
            )
            pl.when(goes)(copy.start)
            waits.append((goes, copy.wait_send))
            copies.append((comes, copy.wait_recv, place, at, reach))
            at += reach
        at_left, at_right = at_left - reach, at_right + reach

    for i in (0, 3, 9, 10):
        loads[i].wait()
    inner, everything = slice(margin, margin + rows), slice(None)

    def weight_grads(target, low):
        for n, (source, span, right) in enumerate(
            (
                (around_t, inner, dq),
                (around_t, everything, dk),
                (around_t, everything, dv),
                (branch_t, everything, att),
            )
        ):
            target[:, n * extent : (n + 1) * extent] = dot(
                source[low : low + half, span], right[...]
            ).astype(BF16)

    weight_grads(send, half)
    swap = remote(send, got.at[pl.ds(0, half), :], core_sem.at[0], core_sem.at[1], (flipped(d, 0), z))
    swap.start()
    sent.append(swap)
    weight_grads(keep, 0)

    def fold(target, source, at, count):
        target[:count, :] = added(target[:count, :], source[pl.ds(at, count), :])

    swap.wait_recv()
    fold(keep, got, 0, half)
    loads[4].wait()
    loads[8].wait()
    own = before_own[...] + before_around[inner, :] + dot(dq[...], wq[...], NT)
    own += dot(dk[inner, :], wk[...], NT) + dot(dv[inner, :], wv[...], NT)
    before_own[...] = own
    count, at_near, at_far = half, half, 0
    loads[11].wait()
    for step in reversed(range(plane.steps)):
        count //= 2
        near = remote(
            keep.at[pl.ds(count, count), :],
            got.at[pl.ds(at_near, count), :],
            near_send.at[step],
            near_recv.at[step],
            partner(step),
        )
        near.start()
        sent.append(near)
        far.wait_recv()
        fold(others, more_got, at_far, count)
        at_far += count
        if step:
            far = remote(
                others.at[pl.ds(count // 2, count // 2), :],
                more_got.at[pl.ds(at_far, count // 2), :],
                far_send.at[step - 1],
                far_recv.at[step - 1],
                partner(step - 1),
            )
            far.start()
            sent.append(far)
        near.wait_recv()
        fold(keep, got, at_near, count)
        at_near += count
    for r in range(1, mp):
        copy = remote(
            others.at[pl.ds(0, block), pl.ds((r - 1) * columns, columns)],
            shards.at[r],
            z_send.at[r],
            z_recv.at[r],
            (d, lax.rem(z - r + mp, mp)),
        )
        copy.start()
        sent.append(copy)

    for i in range(12, 17):
        loads[i].wait()
    for comes, wait, *_ in copies:
        pl.when(comes)(wait)
    for _, _, place, at, reach in copies:
        span = slice(place, place + reach)
        before_own[span, :] = before_own[span, :] + halo_in[at : at + reach, :].astype(F32)
    hat, factor = norm_parts(stream[...])
    upstream = before_own[...]
    add = lambda v: jnp.sum(v, axis=0, keepdims=True)
    back = grad_mid[...] + norm_back(upstream, hat, factor, narrow[0:1, :])
    grad_tokens[...] = back.astype(BF16)
    table[...] = early[...]
    table[0:1, :] = add(upstream * hat)
    table[1:2, :] = add(upstream)
    mine = pl.ds(pl.multiple_of(z * extent, extent), extent)
    table[6:7, mine] = add(dq[...].astype(F32))
    table[7:8, mine] = add(dv[...].astype(F32))
    each = dp // (early.shape[1] // 128)
    for i in range(dp):
        c = i // each
        sheets[i, 0:8, :] = table[:, c * 128 : (c + 1) * 128]
        sheets[i, 8:16, :] = broad[i]
    along_dp = lambda step: (lax.rem(d + step, dp), z)
    along_mp = lambda step: (d, lax.rem(z + step, mp))
    out = peers_start(sheets, second, send_two, recv_two, along_dp, d, dp, True)
    peers_finish(out, second, recv_two, d, dp)
    middle[0] = jnp.sum(second[...], axis=0)
    out = peers_start(middle, first, send_one, recv_one, along_mp, z, mp, False)

    full = keep[:block, :].astype(F32)
    for r in range(1, mp):
        pltpu.make_async_copy(shards.at[r], shards.at[r], z_recv.at[r]).wait()
        full += shards[r].astype(F32)
    total[...] = full
    peers_finish(out, first, recv_one, z, mp)
    vectors[...] = jnp.sum(first[...], axis=0)
    for copy in sent:
        copy.wait_send()
    for when, wait in waits:
        pl.when(when)(wait)


def finish(arrays, upper, plane, mp, hops, margin):
    dp = plane.size
    rows, extent = arrays[0].shape
    width = arrays[4].shape[0]
    block, half, columns = width // dp, width // 2, 4 * extent
    vmem, anywhere = pl.BlockSpec(memory_space=pltpu.VMEM), pl.BlockSpec(memory_space=pl.ANY)
    dma = pltpu.SemaphoreType.DMA
    left = sum(hops)
    return pl.pallas_call(
        functools.partial(finish_kernel, plane, mp, hops, margin),
        out_shape=[
            jax.ShapeDtypeStruct((rows, width), BF16),
            jax.ShapeDtypeStruct((block, columns), F32),
            jax.ShapeDtypeStruct((16, 128), F32),
        ],
        in_specs=[anywhere] * (len(arrays) + 1),
        out_specs=[vmem] * 3,
        scratch_shapes=[pltpu.VMEM(item.shape, item.dtype) for item in arrays]
        + [
            pltpu.VMEM((2 * left, width), BF16),
            pltpu.VMEM((2 * left, width), BF16),
            pltpu.VMEM((half, columns), BF16),
            pltpu.VMEM((half, columns), BF16),
            pltpu.VMEM((2 * half, columns), BF16),
            pltpu.VMEM((half, (mp - 1) * columns), BF16),
            pltpu.VMEM((mp, block, columns), BF16),
            pltpu.VMEM((8, width), F32),
            pltpu.VMEM((dp, 16, 128), F32),
            pltpu.VMEM((1, 16, 128), F32),
            pltpu.VMEM((mp, 16, 128), F32),
            pltpu.VMEM((dp, 16, 128), F32),
            dma((len(arrays),)),
            dma((2 * len(hops),)),
            dma((2 * len(hops),)),
            dma((2,)),
            dma((plane.steps,)),
            dma((plane.steps,)),
            dma((plane.steps,)),
            dma((plane.steps,)),
            dma((mp,)),
            dma((mp,)),
            dma((mp,)),
            dma((mp,)),
            dma((dp,)),
            dma((dp,)),
        ],
        compiler_params=pltpu.CompilerParams(
            collective_id=2, has_side_effects=True, vmem_limit_bytes=60 * MIB
        ),
        cost_estimate=pl.CostEstimate(flops=5 * 10**10, bytes_accessed=0, transcendentals=0),
        name="finish",
    )(*arrays, upper)


def local(
    tokens,
    kept_index,
    lengths,
    first_gain,
    first_shift,
    query_weight,
    key_weight,
    value_weight,
    query_bias,
    value_bias,
    output_weight,
    output_bias,
    second_gain,
    second_shift,
    expand_weight,
    expand_bias,
    reduce_weight,
    reduce_bias,
    cotangent,
):
    dp, mp = lax.axis_size("dp"), lax.axis_size("mp")
    d, z = lax.axis_index("dp"), lax.axis_index("mp")
    plane = Plane(dp)
    rows, width = tokens.shape
    group_rows = rows * mp
    block = width // dp
    full_hidden = expand_weight.shape[1] * mp
    meta = jnp.concatenate([z[None], plane.order(d)]).astype(jnp.int32)

    own_rows = lambda w: lax.dynamic_slice_in_dim(w, d * block, block, 0)
    own_columns = lambda w: lax.dynamic_slice_in_dim(w, d * block, block, 1).T
    first = jnp.concatenate(
        [
            own_rows(query_weight),
            own_rows(key_weight),
            own_rows(value_weight),
            own_columns(output_weight),
        ],
        axis=1,
    )
    second = jnp.concatenate([own_rows(expand_weight), own_columns(reduce_weight)], axis=1)
    singles = (
        first_gain,
        first_shift,
        output_bias,
        second_gain,
        second_shift,
        reduce_bias,
        query_bias,
        value_bias,
    )
    single, wide = first_gain.shape[0], expand_bias.shape[0]
    me = d * mp + z
    lane = jnp.arange(128, dtype=jnp.int32)
    lines = full_hidden // dp // 128

    def placed(stack):
        count = 128 // stack.shape[1]
        return jnp.where(lane // stack.shape[1] == me % count, jnp.tile(stack, (1, count)), 0.0)

    line = placed(expand_bias[None].astype(F32))
    at_line = (jnp.arange(8, dtype=jnp.int32) == me * wide // 128 % lines)[:, None]
    sheet = jnp.concatenate(
        [placed(jnp.stack(singles).astype(F32)), jnp.where(at_line, line, 0.0)], axis=0
    )
    length = lengths[0]
    clips = length.shape[0]
    index = jnp.arange(clips, dtype=jnp.int32)
    ends = jnp.sum(jnp.where(index[None, :] <= index[:, None], length[None, :], 0), axis=1)
    starts = ends - length
    reach, hops, left = LONGEST - 1, [], 0
    while reach > 0:
        extent = min(rows, -(-reach // 64) * 64)
        hops.append(extent)
        left, reach = left + extent, reach - extent
    margin = -(-left // 128) * 128
    while (2 * margin + rows) % TILE:
        margin += 128
    window = 2 * margin + rows
    base = z * rows - margin
    places = base + jnp.arange(window, dtype=jnp.int32)
    labels = jnp.sum((places[:, None] >= ends[None, :]).astype(jnp.int32), axis=1)
    labels = jnp.where((places >= 0) & (places < group_rows), labels, -1)
    label_own = labels[margin : margin + rows]
    limits = []
    for i in range(rows // TILE):
        low = z * rows + i * TILE
        last = low + TILE - 1
        start = jnp.sum(jnp.where(ends <= low, length, 0))
        end = jnp.sum(jnp.where(starts <= last, length, 0))
        limits.append(lax.div(start - base, TILE))
        limits.append(lax.div(end - base + TILE - 1, TILE))
    bounds = jnp.stack(limits).astype(jnp.int32)

    begun = begin(
        sheet[None],
        first,
        tokens,
        jnp.broadcast_to(kept_index[:, None], (rows, 128)),
        jnp.asarray(position_lines(width)),
        plane,
        mp,
        hops,
        margin,
        full_hidden,
    )
    narrow, broad, stream, around = begun[:4]
    buffers = begun[4:]
    normed_one = around[margin : margin + rows]
    scale = 1.0 / math.sqrt(HEAD_SIZE)
    shares = {1: shifted(second, 1, mp)}
    around_t = turned_rows(around, meta, block)
    projections = (query_weight, key_weight, value_weight)
    label_rows = jnp.broadcast_to(label_own[:, None], (rows, 128))
    label_line = jnp.broadcast_to(labels[None, :], (8, window))
    pairs = width // (2 * HEAD_SIZE) // mp
    heads = [
        project(normed_one, around, projections if own else buffers, narrow, meta, block, mp, own)
        for own in (True, False)
    ]
    heads[1] = lax.optimization_barrier((*heads[1], shares[1]))[:3]
    for r in range(2, mp):
        shares[r] = shifted(after(second, shares[1]), r, mp)
    early = spread_chips(shares[1], plane)
    later = [early[1]] + [shares[r] for r in range(2, mp)]
    far, late = (), []
    for r in range(1, mp):
        part = ((r - 1) * pairs, pairs, (mp - 1) * pairs)
        far = attention_forward(
            after(bounds, *far, *later[: r - 1]), *heads[1], label_rows, label_line, part, far
        )
        if r == 1:
            early = join(early, 0)
            early = (early, lax.ppermute(early, "dp", plane.pairs(plane.steps - 1)))
        else:
            late.extend(spread_chips(shares[r], plane))
    near = attention_forward(
        after(bounds, *far, *late[: 2 * mp - 6]), *heads[0], label_rows, label_line, (0, pairs, pairs)
    )
    attended, lses = [near[0], far[0]], [near[1], far[1]]

    results = middle(
        (stream, *attended, cotangent, narrow, broad),
        (output_weight, expand_weight, reduce_weight),
        buffers,
        (*early, *late),
        plane,
        mp,
        full_hidden,
    )
    sums_mid, grad_bias, own_two, ready = results[:4]
    activations, grad_middle, branch_t, grad_near, grad_far, kept, upper = results[4:11]
    full = mp // 2
    moved_one = [
        lax.ppermute(ready[r - 1], "mp", [(j, (j - r) % mp) for j in range(mp)])
        for r in range(1, full)
    ]
    sums_two = Scatter(kept, upper, list(range(full, mp)), plane, mp)

    label_line = jnp.broadcast_to(label_own[None, :], (8, rows))
    label_rows = jnp.broadcast_to(labels[:, None], (window, 128))
    grads_far = ()
    for r in range(1, mp):
        part = ((r - 1) * pairs, pairs, (mp - 1) * pairs)
        tied = after(bounds, *grads_far, sums_two.got) if r == mp - 1 else after(bounds, *grads_far)
        grads_far = attention_backward(
            tied,
            *heads[1],
            grad_far,
            attended[1],
            lses[1],
            label_line,
            label_rows,
            part,
            tuple(grads_far),
        )
    while sums_two.step > 0:
        sums_two.next()
    grads_far = lax.optimization_barrier((*grads_far, sums_two.got))[:3]
    sums_two.last()
    partial = tail(around_t, branch_t, grads_far, attended[1], buffers, meta, block, mp, margin)
    swapped = lax.ppermute(partial[3], "dp", plane.siblings())
    grads_near = attention_backward(
        after(bounds, partial[0]),
        *heads[0],
        grad_near,
        attended[0],
        lses[0],
        label_line,
        label_rows,
        (0, pairs, pairs),
    )

    turned = jnp.mod(z - jnp.arange(mp, dtype=jnp.int32), mp)
    pick = turned[:, None] == jnp.arange(mp, dtype=jnp.int32)[None, :]

    def in_turn(v):
        parts = v.reshape(v.shape[0], 1, mp, v.shape[1] // mp)
        return jnp.sum(jnp.where(pick[None, :, :, None], parts, 0.0), axis=2).reshape(v.shape)

    bias_sums = in_turn(jnp.pad(partial[4][:2], ((0, 0), (width // mp, 0))))
    early = jnp.concatenate([jnp.zeros((2, width), F32), sums_mid[:4], bias_sums], axis=0)
    broad_sum = in_turn(grad_bias[:1])
    broad_part = jnp.pad(broad_sum.reshape(dp, lines, 128), ((0, 0), (0, 8 - lines), (0, 0)))
    lower, upper = folded(partial[2], swapped)
    grad_tokens, total_one, summed = finish(
        (
            *grads_near,
            attended[0],
            *projections,
            partial[1],
            partial[0],
            around_t,
            branch_t,
            lower,
            stream,
            grad_middle,
            narrow,
            early,
            broad_part,
        ),
        upper,
        plane,
        mp,
        hops,
        margin,
    )

    extent = width // mp
    grad_query, grad_key, grad_value, grad_out = [
        total_one[:, i * extent : (i + 1) * extent] for i in range(4)
    ]
    total_two = own_two
    for item in lax.optimization_barrier((*moved_one, *sums_two.moved, total_one))[:-1]:
        total_two = total_two + item.astype(F32)
    extent = full_hidden // mp
    tile = min(512, extent)
    slabs = [total_two[:, i * tile : (i + 1) * tile] for i in range(2 * extent // tile)]
    grad_expand = jnp.concatenate(slabs[0::2], axis=1)
    grad_reduce = jnp.concatenate(slabs[1::2], axis=1)

    taken = lambda stack, extent: lax.dynamic_slice_in_dim(
        stack, me % (128 // extent) * extent, extent, 1
    )
    small = taken(summed[:8], single)
    broad_row = lax.dynamic_slice_in_dim(summed[8:], me * wide // 128 % lines, 1, 0)
    return (
        activations,
        grad_tokens,
        grad_query,
        grad_key,
        grad_value,
        grad_out.T,
        grad_expand,
        grad_reduce.T,
        small[0],
        small[1],
        small[6],
        small[7],
        small[2],
        small[3],
        small[4],
        taken(broad_row, wide)[0],
        small[5],
    )


def solution(mesh):
    vector = P(("dp", "mp"))
    tall = P(("dp", "mp"), None)
    in_specs = (
        tall,
        vector,
        P("dp", None),
        vector,
        vector,
        P(None, "mp"),
        P(None, "mp"),
        P(None, "mp"),
        vector,
        vector,
        P("mp", None),
        vector,
        vector,
        vector,
        P(None, "mp"),
        vector,
        P("mp", None),
        vector,
        tall,
    )
    out_specs = (
        tall,
        tall,
        P("dp", "mp"),
        P("dp", "mp"),
        P("dp", "mp"),
        P("mp", "dp"),
        P("dp", "mp"),
        P("mp", "dp"),
    ) + (vector,) * 9
    return jax.shard_map(local, mesh=mesh, in_specs=in_specs, out_specs=out_specs, check_vma=False)
```

```python
import functools
import math

import jax
import jax.numpy as jnp
import numpy as np
from jax import lax
from jax.experimental import pallas as pl
from jax.experimental.pallas import tpu as pltpu
from jax.sharding import PartitionSpec as P

HEAD_SIZE = 64
LONGEST = 549
EPSILON = 1e-06
TILE = 256
PAIR = 2 * HEAD_SIZE
PAIRS = 2
MIB = 1024 * 1024
F32 = jnp.float32
BF16 = jnp.bfloat16

NN = (((1,), (0,)), ((), ()))
NT = (((1,), (1,)), ((), ()))
TN = (((0,), (0,)), ((), ()))


def dot(left, right, dims=NN):
    return lax.dot_general(left, right, dims, preferred_element_type=F32)


def position_lines(extent):
    quarter = extent // 4
    spatial = (extent - quarter) // 2
    table = np.zeros((128, extent), np.float32)
    at, first = 0, 0
    for count, part in ((8, quarter), (14, spatial), (14, spatial)):
        half = part // 2
        inverse = np.exp(np.arange(half, dtype=np.float32) * np.float32(-math.log(10000.0) / half))
        angles = np.arange(count, dtype=np.float32)[:, None] * inverse[None, :]
        table[first : first + count, at : at + half] = np.sin(angles)
        table[first : first + count, at + half : at + part] = np.cos(angles)
        at, first = at + part, first + count
    return table


def norm_parts(values):
    center = values - jnp.mean(values, axis=-1, keepdims=True)
    spread = jnp.mean(center * center, axis=-1, keepdims=True)
    factor = lax.rsqrt(spread + EPSILON)
    return center * factor, factor


def norm_back(upstream, hat, factor, gain):
    scaled = upstream * gain
    first = jnp.mean(scaled, axis=-1, keepdims=True)
    second = jnp.mean(scaled * hat, axis=-1, keepdims=True)
    return factor * (scaled - first - hat * second)


def clip_label(places, scal, clips, rows, mp):
    label, end = jnp.zeros_like(places), 0
    for c in range(clips):
        end = end + scal[1 + c]
        label = label + (places >= end).astype(jnp.int32)
    return jnp.where((places >= 0) & (places < rows * mp), label, -1)


def tile_range(first, last, base, scal, clips):
    start, end, stop = 0, 0, 0
    for c in range(clips):
        length = scal[1 + c]
        stop = jnp.where(end <= last, end + length, stop)
        end = end + length
        start = jnp.where(end <= first, end, start)
    return lax.div(start - base, TILE), lax.div(stop - base + TILE - 1, TILE)


def forward_kernel(layout, scal, q_ref, k_ref, v_ref, o_ref, lse_ref, s_ref, lq_ref, lk_ref):
    clips, mp = layout
    rows, window = q_ref.shape[0], k_ref.shape[0]
    base = scal[0] * rows - (window - rows) // 2

    @pl.when(pl.program_id(0) == 0)
    def _():
        own = scal[0] * rows + lax.broadcasted_iota(jnp.int32, lq_ref.shape, 1)
        lq_ref[...] = clip_label(own, scal, clips, rows, mp)
        around = base + lax.broadcasted_iota(jnp.int32, lk_ref.shape, 0)
        lk_ref[...] = clip_label(around, scal, clips, rows, mp)

    row = lax.broadcasted_iota(jnp.int32, (2 * HEAD_SIZE, TILE), 0)
    beside = lambda pair: jnp.concatenate(pair, axis=1)
    groups = lambda array: array.reshape(TILE // 8, 8, 2 * TILE)
    pairs = q_ref.shape[1] // PAIR
    for block in range(rows // TILE):
        first = scal[0] * rows + block * TILE
        low, high = tile_range(first, first + TILE - 1, base, scal, clips)
        span = slice(block * TILE, (block + 1) * TILE)
        query_th = []
        for g in range(pairs):
            query_t = q_ref[span, g * PAIR : (g + 1) * PAIR].T
            zero = jnp.zeros_like(query_t)
            query_th.append(
                beside(
                    [
                        jnp.where(row < HEAD_SIZE, query_t, zero),
                        jnp.where(row < HEAD_SIZE, zero, query_t),
                    ]
                )
            )
        label = lq_ref[0:1, span]
        label = beside([label, label])

        def scores(t, carry):
            at = pl.multiple_of(t * TILE, TILE)
            same = beside([lk_ref[pl.ds(at, TILE), :]] * 4) == label
            out = []
            for g in range(pairs):
                key = k_ref[pl.ds(at, TILE), g * PAIR : (g + 1) * PAIR]
                s = jnp.where(same, dot(key, query_th[g]), -1e30)
                s_ref[g, pl.ds(at, TILE), :] = s
                out.append(jnp.maximum(carry[g], jnp.max(groups(s), axis=0)))
            return tuple(out)

        least = jnp.full((8, 2 * TILE), -1e30, F32)
        peaks = lax.fori_loop(low, high, scores, (least,) * pairs)
        peaks = [jnp.max(item, axis=0, keepdims=True) for item in peaks]

        def blend(t, carry):
            at = pl.multiple_of(t * TILE, TILE)
            out = []
            for g in range(pairs):
                total, *accs = carry[g]
                p = jnp.exp(s_ref[g, pl.ds(at, TILE), :] - peaks[g])
                weights = p.astype(BF16)
                value_t = v_ref[pl.ds(at, TILE), g * PAIR : (g + 1) * PAIR].T
                total = total + jnp.sum(groups(p), axis=0)
                parts = [
                    accs[h]
                    + dot(
                        value_t[h * HEAD_SIZE : (h + 1) * HEAD_SIZE],
                        weights[:, h * TILE : (h + 1) * TILE],
                    )
                    for h in range(2)
                ]
                out.append((total, *parts))
            return tuple(out)

        zero = jnp.zeros((HEAD_SIZE, TILE), F32)
        start = (jnp.zeros((8, 2 * TILE), F32), zero, zero)
        done = lax.fori_loop(low, high, blend, (start,) * pairs)
        for g in range(pairs):
            total, *accs = done[g]
            total = jnp.sum(total, axis=0, keepdims=True)
            lse = peaks[g] + jnp.log(total)
            for h in range(2):
                columns = slice(h * TILE, (h + 1) * TILE)
                lse_ref[g, h : h + 1, span] = lse[:, columns]
                accs[h] = accs[h] / total[:, columns]
            o_ref[span, g * PAIR : (g + 1) * PAIR] = jnp.concatenate(accs, axis=0).T.astype(BF16)


def backward_kernel(
    layout,
    scal,
    q_ref,
    k_ref,
    v_ref,
    do_ref,
    o_ref,
    lse_ref,
    dq_ref,
    dk_ref,
    dv_ref,
    dk_acc,
    dv_acc,
    lq_ref,
    lk_ref,
):
    clips, mp = layout
    rows, window = q_ref.shape[0], k_ref.shape[0]
    base = scal[0] * rows - (window - rows) // 2

    @pl.when(pl.program_id(0) == 0)
    def _():
        own = scal[0] * rows + lax.broadcasted_iota(jnp.int32, lq_ref.shape, 1)
        lq_ref[...] = clip_label(own, scal, clips, rows, mp)
        around = base + lax.broadcasted_iota(jnp.int32, lk_ref.shape, 0)
        lk_ref[...] = clip_label(around, scal, clips, rows, mp)

    lane = lax.broadcasted_iota(jnp.int32, (TILE, 2 * HEAD_SIZE), 1)
    row = lax.broadcasted_iota(jnp.int32, (2 * HEAD_SIZE, TILE), 0)
    dk_acc[...] = jnp.zeros_like(dk_acc)
    dv_acc[...] = jnp.zeros_like(dv_acc)

    def halves(array, where):
        zero = jnp.zeros_like(array)
        return [jnp.where(where < HEAD_SIZE, array, zero), jnp.where(where < HEAD_SIZE, zero, array)]

    beside = lambda pair: jnp.concatenate(pair, axis=1)
    pairs = q_ref.shape[1] // PAIR
    for block in range(rows // TILE):
        first = scal[0] * rows + block * TILE
        low, high = tile_range(first, first + TILE - 1, base, scal, clips)
        span = slice(block * TILE, (block + 1) * TILE)
        label = lq_ref[0:1, span]
        label = beside([label, label])
        fixed = []
        for g in range(pairs):
            own = slice(g * PAIR, (g + 1) * PAIR)
            query, grad = q_ref[span, own], do_ref[span, own]
            query_t, grad_t = query.T, grad.T
            product = grad_t.astype(F32) * o_ref[span, own].T.astype(F32)
            delta = beside(
                [
                    jnp.sum(product[h * HEAD_SIZE : (h + 1) * HEAD_SIZE], axis=0, keepdims=True)
                    for h in range(2)
                ]
            )
            lse = beside([lse_ref[g, h : h + 1, span] for h in range(2)])
            query_h = jnp.concatenate(halves(query, lane), axis=0)
            grad_h = jnp.concatenate(halves(grad, lane), axis=0)
            query_th, grad_th = beside(halves(query_t, row)), beside(halves(grad_t, row))
            fixed.append((own, delta, lse, query_h, grad_h, query_th, grad_th))

        def step(t, carry):
            at = pl.multiple_of(t * TILE, TILE)
            same = beside([lk_ref[pl.ds(at, TILE), :]] * 4) == label
            out = []
            for g in range(pairs):
                own, delta, lse, query_h, grad_h, query_th, grad_th = fixed[g]
                key, value = k_ref[pl.ds(at, TILE), own], v_ref[pl.ds(at, TILE), own]
                key_t = key.T
                p = jnp.where(same, jnp.exp(dot(key, query_th) - lse), 0.0)
                ds = (p * (dot(value, grad_th) - delta)).astype(BF16)
                dv_acc[pl.ds(at, TILE), own] += dot(p.astype(BF16), grad_h)
                dk_acc[pl.ds(at, TILE), own] += dot(ds, query_h)
                out.extend(
                    carry[2 * g + h]
                    + dot(
                        key_t[h * HEAD_SIZE : (h + 1) * HEAD_SIZE], ds[:, h * TILE : (h + 1) * TILE]
                    )
                    for h in range(2)
                )
            return tuple(out)

        zero = jnp.zeros((HEAD_SIZE, TILE), F32)
        parts = lax.fori_loop(low, high, step, (zero,) * (2 * pairs))
        for g in range(pairs):
            total = jnp.concatenate(parts[2 * g : 2 * g + 2], axis=0) * (1.0 / math.sqrt(HEAD_SIZE))
            dq_ref[span, fixed[g][0]] = total.T.astype(BF16)
    dk_ref[...] = dk_acc[...].astype(BF16)
    dv_ref[...] = dv_acc[...].astype(BF16)


def attention_call(kernel, name, scal, columns, others, outs, scratch, part, before, work):
    first, count, total = part
    each = min(PAIRS, count)
    pair, first, count = each * PAIR, first // each, count // each
    anywhere = pl.BlockSpec(memory_space=pl.ANY)
    column = lambda item: pl.BlockSpec((item.shape[0], pair), lambda p, b: (0, first + p))
    result = pl.pallas_call(
        kernel,
        grid_spec=pltpu.PrefetchScalarGridSpec(
            num_scalar_prefetch=1,
            grid=(count,),
            in_specs=[column(item) for item in columns]
            + [
                pl.BlockSpec((each,) + item.shape[1:], lambda p, b: (first + p, 0, 0))
                if item.ndim == 3
                else pl.BlockSpec(item.shape, lambda p, b: (0, 0))
                for item in others
            ]
            + [anywhere] * len(before),
            out_specs=[
                pl.BlockSpec((each,) + shape[1:], lambda p, b: (first + p, 0, 0))
                if len(shape) == 3
                else pl.BlockSpec((shape[0], pair), lambda p, b: (0, first + p))
                for shape, _ in outs
            ],
            scratch_shapes=scratch,
        ),
        out_shape=[jax.ShapeDtypeStruct(shape, kind) for shape, kind in outs],
        input_output_aliases={
            1 + len(columns) + len(others) + i: i for i in range(len(before))
        },
        compiler_params=pltpu.CompilerParams(vmem_limit_bytes=32 * MIB),
        cost_estimate=pl.CostEstimate(flops=count * each * work, bytes_accessed=0, transcendentals=0),
        name=name,
    )(scal, *columns, *others, *before)
    return result


def attention_forward(scal, mp, queries, keys, values, part, before=()):
    rows, width = queries.shape
    window = keys.shape[0]

    def kernel(*refs):
        forward_kernel((scal.shape[0] - 1, mp), *refs[:4], *refs[4 + len(before) :])

    return attention_call(
        kernel,
        "attention_forward",
        scal,
        (queries, keys, values),
        (),
        [((rows, width), BF16), ((part[2], 2, rows), F32)],
        [
            pltpu.VMEM((min(PAIRS, part[1]), window, 2 * TILE), F32),
            pltpu.VMEM((8, rows), jnp.int32),
            pltpu.VMEM((window, 128), jnp.int32),
        ],
        part,
        before,
        5 * 10**9,
    )


def attention_backward(scal, mp, queries, keys, values, grads, attended, lse, part, before=()):
    rows, width = queries.shape
    window = keys.shape[0]

    def kernel(*refs):
        backward_kernel((scal.shape[0] - 1, mp), *refs[:7], *refs[7 + len(before) :])

    return attention_call(
        kernel,
        "attention_backward",
        scal,
        (queries, keys, values, grads, attended),
        (lse,),
        [((rows, width), BF16), ((window, width), BF16), ((window, width), BF16)],
        [pltpu.VMEM((window, min(PAIRS, part[1]) * PAIR), F32)] * 2
        + [pltpu.VMEM((8, rows), jnp.int32), pltpu.VMEM((window, 128), jnp.int32)],
        part,
        before,
        6 * 10**9,
    )


def assemble(target, buffers, meta, block, first=0):
    each = buffers[0].shape[0] // block
    span = slice(first, first + buffers[0].shape[1])
    for i in range(len(buffers) * each):
        at = pl.multiple_of(meta[1 + i] * block, block)
        source = buffers[i // each]
        target[pl.ds(at, block), span] = source[i % each * block : (i % each + 1) * block, :]


def turn(target, source, meta, block, lead):
    lead[...] = source.T
    for i in range(target.shape[0] // block):
        at = pl.multiple_of(meta[1 + i] * block, block)
        target[i * block : (i + 1) * block, :] = lead[pl.ds(at, block), :]


def fixed(shape):
    return pl.BlockSpec(shape, lambda *_: (0,) * len(shape), pipeline_mode=pl.Buffered(1))


def call(kernel, name, grid, meta, ins, outs, scratch, vmem, flops, moved=0):
    return pl.pallas_call(
        kernel,
        grid_spec=pltpu.PrefetchScalarGridSpec(
            num_scalar_prefetch=1,
            grid=grid,
            in_specs=[spec for _, spec in ins],
            out_specs=[spec for _, _, spec in outs],
            scratch_shapes=scratch,
        ),
        out_shape=[jax.ShapeDtypeStruct(shape, kind) for shape, kind, _ in outs],
        compiler_params=pltpu.CompilerParams(vmem_limit_bytes=vmem * MIB),
        cost_estimate=pl.CostEstimate(flops=flops, bytes_accessed=moved, transcendentals=0),
        name=name,
    )(meta, *[array for array, _ in ins])


def turn_kernel(block, meta, source, target, lead):
    turn(target, source[...], meta, block, lead)


def turned_rows(source, meta, block):
    rows, width = source.shape
    return call(
        functools.partial(turn_kernel, block),
        "turn",
        (1,),
        meta,
        [(source, fixed(source.shape))],
        [((width, rows), BF16, fixed((width, rows)))],
        [pltpu.VMEM((width, rows), BF16)],
        24,
        4 * 10**9,
    )[0]


def project_kernel(block, scale, own, meta, x, around, bias, *refs):
    weights, (q, k, v), scratch = refs[:-6], refs[-6:-3], refs[-3:]
    if own:
        scratch = weights
    else:
        for w in range(3):
            assemble(scratch[w], weights[4 * w : 4 * w + 4], meta, block)
    q[...] = (dot(x[...], scratch[0][...]) + bias[6:7, :]).astype(BF16) * jnp.asarray(scale, BF16)
    k[...] = dot(around[...], scratch[1][...]).astype(BF16)
    v[...] = (dot(around[...], scratch[2][...]) + bias[7:8, :]).astype(BF16)


def gathered_specs(buffers, kinds, extent, stride):
    return [
        (item, pl.BlockSpec((item.shape[0], extent), lambda i, m, kind=kind: (0, i * stride + kind)))
        for kind in kinds
        for item in buffers
    ]


def project(x, around, weights, narrow, meta, block, mp, own):
    rows, width = x.shape
    window = around.shape[0]
    extent = width // mp
    first, count = (0, 1) if own else (1, mp - 1)
    column = lambda n: pl.BlockSpec((n, extent), lambda i, m: (0, i))
    turned = lambda i, m: (0, lax.rem(m[0] - first - i + mp, mp))
    return call(
        functools.partial(project_kernel, block, 1.0 / math.sqrt(HEAD_SIZE), own),
        "project",
        (count,),
        meta,
        [
            (x, fixed(x.shape)),
            (around, fixed(around.shape)),
            (narrow, pl.BlockSpec((8, extent), turned)),
        ]
        + (
            [(w, fixed(w.shape)) for w in weights]
            if own
            else gathered_specs(weights, (0, 1, 2), extent, 4)
        ),
        [
            ((rows, count * extent), BF16, column(rows)),
            ((window, count * extent), BF16, column(window)),
            ((window, count * extent), BF16, column(window)),
        ],
        [pltpu.VMEM((width, extent), BF16)] * 3,
        40,
        count * 4 * 10**9,
    )


def tail_kernel(block, margin, meta, around_t, branch_t, dq, dk, dv, att, *refs):
    got, (own_out, around_out, keep, send, bias), weights = refs[:12], refs[12:17], refs[17:]
    for w in range(3):
        assemble(weights[w], got[4 * w : 4 * w + 4], meta, block)
    step = pl.program_id(0)
    rows, half, extent = dq.shape[0], keep.shape[0], dq.shape[1]
    back = dot(dk[...], weights[1][...], NT) + dot(dv[...], weights[2][...], NT)
    more = dot(dq[...], weights[0][...], NT)

    @pl.when(step == 0)
    def _():
        around_out[...] = back
        own_out[...] = more

    @pl.when(step > 0)
    def _():
        around_out[...] += back
        own_out[...] += more

    middle, everything = slice(margin, margin + rows), slice(None)
    for at, (left, span, right) in enumerate(
        (
            (around_t, middle, dq),
            (around_t, everything, dk),
            (around_t, everything, dv),
            (branch_t, everything, att),
        )
    ):
        columns = slice(at * extent, (at + 1) * extent)
        keep[:, columns] = dot(left[:half, span], right[...]).astype(BF16)
        send[:, columns] = dot(left[half:, span], right[...]).astype(BF16)
    add = lambda v: jnp.sum(v[...].astype(F32), axis=0, keepdims=True)
    bias[...] = jnp.concatenate([add(dq), add(dv), jnp.zeros((6, extent), F32)], axis=0)


def tail(around_t, branch_t, grads, att, weights, meta, block, mp, margin):
    dq, dk, dv = grads
    rows, width = dq.shape[0], around_t.shape[0]
    window = around_t.shape[1]
    extent = width // mp
    half = width // 2
    count = mp - 1
    column = lambda n: pl.BlockSpec((n, extent), lambda i, m: (0, i))
    wide = pl.BlockSpec((half, 4 * extent), lambda i, m: (0, i))
    return call(
        functools.partial(tail_kernel, block, margin),
        "tail",
        (count,),
        meta,
        [(item, fixed(item.shape)) for item in (around_t, branch_t)]
        + [(dq, column(rows)), (dk, column(window)), (dv, column(window)), (att, column(rows))]
        + gathered_specs(weights, (0, 1, 2), extent, 4),
        [
            ((rows, width), F32, fixed((rows, width))),
            ((window, width), F32, fixed((window, width))),
            ((half, 4 * count * extent), BF16, wide),
            ((half, 4 * count * extent), BF16, wide),
            ((8, count * extent), F32, column(8)),
        ],
        [pltpu.VMEM((width, extent), BF16)] * 3,
        60,
        count * 8 * 10**9,
    )


def join(parts, axis):
    return jnp.concatenate(parts, axis=axis)


class Plane:
    def __init__(self, size):
        self.size = size
        bits = list(range(1, size.bit_length() - 1))
        turn = len(bits) // 2
        self.orders = [bits, bits[turn:] + bits[:turn]]
        held = []
        for order in self.orders:
            masks = [0]
            for bit in order:
                masks = masks + [m ^ (1 << bit) for m in masks]
            held.append(masks)
        self.masks = [held[c] + [1 ^ m for m in held[1 - c]] for c in range(2)]
        self.steps = len(bits)

    def pairs(self, step):
        return [(i, i ^ (1 << self.orders[i % 2][step])) for i in range(self.size)]

    def siblings(self):
        return [(i, i ^ 1) for i in range(self.size)]

    def order(self, d):
        return jnp.bitwise_xor(jnp.array(self.masks, jnp.int32)[d % 2], d)


def shifted(payload, r, mp):
    return lax.ppermute(payload, "mp", [(i, (i + r) % mp) for i in range(mp)])


def spread_chips(held, plane):
    for step in range(plane.steps - 2):
        held = join([held, lax.ppermute(held, "dp", plane.pairs(step))], 0)
    return held, lax.ppermute(held, "dp", plane.pairs(plane.steps - 2))


def added(left, right):
    return (left.astype(F32) + right.astype(F32)).astype(BF16)


def folded(keep, got):
    half = keep.shape[0] // 2
    return added(keep[:half], got[:half]), added(keep[half:], got[half:])


def after(value, *others):
    return lax.optimization_barrier((value,) + others)[0]


class Scatter:
    def __init__(self, keep, upper, shifts, plane, mp):
        self.keep, self.shifts, self.plane, self.mp = keep, shifts, plane, mp
        self.step = plane.steps - 1
        self.got = lax.ppermute(upper, "dp", plane.pairs(self.step))

    def next(self):
        self.step -= 1
        self.keep, upper = folded(self.keep, self.got)
        self.got = lax.ppermute(upper, "dp", self.plane.pairs(self.step))
        return self

    def last(self):
        while self.step > 0:
            self.next()
        extent = self.keep.shape[1] // len(self.shifts)
        self.moved = []
        for i, r in enumerate(self.shifts):
            span = slice(i * extent, (i + 1) * extent)
            pairs = [(j, (j - r) % self.mp) for j in range(self.mp)]
            part = added(self.keep[:, span], self.got[:, span])
            self.moved.append(lax.ppermute(part, "mp", pairs))
        return self


MESH = pl.DeviceIdType.MESH


def flipped(d, bit):
    return d + (1 - 2 * lax.rem(lax.div(d, 1 << bit), 2)) * (1 << bit)


def meet(d, z, dp, mp):
    barrier = pltpu.get_barrier_semaphore()
    for step in range(1, dp):
        there = (lax.rem(d + step, dp), z)
        pl.semaphore_signal(barrier, inc=1, device_id=there, device_id_type=MESH)
    for step in range(1, mp):
        there = (d, lax.rem(z + step, mp))
        pl.semaphore_signal(barrier, inc=1, device_id=there, device_id_type=MESH)
    pl.semaphore_wait(barrier, dp + mp - 2)


def remote(source, target, send_sem, recv_sem, device):
    return pltpu.make_async_remote_copy(
        src_ref=source,
        dst_ref=target,
        send_sem=send_sem,
        recv_sem=recv_sem,
        device_id=device,
        device_id_type=MESH,
    )


def peers_start(source, slots, send_sem, recv_sem, along, me, extent, each):
    copies = []
    for step in range(1, extent):
        place = lax.rem(me + step, extent)
        copies.append(
            remote(
                source.at[place if each else 0],
                slots.at[me],
                send_sem.at[step],
                recv_sem.at[me],
                along(step),
            )
        )
        copies[-1].start()
    slots[me] = source[me if each else 0]
    return copies


def peers_finish(copies, slots, recv_sem, me, extent):
    for step in range(1, extent):
        copies[step - 1].wait_send()
        sender = lax.rem(me + step, extent)
        pltpu.make_async_copy(slots.at[sender], slots.at[sender], recv_sem.at[sender]).wait()


def begin_kernel(plane, mp, hops, margin, *refs):
    (sheet, tokens, index, table), shards_in, refs = refs[:4], refs[4:10], refs[10:]
    (narrow, broad, stream, around, normed_out, second_out), buffers = refs[:6], refs[6:10]
    (middle, first, second, normed, zeros, payload, out_in, out_t), refs = refs[10:18], refs[18:]
    (reduce_in, reduce_t, take), refs = refs[:3], refs[3:]
    send_one, recv_one, send_two, recv_two, refs = *refs[:4], refs[4:]
    z_send, z_recv, chip_send, chip_recv, core_send, core_recv, halo_send, halo_recv, local = refs
    dp = plane.size
    d, z = lax.axis_index("dp"), lax.axis_index("mp")
    core = lax.rem(d, 2)
    rows, width = tokens.shape
    block, columns = payload.shape
    along_dp = lambda step: (lax.rem(d + step, dp), z)
    along_mp = lambda step: (d, lax.rem(z + step, mp))

    query, key, value, output, expand, reduce = shards_in
    extent, hidden_extent = query.shape[1], expand.shape[1]
    mine = pl.ds(pl.multiple_of(d * block, block), block)
    line = pl.ds(pl.multiple_of(lax.div(d * block, 128) * 128, 128), 128)
    taken = [
        pltpu.make_async_copy(
            source.at[mine, :], payload.at[:, pl.ds(w * extent, extent)], take.at[w]
        )
        for w, source in enumerate((query, key, value))
    ]
    taken.append(pltpu.make_async_copy(output.at[:, line], out_in, take.at[3]))
    taken.append(pltpu.make_async_copy(reduce.at[:, line], reduce_in, take.at[4]))
    taken.append(
        pltpu.make_async_copy(
            expand.at[mine, :], second_out.at[:, pl.ds(0, hidden_extent)], take.at[5]
        )
    )
    for copy in taken:
        copy.start()
    zeros[...] = jnp.zeros_like(zeros)
    meet(d, z, dp, mp)
    vectors = peers_start(sheet, first, send_one, recv_one, along_mp, z, mp, False)
    for copy in taken[:4]:
        copy.wait()
    out_t[...] = out_in[...].T
    within = pl.ds(pl.multiple_of(lax.rem(d * block, 128), block), block)
    payload[:, 3 * extent :] = out_t[within, :]

    each = dp // 4

    def place(j, r, other=False):
        return buffers[j // each + (2 if other else 0)].at[
            pl.ds(j % each * block, block), pl.ds((r - 1) * columns, columns)
        ]

    def passed_on(way, r):
        before = r - 1 if way == 0 else (r + 1) % mp
        source = place(0, before) if before else payload
        return remote(
            source, place(0, r), z_send.at[way, r], z_recv.at[r], (d, z + 1 if way == 0 else z - 1)
        )

    last, least = z + 1 < mp, z > 0
    line_sends = [(last & (z >= r - 1), passed_on(0, r).wait_send) for r in range(1, mp)]
    line_sends += [(least & (z <= r), passed_on(1, r).wait_send) for r in range(1, mp)]
    pl.when(last)(passed_on(0, 1).start)
    pl.when(least)(passed_on(1, mp - 1).start)

    count = lax.broadcasted_iota(jnp.int32, index.shape, 1)
    kept = index[...]
    coarse = lax.div(kept, 14)
    frame = lax.div(kept, 196)
    across = coarse - frame * 14
    line = kept - coarse * 14
    hot = ((count == frame) | (count == across + 8) | (count == line + 22)).astype(F32)
    hidden = tokens[...].astype(F32) + lax.dot_general(
        hot, table[...], NN, precision=lax.Precision.HIGHEST, preferred_element_type=F32
    )
    stream[...] = hidden

    peers_finish(vectors, first, recv_one, z, mp)
    middle[0] = jnp.sum(first[...], axis=0)
    vectors = peers_start(middle, second, send_two, recv_two, along_dp, d, dp, False)
    hat, _ = norm_parts(hidden)
    peers_finish(vectors, second, recv_two, d, dp)
    share = dp // (width // 128)
    for c in range(width // 128):
        narrow[:, c * 128 : (c + 1) * 128] = jnp.sum(
            second[c * share : (c + 1) * share, 0:8, :], axis=0
        )
    lines = broad.shape[1] // 128
    per = lines // dp
    for c in range(lines):
        row = second[c // per, 8 + c % per : 9 + c % per, :]
        broad[:, c * 128 : (c + 1) * 128] = jnp.broadcast_to(row, (8, 128))
    normed[...] = (hat * narrow[0:1, :] + narrow[1:2, :]).astype(BF16)
    taken[4].wait()
    reduce_t[...] = reduce_in[...].T
    shares = (
        pltpu.make_async_copy(
            reduce_t.at[within, :],
            second_out.at[:, pl.ds(hidden_extent, hidden_extent)],
            take.at[6],
        ),
        pltpu.make_async_copy(normed, normed_out, take.at[7]),
    )
    for copy in shares:
        copy.start()

    sent = []

    def arrived(j, r):
        pltpu.make_async_copy(place(j, r), place(j, r), z_recv.at[r]).wait()

    def copies_of(j, r):
        copies = []
        for step in range(plane.steps):
            if j < 1 << step:
                there = (1 - core) * flipped(d, plane.orders[0][step]) + core * flipped(
                    d, plane.orders[1][step]
                )
                to = (1 << step) + j
                copies.append(
                    remote(
                        place(j, r),
                        place(to, r),
                        chip_send.at[r, to],
                        chip_recv.at[r, to],
                        (there, z),
                    )
                )
        copies.append(
            remote(
                place(j, r),
                place(j, r, True),
                core_send.at[r, j],
                core_recv.at[r, j],
                (flipped(d, 0), z),
            )
        )
        return copies

    def forward(j, r):
        for copy in copies_of(j, r):
            copy.start()

    def handle(h):

        @pl.when(z >= h)
        def _():
            arrived(0, h)
            if h + 1 < mp:
                pl.when(last)(passed_on(0, h + 1).start)
            forward(0, h)

        @pl.when(z + h < mp)
        def _():
            arrived(0, mp - h)
            if mp - h > 1:
                pl.when(least)(passed_on(1, mp - h - 1).start)
            forward(0, mp - h)

    for h in range(1, mp - 1):
        handle(h)

    waits, at_left, at_right = [], margin, margin + rows
    inside = pltpu.make_async_copy(
        normed, around.at[pl.ds(margin, rows), :], local.at[0]
    )
    inside.start()
    waits.append((None, inside.wait))
    for hop, extent in enumerate(hops, 1):
        left = around.at[pl.ds(at_left - extent, extent), :]
        right = around.at[pl.ds(at_right, extent), :]
        sides = (
            (left, normed.at[pl.ds(rows - extent, extent), :], z + hop, z - hop, 2 * hop - 2),
            (right, normed.at[pl.ds(0, extent), :], z - hop, z + hop, 2 * hop - 1),
        )
        for target, source, there, back, n in sides:
            goes = (there >= 0) & (there < mp)
            comes = (back >= 0) & (back < mp)
            copy = remote(source, target, halo_send.at[n], halo_recv.at[n], (d, there))
            blank = pltpu.make_async_copy(zeros.at[pl.ds(0, extent), :], target, local.at[1 + n])
            pl.when(goes)(copy.start)
            pl.when(jnp.logical_not(comes))(blank.start)
            waits.append((goes, copy.wait_send))
            waits.append((comes, copy.wait_recv))
            waits.append((jnp.logical_not(comes), blank.wait))
        at_left, at_right = at_left - extent, at_right + extent
    if at_left:
        for n, at in enumerate((0, at_right)):
            blank = pltpu.make_async_copy(
                zeros.at[pl.ds(0, at_left), :],
                around.at[pl.ds(at, at_left), :],
                local.at[1 + 2 * len(hops) + n],
            )
            blank.start()
            waits.append((None, blank.wait))

    for h in range(mp - 1, mp):
        handle(h)
    for r in range(1, mp):
        sent.extend(copies_of(0, r))
    for j in range(1, 1 << plane.steps):
        for r in range(1, mp):
            pltpu.make_async_copy(place(j, r), place(j, r), chip_recv.at[r, j]).wait()
            forward(j, r)
            sent.extend(copies_of(j, r))
    for j in range(1 << plane.steps):
        for r in range(1, mp):
            pltpu.make_async_copy(place(j, r, True), place(j, r, True), core_recv.at[r, j]).wait()
    for copy in sent:
        copy.wait_send()
    for when, wait in line_sends:
        pl.when(when)(wait)
    taken[5].wait()
    for copy in shares:
        copy.wait()
    for when, wait in waits:
        wait() if when is None else pl.when(when)(wait)


def begin(sheet, tokens, index, table, shards, plane, mp, hops, margin):
    dp = plane.size
    rows, width = tokens.shape
    extent, hidden = shards[0].shape[1], shards[4].shape[1]
    block, columns, full_hidden = width // dp, 4 * extent, hidden * mp
    vmem, anywhere = pl.BlockSpec(memory_space=pltpu.VMEM), pl.BlockSpec(memory_space=pl.ANY)
    window = 2 * margin + rows
    dma = pltpu.SemaphoreType.DMA
    blocks = dp // 2
    return pl.pallas_call(
        functools.partial(begin_kernel, plane, mp, hops, margin),
        out_shape=[
            jax.ShapeDtypeStruct((8, width), F32),
            jax.ShapeDtypeStruct((8, full_hidden), F32),
            jax.ShapeDtypeStruct((rows, width), F32),
            jax.ShapeDtypeStruct((window, width), BF16),
            jax.ShapeDtypeStruct((rows, width), BF16),
            jax.ShapeDtypeStruct((block, 2 * hidden), BF16),
        ]
        + [jax.ShapeDtypeStruct((width // 4, (mp - 1) * columns), BF16)] * 4,
        in_specs=[vmem] * 4 + [anywhere] * 6,
        out_specs=[vmem] * 3 + [anywhere] * 7,
        scratch_shapes=[
            pltpu.VMEM((1, 16, 128), F32),
            pltpu.VMEM((mp, 16, 128), F32),
            pltpu.VMEM((dp, 16, 128), F32),
            pltpu.VMEM((rows, width), BF16),
            pltpu.VMEM((rows, width), BF16),
            pltpu.VMEM((block, columns), BF16),
            pltpu.VMEM((extent, 128), BF16),
            pltpu.VMEM((128, extent), BF16),
            pltpu.VMEM((hidden, 128), BF16),
            pltpu.VMEM((128, hidden), BF16),
            dma((8,)),
            dma((mp,)),
            dma((mp,)),
            dma((dp,)),
            dma((dp,)),
            dma((2, mp)),
            dma((mp,)),
            dma((mp, blocks)),
            dma((mp, blocks)),
            dma((mp, blocks)),
            dma((mp, blocks)),
            dma((2 * len(hops),)),
            dma((2 * len(hops),)),
            dma((3 + 2 * len(hops),)),
        ],
        compiler_params=pltpu.CompilerParams(
            collective_id=1, has_side_effects=True, vmem_limit_bytes=60 * MIB
        ),
        cost_estimate=pl.CostEstimate(flops=4 * 10**10, bytes_accessed=0, transcendentals=0),
        name="begin",
    )(sheet, tokens, index, table, *shards)


def xored(d, mask):
    for bit in range(mask.bit_length()):
        if mask >> bit & 1:
            d = flipped(d, bit)
    return d


def middle_kernel(plane, mp, tile, *refs):
    (stream_in, near_in, far_in, g_in, narrow_in, broad_in), refs = refs[:6], refs[6:]
    own_o, own_e, own_r, out_parts, refs = *refs[:3], refs[3:7], refs[7:]
    (early_a, early_b), late_a, refs = refs[:2], refs[2 : 2 * mp - 2], refs[2 * mp - 2 :]
    (sums, db, own_total, moved, act, grad_mid, branch_t, grad_near, grad_far), refs = refs[:9], refs[9:]
    (keep_out, upper_out, early_o, late_b, late_c, late_d), refs = refs[:6], refs[6:]
    (mid, near, far, g, narrow, broad, o_temp, weight_o, weights, r_temp), refs = refs[:10], refs[10:]
    (x, x_t, g_t, lead, out_acc, dx_acc, keep, send, got, more), refs = refs[:10], refs[10:]
    load, weight_sem, own_sem, core_send, core_recv, chip_send, chip_recv, refs = *refs[:7], refs[7:]
    sum_send, sum_recv, near_send, near_recv, store = refs
    dp, steps = plane.size, plane.steps
    d, z = lax.axis_index("dp"), lax.axis_index("mp")
    core = lax.rem(d, 2)
    rows, width = x.shape
    block, half, quarter = width // dp, width // 2, width // 4
    extent = own_e.shape[1]
    per = extent // tile
    tiles = mp * per
    wide = 2 * extent
    full = mp // 2
    orders = [
        (1 - core) * xored(d, plane.masks[0][i]) + core * xored(d, plane.masks[1][i])
        for i in range(dp)
    ]
    sibling = (flipped(d, 0), z)

    def partner(step):
        there = (1 - core) * flipped(d, plane.orders[0][step]) + core * flipped(
            d, plane.orders[1][step]
        )
        return there, z

    def home(i):
        return pl.ds(pl.multiple_of(orders[i] * block, block), block)

    def turned(target, source):
        lead[...] = source.T
        for i in range(dp):
            target[i * block : (i + 1) * block, :] = lead[home(i), :]

    loads = [
        pltpu.make_async_copy(source, target, load.at[i])
        for i, (source, target) in enumerate(
            (
                (stream_in, mid),
                (near_in, near),
                (far_in, far),
                (g_in, g),
                (narrow_in, narrow),
                (broad_in, broad),
                (own_o, o_temp),
            )
        )
    ]
    each = dp // 4
    part_o = own_o.shape[0]
    for i in range(dp):
        for r in range(1, mp):
            pltpu.make_async_copy(
                out_parts[i // each].at[
                    pl.ds(i % each * block, block), pl.ds((4 * r - 1) * part_o, part_o)
                ],
                weight_o.at[home(i), pl.ds(r * part_o, part_o)],
                load.at[7],
            ).start()
    rest_o = weight_o.at[:, pl.ds(part_o, width - part_o)]
    for copy in loads:
        copy.start()

    def fetch(i):
        slot, r, t = i % 2, i // per, i % per
        if r == 0:
            return [
                pltpu.make_async_copy(
                    own_e.at[:, pl.ds(t * tile, tile)], weights.at[slot, 0], own_sem.at[0]
                ),
                pltpu.make_async_copy(own_r.at[pl.ds(t * tile, tile), :], r_temp, own_sem.at[1]),
            ]
        if r == 1:
            parts = (early_a, early_b) + tuple(
                early_o.at[pl.ds(n * quarter, quarter), :] for n in range(2)
            )
            first = 0
        else:
            parts, first = (None, late_b, late_c, late_d), (r - 2) * wide

        def piece(n, kind):
            column = kind * extent + t * tile
            if r > 1 and n < each:
                few = each // 2
                return late_a[2 * (r - 2) + n // few].at[
                    pl.ds(n % few * block, block), pl.ds(column, tile)
                ]
            return parts[n // each].at[pl.ds(n % each * block, block), pl.ds(first + column, tile)]

        return [
            pltpu.make_async_copy(
                piece(n, kind),
                weights.at[slot, kind, home(n), :],
                weight_sem.at[slot],
            )
            for kind in range(2)
            for n in range(dp)
        ]

    for copy in fetch(0):
        copy.start()
    meet(d, z, dp, mp)

    def late(buffer, r):
        return buffer.at[:, pl.ds((r - 2) * wide, wide)]

    sent = []
    swaps, hops = {}, {}
    for n, part in enumerate((early_a, early_b)):
        swaps[1, n] = remote(
            part,
            early_o.at[pl.ds(n * quarter, quarter), :],
            core_send.at[1, n],
            core_recv.at[1, n],
            sibling,
        )
    for r in range(2, mp):
        for n in range(2):
            part = late_a[2 * (r - 2) + n]
            span = pl.ds(n * quarter // 2, quarter // 2)
            columns = pl.ds((r - 2) * wide, wide)
            hops[r, n] = remote(
                part,
                late_b.at[span, columns],
                chip_send.at[r, n],
                chip_recv.at[r, n],
                partner(steps - 1),
            )
            swaps[r, n] = remote(
                part, late_c.at[span, columns], core_send.at[r, n], core_recv.at[r, n], sibling
            )
        swaps[r, 2] = remote(
            late(late_b, r), late(late_d, r), core_send.at[r, 2], core_recv.at[r, 2], sibling
        )
    swaps[1, 0].start()
    swaps[1, 1].start()
    for r in range(2, mp):
        for n in range(2):
            hops[r, n].start()
        for n in range(2):
            swaps[r, n].start()

    for i in range(7):
        loads[i].wait()
    pltpu.make_async_copy(rest_o, rest_o, load.at[7]).wait()
    weight_o[:, :part_o] = o_temp[...].T
    cut = near.shape[1]
    mixed = dot(near[...], weight_o[:, :cut], NT) + dot(far[...], weight_o[:, cut:], NT)
    mid[...] = mid[...] + mixed + narrow[2:3, :]
    hat, _ = norm_parts(mid[...])
    x[...] = (hat * narrow[3:4, :] + narrow[4:5, :]).astype(BF16)
    turned(x_t, x[...])
    turned(g_t, g[...])
    out_acc[...] = jnp.zeros_like(out_acc)
    dx_acc[...] = jnp.zeros_like(dx_acc)

    def swap_of(c):
        return remote(
            send.at[c % 2], got.at[c], near_send.at[c], near_recv.at[c], sibling
        )

    def rows_of(step):
        count = half >> (steps - step)
        return count, half - 2 * count

    def sum_of(c, step):
        count, at = rows_of(step)
        return remote(
            keep.at[c, pl.ds(count, count), :],
            more.at[c // 2, pl.ds(at, count), :],
            sum_send.at[c // 2, step],
            sum_recv.at[c // 2, step],
            partner(step),
        )

    def outs_of(c):
        span = pl.ds(c // 2 * wide, wide)
        return [
            pltpu.make_async_copy(
                keep.at[c, pl.ds(n * quarter, quarter), :], target.at[:, span], store.at[c, n]
            )
            for n, target in enumerate((keep_out, upper_out))
        ]

    def core_done(c):
        swap_of(c).wait_recv()
        keep[c] = added(keep[c], got[c])
        if c % 2 == 0:
            sum_of(c, steps - 1).start()
        else:
            for copy in outs_of(c):
                copy.start()

    def chips_done(c, step):
        sum_of(c, step).wait_recv()
        count, at = rows_of(step)
        keep[c, :count, :] = added(keep[c, :count, :], more[c // 2, pl.ds(at, count), :])
        if step:
            sum_of(c, step - 1).start()

    events = {}
    for r in range(2, mp):

        def passed(r=r):
            hops[r, 0].wait_recv()
            hops[r, 1].wait_recv()
            swaps[r, 2].start()

        events.setdefault((r - 1) * per, []).append(passed)
    for r in range(1, mp):

        def arrived(r=r):
            for n in range(2 if r == 1 else 3):
                swaps[r, n].wait_recv()

        events.setdefault(r * per - 1, []).append(arrived)
    for i in range(1, tiles):

        def ahead(i=i):
            for copy in fetch(i):
                copy.start()

        if i >= per:
            events.setdefault(i - 1, []).append(ahead)
    for c in range(mp - 1):
        events.setdefault((c + 2) * per - 1, []).append(functools.partial(core_done, c))
    events.setdefault(tiles - per, []).append(functools.partial(chips_done, 0, steps - 1))

    def body(i, carry):
        slot, c, t = lax.rem(i, 2), lax.div(i, per), lax.rem(i, per)

        @pl.when(c == 0)
        def _():
            pltpu.make_async_copy(weights.at[0, 0], weights.at[0, 0], own_sem.at[0]).wait()
            pltpu.make_async_copy(r_temp, r_temp, own_sem.at[1]).wait()
            weights[slot, 1] = r_temp[...].T

        @pl.when(c > 0)
        def _():
            pltpu.make_async_copy(weights.at[slot], weights.at[slot], weight_sem.at[slot]).wait()

        for n in range(1, per):

            @pl.when(i == n - 1)
            def _():
                for copy in fetch(n):
                    copy.start()

        for n, actions in events.items():

            @pl.when(i == n)
            def _():
                for action in actions:
                    action()

        @pl.when((t == 0) & (c >= 2))
        def _():
            remote(
                send.at[lax.rem(c, 2)], got.at[c], near_send.at[c - 2], near_recv.at[c], sibling
            ).wait_send()

        weight_e, weight_r = weights[slot, 0], weights[slot, 1]
        at = pl.multiple_of(lax.rem(z - c + mp, mp) * extent + t * tile, tile)
        pre = dot(x[...], weight_e) + broad[0:1, pl.ds(at, tile)]
        cumulative = 0.5 * (1.0 + lax.erf(pre * 0.7071067811865476))
        hidden = (pre * cumulative).astype(BF16)
        slope = cumulative + pre * jnp.exp(-0.5 * pre * pre) * (1.0 / math.sqrt(2.0 * math.pi))
        grad_pre = (dot(g[...], weight_r) * slope).astype(BF16)
        line = jnp.sum(grad_pre.astype(F32), axis=0, keepdims=True)
        db[:, pl.ds(pl.multiple_of(i * tile, tile), tile)] = jnp.broadcast_to(line, (8, tile))
        first = pl.ds(pl.multiple_of(2 * t * tile, tile), tile)
        second = pl.ds(pl.multiple_of((2 * t + 1) * tile, tile), tile)
        out = lax.rem(c, 2)
        send[out, :, first] = dot(x_t[half:, :], grad_pre).astype(BF16)
        send[out, :, second] = dot(g_t[half:, :], hidden).astype(BF16)
        keep[c, :, first] = dot(x_t[:half, :], grad_pre).astype(BF16)
        keep[c, :, second] = dot(g_t[:half, :], hidden).astype(BF16)

        @pl.when(t == per - 1)
        def _():
            remote(send.at[out], got.at[c], near_send.at[c], near_recv.at[c], sibling).start()

        out_acc[...] += dot(hidden, weight_r, NT)
        dx_acc[...] += dot(grad_pre, weight_e, NT)
        return carry

    lax.fori_loop(0, tiles, body, 0)

    value, grad, dy = mid[...], g[...].astype(F32), dx_acc[...]
    x[...] = (value + out_acc[...] + narrow[5:6, :]).astype(BF16)
    hat, factor = norm_parts(value)
    back = grad + norm_back(dy, hat, factor, narrow[3:4, :])
    add = lambda v: jnp.sum(v, axis=0, keepdims=True)
    zero = jnp.zeros((4, width), F32)
    sums[...] = jnp.concatenate([add(back), add(dy * hat), add(dy), add(grad), zero], axis=0)
    mid[...] = back
    rounded = back.astype(BF16)
    turned(x_t, rounded)
    near[...] = dot(rounded, weight_o[:, :cut]).astype(BF16)
    far[...] = dot(rounded, weight_o[:, cut:]).astype(BF16)
    results = [
        pltpu.make_async_copy(source, target, load.at[i])
        for i, (source, target) in enumerate(
            ((x, act), (mid, grad_mid), (x_t, branch_t), (near, grad_near), (far, grad_far))
        )
    ]
    for copy in results:
        copy.start()

    core_done(mp - 1)
    for c in range(2, mp, 2):
        chips_done(c, steps - 1)
    for step in reversed(range(steps - 1)):
        for c in range(0, mp, 2):
            chips_done(c, step)
    own_total[...] = keep[0, :block, :].astype(F32)
    for c in range(2, mp, 2):
        moved[c // 2 - 1] = keep[c, :block, :]
    for c in range(max(0, mp - 2), mp):
        swap_of(c).wait_send()
    for c in range(0, mp, 2):
        for step in range(steps):
            sum_of(c, step).wait_send()
    for c in range(1, mp, 2):
        for copy in outs_of(c):
            copy.wait()
    for copy in list(hops.values()) + list(swaps.values()):
        copy.wait_send()
    for copy in results:
        copy.wait()


def middle(arrays, weights, buffers, parts, plane, mp, hidden):
    dp = plane.size
    rows, width = arrays[0].shape
    extent = hidden // mp
    tile = min(512, extent)
    wide, half, quarter, full = 2 * extent, width // 2, width // 4, mp // 2
    vmem, anywhere = pl.BlockSpec(memory_space=pltpu.VMEM), pl.BlockSpec(memory_space=pl.ANY)
    dma = pltpu.SemaphoreType.DMA
    shape = jax.ShapeDtypeStruct
    near = arrays[1].shape[1]
    late = (quarter, (mp - 2) * wide)
    return pl.pallas_call(
        functools.partial(middle_kernel, plane, mp, tile),
        out_shape=[
            shape((8, width), F32),
            shape((8, hidden), F32),
            shape((width // dp, wide), F32),
            shape((max(full - 1, 1), width // dp, wide), BF16),
            shape((rows, width), BF16),
            shape((rows, width), F32),
            shape((width, rows), BF16),
            shape((rows, near), BF16),
            shape((rows, width - near), BF16),
            shape((quarter, (mp - full) * wide), BF16),
            shape((quarter, (mp - full) * wide), BF16),
            shape((half, wide), BF16),
            shape(late, BF16),
            shape(late, BF16),
            shape(late, BF16),
        ],
        in_specs=[anywhere] * (len(arrays) + len(weights) + len(buffers) + len(parts)),
        out_specs=[vmem] * 4 + [anywhere] * 11,
        scratch_shapes=[
            pltpu.VMEM((rows, width), F32),
            pltpu.VMEM(arrays[1].shape, BF16),
            pltpu.VMEM(arrays[2].shape, BF16),
            pltpu.VMEM((rows, width), BF16),
            pltpu.VMEM((8, width), F32),
            pltpu.VMEM((8, hidden), F32),
            pltpu.VMEM(weights[0].shape, BF16),
            pltpu.VMEM((width, width), BF16),
            pltpu.VMEM((2, 2, width, tile), BF16),
            pltpu.VMEM((tile, width), BF16),
            pltpu.VMEM((rows, width), BF16),
            pltpu.VMEM((width, rows), BF16),
            pltpu.VMEM((width, rows), BF16),
            pltpu.VMEM((width, rows), BF16),
            pltpu.VMEM((rows, width), F32),
            pltpu.VMEM((rows, width), F32),
            pltpu.VMEM((mp, half, wide), BF16),
            pltpu.VMEM((2, half, wide), BF16),
            pltpu.VMEM((mp, half, wide), BF16),
            pltpu.VMEM((full, half, wide), BF16),
            dma((8,)),
            dma((2,)),
            dma((2,)),
            dma((mp, 3)),
            dma((mp, 3)),
            dma((mp, 2)),
            dma((mp, 2)),
            dma((full, plane.steps)),
            dma((full, plane.steps)),
            dma((mp,)),
            dma((mp,)),
            dma((mp, 2)),
        ],
        compiler_params=pltpu.CompilerParams(
            collective_id=3, has_side_effects=True, vmem_limit_bytes=60 * MIB
        ),
        cost_estimate=pl.CostEstimate(flops=6 * 10**10, bytes_accessed=0, transcendentals=0),
        name="middle",
    )(*arrays, *weights, *buffers, *parts)


def finish_kernel(plane, mp, hops, margin, *refs):
    hbm, refs = refs[:17], refs[17:]
    upper, refs = refs[0], refs[1:]
    (grad_tokens, total, vectors), refs = refs[:3], refs[3:]
    loaded, refs = refs[:17], refs[17:]
    (halo_out, halo_in, keep, send, got, more_got, shards, table, sheets), refs = refs[:9], refs[9:]
    (middle, first, second), refs = refs[:3], refs[3:]
    load_sem, halo_send, halo_recv, core_sem, near_send, near_recv, far_send, far_recv = refs[:8]
    z_send, z_recv, send_one, recv_one, send_two, recv_two = refs[8:]
    (dq, dk, dv, att, wq, wk, wv, before_around, before_own) = loaded[:9]
    (around_t, branch_t, others, stream, grad_mid, narrow, early, broad) = loaded[9:]
    dp = plane.size
    d, z = lax.axis_index("dp"), lax.axis_index("mp")
    core = lax.rem(d, 2)
    rows, extent = dq.shape
    half = keep.shape[0]
    block = total.shape[0]
    columns = total.shape[1]
    left = sum(hops)

    loads = [
        pltpu.make_async_copy(source, target, load_sem.at[i])
        for i, (source, target) in enumerate(zip(hbm, loaded))
    ]
    for copy in loads:
        copy.start()
    halo_in[...] = jnp.zeros_like(halo_in)
    meet(d, z, dp, mp)

    def partner(step):
        there = (1 - core) * flipped(d, plane.orders[0][step]) + core * flipped(
            d, plane.orders[1][step]
        )
        return there, z

    top = half // 2
    far = remote(
        upper,
        more_got.at[pl.ds(0, top), :],
        far_send.at[plane.steps - 1],
        far_recv.at[plane.steps - 1],
        partner(plane.steps - 1),
    )
    far.start()
    sent = [far]

    for i in (1, 2, 5, 6, 7):
        loads[i].wait()
    waits, at_left, at_right, at = [], margin, margin + rows, 0
    copies = []
    for hop, reach in enumerate(hops, 1):
        sides = (
            (at_left - reach, z - hop, z + hop, 2 * hop - 2, rows - reach),
            (at_right, z + hop, z - hop, 2 * hop - 1, 0),
        )
        for start, there, back, n, place in sides:
            span = slice(start, start + reach)
            here = pl.ds(at, reach)
            part = dot(dk[span, :], wk[...], NT) + dot(dv[span, :], wv[...], NT)
            halo_out[here, :] = (before_around[span, :] + part).astype(BF16)
            goes = (there >= 0) & (there < mp)
            comes = (back >= 0) & (back < mp)
            copy = remote(
                halo_out.at[here, :],
                halo_in.at[here, :],
                halo_send.at[n],
                halo_recv.at[n],
                (d, there),
            )
            pl.when(goes)(copy.start)
            waits.append((goes, copy.wait_send))
            copies.append((comes, copy.wait_recv, place, at, reach))
            at += reach
        at_left, at_right = at_left - reach, at_right + reach

    for i in (0, 3, 9, 10):
        loads[i].wait()
    inner, everything = slice(margin, margin + rows), slice(None)

    def weight_grads(target, low):
        for n, (source, span, right) in enumerate(
            (
                (around_t, inner, dq),
                (around_t, everything, dk),
                (around_t, everything, dv),
                (branch_t, everything, att),
            )
        ):
            target[:, n * extent : (n + 1) * extent] = dot(
                source[low : low + half, span], right[...]
            ).astype(BF16)

    weight_grads(send, half)
    swap = remote(send, got.at[pl.ds(0, half), :], core_sem.at[0], core_sem.at[1], (flipped(d, 0), z))
    swap.start()
    sent.append(swap)
    weight_grads(keep, 0)

    def fold(target, source, at, count):
        target[:count, :] = added(target[:count, :], source[pl.ds(at, count), :])

    swap.wait_recv()
    fold(keep, got, 0, half)
    loads[4].wait()
    loads[8].wait()
    own = before_own[...] + before_around[inner, :] + dot(dq[...], wq[...], NT)
    own += dot(dk[inner, :], wk[...], NT) + dot(dv[inner, :], wv[...], NT)
    before_own[...] = own
    count, at_near, at_far = half, half, 0
    loads[11].wait()
    for step in reversed(range(plane.steps)):
        count //= 2
        near = remote(
            keep.at[pl.ds(count, count), :],
            got.at[pl.ds(at_near, count), :],
            near_send.at[step],
            near_recv.at[step],
            partner(step),
        )
        near.start()
        sent.append(near)
        far.wait_recv()
        fold(others, more_got, at_far, count)
        at_far += count
        if step:
            far = remote(
                others.at[pl.ds(count // 2, count // 2), :],
                more_got.at[pl.ds(at_far, count // 2), :],
                far_send.at[step - 1],
                far_recv.at[step - 1],
                partner(step - 1),
            )
            far.start()
            sent.append(far)
        near.wait_recv()
        fold(keep, got, at_near, count)
        at_near += count
    for r in range(1, mp):
        copy = remote(
            others.at[pl.ds(0, block), pl.ds((r - 1) * columns, columns)],
            shards.at[r],
            z_send.at[r],
            z_recv.at[r],
            (d, lax.rem(z - r + mp, mp)),
        )
        copy.start()
        sent.append(copy)

    for i in range(12, 17):
        loads[i].wait()
    for comes, wait, *_ in copies:
        pl.when(comes)(wait)
    for _, _, place, at, reach in copies:
        span = slice(place, place + reach)
        before_own[span, :] = before_own[span, :] + halo_in[at : at + reach, :].astype(F32)
    hat, factor = norm_parts(stream[...])
    upstream = before_own[...]
    add = lambda v: jnp.sum(v, axis=0, keepdims=True)
    back = grad_mid[...] + norm_back(upstream, hat, factor, narrow[0:1, :])
    grad_tokens[...] = back.astype(BF16)
    table[...] = early[...]
    table[0:1, :] = add(upstream * hat)
    table[1:2, :] = add(upstream)
    mine = pl.ds(pl.multiple_of(z * extent, extent), extent)
    table[6:7, mine] = add(dq[...].astype(F32))
    table[7:8, mine] = add(dv[...].astype(F32))
    each = dp // (early.shape[1] // 128)
    for i in range(dp):
        c = i // each
        sheets[i, 0:8, :] = table[:, c * 128 : (c + 1) * 128]
        sheets[i, 8:16, :] = broad[i]
    along_dp = lambda step: (lax.rem(d + step, dp), z)
    along_mp = lambda step: (d, lax.rem(z + step, mp))
    out = peers_start(sheets, second, send_two, recv_two, along_dp, d, dp, True)
    peers_finish(out, second, recv_two, d, dp)
    middle[0] = jnp.sum(second[...], axis=0)
    out = peers_start(middle, first, send_one, recv_one, along_mp, z, mp, False)

    full = keep[:block, :].astype(F32)
    for r in range(1, mp):
        pltpu.make_async_copy(shards.at[r], shards.at[r], z_recv.at[r]).wait()
        full += shards[r].astype(F32)
    total[...] = full
    peers_finish(out, first, recv_one, z, mp)
    vectors[...] = jnp.sum(first[...], axis=0)
    for copy in sent:
        copy.wait_send()
    for when, wait in waits:
        pl.when(when)(wait)


def finish(arrays, upper, plane, mp, hops, margin):
    dp = plane.size
    rows, extent = arrays[0].shape
    width = arrays[4].shape[0]
    block, half, columns = width // dp, width // 2, 4 * extent
    vmem, anywhere = pl.BlockSpec(memory_space=pltpu.VMEM), pl.BlockSpec(memory_space=pl.ANY)
    dma = pltpu.SemaphoreType.DMA
    left = sum(hops)
    return pl.pallas_call(
        functools.partial(finish_kernel, plane, mp, hops, margin),
        out_shape=[
            jax.ShapeDtypeStruct((rows, width), BF16),
            jax.ShapeDtypeStruct((block, columns), F32),
            jax.ShapeDtypeStruct((16, 128), F32),
        ],
        in_specs=[anywhere] * (len(arrays) + 1),
        out_specs=[vmem] * 3,
        scratch_shapes=[pltpu.VMEM(item.shape, item.dtype) for item in arrays]
        + [
            pltpu.VMEM((2 * left, width), BF16),
            pltpu.VMEM((2 * left, width), BF16),
            pltpu.VMEM((half, columns), BF16),
            pltpu.VMEM((half, columns), BF16),
            pltpu.VMEM((2 * half, columns), BF16),
            pltpu.VMEM((half, (mp - 1) * columns), BF16),
            pltpu.VMEM((mp, block, columns), BF16),
            pltpu.VMEM((8, width), F32),
            pltpu.VMEM((dp, 16, 128), F32),
            pltpu.VMEM((1, 16, 128), F32),
            pltpu.VMEM((mp, 16, 128), F32),
            pltpu.VMEM((dp, 16, 128), F32),
            dma((len(arrays),)),
            dma((2 * len(hops),)),
            dma((2 * len(hops),)),
            dma((2,)),
            dma((plane.steps,)),
            dma((plane.steps,)),
            dma((plane.steps,)),
            dma((plane.steps,)),
            dma((mp,)),
            dma((mp,)),
            dma((mp,)),
            dma((mp,)),
            dma((dp,)),
            dma((dp,)),
        ],
        compiler_params=pltpu.CompilerParams(
            collective_id=2, has_side_effects=True, vmem_limit_bytes=60 * MIB
        ),
        cost_estimate=pl.CostEstimate(flops=5 * 10**10, bytes_accessed=0, transcendentals=0),
        name="finish",
    )(*arrays, upper)


def local(
    tokens,
    kept_index,
    lengths,
    first_gain,
    first_shift,
    query_weight,
    key_weight,
    value_weight,
    query_bias,
    value_bias,
    output_weight,
    output_bias,
    second_gain,
    second_shift,
    expand_weight,
    expand_bias,
    reduce_weight,
    reduce_bias,
    cotangent,
):
    dp, mp = lax.axis_size("dp"), lax.axis_size("mp")
    d, z = lax.axis_index("dp"), lax.axis_index("mp")
    plane = Plane(dp)
    rows, width = tokens.shape
    group_rows = rows * mp
    block = width // dp
    full_hidden = expand_weight.shape[1] * mp
    meta = jnp.concatenate([z[None], plane.order(d)]).astype(jnp.int32)

    singles = (
        first_gain,
        first_shift,
        output_bias,
        second_gain,
        second_shift,
        reduce_bias,
        query_bias,
        value_bias,
    )
    single, wide = first_gain.shape[0], expand_bias.shape[0]
    me = d * mp + z
    lane = jnp.arange(128, dtype=jnp.int32)
    lines = full_hidden // dp // 128

    def placed(stack):
        count = 128 // stack.shape[1]
        return jnp.where(lane // stack.shape[1] == me % count, jnp.tile(stack, (1, count)), 0.0)

    line = placed(expand_bias[None].astype(F32))
    at_line = (jnp.arange(8, dtype=jnp.int32) == me * wide // 128 % lines)[:, None]
    sheet = jnp.concatenate(
        [placed(jnp.stack(singles).astype(F32)), jnp.where(at_line, line, 0.0)], axis=0
    )
    scal = jnp.concatenate([z[None], lengths[0]]).astype(jnp.int32)
    reach, hops, left = LONGEST - 1, [], 0
    while reach > 0:
        extent = min(rows, -(-reach // 16) * 16)
        hops.append(extent)
        left, reach = left + extent, reach - extent
    margin = -(-left // 128) * 128
    while (2 * margin + rows) % TILE:
        margin += 128

    begun = begin(
        sheet[None],
        tokens,
        jnp.broadcast_to(kept_index[:, None], (rows, 128)),
        jnp.asarray(position_lines(width)),
        (query_weight, key_weight, value_weight, output_weight, expand_weight, reduce_weight),
        plane,
        mp,
        hops,
        margin,
    )
    narrow, broad, stream, around, normed_one, second = begun[:6]
    buffers = begun[6:]
    shares = {1: shifted(second, 1, mp)}
    around_t = turned_rows(around, meta, block)
    projections = (query_weight, key_weight, value_weight)
    pairs = width // (2 * HEAD_SIZE) // mp
    heads = [
        project(normed_one, around, projections if own else buffers, narrow, meta, block, mp, own)
        for own in (True, False)
    ]
    heads[1] = lax.optimization_barrier((*heads[1], shares[1]))[:3]
    for r in range(2, mp):
        shares[r] = shifted(after(second, shares[1]), r, mp)
    early = spread_chips(shares[1], plane)
    later = [early[1]] + [shares[r] for r in range(2, mp)]
    far, late = (), []
    for r in range(1, mp):
        part = ((r - 1) * pairs, pairs, (mp - 1) * pairs)
        far = attention_forward(
            after(scal, *far, *later[: r - 1]), mp, *heads[1], part, far
        )
        if r == 1:
            early = join(early, 0)
            early = (early, lax.ppermute(early, "dp", plane.pairs(plane.steps - 1)))
        else:
            late.extend(spread_chips(shares[r], plane))
    near = attention_forward(
        after(scal, *far, *late[: 2 * mp - 6]), mp, *heads[0], (0, pairs, pairs)
    )
    attended, lses = [near[0], far[0]], [near[1], far[1]]

    results = middle(
        (stream, *attended, cotangent, narrow, broad),
        (output_weight, expand_weight, reduce_weight),
        buffers,
        (*early, *late),
        plane,
        mp,
        full_hidden,
    )
    sums_mid, grad_bias, own_two, ready = results[:4]
    activations, grad_middle, branch_t, grad_near, grad_far, kept, upper = results[4:11]
    moved_one = [
        lax.ppermute(ready[r // 2 - 1], "mp", [(j, (j - r) % mp) for j in range(mp)])
        for r in range(2, mp, 2)
    ]
    sums_two = Scatter(kept, upper, list(range(1, mp, 2)), plane, mp)

    grads_far = ()
    for r in range(1, mp):
        part = ((r - 1) * pairs, pairs, (mp - 1) * pairs)
        tied = after(scal, *grads_far, sums_two.got) if r == mp - 1 else after(scal, *grads_far)
        grads_far = attention_backward(
            tied,
            mp,
            *heads[1],
            grad_far,
            attended[1],
            lses[1],
            part,
            tuple(grads_far),
        )
    while sums_two.step > 0:
        sums_two.next()
    grads_far = lax.optimization_barrier((*grads_far, sums_two.got))[:3]
    sums_two.last()
    partial = tail(around_t, branch_t, grads_far, attended[1], buffers, meta, block, mp, margin)
    swapped = lax.ppermute(partial[3], "dp", plane.siblings())
    grads_near = attention_backward(
        after(scal, partial[0]),
        mp,
        *heads[0],
        grad_near,
        attended[0],
        lses[0],
        (0, pairs, pairs),
    )

    turned = jnp.mod(z - jnp.arange(mp, dtype=jnp.int32), mp)
    pick = turned[:, None] == jnp.arange(mp, dtype=jnp.int32)[None, :]

    def in_turn(v):
        parts = v.reshape(v.shape[0], 1, mp, v.shape[1] // mp)
        return jnp.sum(jnp.where(pick[None, :, :, None], parts, 0.0), axis=2).reshape(v.shape)

    bias_sums = in_turn(jnp.pad(partial[4][:2], ((0, 0), (width // mp, 0))))
    early = jnp.concatenate([jnp.zeros((2, width), F32), sums_mid[:4], bias_sums], axis=0)
    broad_sum = in_turn(grad_bias[:1])
    broad_part = jnp.pad(broad_sum.reshape(dp, lines, 128), ((0, 0), (0, 8 - lines), (0, 0)))
    lower, upper = folded(partial[2], swapped)
    grad_tokens, total_one, summed = finish(
        (
            *grads_near,
            attended[0],
            *projections,
            partial[1],
            partial[0],
            around_t,
            branch_t,
            lower,
            stream,
            grad_middle,
            narrow,
            early,
            broad_part,
        ),
        upper,
        plane,
        mp,
        hops,
        margin,
    )

    extent = width // mp
    grad_query, grad_key, grad_value, grad_out = [
        total_one[:, i * extent : (i + 1) * extent] for i in range(4)
    ]
    total_two = own_two
    for item in lax.optimization_barrier((*moved_one, *sums_two.moved, total_one))[:-1]:
        total_two = total_two + item.astype(F32)
    extent = full_hidden // mp
    tile = min(512, extent)
    slabs = [total_two[:, i * tile : (i + 1) * tile] for i in range(2 * extent // tile)]
    grad_expand = jnp.concatenate(slabs[0::2], axis=1)
    grad_reduce = jnp.concatenate(slabs[1::2], axis=1)

    taken = lambda stack, extent: lax.dynamic_slice_in_dim(
        stack, me % (128 // extent) * extent, extent, 1
    )
    small = taken(summed[:8], single)
    broad_row = lax.dynamic_slice_in_dim(summed[8:], me * wide // 128 % lines, 1, 0)
    return (
        activations,
        grad_tokens,
        grad_query,
        grad_key,
        grad_value,
        grad_out.T,
        grad_expand,
        grad_reduce.T,
        small[0],
        small[1],
        small[6],
        small[7],
        small[2],
        small[3],
        small[4],
        taken(broad_row, wide)[0],
        small[5],
    )


def solution(mesh):
    vector = P(("dp", "mp"))
    tall = P(("dp", "mp"), None)
    in_specs = (
        tall,
        vector,
        P("dp", None),
        vector,
        vector,
        P(None, "mp"),
        P(None, "mp"),
        P(None, "mp"),
        vector,
        vector,
        P("mp", None),
        vector,
        vector,
        vector,
        P(None, "mp"),
        vector,
        P("mp", None),
        vector,
        tall,
    )
    out_specs = (
        tall,
        tall,
        P("dp", "mp"),
        P("dp", "mp"),
        P("dp", "mp"),
        P("mp", "dp"),
        P("dp", "mp"),
        P("mp", "dp"),
    ) + (vector,) * 9
    return jax.shard_map(local, mesh=mesh, in_specs=in_specs, out_specs=out_specs, check_vma=False)
```

```python
import functools
import math

import jax
import jax.numpy as jnp
import numpy as np
from jax import lax
from jax.experimental import pallas as pl
from jax.experimental.pallas import tpu as pltpu
from jax.sharding import PartitionSpec as P

HEAD_SIZE = 64
LONGEST = 549
EPSILON = 1e-06
TILE = 256
PAIR = 2 * HEAD_SIZE
PAIRS = 2
MIB = 1024 * 1024
F32 = jnp.float32
BF16 = jnp.bfloat16

NN = (((1,), (0,)), ((), ()))
NT = (((1,), (1,)), ((), ()))
TN = (((0,), (0,)), ((), ()))


def dot(left, right, dims=NN):
    return lax.dot_general(left, right, dims, preferred_element_type=F32)


def position_lines(extent):
    quarter = extent // 4
    spatial = (extent - quarter) // 2
    table = np.zeros((128, extent), np.float32)
    at, first = 0, 0
    for count, part in ((8, quarter), (14, spatial), (14, spatial)):
        half = part // 2
        inverse = np.exp(np.arange(half, dtype=np.float32) * np.float32(-math.log(10000.0) / half))
        angles = np.arange(count, dtype=np.float32)[:, None] * inverse[None, :]
        table[first : first + count, at : at + half] = np.sin(angles)
        table[first : first + count, at + half : at + part] = np.cos(angles)
        at, first = at + part, first + count
    return table


def norm_parts(values):
    center = values - jnp.mean(values, axis=-1, keepdims=True)
    spread = jnp.mean(center * center, axis=-1, keepdims=True)
    factor = lax.rsqrt(spread + EPSILON)
    return center * factor, factor


def norm_back(upstream, hat, factor, gain):
    scaled = upstream * gain
    first = jnp.mean(scaled, axis=-1, keepdims=True)
    second = jnp.mean(scaled * hat, axis=-1, keepdims=True)
    return factor * (scaled - first - hat * second)


def clip_label(places, scal, clips, rows, mp):
    label, end = jnp.zeros_like(places), 0
    for c in range(clips):
        end = end + scal[1 + c]
        label = label + (places >= end).astype(jnp.int32)
    return jnp.where((places >= 0) & (places < rows * mp), label, -1)


def tile_range(first, last, base, scal, clips):
    start, end, stop = 0, 0, 0
    for c in range(clips):
        length = scal[1 + c]
        stop = jnp.where(end <= last, end + length, stop)
        end = end + length
        start = jnp.where(end <= first, end, start)
    return lax.div(start - base, TILE), lax.div(stop - base + TILE - 1, TILE)


def forward_kernel(layout, scal, q_ref, k_ref, v_ref, o_ref, lse_ref, s_ref, lq_ref, lk_ref):
    clips, mp = layout
    rows, window = q_ref.shape[0], k_ref.shape[0]
    base = scal[0] * rows - (window - rows) // 2

    @pl.when(pl.program_id(0) == 0)
    def _():
        own = scal[0] * rows + lax.broadcasted_iota(jnp.int32, lq_ref.shape, 1)
        lq_ref[...] = clip_label(own, scal, clips, rows, mp)
        around = base + lax.broadcasted_iota(jnp.int32, lk_ref.shape, 0)
        lk_ref[...] = clip_label(around, scal, clips, rows, mp)

    row = lax.broadcasted_iota(jnp.int32, (2 * HEAD_SIZE, TILE), 0)
    beside = lambda pair: jnp.concatenate(pair, axis=1)
    groups = lambda array: array.reshape(TILE // 8, 8, 2 * TILE)
    pairs = q_ref.shape[1] // PAIR
    for block in range(rows // TILE):
        first = scal[0] * rows + block * TILE
        low, high = tile_range(first, first + TILE - 1, base, scal, clips)
        span = slice(block * TILE, (block + 1) * TILE)
        query_th = []
        for g in range(pairs):
            query_t = q_ref[span, g * PAIR : (g + 1) * PAIR].T
            zero = jnp.zeros_like(query_t)
            query_th.append(
                beside(
                    [
                        jnp.where(row < HEAD_SIZE, query_t, zero),
                        jnp.where(row < HEAD_SIZE, zero, query_t),
                    ]
                )
            )
        label = lq_ref[0:1, span]
        label = beside([label, label])

        def scores(t, carry):
            at = pl.multiple_of(t * TILE, TILE)
            same = beside([lk_ref[pl.ds(at, TILE), :]] * 4) == label
            out = []
            for g in range(pairs):
                key = k_ref[pl.ds(at, TILE), g * PAIR : (g + 1) * PAIR]
                s = jnp.where(same, dot(key, query_th[g]), -1e30)
                s_ref[g, pl.ds(at, TILE), :] = s
                out.append(jnp.maximum(carry[g], jnp.max(groups(s), axis=0)))
            return tuple(out)

        least = jnp.full((8, 2 * TILE), -1e30, F32)
        peaks = lax.fori_loop(low, high, scores, (least,) * pairs)
        peaks = [jnp.max(item, axis=0, keepdims=True) for item in peaks]

        def blend(t, carry):
            at = pl.multiple_of(t * TILE, TILE)
            out = []
            for g in range(pairs):
                total, *accs = carry[g]
                p = jnp.exp(s_ref[g, pl.ds(at, TILE), :] - peaks[g])
                weights = p.astype(BF16)
                value_t = v_ref[pl.ds(at, TILE), g * PAIR : (g + 1) * PAIR].T
                total = total + jnp.sum(groups(p), axis=0)
                parts = [
                    accs[h]
                    + dot(
                        value_t[h * HEAD_SIZE : (h + 1) * HEAD_SIZE],
                        weights[:, h * TILE : (h + 1) * TILE],
                    )
                    for h in range(2)
                ]
                out.append((total, *parts))
            return tuple(out)

        zero = jnp.zeros((HEAD_SIZE, TILE), F32)
        start = (jnp.zeros((8, 2 * TILE), F32), zero, zero)
        done = lax.fori_loop(low, high, blend, (start,) * pairs)
        for g in range(pairs):
            total, *accs = done[g]
            total = jnp.sum(total, axis=0, keepdims=True)
            lse = peaks[g] + jnp.log(total)
            for h in range(2):
                columns = slice(h * TILE, (h + 1) * TILE)
                lse_ref[g, h : h + 1, span] = lse[:, columns]
                accs[h] = accs[h] / total[:, columns]
            o_ref[span, g * PAIR : (g + 1) * PAIR] = jnp.concatenate(accs, axis=0).T.astype(BF16)


def backward_kernel(
    layout,
    scal,
    q_ref,
    k_ref,
    v_ref,
    do_ref,
    o_ref,
    lse_ref,
    dq_ref,
    dk_ref,
    dv_ref,
    dk_acc,
    dv_acc,
    lq_ref,
    lk_ref,
):
    clips, mp = layout
    rows, window = q_ref.shape[0], k_ref.shape[0]
    base = scal[0] * rows - (window - rows) // 2

    @pl.when(pl.program_id(0) == 0)
    def _():
        own = scal[0] * rows + lax.broadcasted_iota(jnp.int32, lq_ref.shape, 1)
        lq_ref[...] = clip_label(own, scal, clips, rows, mp)
        around = base + lax.broadcasted_iota(jnp.int32, lk_ref.shape, 0)
        lk_ref[...] = clip_label(around, scal, clips, rows, mp)

    lane = lax.broadcasted_iota(jnp.int32, (TILE, 2 * HEAD_SIZE), 1)
    row = lax.broadcasted_iota(jnp.int32, (2 * HEAD_SIZE, TILE), 0)
    dk_acc[...] = jnp.zeros_like(dk_acc)
    dv_acc[...] = jnp.zeros_like(dv_acc)

    def halves(array, where):
        zero = jnp.zeros_like(array)
        return [jnp.where(where < HEAD_SIZE, array, zero), jnp.where(where < HEAD_SIZE, zero, array)]

    beside = lambda pair: jnp.concatenate(pair, axis=1)
    pairs = q_ref.shape[1] // PAIR
    for block in range(rows // TILE):
        first = scal[0] * rows + block * TILE
        low, high = tile_range(first, first + TILE - 1, base, scal, clips)
        span = slice(block * TILE, (block + 1) * TILE)
        label = lq_ref[0:1, span]
        label = beside([label, label])
        fixed = []
        for g in range(pairs):
            own = slice(g * PAIR, (g + 1) * PAIR)
            query, grad = q_ref[span, own], do_ref[span, own]
            query_t, grad_t = query.T, grad.T
            product = grad_t.astype(F32) * o_ref[span, own].T.astype(F32)
            delta = beside(
                [
                    jnp.sum(product[h * HEAD_SIZE : (h + 1) * HEAD_SIZE], axis=0, keepdims=True)
                    for h in range(2)
                ]
            )
            lse = beside([lse_ref[g, h : h + 1, span] for h in range(2)])
            query_h = jnp.concatenate(halves(query, lane), axis=0)
            grad_h = jnp.concatenate(halves(grad, lane), axis=0)
            query_th, grad_th = beside(halves(query_t, row)), beside(halves(grad_t, row))
            fixed.append((own, delta, lse, query_h, grad_h, query_th, grad_th))

        def step(t, carry):
            at = pl.multiple_of(t * TILE, TILE)
            same = beside([lk_ref[pl.ds(at, TILE), :]] * 4) == label
            out = []
            for g in range(pairs):
                own, delta, lse, query_h, grad_h, query_th, grad_th = fixed[g]
                key, value = k_ref[pl.ds(at, TILE), own], v_ref[pl.ds(at, TILE), own]
                key_t = key.T
                p = jnp.where(same, jnp.exp(dot(key, query_th) - lse), 0.0)
                ds = (p * (dot(value, grad_th) - delta)).astype(BF16)
                dv_acc[pl.ds(at, TILE), own] += dot(p.astype(BF16), grad_h)
                dk_acc[pl.ds(at, TILE), own] += dot(ds, query_h)
                out.extend(
                    carry[2 * g + h]
                    + dot(
                        key_t[h * HEAD_SIZE : (h + 1) * HEAD_SIZE], ds[:, h * TILE : (h + 1) * TILE]
                    )
                    for h in range(2)
                )
            return tuple(out)

        zero = jnp.zeros((HEAD_SIZE, TILE), F32)
        parts = lax.fori_loop(low, high, step, (zero,) * (2 * pairs))
        for g in range(pairs):
            total = jnp.concatenate(parts[2 * g : 2 * g + 2], axis=0) * (1.0 / math.sqrt(HEAD_SIZE))
            dq_ref[span, fixed[g][0]] = total.T.astype(BF16)
    dk_ref[...] = dk_acc[...].astype(BF16)
    dv_ref[...] = dv_acc[...].astype(BF16)


def attention_call(kernel, name, scal, columns, others, outs, scratch, part, before, work):
    first, count, total = part
    each = min(PAIRS, count)
    pair, first, count = each * PAIR, first // each, count // each
    anywhere = pl.BlockSpec(memory_space=pl.ANY)
    column = lambda item: pl.BlockSpec((item.shape[0], pair), lambda p, b: (0, first + p))
    result = pl.pallas_call(
        kernel,
        grid_spec=pltpu.PrefetchScalarGridSpec(
            num_scalar_prefetch=1,
            grid=(count,),
            in_specs=[column(item) for item in columns]
            + [
                pl.BlockSpec((each,) + item.shape[1:], lambda p, b: (first + p, 0, 0))
                if item.ndim == 3
                else pl.BlockSpec(item.shape, lambda p, b: (0, 0))
                for item in others
            ]
            + [anywhere] * len(before),
            out_specs=[
                pl.BlockSpec((each,) + shape[1:], lambda p, b: (first + p, 0, 0))
                if len(shape) == 3
                else pl.BlockSpec((shape[0], pair), lambda p, b: (0, first + p))
                for shape, _ in outs
            ],
            scratch_shapes=scratch,
        ),
        out_shape=[jax.ShapeDtypeStruct(shape, kind) for shape, kind in outs],
        input_output_aliases={
            1 + len(columns) + len(others) + i: i for i in range(len(before))
        },
        compiler_params=pltpu.CompilerParams(vmem_limit_bytes=32 * MIB),
        cost_estimate=pl.CostEstimate(flops=count * each * work, bytes_accessed=0, transcendentals=0),
        name=name,
    )(scal, *columns, *others, *before)
    return result


def attention_forward(scal, mp, queries, keys, values, part, before=()):
    rows, width = queries.shape
    window = keys.shape[0]

    def kernel(*refs):
        forward_kernel((scal.shape[0] - 1, mp), *refs[:4], *refs[4 + len(before) :])

    return attention_call(
        kernel,
        "attention_forward",
        scal,
        (queries, keys, values),
        (),
        [((rows, width), BF16), ((part[2], 2, rows), F32)],
        [
            pltpu.VMEM((min(PAIRS, part[1]), window, 2 * TILE), F32),
            pltpu.VMEM((8, rows), jnp.int32),
            pltpu.VMEM((window, 128), jnp.int32),
        ],
        part,
        before,
        5 * 10**9,
    )


def attention_backward(scal, mp, queries, keys, values, grads, attended, lse, part, before=()):
    rows, width = queries.shape
    window = keys.shape[0]

    def kernel(*refs):
        backward_kernel((scal.shape[0] - 1, mp), *refs[:7], *refs[7 + len(before) :])

    return attention_call(
        kernel,
        "attention_backward",
        scal,
        (queries, keys, values, grads, attended),
        (lse,),
        [((rows, width), BF16), ((window, width), BF16), ((window, width), BF16)],
        [pltpu.VMEM((window, min(PAIRS, part[1]) * PAIR), F32)] * 2
        + [pltpu.VMEM((8, rows), jnp.int32), pltpu.VMEM((window, 128), jnp.int32)],
        part,
        before,
        6 * 10**9,
    )


def assemble(target, buffers, meta, block, first=0):
    each = buffers[0].shape[0] // block
    span = slice(first, first + buffers[0].shape[1])
    for i in range(len(buffers) * each):
        at = pl.multiple_of(meta[1 + i] * block, block)
        source = buffers[i // each]
        target[pl.ds(at, block), span] = source[i % each * block : (i % each + 1) * block, :]


def turn(target, source, meta, block, lead):
    lead[...] = source.T
    for i in range(target.shape[0] // block):
        at = pl.multiple_of(meta[1 + i] * block, block)
        target[i * block : (i + 1) * block, :] = lead[pl.ds(at, block), :]


def fixed(shape):
    return pl.BlockSpec(shape, lambda *_: (0,) * len(shape), pipeline_mode=pl.Buffered(1))


def call(kernel, name, grid, meta, ins, outs, scratch, vmem, flops, moved=0):
    return pl.pallas_call(
        kernel,
        grid_spec=pltpu.PrefetchScalarGridSpec(
            num_scalar_prefetch=1,
            grid=grid,
            in_specs=[spec for _, spec in ins],
            out_specs=[spec for _, _, spec in outs],
            scratch_shapes=scratch,
        ),
        out_shape=[jax.ShapeDtypeStruct(shape, kind) for shape, kind, _ in outs],
        compiler_params=pltpu.CompilerParams(vmem_limit_bytes=vmem * MIB),
        cost_estimate=pl.CostEstimate(flops=flops, bytes_accessed=moved, transcendentals=0),
        name=name,
    )(meta, *[array for array, _ in ins])


def turn_kernel(block, meta, source, target, lead):
    turn(target, source[...], meta, block, lead)


def turned_rows(source, meta, block):
    rows, width = source.shape
    return call(
        functools.partial(turn_kernel, block),
        "turn",
        (1,),
        meta,
        [(source, fixed(source.shape))],
        [((width, rows), BF16, fixed((width, rows)))],
        [pltpu.VMEM((width, rows), BF16)],
        24,
        4 * 10**9,
    )[0]


def project_kernel(block, scale, own, meta, x, around, bias, *refs):
    weights, (q, k, v), scratch = refs[:-6], refs[-6:-3], refs[-3:]
    if own:
        scratch = weights
    else:
        for w in range(3):
            assemble(scratch[w], weights[4 * w : 4 * w + 4], meta, block)
    q[...] = (dot(x[...], scratch[0][...]) + bias[6:7, :]).astype(BF16) * jnp.asarray(scale, BF16)
    k[...] = dot(around[...], scratch[1][...]).astype(BF16)
    v[...] = (dot(around[...], scratch[2][...]) + bias[7:8, :]).astype(BF16)


def gathered_specs(buffers, kinds, extent, stride):
    return [
        (item, pl.BlockSpec((item.shape[0], extent), lambda i, m, kind=kind: (0, i * stride + kind)))
        for kind in kinds
        for item in buffers
    ]


def project(x, around, weights, narrow, meta, block, mp, own):
    rows, width = x.shape
    window = around.shape[0]
    extent = width // mp
    first, count = (0, 1) if own else (1, mp - 1)
    column = lambda n: pl.BlockSpec((n, extent), lambda i, m: (0, i))
    turned = lambda i, m: (0, lax.rem(m[0] - first - i + mp, mp))
    return call(
        functools.partial(project_kernel, block, 1.0 / math.sqrt(HEAD_SIZE), own),
        "project",
        (count,),
        meta,
        [
            (x, fixed(x.shape)),
            (around, fixed(around.shape)),
            (narrow, pl.BlockSpec((8, extent), turned)),
        ]
        + (
            [(w, fixed(w.shape)) for w in weights]
            if own
            else gathered_specs(weights, (0, 1, 2), extent, 4)
        ),
        [
            ((rows, count * extent), BF16, column(rows)),
            ((window, count * extent), BF16, column(window)),
            ((window, count * extent), BF16, column(window)),
        ],
        [pltpu.VMEM((width, extent), BF16)] * 3,
        40,
        count * 4 * 10**9,
    )


def join(parts, axis):
    return jnp.concatenate(parts, axis=axis)


class Plane:
    def __init__(self, size):
        self.size = size
        bits = list(range(1, size.bit_length() - 1))
        turn = len(bits) // 2
        self.orders = [bits, bits[turn:] + bits[:turn]]
        held = []
        for order in self.orders:
            masks = [0]
            for bit in order:
                masks = masks + [m ^ (1 << bit) for m in masks]
            held.append(masks)
        self.masks = [held[c] + [1 ^ m for m in held[1 - c]] for c in range(2)]
        self.steps = len(bits)

    def pairs(self, step):
        return [(i, i ^ (1 << self.orders[i % 2][step])) for i in range(self.size)]

    def siblings(self):
        return [(i, i ^ 1) for i in range(self.size)]

    def order(self, d):
        return jnp.bitwise_xor(jnp.array(self.masks, jnp.int32)[d % 2], d)


def shifted(payload, r, mp):
    return lax.ppermute(payload, "mp", [(i, (i + r) % mp) for i in range(mp)])


def spread_chips(held, plane):
    for step in range(plane.steps - 2):
        held = join([held, lax.ppermute(held, "dp", plane.pairs(step))], 0)
    return held, lax.ppermute(held, "dp", plane.pairs(plane.steps - 2))


def added(left, right):
    return (left.astype(F32) + right.astype(F32)).astype(BF16)


def folded(keep, got):
    half = keep.shape[0] // 2
    return added(keep[:half], got[:half]), added(keep[half:], got[half:])


def after(value, *others):
    return lax.optimization_barrier((value,) + others)[0]


class Scatter:
    def __init__(self, keep, upper, shifts, plane, mp):
        self.keep, self.shifts, self.plane, self.mp = keep, shifts, plane, mp
        self.step = plane.steps - 1
        self.got = lax.ppermute(upper, "dp", plane.pairs(self.step))

    def next(self):
        self.step -= 1
        self.keep, upper = folded(self.keep, self.got)
        self.got = lax.ppermute(upper, "dp", self.plane.pairs(self.step))
        return self


MESH = pl.DeviceIdType.MESH


def flipped(d, bit):
    return d + (1 - 2 * lax.rem(lax.div(d, 1 << bit), 2)) * (1 << bit)


def meet(d, z, dp, mp):
    barrier = pltpu.get_barrier_semaphore()
    for step in range(1, dp):
        there = (lax.rem(d + step, dp), z)
        pl.semaphore_signal(barrier, inc=1, device_id=there, device_id_type=MESH)
    for step in range(1, mp):
        there = (d, lax.rem(z + step, mp))
        pl.semaphore_signal(barrier, inc=1, device_id=there, device_id_type=MESH)
    pl.semaphore_wait(barrier, dp + mp - 2)


def remote(source, target, send_sem, recv_sem, device):
    return pltpu.make_async_remote_copy(
        src_ref=source,
        dst_ref=target,
        send_sem=send_sem,
        recv_sem=recv_sem,
        device_id=device,
        device_id_type=MESH,
    )


def peers_start(source, slots, send_sem, recv_sem, along, me, extent, each):
    copies = []
    for step in range(1, extent):
        place = lax.rem(me + step, extent)
        copies.append(
            remote(
                source.at[place if each else 0],
                slots.at[me],
                send_sem.at[step],
                recv_sem.at[me],
                along(step),
            )
        )
        copies[-1].start()
    slots[me] = source[me if each else 0]
    return copies


def peers_finish(copies, slots, recv_sem, me, extent):
    for step in range(1, extent):
        copies[step - 1].wait_send()
        sender = lax.rem(me + step, extent)
        pltpu.make_async_copy(slots.at[sender], slots.at[sender], recv_sem.at[sender]).wait()


def begin_kernel(plane, mp, hops, margin, *refs):
    (sheet, tokens, index, table), shards_in, refs = refs[:4], refs[4:10], refs[10:]
    (narrow, broad, stream, around, normed_out, second_out), buffers = refs[:6], refs[6:10]
    (middle, first, second, normed, zeros, payload, out_in, out_t), refs = refs[10:18], refs[18:]
    (reduce_in, reduce_t, take), refs = refs[:3], refs[3:]
    send_one, recv_one, send_two, recv_two, refs = *refs[:4], refs[4:]
    z_send, z_recv, chip_send, chip_recv, core_send, core_recv, halo_send, halo_recv, local = refs
    dp = plane.size
    d, z = lax.axis_index("dp"), lax.axis_index("mp")
    core = lax.rem(d, 2)
    rows, width = tokens.shape
    block, columns = payload.shape
    along_dp = lambda step: (lax.rem(d + step, dp), z)
    along_mp = lambda step: (d, lax.rem(z + step, mp))

    query, key, value, output, expand, reduce = shards_in
    extent, hidden_extent = query.shape[1], expand.shape[1]
    mine = pl.ds(pl.multiple_of(d * block, block), block)
    line = pl.ds(pl.multiple_of(lax.div(d * block, 128) * 128, 128), 128)
    taken = [
        pltpu.make_async_copy(
            source.at[mine, :], payload.at[:, pl.ds(w * extent, extent)], take.at[w]
        )
        for w, source in enumerate((query, key, value))
    ]
    taken.append(pltpu.make_async_copy(output.at[:, line], out_in, take.at[3]))
    taken.append(pltpu.make_async_copy(reduce.at[:, line], reduce_in, take.at[4]))
    taken.append(
        pltpu.make_async_copy(
            expand.at[mine, :], second_out.at[:, pl.ds(0, hidden_extent)], take.at[5]
        )
    )
    for copy in taken:
        copy.start()
    zeros[...] = jnp.zeros_like(zeros)
    meet(d, z, dp, mp)
    vectors = peers_start(sheet, first, send_one, recv_one, along_mp, z, mp, False)
    for copy in taken[:4]:
        copy.wait()
    out_t[...] = out_in[...].T
    within = pl.ds(pl.multiple_of(lax.rem(d * block, 128), block), block)
    payload[:, 3 * extent :] = out_t[within, :]

    each = dp // 4

    def place(j, r, other=False):
        return buffers[j // each + (2 if other else 0)].at[
            pl.ds(j % each * block, block), pl.ds((r - 1) * columns, columns)
        ]

    def passed_on(way, r):
        before = r - 1 if way == 0 else (r + 1) % mp
        source = place(0, before) if before else payload
        return remote(
            source, place(0, r), z_send.at[way, r], z_recv.at[r], (d, z + 1 if way == 0 else z - 1)
        )

    last, least = z + 1 < mp, z > 0
    line_sends = [(last & (z >= r - 1), passed_on(0, r).wait_send) for r in range(1, mp)]
    line_sends += [(least & (z <= r), passed_on(1, r).wait_send) for r in range(1, mp)]
    pl.when(last)(passed_on(0, 1).start)
    pl.when(least)(passed_on(1, mp - 1).start)

    kept = index[...]
    coarse = lax.div(kept, 14)
    frame = lax.div(kept, 196)
    across = coarse - frame * 14
    line = kept - coarse * 14
    count = lax.broadcasted_iota(jnp.int32, (table.shape[0], rows), 0)
    hot = ((count == frame) | (count == across + 8) | (count == line + 22)).astype(F32)
    hidden = tokens[...].astype(F32) + lax.dot_general(
        hot, table[...], TN, precision=lax.Precision.HIGHEST, preferred_element_type=F32
    )
    stream[...] = hidden

    peers_finish(vectors, first, recv_one, z, mp)
    middle[0] = jnp.sum(first[...], axis=0)
    vectors = peers_start(middle, second, send_two, recv_two, along_dp, d, dp, False)
    hat, _ = norm_parts(hidden)
    peers_finish(vectors, second, recv_two, d, dp)
    share = dp // (width // 128)
    for c in range(width // 128):
        narrow[:, c * 128 : (c + 1) * 128] = jnp.sum(
            second[c * share : (c + 1) * share, 0:8, :], axis=0
        )
    lines = broad.shape[1] // 128
    per = lines // dp
    for c in range(lines):
        row = second[c // per, 8 + c % per : 9 + c % per, :]
        broad[:, c * 128 : (c + 1) * 128] = jnp.broadcast_to(row, (8, 128))
    normed[...] = (hat * narrow[0:1, :] + narrow[1:2, :]).astype(BF16)
    taken[4].wait()
    reduce_t[...] = reduce_in[...].T
    shares = (
        pltpu.make_async_copy(
            reduce_t.at[within, :],
            second_out.at[:, pl.ds(hidden_extent, hidden_extent)],
            take.at[6],
        ),
        pltpu.make_async_copy(normed, normed_out, take.at[7]),
    )
    for copy in shares:
        copy.start()

    sent = []

    def arrived(j, r):
        pltpu.make_async_copy(place(j, r), place(j, r), z_recv.at[r]).wait()

    def copies_of(j, r):
        copies = []
        for step in range(plane.steps):
            if j < 1 << step:
                there = (1 - core) * flipped(d, plane.orders[0][step]) + core * flipped(
                    d, plane.orders[1][step]
                )
                to = (1 << step) + j
                copies.append(
                    remote(
                        place(j, r),
                        place(to, r),
                        chip_send.at[r, to],
                        chip_recv.at[r, to],
                        (there, z),
                    )
                )
        copies.append(
            remote(
                place(j, r),
                place(j, r, True),
                core_send.at[r, j],
                core_recv.at[r, j],
                (flipped(d, 0), z),
            )
        )
        return copies

    def forward(j, r):
        for copy in copies_of(j, r):
            copy.start()

    def handle(h):

        @pl.when(z >= h)
        def _():
            arrived(0, h)
            if h + 1 < mp:
                pl.when(last)(passed_on(0, h + 1).start)
            forward(0, h)

        @pl.when(z + h < mp)
        def _():
            arrived(0, mp - h)
            if mp - h > 1:
                pl.when(least)(passed_on(1, mp - h - 1).start)
            forward(0, mp - h)

    for h in range(1, mp - 1):
        handle(h)

    waits, at_left, at_right = [], margin, margin + rows
    inside = pltpu.make_async_copy(
        normed, around.at[pl.ds(margin, rows), :], local.at[0]
    )
    inside.start()
    waits.append((None, inside.wait))
    for hop, extent in enumerate(hops, 1):
        left = around.at[pl.ds(at_left - extent, extent), :]
        right = around.at[pl.ds(at_right, extent), :]
        sides = (
            (left, normed.at[pl.ds(rows - extent, extent), :], z + hop, z - hop, 2 * hop - 2),
            (right, normed.at[pl.ds(0, extent), :], z - hop, z + hop, 2 * hop - 1),
        )
        for target, source, there, back, n in sides:
            goes = (there >= 0) & (there < mp)
            comes = (back >= 0) & (back < mp)
            copy = remote(source, target, halo_send.at[n], halo_recv.at[n], (d, there))
            blank = pltpu.make_async_copy(zeros.at[pl.ds(0, extent), :], target, local.at[1 + n])
            pl.when(goes)(copy.start)
            pl.when(jnp.logical_not(comes))(blank.start)
            waits.append((goes, copy.wait_send))
            waits.append((comes, copy.wait_recv))
            waits.append((jnp.logical_not(comes), blank.wait))
        at_left, at_right = at_left - extent, at_right + extent
    if at_left:
        for n, at in enumerate((0, at_right)):
            blank = pltpu.make_async_copy(
                zeros.at[pl.ds(0, at_left), :],
                around.at[pl.ds(at, at_left), :],
                local.at[1 + 2 * len(hops) + n],
            )
            blank.start()
            waits.append((None, blank.wait))

    for h in range(mp - 1, mp):
        handle(h)
    for r in range(1, mp):
        sent.extend(copies_of(0, r))
    for j in range(1, 1 << plane.steps):
        for r in range(1, mp):
            pltpu.make_async_copy(place(j, r), place(j, r), chip_recv.at[r, j]).wait()
            forward(j, r)
            sent.extend(copies_of(j, r))
    for j in range(1 << plane.steps):
        for r in range(1, mp):
            pltpu.make_async_copy(place(j, r, True), place(j, r, True), core_recv.at[r, j]).wait()
    for copy in sent:
        copy.wait_send()
    for when, wait in line_sends:
        pl.when(when)(wait)
    taken[5].wait()
    for copy in shares:
        copy.wait()
    for when, wait in waits:
        wait() if when is None else pl.when(when)(wait)


def begin(sheet, tokens, index, table, shards, plane, mp, hops, margin):
    dp = plane.size
    rows, width = tokens.shape
    extent, hidden = shards[0].shape[1], shards[4].shape[1]
    block, columns, full_hidden = width // dp, 4 * extent, hidden * mp
    vmem, anywhere = pl.BlockSpec(memory_space=pltpu.VMEM), pl.BlockSpec(memory_space=pl.ANY)
    window = 2 * margin + rows
    dma = pltpu.SemaphoreType.DMA
    blocks = dp // 2
    return pl.pallas_call(
        functools.partial(begin_kernel, plane, mp, hops, margin),
        out_shape=[
            jax.ShapeDtypeStruct((8, width), F32),
            jax.ShapeDtypeStruct((8, full_hidden), F32),
            jax.ShapeDtypeStruct((rows, width), F32),
            jax.ShapeDtypeStruct((window, width), BF16),
            jax.ShapeDtypeStruct((rows, width), BF16),
            jax.ShapeDtypeStruct((block, 2 * hidden), BF16),
        ]
        + [jax.ShapeDtypeStruct((width // 4, (mp - 1) * columns), BF16)] * 4,
        in_specs=[vmem] * 4 + [anywhere] * 6,
        out_specs=[vmem] * 3 + [anywhere] * 7,
        scratch_shapes=[
            pltpu.VMEM((1, 16, 128), F32),
            pltpu.VMEM((mp, 16, 128), F32),
            pltpu.VMEM((dp, 16, 128), F32),
            pltpu.VMEM((rows, width), BF16),
            pltpu.VMEM((rows, width), BF16),
            pltpu.VMEM((block, columns), BF16),
            pltpu.VMEM((extent, 128), BF16),
            pltpu.VMEM((128, extent), BF16),
            pltpu.VMEM((hidden, 128), BF16),
            pltpu.VMEM((128, hidden), BF16),
            dma((8,)),
            dma((mp,)),
            dma((mp,)),
            dma((dp,)),
            dma((dp,)),
            dma((2, mp)),
            dma((mp,)),
            dma((mp, blocks)),
            dma((mp, blocks)),
            dma((mp, blocks)),
            dma((mp, blocks)),
            dma((2 * len(hops),)),
            dma((2 * len(hops),)),
            dma((3 + 2 * len(hops),)),
        ],
        compiler_params=pltpu.CompilerParams(
            collective_id=1, has_side_effects=True, vmem_limit_bytes=60 * MIB
        ),
        cost_estimate=pl.CostEstimate(flops=4 * 10**10, bytes_accessed=0, transcendentals=0),
        name="begin",
    )(sheet, tokens, index, table, *shards)


def xored(d, mask):
    for bit in range(mask.bit_length()):
        if mask >> bit & 1:
            d = flipped(d, bit)
    return d


def middle_kernel(plane, mp, tile, *refs):
    (stream_in, near_in, far_in, g_in, narrow_in, broad_in), refs = refs[:6], refs[6:]
    own_o, own_e, own_r, out_parts, refs = *refs[:3], refs[3:7], refs[7:]
    (early_a, early_b), late_a, refs = refs[:2], refs[2 : 2 * mp - 2], refs[2 * mp - 2 :]
    (sums, db, own_total, moved, act, grad_mid, branch_t, grad_near, grad_far), refs = refs[:9], refs[9:]
    (keep_out, upper_out, early_o, late_b, late_c, late_d), refs = refs[:6], refs[6:]
    (mid, near, far, g, narrow, broad, o_temp, weight_o, weights, r_temp), refs = refs[:10], refs[10:]
    (x, x_t, g_t, lead, out_acc, dx_acc, keep, send, got, more), refs = refs[:10], refs[10:]
    load, weight_sem, own_sem, core_send, core_recv, chip_send, chip_recv, refs = *refs[:7], refs[7:]
    sum_send, sum_recv, near_send, near_recv, store = refs
    dp, steps = plane.size, plane.steps
    d, z = lax.axis_index("dp"), lax.axis_index("mp")
    core = lax.rem(d, 2)
    rows, width = x.shape
    block, half, quarter = width // dp, width // 2, width // 4
    extent = own_e.shape[1]
    per = extent // tile
    tiles = mp * per
    wide = 2 * extent
    full = mp // 2
    orders = [
        (1 - core) * xored(d, plane.masks[0][i]) + core * xored(d, plane.masks[1][i])
        for i in range(dp)
    ]
    sibling = (flipped(d, 0), z)

    def partner(step):
        there = (1 - core) * flipped(d, plane.orders[0][step]) + core * flipped(
            d, plane.orders[1][step]
        )
        return there, z

    def home(i):
        return pl.ds(pl.multiple_of(orders[i] * block, block), block)

    def turned(target, source):
        lead[...] = source.T
        for i in range(dp):
            target[i * block : (i + 1) * block, :] = lead[home(i), :]

    loads = [
        pltpu.make_async_copy(source, target, load.at[i])
        for i, (source, target) in enumerate(
            (
                (stream_in, mid),
                (near_in, near),
                (far_in, far),
                (g_in, g),
                (narrow_in, narrow),
                (broad_in, broad),
                (own_o, o_temp),
            )
        )
    ]
    each = dp // 4
    part_o = own_o.shape[0]
    for i in range(dp):
        for r in range(1, mp):
            pltpu.make_async_copy(
                out_parts[i // each].at[
                    pl.ds(i % each * block, block), pl.ds((4 * r - 1) * part_o, part_o)
                ],
                weight_o.at[home(i), pl.ds(r * part_o, part_o)],
                load.at[7],
            ).start()
    rest_o = weight_o.at[:, pl.ds(part_o, width - part_o)]
    for copy in loads:
        copy.start()

    def fetch(i):
        slot, r, t = i % 2, i // per, i % per
        if r == 0:
            return [
                pltpu.make_async_copy(
                    own_e.at[:, pl.ds(t * tile, tile)], weights.at[slot, 0], own_sem.at[0]
                ),
                pltpu.make_async_copy(own_r.at[pl.ds(t * tile, tile), :], r_temp, own_sem.at[1]),
            ]
        if r == 1:
            parts = (early_a, early_b) + tuple(
                early_o.at[pl.ds(n * quarter, quarter), :] for n in range(2)
            )
            first = 0
        else:
            parts, first = (None, late_b, late_c, late_d), (r - 2) * wide

        def piece(n, kind):
            column = kind * extent + t * tile
            if r > 1 and n < each:
                few = each // 2
                return late_a[2 * (r - 2) + n // few].at[
                    pl.ds(n % few * block, block), pl.ds(column, tile)
                ]
            return parts[n // each].at[pl.ds(n % each * block, block), pl.ds(first + column, tile)]

        return [
            pltpu.make_async_copy(
                piece(n, kind),
                weights.at[slot, kind, home(n), :],
                weight_sem.at[slot],
            )
            for kind in range(2)
            for n in range(dp)
        ]

    for copy in fetch(0):
        copy.start()
    meet(d, z, dp, mp)

    def late(buffer, r):
        return buffer.at[:, pl.ds((r - 2) * wide, wide)]

    sent = []
    swaps, hops = {}, {}
    for n, part in enumerate((early_a, early_b)):
        swaps[1, n] = remote(
            part,
            early_o.at[pl.ds(n * quarter, quarter), :],
            core_send.at[1, n],
            core_recv.at[1, n],
            sibling,
        )
    for r in range(2, mp):
        for n in range(2):
            part = late_a[2 * (r - 2) + n]
            span = pl.ds(n * quarter // 2, quarter // 2)
            columns = pl.ds((r - 2) * wide, wide)
            hops[r, n] = remote(
                part,
                late_b.at[span, columns],
                chip_send.at[r, n],
                chip_recv.at[r, n],
                partner(steps - 1),
            )
            swaps[r, n] = remote(
                part, late_c.at[span, columns], core_send.at[r, n], core_recv.at[r, n], sibling
            )
        swaps[r, 2] = remote(
            late(late_b, r), late(late_d, r), core_send.at[r, 2], core_recv.at[r, 2], sibling
        )
    swaps[1, 0].start()
    swaps[1, 1].start()
    for r in range(2, mp):
        for n in range(2):
            hops[r, n].start()
        for n in range(2):
            swaps[r, n].start()

    for i in range(7):
        loads[i].wait()
    pltpu.make_async_copy(rest_o, rest_o, load.at[7]).wait()
    weight_o[:, :part_o] = o_temp[...].T
    cut = near.shape[1]
    mixed = dot(near[...], weight_o[:, :cut], NT) + dot(far[...], weight_o[:, cut:], NT)
    mid[...] = mid[...] + mixed + narrow[2:3, :]
    hat, _ = norm_parts(mid[...])
    x[...] = (hat * narrow[3:4, :] + narrow[4:5, :]).astype(BF16)
    turned(x_t, x[...])
    turned(g_t, g[...])
    out_acc[...] = jnp.zeros_like(out_acc)
    dx_acc[...] = jnp.zeros_like(dx_acc)

    def swap_of(c):
        return remote(
            send.at[c % 2], got.at[c], near_send.at[c], near_recv.at[c], sibling
        )

    def rows_of(step):
        count = half >> (steps - step)
        return count, half - 2 * count

    def sum_of(c, step):
        count, at = rows_of(step)
        return remote(
            keep.at[c, pl.ds(count, count), :],
            more.at[c // 2, pl.ds(at, count), :],
            sum_send.at[c // 2, step],
            sum_recv.at[c // 2, step],
            partner(step),
        )

    def outs_of(c):
        span = pl.ds(c // 2 * wide, wide)
        return [
            pltpu.make_async_copy(
                keep.at[c, pl.ds(n * quarter, quarter), :], target.at[:, span], store.at[c, n]
            )
            for n, target in enumerate((keep_out, upper_out))
        ]

    def core_done(c):
        swap_of(c).wait_recv()
        keep[c] = added(keep[c], got[c])
        if c % 2 == 0:
            sum_of(c, steps - 1).start()
        else:
            for copy in outs_of(c):
                copy.start()

    def chips_done(c, step):
        sum_of(c, step).wait_recv()
        count, at = rows_of(step)
        keep[c, :count, :] = added(keep[c, :count, :], more[c // 2, pl.ds(at, count), :])
        if step:
            sum_of(c, step - 1).start()

    events = {}
    for r in range(2, mp):

        def passed(r=r):
            hops[r, 0].wait_recv()
            hops[r, 1].wait_recv()
            swaps[r, 2].start()

        events.setdefault((r - 1) * per, []).append(passed)
    for r in range(1, mp):

        def arrived(r=r):
            for n in range(2 if r == 1 else 3):
                swaps[r, n].wait_recv()

        events.setdefault(r * per - 1, []).append(arrived)
    for i in range(1, tiles):

        def ahead(i=i):
            for copy in fetch(i):
                copy.start()

        if i >= per:
            events.setdefault(i - 1, []).append(ahead)
    for c in range(mp - 1):
        events.setdefault((c + 2) * per - 1, []).append(functools.partial(core_done, c))
    events.setdefault(tiles - per, []).append(functools.partial(chips_done, 0, steps - 1))

    def body(i, carry):
        slot, c, t = lax.rem(i, 2), lax.div(i, per), lax.rem(i, per)

        @pl.when(c == 0)
        def _():
            pltpu.make_async_copy(weights.at[0, 0], weights.at[0, 0], own_sem.at[0]).wait()
            pltpu.make_async_copy(r_temp, r_temp, own_sem.at[1]).wait()
            weights[slot, 1] = r_temp[...].T

        @pl.when(c > 0)
        def _():
            pltpu.make_async_copy(weights.at[slot], weights.at[slot], weight_sem.at[slot]).wait()

        for n in range(1, per):

            @pl.when(i == n - 1)
            def _():
                for copy in fetch(n):
                    copy.start()

        for n, actions in events.items():

            @pl.when(i == n)
            def _():
                for action in actions:
                    action()

        @pl.when((t == 0) & (c >= 2))
        def _():
            remote(
                send.at[lax.rem(c, 2)], got.at[c], near_send.at[c - 2], near_recv.at[c], sibling
            ).wait_send()

        at = pl.multiple_of(lax.rem(z - c + mp, mp) * extent + t * tile, tile)
        bias = broad[0:1, pl.ds(at, tile)]
        out = lax.rem(c, 2)
        hiddens, grads = [], []
        few = tile // 2
        for part in range(2):
            span = slice(part * few, (part + 1) * few)
            pre = dot(x[...], weights[slot, 0, :, span]) + bias[:, span]
            cumulative = 0.5 * (1.0 + lax.erf(pre * 0.7071067811865476))
            hidden = (pre * cumulative).astype(BF16)
            slope = cumulative + pre * jnp.exp(-0.5 * pre * pre) * (1.0 / math.sqrt(2.0 * math.pi))
            grad_pre = (dot(g[...], weights[slot, 1, :, span]) * slope).astype(BF16)
            line = jnp.sum(grad_pre.astype(F32), axis=0, keepdims=True)
            db[:, pl.ds(pl.multiple_of(i * tile + part * few, few), few)] = jnp.broadcast_to(
                line, (8, few)
            )
            first = pl.ds(pl.multiple_of(2 * t * tile + part * few, few), few)
            second = pl.ds(pl.multiple_of((2 * t + 1) * tile + part * few, few), few)
            send[out, :, first] = dot(x_t[half:, :], grad_pre).astype(BF16)
            send[out, :, second] = dot(g_t[half:, :], hidden).astype(BF16)
            keep[c, :, first] = dot(x_t[:half, :], grad_pre).astype(BF16)
            keep[c, :, second] = dot(g_t[:half, :], hidden).astype(BF16)
            hiddens.append(hidden)
            grads.append(grad_pre)
        hidden, grad_pre = jnp.concatenate(hiddens, axis=1), jnp.concatenate(grads, axis=1)
        weight_e, weight_r = weights[slot, 0], weights[slot, 1]

        @pl.when(t == per - 1)
        def _():
            remote(send.at[out], got.at[c], near_send.at[c], near_recv.at[c], sibling).start()

        out_acc[...] += dot(hidden, weight_r, NT)
        dx_acc[...] += dot(grad_pre, weight_e, NT)
        return carry

    lax.fori_loop(0, tiles, body, 0)

    value, grad, dy = mid[...], g[...].astype(F32), dx_acc[...]
    x[...] = (value + out_acc[...] + narrow[5:6, :]).astype(BF16)
    hat, factor = norm_parts(value)
    back = grad + norm_back(dy, hat, factor, narrow[3:4, :])
    add = lambda v: jnp.sum(v, axis=0, keepdims=True)
    zero = jnp.zeros((4, width), F32)
    sums[...] = jnp.concatenate([add(back), add(dy * hat), add(dy), add(grad), zero], axis=0)
    mid[...] = back
    rounded = back.astype(BF16)
    turned(x_t, rounded)
    near[...] = dot(rounded, weight_o[:, :cut]).astype(BF16)
    far[...] = dot(rounded, weight_o[:, cut:]).astype(BF16)
    results = [
        pltpu.make_async_copy(source, target, load.at[i])
        for i, (source, target) in enumerate(
            ((x, act), (mid, grad_mid), (x_t, branch_t), (near, grad_near), (far, grad_far))
        )
    ]
    for copy in results:
        copy.start()

    core_done(mp - 1)
    for c in range(2, mp, 2):
        chips_done(c, steps - 1)
    for step in reversed(range(steps - 1)):
        for c in range(0, mp, 2):
            chips_done(c, step)
    own_total[...] = keep[0, :block, :].astype(F32)
    for c in range(2, mp, 2):
        moved[c // 2 - 1] = keep[c, :block, :]
    for c in range(max(0, mp - 2), mp):
        swap_of(c).wait_send()
    for c in range(0, mp, 2):
        for step in range(steps):
            sum_of(c, step).wait_send()
    for c in range(1, mp, 2):
        for copy in outs_of(c):
            copy.wait()
    for copy in list(hops.values()) + list(swaps.values()):
        copy.wait_send()
    for copy in results:
        copy.wait()


def middle(arrays, weights, buffers, parts, plane, mp, hidden):
    dp = plane.size
    rows, width = arrays[0].shape
    extent = hidden // mp
    tile = min(512, extent)
    wide, half, quarter, full = 2 * extent, width // 2, width // 4, mp // 2
    vmem, anywhere = pl.BlockSpec(memory_space=pltpu.VMEM), pl.BlockSpec(memory_space=pl.ANY)
    dma = pltpu.SemaphoreType.DMA
    shape = jax.ShapeDtypeStruct
    near = arrays[1].shape[1]
    late = (quarter, (mp - 2) * wide)
    return pl.pallas_call(
        functools.partial(middle_kernel, plane, mp, tile),
        out_shape=[
            shape((8, width), F32),
            shape((8, hidden), F32),
            shape((width // dp, wide), F32),
            shape((max(full - 1, 1), width // dp, wide), BF16),
            shape((rows, width), BF16),
            shape((rows, width), F32),
            shape((width, rows), BF16),
            shape((rows, near), BF16),
            shape((rows, width - near), BF16),
            shape((quarter, (mp - full) * wide), BF16),
            shape((quarter, (mp - full) * wide), BF16),
            shape((half, wide), BF16),
            shape(late, BF16),
            shape(late, BF16),
            shape(late, BF16),
        ],
        in_specs=[anywhere] * (len(arrays) + len(weights) + len(buffers) + len(parts)),
        out_specs=[vmem] * 4 + [anywhere] * 11,
        scratch_shapes=[
            pltpu.VMEM((rows, width), F32),
            pltpu.VMEM(arrays[1].shape, BF16),
            pltpu.VMEM(arrays[2].shape, BF16),
            pltpu.VMEM((rows, width), BF16),
            pltpu.VMEM((8, width), F32),
            pltpu.VMEM((8, hidden), F32),
            pltpu.VMEM(weights[0].shape, BF16),
            pltpu.VMEM((width, width), BF16),
            pltpu.VMEM((2, 2, width, tile), BF16),
            pltpu.VMEM((tile, width), BF16),
            pltpu.VMEM((rows, width), BF16),
            pltpu.VMEM((width, rows), BF16),
            pltpu.VMEM((width, rows), BF16),
            pltpu.VMEM((width, rows), BF16),
            pltpu.VMEM((rows, width), F32),
            pltpu.VMEM((rows, width), F32),
            pltpu.VMEM((mp, half, wide), BF16),
            pltpu.VMEM((2, half, wide), BF16),
            pltpu.VMEM((mp, half, wide), BF16),
            pltpu.VMEM((full, half, wide), BF16),
            dma((8,)),
            dma((2,)),
            dma((2,)),
            dma((mp, 3)),
            dma((mp, 3)),
            dma((mp, 2)),
            dma((mp, 2)),
            dma((full, plane.steps)),
            dma((full, plane.steps)),
            dma((mp,)),
            dma((mp,)),
            dma((mp, 2)),
        ],
        compiler_params=pltpu.CompilerParams(
            collective_id=3, has_side_effects=True, vmem_limit_bytes=60 * MIB
        ),
        cost_estimate=pl.CostEstimate(flops=6 * 10**10, bytes_accessed=0, transcendentals=0),
        name="middle",
    )(*arrays, *weights, *buffers, *parts)


def orders_of(plane, d, core):
    return [
        (1 - core) * xored(d, plane.masks[0][i]) + core * xored(d, plane.masks[1][i])
        for i in range(plane.size)
    ]


def tail_kernel(plane, mp, margin, *refs):
    (around_t, branch_t, dq, dk, dv, att), got, refs = refs[:6], refs[6:18], refs[18:]
    (kept, came, own_two), even, refs = refs[:3], refs[3 : 2 + mp // 2], refs[2 + mp // 2 :]
    (own_out, around_out, lower, upper, bias, total_out, rest_out), refs = refs[:7], refs[7:]
    weights, (payload, shards, keep, send, arrived), refs = refs[:3], refs[3:8], refs[8:]
    z_send, z_recv, core_send, core_recv = refs
    dp = plane.size
    d, z = lax.axis_index("dp"), lax.axis_index("mp")
    step, last = pl.program_id(0), mp - 2
    rows, extent = dq.shape
    width = around_t.shape[0]
    half, quarter, block = width // 2, width // 4, width // dp
    wide = own_two.shape[1]
    sibling = (flipped(d, 0), z)

    def sum_of():
        return remote(
            payload, shards, z_send.at[0], z_recv.at[0], (d, lax.rem(z - 1 + mp, mp))
        )

    @pl.when(step == 0)
    def _():
        meet(d, z, dp, mp)
        payload[...] = added(kept[:, :wide], came[:, :wide])
        sum_of().start()
        rest_out[...] = added(kept[:, wide:], came[:, wide:])

    orders = orders_of(plane, d, lax.rem(d, 2))
    each = dp // 4
    for w in range(3):
        for i in range(dp):
            source = got[4 * w + i // each]
            at = pl.multiple_of(orders[i] * block, block)
            weights[w][pl.ds(at, block), :] = source[i % each * block : (i % each + 1) * block, :]

    middle, everything = slice(margin, margin + rows), slice(None)
    for low, target in ((half, send), (0, keep)):
        for at, (left, span, right) in enumerate(
            (
                (around_t, middle, dq),
                (around_t, everything, dk),
                (around_t, everything, dv),
                (branch_t, everything, att),
            )
        ):
            target[step, :, at * extent : (at + 1) * extent] = dot(
                left[low : low + half, span], right[...]
            ).astype(BF16)
        if low:
            remote(
                send.at[step], arrived.at[step], core_send.at[step], core_recv.at[step], sibling
            ).start()
    add = lambda v: jnp.sum(v[...].astype(F32), axis=0, keepdims=True)
    bias[...] = jnp.concatenate([add(dq), add(dv), jnp.zeros((6, extent), F32)], axis=0)
    back = dot(dk[...], weights[1][...], NT) + dot(dv[...], weights[2][...], NT)
    more = dot(dq[...], weights[0][...], NT)

    @pl.when(step == 0)
    def _():
        around_out[...] = back
        own_out[...] = more

    @pl.when(step > 0)
    def _():
        around_out[...] += back
        own_out[...] += more

    def fold(n):
        swap = remote(send.at[n], arrived.at[n], core_send.at[n], core_recv.at[n], sibling)
        swap.wait_recv()
        span = slice(n * 4 * extent, (n + 1) * 4 * extent)
        lower[:, span] = added(keep[n, :quarter, :], arrived[n, :quarter, :])
        upper[:, span] = added(keep[n, quarter:, :], arrived[n, quarter:, :])

    for n in range(last):
        pl.when(step == n + 1)(functools.partial(fold, n))

    @pl.when(step == last)
    def _():
        fold(last)
        total = own_two[...]
        for item in even:
            total = total + item[...].astype(F32)
        sum_of().wait_recv()
        total_out[...] = total + shards[...].astype(F32)
        sum_of().wait_send()
        for n in range(mp - 1):
            remote(
                send.at[n], arrived.at[n], core_send.at[n], core_recv.at[n], sibling
            ).wait_send()


def tail(around_t, branch_t, grads, att, weights, sums, own_two, even, plane, mp, margin):
    dq, dk, dv = grads
    rows, width = dq.shape[0], around_t.shape[0]
    window = around_t.shape[1]
    extent = width // mp
    half, quarter, block = width // 2, width // 4, width // plane.size
    count, wide = mp - 1, own_two.shape[1]
    column = lambda item: pl.BlockSpec((item.shape[0], extent), lambda i: (0, i))
    whole = lambda shape: pl.BlockSpec(
        shape, lambda i: (0,) * len(shape), pipeline_mode=pl.Buffered(1)
    )
    pieces = [
        pl.BlockSpec((item.shape[0], extent), lambda i, kind=kind: (0, i * 4 + kind))
        for kind in range(3)
        for item in weights
    ]
    outs = [
        ((rows, width), F32),
        ((window, width), F32),
        ((quarter, 4 * count * extent), BF16),
        ((quarter, 4 * count * extent), BF16),
        ((8, count * extent), F32),
        ((block, wide), F32),
        ((block, (mp // 2 - 1) * wide), BF16),
    ]
    specs = [whole(shape) for shape, _ in outs]
    specs[4] = pl.BlockSpec((8, extent), lambda i: (0, i))
    stack = pltpu.VMEM((count, half, 4 * extent), BF16)
    dma = pltpu.SemaphoreType.DMA
    constant = (*sums, own_two, *even)
    return pl.pallas_call(
        functools.partial(tail_kernel, plane, mp, margin),
        grid=(count,),
        in_specs=[whole(around_t.shape), whole(branch_t.shape)]
        + [column(item) for item in (dq, dk, dv, att)]
        + pieces
        + [whole(item.shape) for item in constant],
        out_specs=specs,
        out_shape=[jax.ShapeDtypeStruct(shape, kind) for shape, kind in outs],
        scratch_shapes=[pltpu.VMEM((width, extent), BF16)] * 3
        + [
            pltpu.VMEM((block, wide), BF16),
            pltpu.VMEM((block, wide), BF16),
            stack,
            stack,
            stack,
            dma((1,)),
            dma((1,)),
            dma((count,)),
            dma((count,)),
        ],
        compiler_params=pltpu.CompilerParams(
            collective_id=4, has_side_effects=True, vmem_limit_bytes=60 * MIB
        ),
        cost_estimate=pl.CostEstimate(flops=24 * 10**9, bytes_accessed=0, transcendentals=0),
        name="tail",
    )(around_t, branch_t, dq, dk, dv, att, *(list(weights) * 3), *constant)


def finish_kernel(plane, mp, hops, margin, *refs):
    inputs = 18 + mp // 2
    hbm, refs = refs[:inputs], refs[inputs:]
    upper, refs = refs[0], refs[1:]
    (grad_tokens, *totals, grad_expand, grad_reduce, vectors), refs = refs[:8], refs[8:]
    loaded, refs = refs[:inputs], refs[inputs:]
    (halo_out, halo_in, keep, send, got, more_got, shards, table, sheets), refs = refs[:9], refs[9:]
    (middle, first, second), refs = refs[:3], refs[3:]
    load_sem, halo_send, halo_recv, core_sem, near_send, near_recv, far_send, far_recv = refs[:8]
    z_send, z_recv, send_one, recv_one, send_two, recv_two = refs[8:]
    (dq, dk, dv, att, wq, wk, wv, before_around, before_own) = loaded[:9]
    (around_t, branch_t, others, stream, grad_mid, narrow, sums, bias, broad) = loaded[9:18]
    dp = plane.size
    d, z = lax.axis_index("dp"), lax.axis_index("mp")
    core = lax.rem(d, 2)
    rows, extent = dq.shape
    half = keep.shape[0]
    block = totals[0].shape[0]
    columns = 4 * extent

    loads = [
        pltpu.make_async_copy(source, target, load_sem.at[i])
        for i, (source, target) in enumerate(zip(hbm, loaded))
    ]
    for copy in loads:
        copy.start()
    width = wq.shape[0]
    halo_in[...] = jnp.zeros_like(halo_in)
    meet(d, z, dp, mp)

    def partner(step):
        there = (1 - core) * flipped(d, plane.orders[0][step]) + core * flipped(
            d, plane.orders[1][step]
        )
        return there, z

    def fold(target, source, at, count):
        target[:count, :] = added(target[:count, :], source[pl.ds(at, count), :])

    sent = []
    top = half // 2

    def far_of(step):
        count = half >> (plane.steps - step)
        return remote(
            others.at[pl.ds(count, count), :],
            more_got.at[pl.ds(half - 2 * count, count), :],
            far_send.at[step],
            far_recv.at[step],
            partner(step),
        )

    came = pltpu.make_async_copy(upper, more_got.at[pl.ds(0, top), :], core_sem.at[2])
    came.start()
    came.wait()
    loads[11].wait()
    fold(others, more_got, 0, top)
    if plane.steps > 1:
        far_of(plane.steps - 2).start()

    for i in (1, 2, 5, 6, 7):
        loads[i].wait()
    waits, at_left, at_right, at = [], margin, margin + rows, 0
    copies = []
    for hop, reach in enumerate(hops, 1):
        sides = (
            (at_left - reach, z - hop, z + hop, 2 * hop - 2, rows - reach),
            (at_right, z + hop, z - hop, 2 * hop - 1, 0),
        )
        for start, there, back, n, place in sides:
            span = slice(start, start + reach)
            here = pl.ds(at, reach)
            part = dot(dk[span, :], wk[...], NT) + dot(dv[span, :], wv[...], NT)
            halo_out[here, :] = (before_around[span, :] + part).astype(BF16)
            goes = (there >= 0) & (there < mp)
            comes = (back >= 0) & (back < mp)
            copy = remote(
                halo_out.at[here, :],
                halo_in.at[here, :],
                halo_send.at[n],
                halo_recv.at[n],
                (d, there),
            )
            pl.when(goes)(copy.start)
            waits.append((goes, copy.wait_send))
            copies.append((comes, copy.wait_recv, place, at, reach))
            at += reach
        at_left, at_right = at_left - reach, at_right + reach

    for i in (0, 3, 9, 10):
        loads[i].wait()
    inner, everything = slice(margin, margin + rows), slice(None)

    def weight_grads(target, low):
        for n, (source, span, right) in enumerate(
            (
                (around_t, inner, dq),
                (around_t, everything, dk),
                (around_t, everything, dv),
                (branch_t, everything, att),
            )
        ):
            target[:, n * extent : (n + 1) * extent] = dot(
                source[low : low + half, span], right[...]
            ).astype(BF16)

    weight_grads(send, half)
    swap = remote(send, got.at[pl.ds(0, half), :], core_sem.at[0], core_sem.at[1], (flipped(d, 0), z))
    swap.start()
    sent.append(swap)
    weight_grads(keep, 0)

    for step in reversed(range(plane.steps - 1)):
        far_of(step).wait_recv()
        count = half >> (plane.steps - step)
        fold(others, more_got, half - 2 * count, count)
        if step:
            far_of(step - 1).start()
        sent.append(far_of(step))
    for r in range(1, mp):
        copy = remote(
            others.at[pl.ds(0, block), pl.ds((r - 1) * columns, columns)],
            shards.at[r],
            z_send.at[r],
            z_recv.at[r],
            (d, lax.rem(z - r + mp, mp)),
        )
        copy.start()
        sent.append(copy)

    swap.wait_recv()
    fold(keep, got, 0, half)
    count, at_near = half, half
    for step in reversed(range(plane.steps)):
        count //= 2
        near = remote(
            keep.at[pl.ds(count, count), :],
            got.at[pl.ds(at_near, count), :],
            near_send.at[step],
            near_recv.at[step],
            partner(step),
        )
        near.start()
        sent.append(near)
        if step == plane.steps - 1:
            loads[4].wait()
            loads[8].wait()
            own = before_own[...] + before_around[inner, :] + dot(dq[...], wq[...], NT)
            own += dot(dk[inner, :], wk[...], NT) + dot(dv[inner, :], wv[...], NT)
            before_own[...] = own
        near.wait_recv()
        fold(keep, got, at_near, count)
        at_near += count

    for i in range(12, 18):
        loads[i].wait()
    for comes, wait, *_ in copies:
        pl.when(comes)(wait)
    for _, _, place, at, reach in copies:
        span = slice(place, place + reach)
        before_own[span, :] = before_own[span, :] + halo_in[at : at + reach, :].astype(F32)
    hat, factor = norm_parts(stream[...])
    upstream = before_own[...]
    add = lambda v: jnp.sum(v, axis=0, keepdims=True)
    back = grad_mid[...] + norm_back(upstream, hat, factor, narrow[0:1, :])
    grad_tokens[...] = back.astype(BF16)
    table[0:1, :] = add(upstream * hat)
    table[1:2, :] = add(upstream)
    table[2:6, :] = sums[0:4, :]
    mine = pl.ds(pl.multiple_of(z * extent, extent), extent)
    table[6:7, mine] = add(dq[...].astype(F32))
    table[7:8, mine] = add(dv[...].astype(F32))
    for r in range(1, mp):
        place = pl.ds(pl.multiple_of(lax.rem(z - r + mp, mp) * extent, extent), extent)
        table[6:8, place] = bias[0:2, (r - 1) * extent : r * extent]
    each = dp // (width // 128)
    hidden = broad.shape[1]
    lines = hidden // dp // 128
    per = hidden // mp // 128
    sheets[...] = jnp.zeros_like(sheets)
    for i in range(dp):
        c = i // each
        sheets[i, 0:8, :] = table[:, c * 128 : (c + 1) * 128]
        for n in range(lines):
            shard, at = (i * lines + n) // per, (i * lines + n) % per
            start = (lax.rem(z - shard + mp, mp) * per + at) * 128
            sheets[i, 8 + n : 9 + n, :] = broad[0:1, pl.ds(pl.multiple_of(start, 128), 128)]
    along_dp = lambda step: (lax.rem(d + step, dp), z)
    along_mp = lambda step: (d, lax.rem(z + step, mp))
    out = peers_start(sheets, second, send_two, recv_two, along_dp, d, dp, True)
    peers_finish(out, second, recv_two, d, dp)
    middle[0] = jnp.sum(second[...], axis=0)
    out = peers_start(middle, first, send_one, recv_one, along_mp, z, mp, False)
    for copy in loads[18:]:
        copy.wait()
    full = loaded[18][...]
    for item in loaded[19:]:
        full = full + item[...].astype(F32)
    tile = min(512, full.shape[1] // 2)
    for n in range(full.shape[1] // tile // 2):
        span = slice(n * tile, (n + 1) * tile)
        grad_expand[:, span] = full[:, 2 * n * tile : (2 * n + 1) * tile]
        grad_reduce[span, :] = full[:, (2 * n + 1) * tile : (2 * n + 2) * tile].T

    full = keep[:block, :].astype(F32)
    for r in range(1, mp):
        pltpu.make_async_copy(shards.at[r], shards.at[r], z_recv.at[r]).wait()
        full += shards[r].astype(F32)
    for n, item in enumerate(totals):
        part = full[:, n * extent : (n + 1) * extent]
        item[...] = part if n < 3 else part.T
    peers_finish(out, first, recv_one, z, mp)
    vectors[...] = jnp.sum(first[...], axis=0)
    for copy in sent:
        copy.wait_send()
    for when, wait in waits:
        pl.when(when)(wait)


def finish(arrays, upper, plane, mp, hops, margin):
    dp = plane.size
    rows, extent = arrays[0].shape
    width = arrays[4].shape[0]
    block, half, columns = width // dp, width // 2, 4 * extent
    hidden = arrays[18].shape[1] // 2
    vmem, anywhere = pl.BlockSpec(memory_space=pltpu.VMEM), pl.BlockSpec(memory_space=pl.ANY)
    dma = pltpu.SemaphoreType.DMA
    left = sum(hops)
    return pl.pallas_call(
        functools.partial(finish_kernel, plane, mp, hops, margin),
        out_shape=[
            jax.ShapeDtypeStruct((rows, width), BF16),
            *[jax.ShapeDtypeStruct((block, extent), F32)] * 3,
            jax.ShapeDtypeStruct((extent, block), F32),
            jax.ShapeDtypeStruct((block, hidden), F32),
            jax.ShapeDtypeStruct((hidden, block), F32),
            jax.ShapeDtypeStruct((16, 128), F32),
        ],
        in_specs=[anywhere] * (len(arrays) + 1),
        out_specs=[vmem] * 8,
        scratch_shapes=[pltpu.VMEM(item.shape, item.dtype) for item in arrays]
        + [
            pltpu.VMEM((2 * left, width), BF16),
            pltpu.VMEM((2 * left, width), BF16),
            pltpu.VMEM((half, columns), BF16),
            pltpu.VMEM((half, columns), BF16),
            pltpu.VMEM((2 * half, columns), BF16),
            pltpu.VMEM((half, (mp - 1) * columns), BF16),
            pltpu.VMEM((mp, block, columns), BF16),
            pltpu.VMEM((8, width), F32),
            pltpu.VMEM((dp, 16, 128), F32),
            pltpu.VMEM((1, 16, 128), F32),
            pltpu.VMEM((mp, 16, 128), F32),
            pltpu.VMEM((dp, 16, 128), F32),
            dma((len(arrays),)),
            dma((2 * len(hops),)),
            dma((2 * len(hops),)),
            dma((3,)),
            dma((plane.steps,)),
            dma((plane.steps,)),
            dma((plane.steps,)),
            dma((plane.steps,)),
            dma((mp,)),
            dma((mp,)),
            dma((mp,)),
            dma((mp,)),
            dma((dp,)),
            dma((dp,)),
        ],
        compiler_params=pltpu.CompilerParams(
            collective_id=2, has_side_effects=True, vmem_limit_bytes=60 * MIB
        ),
        cost_estimate=pl.CostEstimate(flops=5 * 10**10, bytes_accessed=0, transcendentals=0),
        name="finish",
    )(*arrays, upper)


def local(
    tokens,
    kept_index,
    lengths,
    first_gain,
    first_shift,
    query_weight,
    key_weight,
    value_weight,
    query_bias,
    value_bias,
    output_weight,
    output_bias,
    second_gain,
    second_shift,
    expand_weight,
    expand_bias,
    reduce_weight,
    reduce_bias,
    cotangent,
):
    dp, mp = lax.axis_size("dp"), lax.axis_size("mp")
    d, z = lax.axis_index("dp"), lax.axis_index("mp")
    plane = Plane(dp)
    rows, width = tokens.shape
    group_rows = rows * mp
    block = width // dp
    full_hidden = expand_weight.shape[1] * mp
    meta = jnp.concatenate([z[None], plane.order(d)]).astype(jnp.int32)

    singles = (
        first_gain,
        first_shift,
        output_bias,
        second_gain,
        second_shift,
        reduce_bias,
        query_bias,
        value_bias,
    )
    single, wide = first_gain.shape[0], expand_bias.shape[0]
    me = d * mp + z
    lane = jnp.arange(128, dtype=jnp.int32)
    lines = full_hidden // dp // 128

    def placed(stack):
        count = 128 // stack.shape[1]
        return jnp.where(lane // stack.shape[1] == me % count, jnp.tile(stack, (1, count)), 0.0)

    line = placed(expand_bias[None].astype(F32))
    at_line = (jnp.arange(8, dtype=jnp.int32) == me * wide // 128 % lines)[:, None]
    sheet = jnp.concatenate(
        [placed(jnp.stack(singles).astype(F32)), jnp.where(at_line, line, 0.0)], axis=0
    )
    scal = jnp.concatenate([z[None], lengths[0]]).astype(jnp.int32)
    reach, hops, left = LONGEST - 1, [], 0
    while reach > 0:
        extent = min(rows, -(-reach // 16) * 16)
        hops.append(extent)
        left, reach = left + extent, reach - extent
    margin = -(-left // 128) * 128
    while (2 * margin + rows) % TILE:
        margin += 128

    begun = begin(
        sheet[None],
        tokens,
        kept_index[None],
        jnp.asarray(position_lines(width)),
        (query_weight, key_weight, value_weight, output_weight, expand_weight, reduce_weight),
        plane,
        mp,
        hops,
        margin,
    )
    narrow, broad, stream, around, normed_one, second = begun[:6]
    buffers = begun[6:]
    shares = {1: shifted(second, 1, mp)}
    around_t = turned_rows(around, meta, block)
    projections = (query_weight, key_weight, value_weight)
    pairs = width // (2 * HEAD_SIZE) // mp
    own = project(normed_one, around, projections, narrow, meta, block, mp, True)
    tied = after(narrow, shares[1], *own)
    rest = project(normed_one, around, buffers, tied, meta, block, mp, False)
    heads = [own, rest]
    for r in range(2, mp):
        shares[r] = shifted(after(second, shares[1]), r, mp)
    early = spread_chips(shares[1], plane)
    far, late = (), []
    for r in range(1, mp):
        part = ((r - 1) * pairs, pairs, (mp - 1) * pairs)
        if r == 1:
            far = attention_forward(after(scal, early[-1]), mp, *heads[1], part, far)
            early = join(early, 0)
            early = (early, lax.ppermute(early, "dp", plane.pairs(plane.steps - 1)))
            near = attention_forward(after(scal, *far), mp, *heads[0], (0, pairs, pairs))
        else:
            tied = after(scal, *far, *near, shares[r])
            far = attention_forward(tied, mp, *heads[1], part, far)
            late.extend(spread_chips(shares[r], plane))
    attended, lses = [near[0], far[0]], [near[1], far[1]]

    results = middle(
        (stream, *attended, cotangent, narrow, broad),
        (output_weight, expand_weight, reduce_weight),
        buffers,
        (*early, *late),
        plane,
        mp,
        full_hidden,
    )
    sums_mid, grad_bias, own_two, ready = results[:4]
    activations, grad_middle, branch_t, grad_near, grad_far, kept, upper = results[4:11]
    moved_one = [
        lax.ppermute(ready[r // 2 - 1], "mp", [(j, (j - r) % mp) for j in range(mp)])
        for r in range(2, mp, 2)
    ]
    sums_two = Scatter(kept, upper, list(range(1, mp, 2)), plane, mp)

    grads_far = ()
    for r in range(1, mp):
        part = ((r - 1) * pairs, pairs, (mp - 1) * pairs)
        tied = after(scal, *grads_far, sums_two.got) if r == mp - 1 else after(scal, *grads_far)
        grads_far = attention_backward(
            tied,
            mp,
            *heads[1],
            grad_far,
            attended[1],
            lses[1],
            part,
            tuple(grads_far),
        )
    while sums_two.step > 0:
        sums_two.next()
    partial = tail(
        around_t,
        branch_t,
        grads_far,
        attended[1],
        buffers,
        (sums_two.keep, sums_two.got),
        own_two,
        moved_one,
        plane,
        mp,
        margin,
    )
    crossed = lax.ppermute(partial[3], "dp", plane.pairs(plane.steps - 1))
    breadth = own_two.shape[1]
    moved_two = [
        lax.ppermute(
            partial[6][:, i * breadth : (i + 1) * breadth],
            "mp",
            [(j, (j - r) % mp) for j in range(mp)],
        )
        for i, r in enumerate(range(3, mp, 2))
    ]
    grads_near = attention_backward(
        after(scal, partial[0]),
        mp,
        *heads[0],
        grad_near,
        attended[0],
        lses[0],
        (0, pairs, pairs),
    )

    grad_tokens, grad_query, grad_key, grad_value, grad_out, grad_expand, grad_reduce, summed = finish(
        (
            *grads_near,
            attended[0],
            *projections,
            partial[1],
            partial[0],
            around_t,
            branch_t,
            partial[2],
            stream,
            grad_middle,
            narrow,
            sums_mid,
            partial[4],
            grad_bias,
            partial[5],
            *moved_two,
        ),
        crossed,
        plane,
        mp,
        hops,
        margin,
    )

    taken = lambda stack, extent: lax.dynamic_slice_in_dim(
        stack, me % (128 // extent) * extent, extent, 1
    )
    small = taken(summed[:8], single)
    broad_row = lax.dynamic_slice_in_dim(summed[8:], me * wide // 128 % lines, 1, 0)
    return (
        activations,
        grad_tokens,
        grad_query,
        grad_key,
        grad_value,
        grad_out,
        grad_expand,
        grad_reduce,
        small[0],
        small[1],
        small[6],
        small[7],
        small[2],
        small[3],
        small[4],
        taken(broad_row, wide)[0],
        small[5],
    )


def solution(mesh):
    vector = P(("dp", "mp"))
    tall = P(("dp", "mp"), None)
    in_specs = (
        tall,
        vector,
        P("dp", None),
        vector,
        vector,
        P(None, "mp"),
        P(None, "mp"),
        P(None, "mp"),
        vector,
        vector,
        P("mp", None),
        vector,
        vector,
        vector,
        P(None, "mp"),
        vector,
        P("mp", None),
        vector,
        tall,
    )
    out_specs = (
        tall,
        tall,
        P("dp", "mp"),
        P("dp", "mp"),
        P("dp", "mp"),
        P("mp", "dp"),
        P("dp", "mp"),
        P("mp", "dp"),
    ) + (vector,) * 9
    return jax.shard_map(local, mesh=mesh, in_specs=in_specs, out_specs=out_specs, check_vma=False)
```

```python
import functools
import math

import jax
import jax.numpy as jnp
import numpy as np
from jax import lax
from jax.experimental import pallas as pl
from jax.experimental.pallas import tpu as pltpu
from jax.sharding import PartitionSpec as P

HEAD_SIZE = 64
LONGEST = 549
EPSILON = 1e-06
TILE = 256
PAIR = 2 * HEAD_SIZE
PAIRS = 2
MIB = 1024 * 1024
F32 = jnp.float32
BF16 = jnp.bfloat16

NN = (((1,), (0,)), ((), ()))
NT = (((1,), (1,)), ((), ()))
TN = (((0,), (0,)), ((), ()))


def dot(left, right, dims=NN):
    return lax.dot_general(left, right, dims, preferred_element_type=F32)


def position_lines(extent):
    quarter = extent // 4
    spatial = (extent - quarter) // 2
    table = np.zeros((128, extent), np.float32)
    at, first = 0, 0
    for count, part in ((8, quarter), (14, spatial), (14, spatial)):
        half = part // 2
        inverse = np.exp(np.arange(half, dtype=np.float32) * np.float32(-math.log(10000.0) / half))
        angles = np.arange(count, dtype=np.float32)[:, None] * inverse[None, :]
        table[first : first + count, at : at + half] = np.sin(angles)
        table[first : first + count, at + half : at + part] = np.cos(angles)
        at, first = at + part, first + count
    return table


def norm_parts(values):
    center = values - jnp.mean(values, axis=-1, keepdims=True)
    spread = jnp.mean(center * center, axis=-1, keepdims=True)
    factor = lax.rsqrt(spread + EPSILON)
    return center * factor, factor


def norm_back(upstream, hat, factor, gain):
    scaled = upstream * gain
    first = jnp.mean(scaled, axis=-1, keepdims=True)
    second = jnp.mean(scaled * hat, axis=-1, keepdims=True)
    return factor * (scaled - first - hat * second)


def clip_label(places, scal, clips, rows, mp):
    label, end = jnp.zeros_like(places), 0
    for c in range(clips):
        end = end + scal[1 + c]
        label = label + (places >= end).astype(jnp.int32)
    return jnp.where((places >= 0) & (places < rows * mp), label, -1)


def tile_range(first, last, base, scal, clips):
    start, end, stop = 0, 0, 0
    for c in range(clips):
        length = scal[1 + c]
        stop = jnp.where(end <= last, end + length, stop)
        end = end + length
        start = jnp.where(end <= first, end, start)
    return lax.div(start - base, TILE), lax.div(stop - base + TILE - 1, TILE)


def forward_kernel(layout, scal, q_ref, k_ref, v_ref, o_ref, lse_ref, s_ref, lq_ref, lk_ref):
    clips, mp = layout
    rows, window = q_ref.shape[0], k_ref.shape[0]
    base = scal[0] * rows - (window - rows) // 2

    @pl.when(pl.program_id(0) == 0)
    def _():
        own = scal[0] * rows + lax.broadcasted_iota(jnp.int32, lq_ref.shape, 1)
        lq_ref[...] = clip_label(own, scal, clips, rows, mp)
        around = base + lax.broadcasted_iota(jnp.int32, lk_ref.shape, 0)
        lk_ref[...] = clip_label(around, scal, clips, rows, mp)

    row = lax.broadcasted_iota(jnp.int32, (2 * HEAD_SIZE, TILE), 0)
    beside = lambda pair: jnp.concatenate(pair, axis=1)
    groups = lambda array: array.reshape(TILE // 8, 8, 2 * TILE)
    pairs = q_ref.shape[1] // PAIR
    for block in range(rows // TILE):
        first = scal[0] * rows + block * TILE
        low, high = tile_range(first, first + TILE - 1, base, scal, clips)
        span = slice(block * TILE, (block + 1) * TILE)
        query_th = []
        for g in range(pairs):
            query_t = q_ref[span, g * PAIR : (g + 1) * PAIR].T
            zero = jnp.zeros_like(query_t)
            query_th.append(
                beside(
                    [
                        jnp.where(row < HEAD_SIZE, query_t, zero),
                        jnp.where(row < HEAD_SIZE, zero, query_t),
                    ]
                )
            )
        label = lq_ref[0:1, span]
        label = beside([label, label])

        def scores(t, carry):
            at = pl.multiple_of(t * TILE, TILE)
            same = beside([lk_ref[pl.ds(at, TILE), :]] * 4) == label
            out = []
            for g in range(pairs):
                key = k_ref[pl.ds(at, TILE), g * PAIR : (g + 1) * PAIR]
                s = jnp.where(same, dot(key, query_th[g]), -1e30)
                s_ref[g, pl.ds(at, TILE), :] = s
                out.append(jnp.maximum(carry[g], jnp.max(groups(s), axis=0)))
            return tuple(out)

        least = jnp.full((8, 2 * TILE), -1e30, F32)
        peaks = lax.fori_loop(low, high, scores, (least,) * pairs)
        peaks = [jnp.max(item, axis=0, keepdims=True) for item in peaks]

        def blend(t, carry):
            at = pl.multiple_of(t * TILE, TILE)
            out = []
            for g in range(pairs):
                total, *accs = carry[g]
                p = jnp.exp(s_ref[g, pl.ds(at, TILE), :] - peaks[g])
                weights = p.astype(BF16)
                value_t = v_ref[pl.ds(at, TILE), g * PAIR : (g + 1) * PAIR].T
                total = total + jnp.sum(groups(p), axis=0)
                parts = [
                    accs[h]
                    + dot(
                        value_t[h * HEAD_SIZE : (h + 1) * HEAD_SIZE],
                        weights[:, h * TILE : (h + 1) * TILE],
                    )
                    for h in range(2)
                ]
                out.append((total, *parts))
            return tuple(out)

        zero = jnp.zeros((HEAD_SIZE, TILE), F32)
        start = (jnp.zeros((8, 2 * TILE), F32), zero, zero)
        done = lax.fori_loop(low, high, blend, (start,) * pairs)
        for g in range(pairs):
            total, *accs = done[g]
            total = jnp.sum(total, axis=0, keepdims=True)
            lse = peaks[g] + jnp.log(total)
            for h in range(2):
                columns = slice(h * TILE, (h + 1) * TILE)
                lse_ref[g, h : h + 1, span] = lse[:, columns]
                accs[h] = accs[h] / total[:, columns]
            o_ref[span, g * PAIR : (g + 1) * PAIR] = jnp.concatenate(accs, axis=0).T.astype(BF16)


def backward_kernel(
    layout,
    scal,
    q_ref,
    k_ref,
    v_ref,
    do_ref,
    o_ref,
    lse_ref,
    dq_ref,
    dk_ref,
    dv_ref,
    dk_acc,
    dv_acc,
    lq_ref,
    lk_ref,
):
    clips, mp = layout
    rows, window = q_ref.shape[0], k_ref.shape[0]
    base = scal[0] * rows - (window - rows) // 2

    @pl.when(pl.program_id(0) == 0)
    def _():
        own = scal[0] * rows + lax.broadcasted_iota(jnp.int32, lq_ref.shape, 1)
        lq_ref[...] = clip_label(own, scal, clips, rows, mp)
        around = base + lax.broadcasted_iota(jnp.int32, lk_ref.shape, 0)
        lk_ref[...] = clip_label(around, scal, clips, rows, mp)

    lane = lax.broadcasted_iota(jnp.int32, (TILE, 2 * HEAD_SIZE), 1)
    row = lax.broadcasted_iota(jnp.int32, (2 * HEAD_SIZE, TILE), 0)
    dk_acc[...] = jnp.zeros_like(dk_acc)
    dv_acc[...] = jnp.zeros_like(dv_acc)

    def halves(array, where):
        zero = jnp.zeros_like(array)
        return [jnp.where(where < HEAD_SIZE, array, zero), jnp.where(where < HEAD_SIZE, zero, array)]

    beside = lambda pair: jnp.concatenate(pair, axis=1)
    pairs = q_ref.shape[1] // PAIR
    for block in range(rows // TILE):
        first = scal[0] * rows + block * TILE
        low, high = tile_range(first, first + TILE - 1, base, scal, clips)
        span = slice(block * TILE, (block + 1) * TILE)
        label = lq_ref[0:1, span]
        label = beside([label, label])
        fixed = []
        for g in range(pairs):
            own = slice(g * PAIR, (g + 1) * PAIR)
            query, grad = q_ref[span, own], do_ref[span, own]
            query_t, grad_t = query.T, grad.T
            product = grad_t.astype(F32) * o_ref[span, own].T.astype(F32)
            delta = beside(
                [
                    jnp.sum(product[h * HEAD_SIZE : (h + 1) * HEAD_SIZE], axis=0, keepdims=True)
                    for h in range(2)
                ]
            )
            lse = beside([lse_ref[g, h : h + 1, span] for h in range(2)])
            query_h = jnp.concatenate(halves(query, lane), axis=0)
            grad_h = jnp.concatenate(halves(grad, lane), axis=0)
            query_th, grad_th = beside(halves(query_t, row)), beside(halves(grad_t, row))
            fixed.append((own, delta, lse, query_h, grad_h, query_th, grad_th))

        def step(t, carry):
            at = pl.multiple_of(t * TILE, TILE)
            same = beside([lk_ref[pl.ds(at, TILE), :]] * 4) == label
            out = []
            for g in range(pairs):
                own, delta, lse, query_h, grad_h, query_th, grad_th = fixed[g]
                key, value = k_ref[pl.ds(at, TILE), own], v_ref[pl.ds(at, TILE), own]
                key_t = key.T
                p = jnp.where(same, jnp.exp(dot(key, query_th) - lse), 0.0)
                ds = (p * (dot(value, grad_th) - delta)).astype(BF16)
                dv_acc[pl.ds(at, TILE), own] += dot(p.astype(BF16), grad_h)
                dk_acc[pl.ds(at, TILE), own] += dot(ds, query_h)
                out.extend(
                    carry[2 * g + h]
                    + dot(
                        key_t[h * HEAD_SIZE : (h + 1) * HEAD_SIZE], ds[:, h * TILE : (h + 1) * TILE]
                    )
                    for h in range(2)
                )
            return tuple(out)

        zero = jnp.zeros((HEAD_SIZE, TILE), F32)
        parts = lax.fori_loop(low, high, step, (zero,) * (2 * pairs))
        for g in range(pairs):
            total = jnp.concatenate(parts[2 * g : 2 * g + 2], axis=0) * (1.0 / math.sqrt(HEAD_SIZE))
            dq_ref[span, fixed[g][0]] = total.T.astype(BF16)
    dk_ref[...] = dk_acc[...].astype(BF16)
    dv_ref[...] = dv_acc[...].astype(BF16)


def attention_call(kernel, name, scal, columns, others, outs, scratch, part, before, work):
    first, count, total = part
    each = min(PAIRS, count)
    pair, first, count = each * PAIR, first // each, count // each
    anywhere = pl.BlockSpec(memory_space=pl.ANY)
    column = lambda item: pl.BlockSpec((item.shape[0], pair), lambda p, b: (0, first + p))
    result = pl.pallas_call(
        kernel,
        grid_spec=pltpu.PrefetchScalarGridSpec(
            num_scalar_prefetch=1,
            grid=(count,),
            in_specs=[column(item) for item in columns]
            + [
                pl.BlockSpec((each,) + item.shape[1:], lambda p, b: (first + p, 0, 0))
                if item.ndim == 3
                else pl.BlockSpec(item.shape, lambda p, b: (0, 0))
                for item in others
            ]
            + [anywhere] * len(before),
            out_specs=[
                pl.BlockSpec((each,) + shape[1:], lambda p, b: (first + p, 0, 0))
                if len(shape) == 3
                else pl.BlockSpec((shape[0], pair), lambda p, b: (0, first + p))
                for shape, _ in outs
            ],
            scratch_shapes=scratch,
        ),
        out_shape=[jax.ShapeDtypeStruct(shape, kind) for shape, kind in outs],
        input_output_aliases={
            1 + len(columns) + len(others) + i: i for i in range(len(before))
        },
        compiler_params=pltpu.CompilerParams(vmem_limit_bytes=32 * MIB),
        cost_estimate=pl.CostEstimate(flops=count * each * work, bytes_accessed=0, transcendentals=0),
        name=name,
    )(scal, *columns, *others, *before)
    return result


def attention_forward(scal, mp, queries, keys, values, part, before=()):
    rows, width = queries.shape
    window = keys.shape[0]

    def kernel(*refs):
        forward_kernel((scal.shape[0] - 1, mp), *refs[:4], *refs[4 + len(before) :])

    return attention_call(
        kernel,
        "attention_forward",
        scal,
        (queries, keys, values),
        (),
        [((rows, width), BF16), ((part[2], 2, rows), F32)],
        [
            pltpu.VMEM((min(PAIRS, part[1]), window, 2 * TILE), F32),
            pltpu.VMEM((8, rows), jnp.int32),
            pltpu.VMEM((window, 128), jnp.int32),
        ],
        part,
        before,
        5 * 10**9,
    )


def attention_backward(scal, mp, queries, keys, values, grads, attended, lse, part, before=()):
    rows, width = queries.shape
    window = keys.shape[0]

    def kernel(*refs):
        backward_kernel((scal.shape[0] - 1, mp), *refs[:7], *refs[7 + len(before) :])

    return attention_call(
        kernel,
        "attention_backward",
        scal,
        (queries, keys, values, grads, attended),
        (lse,),
        [((rows, width), BF16), ((window, width), BF16), ((window, width), BF16)],
        [pltpu.VMEM((window, min(PAIRS, part[1]) * PAIR), F32)] * 2
        + [pltpu.VMEM((8, rows), jnp.int32), pltpu.VMEM((window, 128), jnp.int32)],
        part,
        before,
        6 * 10**9,
    )


def assemble(target, buffers, meta, block, first=0):
    each = buffers[0].shape[0] // block
    span = slice(first, first + buffers[0].shape[1])
    for i in range(len(buffers) * each):
        at = pl.multiple_of(meta[1 + i] * block, block)
        source = buffers[i // each]
        target[pl.ds(at, block), span] = source[i % each * block : (i % each + 1) * block, :]


def turn(target, source, meta, block, lead):
    lead[...] = source.T
    for i in range(target.shape[0] // block):
        at = pl.multiple_of(meta[1 + i] * block, block)
        target[i * block : (i + 1) * block, :] = lead[pl.ds(at, block), :]


def fixed(shape):
    return pl.BlockSpec(shape, lambda *_: (0,) * len(shape), pipeline_mode=pl.Buffered(1))


def call(kernel, name, grid, meta, ins, outs, scratch, vmem, flops, moved=0):
    return pl.pallas_call(
        kernel,
        grid_spec=pltpu.PrefetchScalarGridSpec(
            num_scalar_prefetch=1,
            grid=grid,
            in_specs=[spec for _, spec in ins],
            out_specs=[spec for _, _, spec in outs],
            scratch_shapes=scratch,
        ),
        out_shape=[jax.ShapeDtypeStruct(shape, kind) for shape, kind, _ in outs],
        compiler_params=pltpu.CompilerParams(vmem_limit_bytes=vmem * MIB),
        cost_estimate=pl.CostEstimate(flops=flops, bytes_accessed=moved, transcendentals=0),
        name=name,
    )(meta, *[array for array, _ in ins])


def turn_kernel(block, meta, source, target, lead):
    turn(target, source[...], meta, block, lead)


def turned_rows(source, meta, block):
    rows, width = source.shape
    return call(
        functools.partial(turn_kernel, block),
        "turn",
        (1,),
        meta,
        [(source, fixed(source.shape))],
        [((width, rows), BF16, fixed((width, rows)))],
        [pltpu.VMEM((width, rows), BF16)],
        24,
        4 * 10**9,
    )[0]


def project_kernel(block, scale, own, meta, x, around, bias, *refs):
    weights, (q, k, v), scratch = refs[:-6], refs[-6:-3], refs[-3:]
    if own:
        scratch = weights
    else:
        for w in range(3):
            assemble(scratch[w], weights[4 * w : 4 * w + 4], meta, block)
    q[...] = (dot(x[...], scratch[0][...]) + bias[6:7, :]).astype(BF16) * jnp.asarray(scale, BF16)
    k[...] = dot(around[...], scratch[1][...]).astype(BF16)
    v[...] = (dot(around[...], scratch[2][...]) + bias[7:8, :]).astype(BF16)


def gathered_specs(buffers, kinds, extent, stride):
    return [
        (item, pl.BlockSpec((item.shape[0], extent), lambda i, m, kind=kind: (0, i * stride + kind)))
        for kind in kinds
        for item in buffers
    ]


def project(x, around, weights, narrow, meta, block, mp, own):
    rows, width = x.shape
    window = around.shape[0]
    extent = width // mp
    first, count = (0, 1) if own else (1, mp - 1)
    column = lambda n: pl.BlockSpec((n, extent), lambda i, m: (0, i))
    turned = lambda i, m: (0, lax.rem(m[0] - first - i + mp, mp))
    return call(
        functools.partial(project_kernel, block, 1.0 / math.sqrt(HEAD_SIZE), own),
        "project",
        (count,),
        meta,
        [
            (x, fixed(x.shape)),
            (around, fixed(around.shape)),
            (narrow, pl.BlockSpec((8, extent), turned)),
        ]
        + (
            [(w, fixed(w.shape)) for w in weights]
            if own
            else gathered_specs(weights, (0, 1, 2), extent, 4)
        ),
        [
            ((rows, count * extent), BF16, column(rows)),
            ((window, count * extent), BF16, column(window)),
            ((window, count * extent), BF16, column(window)),
        ],
        [pltpu.VMEM((width, extent), BF16)] * 3,
        40,
        count * 4 * 10**9,
    )


def join(parts, axis):
    return jnp.concatenate(parts, axis=axis)


class Plane:
    def __init__(self, size):
        self.size = size
        bits = list(range(1, size.bit_length() - 1))
        turn = len(bits) // 2
        self.orders = [bits, bits[turn:] + bits[:turn]]
        held = []
        for order in self.orders:
            masks = [0]
            for bit in order:
                masks = masks + [m ^ (1 << bit) for m in masks]
            held.append(masks)
        self.masks = [held[c] + [1 ^ m for m in held[1 - c]] for c in range(2)]
        self.steps = len(bits)

    def pairs(self, step):
        return [(i, i ^ (1 << self.orders[i % 2][step])) for i in range(self.size)]

    def siblings(self):
        return [(i, i ^ 1) for i in range(self.size)]

    def order(self, d):
        return jnp.bitwise_xor(jnp.array(self.masks, jnp.int32)[d % 2], d)


def shifted(payload, r, mp):
    return lax.ppermute(payload, "mp", [(i, (i + r) % mp) for i in range(mp)])


def spread_chips(held, plane):
    for step in range(plane.steps - 2):
        held = join([held, lax.ppermute(held, "dp", plane.pairs(step))], 0)
    return held, lax.ppermute(held, "dp", plane.pairs(plane.steps - 2))


def added(left, right):
    return (left.astype(F32) + right.astype(F32)).astype(BF16)


def folded(keep, got):
    half = keep.shape[0] // 2
    return added(keep[:half], got[:half]), added(keep[half:], got[half:])


def after(value, *others):
    return lax.optimization_barrier((value,) + others)[0]


class Scatter:
    def __init__(self, keep, upper, shifts, plane, mp):
        self.keep, self.shifts, self.plane, self.mp = keep, shifts, plane, mp
        self.step = plane.steps - 1
        self.got = lax.ppermute(upper, "dp", plane.pairs(self.step))

    def next(self):
        self.step -= 1
        self.keep, upper = folded(self.keep, self.got)
        self.got = lax.ppermute(upper, "dp", self.plane.pairs(self.step))
        return self


MESH = pl.DeviceIdType.MESH


def flipped(d, bit):
    return d + (1 - 2 * lax.rem(lax.div(d, 1 << bit), 2)) * (1 << bit)


def meet(d, z, dp, mp):
    barrier = pltpu.get_barrier_semaphore()
    for step in range(1, dp):
        there = (lax.rem(d + step, dp), z)
        pl.semaphore_signal(barrier, inc=1, device_id=there, device_id_type=MESH)
    for step in range(1, mp):
        there = (d, lax.rem(z + step, mp))
        pl.semaphore_signal(barrier, inc=1, device_id=there, device_id_type=MESH)
    pl.semaphore_wait(barrier, dp + mp - 2)


def remote(source, target, send_sem, recv_sem, device):
    return pltpu.make_async_remote_copy(
        src_ref=source,
        dst_ref=target,
        send_sem=send_sem,
        recv_sem=recv_sem,
        device_id=device,
        device_id_type=MESH,
    )


def peers_start(source, slots, send_sem, recv_sem, along, me, extent, each):
    copies = []
    for step in range(1, extent):
        place = lax.rem(me + step, extent)
        copies.append(
            remote(
                source.at[place if each else 0],
                slots.at[me],
                send_sem.at[step],
                recv_sem.at[me],
                along(step),
            )
        )
        copies[-1].start()
    slots[me] = source[me if each else 0]
    return copies


def peers_finish(copies, slots, recv_sem, me, extent):
    for step in range(1, extent):
        copies[step - 1].wait_send()
        sender = lax.rem(me + step, extent)
        pltpu.make_async_copy(slots.at[sender], slots.at[sender], recv_sem.at[sender]).wait()


def begin_kernel(plane, mp, hops, margin, *refs):
    (sheet, tokens, index, table), shards_in, refs = refs[:4], refs[4:10], refs[10:]
    (narrow, broad, stream, around, normed_out, second_out), buffers = refs[:6], refs[6:10]
    (middle, first, second, normed, zeros, payload, out_in, out_t), refs = refs[10:18], refs[18:]
    (reduce_in, reduce_t, take), refs = refs[:3], refs[3:]
    send_one, recv_one, send_two, recv_two, refs = *refs[:4], refs[4:]
    z_send, z_recv, chip_send, chip_recv, core_send, core_recv, halo_send, halo_recv, local = refs
    dp = plane.size
    d, z = lax.axis_index("dp"), lax.axis_index("mp")
    core = lax.rem(d, 2)
    rows, width = tokens.shape
    block, columns = payload.shape
    along_dp = lambda step: (lax.rem(d + step, dp), z)
    along_mp = lambda step: (d, lax.rem(z + step, mp))

    query, key, value, output, expand, reduce = shards_in
    extent, hidden_extent = query.shape[1], expand.shape[1]
    mine = pl.ds(pl.multiple_of(d * block, block), block)
    line = pl.ds(pl.multiple_of(lax.div(d * block, 128) * 128, 128), 128)
    taken = [
        pltpu.make_async_copy(
            source.at[mine, :], payload.at[:, pl.ds(w * extent, extent)], take.at[w]
        )
        for w, source in enumerate((query, key, value))
    ]
    taken.append(pltpu.make_async_copy(output.at[:, line], out_in, take.at[3]))
    taken.append(pltpu.make_async_copy(reduce.at[:, line], reduce_in, take.at[4]))
    taken.append(
        pltpu.make_async_copy(
            expand.at[mine, :], second_out.at[:, pl.ds(0, hidden_extent)], take.at[5]
        )
    )
    for copy in taken:
        copy.start()
    zeros[...] = jnp.zeros_like(zeros)
    meet(d, z, dp, mp)
    vectors = peers_start(sheet, first, send_one, recv_one, along_mp, z, mp, False)
    for copy in taken[:4]:
        copy.wait()
    out_t[...] = out_in[...].T
    within = pl.ds(pl.multiple_of(lax.rem(d * block, 128), block), block)
    payload[:, 3 * extent :] = out_t[within, :]

    each = dp // 4

    def place(j, r, other=False):
        return buffers[j // each + (2 if other else 0)].at[
            pl.ds(j % each * block, block), pl.ds((r - 1) * columns, columns)
        ]

    def passed_on(way, r):
        before = r - 1 if way == 0 else (r + 1) % mp
        source = place(0, before) if before else payload
        return remote(
            source, place(0, r), z_send.at[way, r], z_recv.at[r], (d, z + 1 if way == 0 else z - 1)
        )

    last, least = z + 1 < mp, z > 0
    line_sends = [(last & (z >= r - 1), passed_on(0, r).wait_send) for r in range(1, mp)]
    line_sends += [(least & (z <= r), passed_on(1, r).wait_send) for r in range(1, mp)]
    pl.when(last)(passed_on(0, 1).start)
    pl.when(least)(passed_on(1, mp - 1).start)

    kept = index[...]
    coarse = lax.div(kept, 14)
    frame = lax.div(kept, 196)
    across = coarse - frame * 14
    line = kept - coarse * 14
    count = lax.broadcasted_iota(jnp.int32, (table.shape[0], rows), 0)
    hot = ((count == frame) | (count == across + 8) | (count == line + 22)).astype(F32)
    hidden = tokens[...].astype(F32) + lax.dot_general(
        hot, table[...], TN, precision=lax.Precision.HIGHEST, preferred_element_type=F32
    )
    stream[...] = hidden

    peers_finish(vectors, first, recv_one, z, mp)
    middle[0] = jnp.sum(first[...], axis=0)
    vectors = peers_start(middle, second, send_two, recv_two, along_dp, d, dp, False)
    hat, _ = norm_parts(hidden)
    peers_finish(vectors, second, recv_two, d, dp)
    share = dp // (width // 128)
    for c in range(width // 128):
        narrow[:, c * 128 : (c + 1) * 128] = jnp.sum(
            second[c * share : (c + 1) * share, 0:8, :], axis=0
        )
    lines = broad.shape[1] // 128
    per = lines // dp
    for c in range(lines):
        row = second[c // per, 8 + c % per : 9 + c % per, :]
        broad[:, c * 128 : (c + 1) * 128] = jnp.broadcast_to(row, (8, 128))
    normed[...] = (hat * narrow[0:1, :] + narrow[1:2, :]).astype(BF16)
    taken[4].wait()
    reduce_t[...] = reduce_in[...].T
    shares = (
        pltpu.make_async_copy(
            reduce_t.at[within, :],
            second_out.at[:, pl.ds(hidden_extent, hidden_extent)],
            take.at[6],
        ),
        pltpu.make_async_copy(normed, normed_out, take.at[7]),
    )
    for copy in shares:
        copy.start()

    sent = []

    def arrived(j, r):
        pltpu.make_async_copy(place(j, r), place(j, r), z_recv.at[r]).wait()

    def copies_of(j, r):
        copies = []
        for step in range(plane.steps):
            if j < 1 << step:
                there = (1 - core) * flipped(d, plane.orders[0][step]) + core * flipped(
                    d, plane.orders[1][step]
                )
                to = (1 << step) + j
                copies.append(
                    remote(
                        place(j, r),
                        place(to, r),
                        chip_send.at[r, to],
                        chip_recv.at[r, to],
                        (there, z),
                    )
                )
        copies.append(
            remote(
                place(j, r),
                place(j, r, True),
                core_send.at[r, j],
                core_recv.at[r, j],
                (flipped(d, 0), z),
            )
        )
        return copies

    def forward(j, r):
        for copy in copies_of(j, r):
            copy.start()

    def handle(h):

        @pl.when(z >= h)
        def _():
            arrived(0, h)
            if h + 1 < mp:
                pl.when(last)(passed_on(0, h + 1).start)
            forward(0, h)

        @pl.when(z + h < mp)
        def _():
            arrived(0, mp - h)
            if mp - h > 1:
                pl.when(least)(passed_on(1, mp - h - 1).start)
            forward(0, mp - h)

    for h in range(1, mp - 1):
        handle(h)

    waits, at_left, at_right = [], margin, margin + rows
    inside = pltpu.make_async_copy(
        normed, around.at[pl.ds(margin, rows), :], local.at[0]
    )
    inside.start()
    waits.append((None, inside.wait))
    for hop, extent in enumerate(hops, 1):
        left = around.at[pl.ds(at_left - extent, extent), :]
        right = around.at[pl.ds(at_right, extent), :]
        sides = (
            (left, normed.at[pl.ds(rows - extent, extent), :], z + hop, z - hop, 2 * hop - 2),
            (right, normed.at[pl.ds(0, extent), :], z - hop, z + hop, 2 * hop - 1),
        )
        for target, source, there, back, n in sides:
            goes = (there >= 0) & (there < mp)
            comes = (back >= 0) & (back < mp)
            copy = remote(source, target, halo_send.at[n], halo_recv.at[n], (d, there))
            blank = pltpu.make_async_copy(zeros.at[pl.ds(0, extent), :], target, local.at[1 + n])
            pl.when(goes)(copy.start)
            pl.when(jnp.logical_not(comes))(blank.start)
            waits.append((goes, copy.wait_send))
            waits.append((comes, copy.wait_recv))
            waits.append((jnp.logical_not(comes), blank.wait))
        at_left, at_right = at_left - extent, at_right + extent
    if at_left:
        for n, at in enumerate((0, at_right)):
            blank = pltpu.make_async_copy(
                zeros.at[pl.ds(0, at_left), :],
                around.at[pl.ds(at, at_left), :],
                local.at[1 + 2 * len(hops) + n],
            )
            blank.start()
            waits.append((None, blank.wait))

    for h in range(mp - 1, mp):
        handle(h)
    for r in range(1, mp):
        sent.extend(copies_of(0, r))
    for j in range(1, 1 << plane.steps):
        for r in range(1, mp):
            pltpu.make_async_copy(place(j, r), place(j, r), chip_recv.at[r, j]).wait()
            forward(j, r)
            sent.extend(copies_of(j, r))
    for j in range(1 << plane.steps):
        for r in range(1, mp):
            pltpu.make_async_copy(place(j, r, True), place(j, r, True), core_recv.at[r, j]).wait()
    for copy in sent:
        copy.wait_send()
    for when, wait in line_sends:
        pl.when(when)(wait)
    taken[5].wait()
    for copy in shares:
        copy.wait()
    for when, wait in waits:
        wait() if when is None else pl.when(when)(wait)


def begin(sheet, tokens, index, table, shards, plane, mp, hops, margin):
    dp = plane.size
    rows, width = tokens.shape
    extent, hidden = shards[0].shape[1], shards[4].shape[1]
    block, columns, full_hidden = width // dp, 4 * extent, hidden * mp
    vmem, anywhere = pl.BlockSpec(memory_space=pltpu.VMEM), pl.BlockSpec(memory_space=pl.ANY)
    window = 2 * margin + rows
    dma = pltpu.SemaphoreType.DMA
    blocks = dp // 2
    return pl.pallas_call(
        functools.partial(begin_kernel, plane, mp, hops, margin),
        out_shape=[
            jax.ShapeDtypeStruct((8, width), F32),
            jax.ShapeDtypeStruct((8, full_hidden), F32),
            jax.ShapeDtypeStruct((rows, width), F32),
            jax.ShapeDtypeStruct((window, width), BF16),
            jax.ShapeDtypeStruct((rows, width), BF16),
            jax.ShapeDtypeStruct((block, 2 * hidden), BF16),
        ]
        + [jax.ShapeDtypeStruct((width // 4, (mp - 1) * columns), BF16)] * 4,
        in_specs=[vmem] * 4 + [anywhere] * 6,
        out_specs=[vmem] * 3 + [anywhere] * 7,
        scratch_shapes=[
            pltpu.VMEM((1, 16, 128), F32),
            pltpu.VMEM((mp, 16, 128), F32),
            pltpu.VMEM((dp, 16, 128), F32),
            pltpu.VMEM((rows, width), BF16),
            pltpu.VMEM((rows, width), BF16),
            pltpu.VMEM((block, columns), BF16),
            pltpu.VMEM((extent, 128), BF16),
            pltpu.VMEM((128, extent), BF16),
            pltpu.VMEM((hidden, 128), BF16),
            pltpu.VMEM((128, hidden), BF16),
            dma((8,)),
            dma((mp,)),
            dma((mp,)),
            dma((dp,)),
            dma((dp,)),
            dma((2, mp)),
            dma((mp,)),
            dma((mp, blocks)),
            dma((mp, blocks)),
            dma((mp, blocks)),
            dma((mp, blocks)),
            dma((2 * len(hops),)),
            dma((2 * len(hops),)),
            dma((3 + 2 * len(hops),)),
        ],
        compiler_params=pltpu.CompilerParams(
            collective_id=1, has_side_effects=True, vmem_limit_bytes=60 * MIB
        ),
        cost_estimate=pl.CostEstimate(flops=4 * 10**10, bytes_accessed=0, transcendentals=0),
        name="begin",
    )(sheet, tokens, index, table, *shards)


def xored(d, mask):
    for bit in range(mask.bit_length()):
        if mask >> bit & 1:
            d = flipped(d, bit)
    return d


def middle_kernel(plane, mp, tile, *refs):
    (stream_in, near_in, far_in, g_in, narrow_in, broad_in), refs = refs[:6], refs[6:]
    own_o, own_e, own_r, out_parts, refs = *refs[:3], refs[3:7], refs[7:]
    (early_a, early_b), late_a, refs = refs[:2], refs[2 : 2 * mp - 2], refs[2 * mp - 2 :]
    (sums, db, own_total, moved, act, grad_mid, branch_t, grad_near, grad_far), refs = refs[:9], refs[9:]
    (keep_out, upper_out, early_o, late_b, late_c, late_d), refs = refs[:6], refs[6:]
    (mid, near, far, g, narrow, broad, o_temp, weight_o, weights, r_temp), refs = refs[:10], refs[10:]
    (x, x_t, g_t, lead, out_acc, dx_acc, keep, send, got, more), refs = refs[:10], refs[10:]
    load, weight_sem, own_sem, core_send, core_recv, chip_send, chip_recv, refs = *refs[:7], refs[7:]
    sum_send, sum_recv, near_send, near_recv, store = refs
    dp, steps = plane.size, plane.steps
    d, z = lax.axis_index("dp"), lax.axis_index("mp")
    core = lax.rem(d, 2)
    rows, width = x.shape
    block, half, quarter = width // dp, width // 2, width // 4
    extent = own_e.shape[1]
    per = extent // tile
    tiles = mp * per
    wide = 2 * extent
    full = mp // 2
    orders = [
        (1 - core) * xored(d, plane.masks[0][i]) + core * xored(d, plane.masks[1][i])
        for i in range(dp)
    ]
    sibling = (flipped(d, 0), z)

    def partner(step):
        there = (1 - core) * flipped(d, plane.orders[0][step]) + core * flipped(
            d, plane.orders[1][step]
        )
        return there, z

    def home(i):
        return pl.ds(pl.multiple_of(orders[i] * block, block), block)

    def turned(target, source):
        lead[...] = source.T
        for i in range(dp):
            target[i * block : (i + 1) * block, :] = lead[home(i), :]

    loads = [
        pltpu.make_async_copy(source, target, load.at[i])
        for i, (source, target) in enumerate(
            (
                (stream_in, mid),
                (near_in, near),
                (far_in, far),
                (g_in, g),
                (narrow_in, narrow),
                (broad_in, broad),
                (own_o, o_temp),
            )
        )
    ]
    each = dp // 4
    part_o = own_o.shape[0]
    for i in range(dp):
        for r in range(1, mp):
            pltpu.make_async_copy(
                out_parts[i // each].at[
                    pl.ds(i % each * block, block), pl.ds((4 * r - 1) * part_o, part_o)
                ],
                weight_o.at[home(i), pl.ds(r * part_o, part_o)],
                load.at[7],
            ).start()
    rest_o = weight_o.at[:, pl.ds(part_o, width - part_o)]
    for copy in loads:
        copy.start()

    def fetch(i):
        slot, r, t = i % 2, i // per, i % per
        if r == 0:
            return [
                pltpu.make_async_copy(
                    own_e.at[:, pl.ds(t * tile, tile)], weights.at[slot, 0], own_sem.at[0]
                ),
                pltpu.make_async_copy(own_r.at[pl.ds(t * tile, tile), :], r_temp, own_sem.at[1]),
            ]
        if r == 1:
            parts = (early_a, early_b) + tuple(
                early_o.at[pl.ds(n * quarter, quarter), :] for n in range(2)
            )
            first = 0
        else:
            parts, first = (None, late_b, late_c, late_d), (r - 2) * wide

        def piece(n, kind):
            column = kind * extent + t * tile
            if r > 1 and n < each:
                few = each // 2
                return late_a[2 * (r - 2) + n // few].at[
                    pl.ds(n % few * block, block), pl.ds(column, tile)
                ]
            return parts[n // each].at[pl.ds(n % each * block, block), pl.ds(first + column, tile)]

        return [
            pltpu.make_async_copy(
                piece(n, kind),
                weights.at[slot, kind, home(n), :],
                weight_sem.at[slot],
            )
            for kind in range(2)
            for n in range(dp)
        ]

    for copy in fetch(0):
        copy.start()
    meet(d, z, dp, mp)

    def late(buffer, r):
        return buffer.at[:, pl.ds((r - 2) * wide, wide)]

    sent = []
    swaps, hops = {}, {}
    for n, part in enumerate((early_a, early_b)):
        swaps[1, n] = remote(
            part,
            early_o.at[pl.ds(n * quarter, quarter), :],
            core_send.at[1, n],
            core_recv.at[1, n],
            sibling,
        )
    for r in range(2, mp):
        for n in range(2):
            part = late_a[2 * (r - 2) + n]
            span = pl.ds(n * quarter // 2, quarter // 2)
            columns = pl.ds((r - 2) * wide, wide)
            hops[r, n] = remote(
                part,
                late_b.at[span, columns],
                chip_send.at[r, n],
                chip_recv.at[r, n],
                partner(steps - 1),
            )
            swaps[r, n] = remote(
                part, late_c.at[span, columns], core_send.at[r, n], core_recv.at[r, n], sibling
            )
        swaps[r, 2] = remote(
            late(late_b, r), late(late_d, r), core_send.at[r, 2], core_recv.at[r, 2], sibling
        )
    swaps[1, 0].start()
    swaps[1, 1].start()
    for r in range(2, mp):
        for n in range(2):
            hops[r, n].start()
        for n in range(2):
            swaps[r, n].start()

    for i in range(7):
        loads[i].wait()
    pltpu.make_async_copy(rest_o, rest_o, load.at[7]).wait()
    weight_o[:, :part_o] = o_temp[...].T
    cut = near.shape[1]
    mixed = dot(near[...], weight_o[:, :cut], NT) + dot(far[...], weight_o[:, cut:], NT)
    mid[...] = mid[...] + mixed + narrow[2:3, :]
    hat, _ = norm_parts(mid[...])
    x[...] = (hat * narrow[3:4, :] + narrow[4:5, :]).astype(BF16)
    turned(x_t, x[...])
    turned(g_t, g[...])
    out_acc[...] = jnp.zeros_like(out_acc)
    dx_acc[...] = jnp.zeros_like(dx_acc)

    def swap_of(c):
        return remote(
            send.at[c % 2], got.at[c], near_send.at[c], near_recv.at[c], sibling
        )

    def rows_of(step):
        count = half >> (steps - step)
        return count, half - 2 * count

    def sum_of(c, step):
        count, at = rows_of(step)
        return remote(
            keep.at[c, pl.ds(count, count), :],
            more.at[c // 2, pl.ds(at, count), :],
            sum_send.at[c // 2, step],
            sum_recv.at[c // 2, step],
            partner(step),
        )

    def outs_of(c):
        span = pl.ds(c // 2 * wide, wide)
        return [
            pltpu.make_async_copy(
                keep.at[c, pl.ds(n * quarter, quarter), :], target.at[:, span], store.at[c, n]
            )
            for n, target in enumerate((keep_out, upper_out))
        ]

    def core_done(c):
        swap_of(c).wait_recv()
        keep[c] = added(keep[c], got[c])
        if c % 2 == 0:
            sum_of(c, steps - 1).start()
        else:
            for copy in outs_of(c):
                copy.start()

    def chips_done(c, step):
        sum_of(c, step).wait_recv()
        count, at = rows_of(step)
        keep[c, :count, :] = added(keep[c, :count, :], more[c // 2, pl.ds(at, count), :])
        if step:
            sum_of(c, step - 1).start()

    events = {}
    for r in range(2, mp):

        def passed(r=r):
            hops[r, 0].wait_recv()
            hops[r, 1].wait_recv()
            swaps[r, 2].start()

        events.setdefault((r - 1) * per, []).append(passed)
    for r in range(1, mp):

        def arrived(r=r):
            for n in range(2 if r == 1 else 3):
                swaps[r, n].wait_recv()

        events.setdefault(r * per - 1, []).append(arrived)
    for i in range(1, tiles):

        def ahead(i=i):
            for copy in fetch(i):
                copy.start()

        if i >= per:
            events.setdefault(i - 1, []).append(ahead)
    for c in range(mp - 1):
        events.setdefault((c + 2) * per - 1, []).append(functools.partial(core_done, c))
    events.setdefault(tiles - per, []).append(functools.partial(chips_done, 0, steps - 1))

    def body(i, carry):
        slot, c, t = lax.rem(i, 2), lax.div(i, per), lax.rem(i, per)

        @pl.when(c == 0)
        def _():
            pltpu.make_async_copy(weights.at[0, 0], weights.at[0, 0], own_sem.at[0]).wait()
            pltpu.make_async_copy(r_temp, r_temp, own_sem.at[1]).wait()
            weights[slot, 1] = r_temp[...].T

        @pl.when(c > 0)
        def _():
            pltpu.make_async_copy(weights.at[slot], weights.at[slot], weight_sem.at[slot]).wait()

        for n in range(1, per):

            @pl.when(i == n - 1)
            def _():
                for copy in fetch(n):
                    copy.start()

        for n, actions in events.items():

            @pl.when(i == n)
            def _():
                for action in actions:
                    action()

        @pl.when((t == 0) & (c >= 2))
        def _():
            remote(
                send.at[lax.rem(c, 2)], got.at[c], near_send.at[c - 2], near_recv.at[c], sibling
            ).wait_send()

        at = pl.multiple_of(lax.rem(z - c + mp, mp) * extent + t * tile, tile)
        bias = broad[0:1, pl.ds(at, tile)]
        out = lax.rem(c, 2)
        hiddens, grads = [], []
        few = tile // 2
        for part in range(2):
            span = slice(part * few, (part + 1) * few)
            pre = dot(x[...], weights[slot, 0, :, span]) + bias[:, span]
            cumulative = 0.5 * (1.0 + lax.erf(pre * 0.7071067811865476))
            hidden = (pre * cumulative).astype(BF16)
            slope = cumulative + pre * jnp.exp(-0.5 * pre * pre) * (1.0 / math.sqrt(2.0 * math.pi))
            grad_pre = (dot(g[...], weights[slot, 1, :, span]) * slope).astype(BF16)
            line = jnp.sum(grad_pre.astype(F32), axis=0, keepdims=True)
            db[:, pl.ds(pl.multiple_of(i * tile + part * few, few), few)] = jnp.broadcast_to(
                line, (8, few)
            )
            first = pl.ds(pl.multiple_of(2 * t * tile + part * few, few), few)
            second = pl.ds(pl.multiple_of((2 * t + 1) * tile + part * few, few), few)
            send[out, :, first] = dot(x_t[half:, :], grad_pre).astype(BF16)
            send[out, :, second] = dot(g_t[half:, :], hidden).astype(BF16)
            keep[c, :, first] = dot(x_t[:half, :], grad_pre).astype(BF16)
            keep[c, :, second] = dot(g_t[:half, :], hidden).astype(BF16)
            hiddens.append(hidden)
            grads.append(grad_pre)
        hidden, grad_pre = jnp.concatenate(hiddens, axis=1), jnp.concatenate(grads, axis=1)
        weight_e, weight_r = weights[slot, 0], weights[slot, 1]

        @pl.when(t == per - 1)
        def _():
            remote(send.at[out], got.at[c], near_send.at[c], near_recv.at[c], sibling).start()

        out_acc[...] += dot(hidden, weight_r, NT)
        dx_acc[...] += dot(grad_pre, weight_e, NT)
        return carry

    lax.fori_loop(0, tiles, body, 0)

    value, grad, dy = mid[...], g[...].astype(F32), dx_acc[...]
    x[...] = (value + out_acc[...] + narrow[5:6, :]).astype(BF16)
    hat, factor = norm_parts(value)
    back = grad + norm_back(dy, hat, factor, narrow[3:4, :])
    add = lambda v: jnp.sum(v, axis=0, keepdims=True)
    zero = jnp.zeros((4, width), F32)
    sums[...] = jnp.concatenate([add(back), add(dy * hat), add(dy), add(grad), zero], axis=0)
    mid[...] = back
    rounded = back.astype(BF16)
    turned(x_t, rounded)
    near[...] = dot(rounded, weight_o[:, :cut]).astype(BF16)
    far[...] = dot(rounded, weight_o[:, cut:]).astype(BF16)
    results = [
        pltpu.make_async_copy(source, target, load.at[i])
        for i, (source, target) in enumerate(
            ((x, act), (mid, grad_mid), (x_t, branch_t), (near, grad_near), (far, grad_far))
        )
    ]
    for copy in results:
        copy.start()

    core_done(mp - 1)
    for c in range(2, mp, 2):
        chips_done(c, steps - 1)
    for step in reversed(range(steps - 1)):
        for c in range(0, mp, 2):
            chips_done(c, step)
    own_total[...] = keep[0, :block, :].astype(F32)
    for c in range(2, mp, 2):
        moved[c // 2 - 1] = keep[c, :block, :]
    for c in range(max(0, mp - 2), mp):
        swap_of(c).wait_send()
    for c in range(0, mp, 2):
        for step in range(steps):
            sum_of(c, step).wait_send()
    for c in range(1, mp, 2):
        for copy in outs_of(c):
            copy.wait()
    for copy in list(hops.values()) + list(swaps.values()):
        copy.wait_send()
    for copy in results:
        copy.wait()


def middle(arrays, weights, buffers, parts, plane, mp, hidden):
    dp = plane.size
    rows, width = arrays[0].shape
    extent = hidden // mp
    tile = min(512, extent)
    wide, half, quarter, full = 2 * extent, width // 2, width // 4, mp // 2
    vmem, anywhere = pl.BlockSpec(memory_space=pltpu.VMEM), pl.BlockSpec(memory_space=pl.ANY)
    dma = pltpu.SemaphoreType.DMA
    shape = jax.ShapeDtypeStruct
    near = arrays[1].shape[1]
    late = (quarter, (mp - 2) * wide)
    return pl.pallas_call(
        functools.partial(middle_kernel, plane, mp, tile),
        out_shape=[
            shape((8, width), F32),
            shape((8, hidden), F32),
            shape((width // dp, wide), F32),
            shape((max(full - 1, 1), width // dp, wide), BF16),
            shape((rows, width), BF16),
            shape((rows, width), F32),
            shape((width, rows), BF16),
            shape((rows, near), BF16),
            shape((rows, width - near), BF16),
            shape((quarter, (mp - full) * wide), BF16),
            shape((quarter, (mp - full) * wide), BF16),
            shape((half, wide), BF16),
            shape(late, BF16),
            shape(late, BF16),
            shape(late, BF16),
        ],
        in_specs=[anywhere] * (len(arrays) + len(weights) + len(buffers) + len(parts)),
        out_specs=[vmem] * 4 + [anywhere] * 11,
        scratch_shapes=[
            pltpu.VMEM((rows, width), F32),
            pltpu.VMEM(arrays[1].shape, BF16),
            pltpu.VMEM(arrays[2].shape, BF16),
            pltpu.VMEM((rows, width), BF16),
            pltpu.VMEM((8, width), F32),
            pltpu.VMEM((8, hidden), F32),
            pltpu.VMEM(weights[0].shape, BF16),
            pltpu.VMEM((width, width), BF16),
            pltpu.VMEM((2, 2, width, tile), BF16),
            pltpu.VMEM((tile, width), BF16),
            pltpu.VMEM((rows, width), BF16),
            pltpu.VMEM((width, rows), BF16),
            pltpu.VMEM((width, rows), BF16),
            pltpu.VMEM((width, rows), BF16),
            pltpu.VMEM((rows, width), F32),
            pltpu.VMEM((rows, width), F32),
            pltpu.VMEM((mp, half, wide), BF16),
            pltpu.VMEM((2, half, wide), BF16),
            pltpu.VMEM((mp, half, wide), BF16),
            pltpu.VMEM((full, half, wide), BF16),
            dma((8,)),
            dma((2,)),
            dma((2,)),
            dma((mp, 3)),
            dma((mp, 3)),
            dma((mp, 2)),
            dma((mp, 2)),
            dma((full, plane.steps)),
            dma((full, plane.steps)),
            dma((mp,)),
            dma((mp,)),
            dma((mp, 2)),
        ],
        compiler_params=pltpu.CompilerParams(
            collective_id=3, has_side_effects=True, vmem_limit_bytes=60 * MIB
        ),
        cost_estimate=pl.CostEstimate(flops=6 * 10**10, bytes_accessed=0, transcendentals=0),
        name="middle",
    )(*arrays, *weights, *buffers, *parts)


def orders_of(plane, d, core):
    return [
        (1 - core) * xored(d, plane.masks[0][i]) + core * xored(d, plane.masks[1][i])
        for i in range(plane.size)
    ]


def tail_kernel(plane, mp, margin, *refs):
    (around_t, branch_t, dq, dk, dv, att), got, refs = refs[:6], refs[6:18], refs[18:]
    (kept, came, own_two), even, refs = refs[:3], refs[3 : 2 + mp // 2], refs[2 + mp // 2 :]
    (own_out, around_out, lower, upper, bias, total_out, rest_out), refs = refs[:7], refs[7:]
    weights, (payload, shards, keep, send, arrived), refs = refs[:3], refs[3:8], refs[8:]
    z_send, z_recv, core_send, core_recv = refs
    dp = plane.size
    d, z = lax.axis_index("dp"), lax.axis_index("mp")
    step, last = pl.program_id(0), mp - 2
    rows, extent = dq.shape
    width = around_t.shape[0]
    half, quarter, block = width // 2, width // 4, width // dp
    wide = own_two.shape[1]
    sibling = (flipped(d, 0), z)

    def sum_of():
        return remote(
            payload, shards, z_send.at[0], z_recv.at[0], (d, lax.rem(z - 1 + mp, mp))
        )

    @pl.when(step == 0)
    def _():
        meet(d, z, dp, mp)
        payload[...] = added(kept[:, :wide], came[:, :wide])
        sum_of().start()
        rest_out[...] = added(kept[:, wide:], came[:, wide:])

    orders = orders_of(plane, d, lax.rem(d, 2))
    each = dp // 4
    for w in range(3):
        for i in range(dp):
            source = got[4 * w + i // each]
            at = pl.multiple_of(orders[i] * block, block)
            weights[w][pl.ds(at, block), :] = source[i % each * block : (i % each + 1) * block, :]

    middle, everything = slice(margin, margin + rows), slice(None)
    for low, target in ((half, send), (0, keep)):
        for at, (left, span, right) in enumerate(
            (
                (around_t, middle, dq),
                (around_t, everything, dk),
                (around_t, everything, dv),
                (branch_t, everything, att),
            )
        ):
            target[step, :, at * extent : (at + 1) * extent] = dot(
                left[low : low + half, span], right[...]
            ).astype(BF16)
        if low:
            remote(
                send.at[step], arrived.at[step], core_send.at[step], core_recv.at[step], sibling
            ).start()
    add = lambda v: jnp.sum(v[...].astype(F32), axis=0, keepdims=True)
    bias[...] = jnp.concatenate([add(dq), add(dv), jnp.zeros((6, extent), F32)], axis=0)
    back = dot(dk[...], weights[1][...], NT) + dot(dv[...], weights[2][...], NT)
    more = dot(dq[...], weights[0][...], NT)

    @pl.when(step == 0)
    def _():
        around_out[...] = back
        own_out[...] = more

    @pl.when(step > 0)
    def _():
        around_out[...] += back
        own_out[...] += more

    def fold(n):
        swap = remote(send.at[n], arrived.at[n], core_send.at[n], core_recv.at[n], sibling)
        swap.wait_recv()
        span = slice(n * 4 * extent, (n + 1) * 4 * extent)
        lower[:, span] = added(keep[n, :quarter, :], arrived[n, :quarter, :])
        upper[:, span] = added(keep[n, quarter:, :], arrived[n, quarter:, :])

    for n in range(last):
        pl.when(step == n + 1)(functools.partial(fold, n))

    @pl.when(step == last)
    def _():
        fold(last)
        total = own_two[...]
        for item in even:
            total = total + item[...].astype(F32)
        sum_of().wait_recv()
        total_out[...] = total + shards[...].astype(F32)
        sum_of().wait_send()
        for n in range(mp - 1):
            remote(
                send.at[n], arrived.at[n], core_send.at[n], core_recv.at[n], sibling
            ).wait_send()


def tail(around_t, branch_t, grads, att, weights, sums, own_two, even, plane, mp, margin):
    dq, dk, dv = grads
    rows, width = dq.shape[0], around_t.shape[0]
    window = around_t.shape[1]
    extent = width // mp
    half, quarter, block = width // 2, width // 4, width // plane.size
    count, wide = mp - 1, own_two.shape[1]
    column = lambda item: pl.BlockSpec((item.shape[0], extent), lambda i: (0, i))
    whole = lambda shape: pl.BlockSpec(
        shape, lambda i: (0,) * len(shape), pipeline_mode=pl.Buffered(1)
    )
    pieces = [
        pl.BlockSpec((item.shape[0], extent), lambda i, kind=kind: (0, i * 4 + kind))
        for kind in range(3)
        for item in weights
    ]
    outs = [
        ((rows, width), F32),
        ((window, width), F32),
        ((quarter, 4 * count * extent), BF16),
        ((quarter, 4 * count * extent), BF16),
        ((8, count * extent), F32),
        ((block, wide), F32),
        ((block, (mp // 2 - 1) * wide), BF16),
    ]
    specs = [whole(shape) for shape, _ in outs]
    specs[4] = pl.BlockSpec((8, extent), lambda i: (0, i))
    stack = pltpu.VMEM((count, half, 4 * extent), BF16)
    dma = pltpu.SemaphoreType.DMA
    constant = (*sums, own_two, *even)
    return pl.pallas_call(
        functools.partial(tail_kernel, plane, mp, margin),
        grid=(count,),
        in_specs=[whole(around_t.shape), whole(branch_t.shape)]
        + [column(item) for item in (dq, dk, dv, att)]
        + pieces
        + [whole(item.shape) for item in constant],
        out_specs=specs,
        out_shape=[jax.ShapeDtypeStruct(shape, kind) for shape, kind in outs],
        scratch_shapes=[pltpu.VMEM((width, extent), BF16)] * 3
        + [
            pltpu.VMEM((block, wide), BF16),
            pltpu.VMEM((block, wide), BF16),
            stack,
            stack,
            stack,
            dma((1,)),
            dma((1,)),
            dma((count,)),
            dma((count,)),
        ],
        compiler_params=pltpu.CompilerParams(
            collective_id=4, has_side_effects=True, vmem_limit_bytes=60 * MIB
        ),
        cost_estimate=pl.CostEstimate(flops=24 * 10**9, bytes_accessed=0, transcendentals=0),
        name="tail",
    )(around_t, branch_t, dq, dk, dv, att, *(list(weights) * 3), *constant)


def finish_kernel(plane, mp, hops, margin, *refs):
    inputs = 18 + mp // 2
    hbm, refs = refs[:inputs], refs[inputs:]
    upper, refs = refs[0], refs[1:]
    (grad_tokens, *totals, grad_expand, grad_reduce, vectors), refs = refs[:8], refs[8:]
    loaded, refs = refs[:inputs], refs[inputs:]
    (halo_out, halo_in, keep, send, got, more_got, shards, table, sheets), refs = refs[:9], refs[9:]
    (middle, first, second), refs = refs[:3], refs[3:]
    load_sem, halo_send, halo_recv, core_sem, near_send, near_recv, far_send, far_recv = refs[:8]
    z_send, z_recv, send_one, recv_one, send_two, recv_two = refs[8:]
    (dq, dk, dv, att, wq, wk, wv, before_around, before_own) = loaded[:9]
    (around_t, branch_t, others, stream, grad_mid, narrow, sums, bias, broad) = loaded[9:18]
    dp = plane.size
    d, z = lax.axis_index("dp"), lax.axis_index("mp")
    core = lax.rem(d, 2)
    rows, extent = dq.shape
    half = keep.shape[0]
    block = totals[0].shape[0]
    columns = 4 * extent

    loads = [
        pltpu.make_async_copy(source, target, load_sem.at[i])
        for i, (source, target) in enumerate(zip(hbm, loaded))
    ]
    for copy in loads:
        copy.start()
    width = wq.shape[0]
    halo_in[...] = jnp.zeros_like(halo_in)
    meet(d, z, dp, mp)

    def partner(step):
        there = (1 - core) * flipped(d, plane.orders[0][step]) + core * flipped(
            d, plane.orders[1][step]
        )
        return there, z

    def fold(target, source, at, count):
        target[:count, :] = added(target[:count, :], source[pl.ds(at, count), :])

    def far_of(step):
        count = half >> (plane.steps - step)
        first = step == plane.steps - 1
        return remote(
            upper if first else others.at[pl.ds(count, count), :],
            more_got.at[pl.ds(half - 2 * count, count), :],
            far_send.at[step],
            far_recv.at[step],
            partner(step),
        )

    sent = [far_of(plane.steps - 1)]
    sent[0].start()

    for i in (1, 2, 5, 6, 7):
        loads[i].wait()
    waits, at_left, at_right, at = [], margin, margin + rows, 0
    copies = []
    for hop, reach in enumerate(hops, 1):
        sides = (
            (at_left - reach, z - hop, z + hop, 2 * hop - 2, rows - reach),
            (at_right, z + hop, z - hop, 2 * hop - 1, 0),
        )
        for start, there, back, n, place in sides:
            span = slice(start, start + reach)
            here = pl.ds(at, reach)
            part = dot(dk[span, :], wk[...], NT) + dot(dv[span, :], wv[...], NT)
            halo_out[here, :] = (before_around[span, :] + part).astype(BF16)
            goes = (there >= 0) & (there < mp)
            comes = (back >= 0) & (back < mp)
            copy = remote(
                halo_out.at[here, :],
                halo_in.at[here, :],
                halo_send.at[n],
                halo_recv.at[n],
                (d, there),
            )
            pl.when(goes)(copy.start)
            waits.append((goes, copy.wait_send))
            copies.append((comes, copy.wait_recv, place, at, reach))
            at += reach
        at_left, at_right = at_left - reach, at_right + reach

    for i in (0, 3, 9, 10):
        loads[i].wait()
    inner, everything = slice(margin, margin + rows), slice(None)

    def weight_grads(target, low):
        for n, (source, span, right) in enumerate(
            (
                (around_t, inner, dq),
                (around_t, everything, dk),
                (around_t, everything, dv),
                (branch_t, everything, att),
            )
        ):
            target[:, n * extent : (n + 1) * extent] = dot(
                source[low : low + half, span], right[...]
            ).astype(BF16)

    weight_grads(send, half)
    swap = remote(send, got.at[pl.ds(0, half), :], core_sem.at[0], core_sem.at[1], (flipped(d, 0), z))
    swap.start()
    sent.append(swap)
    weight_grads(keep, 0)

    swap.wait_recv()
    fold(keep, got, 0, half)
    count, at_near = half, half
    for step in reversed(range(plane.steps)):
        count //= 2
        near = remote(
            keep.at[pl.ds(count, count), :],
            got.at[pl.ds(at_near, count), :],
            near_send.at[step],
            near_recv.at[step],
            partner(step),
        )
        near.start()
        sent.append(near)
        if step == plane.steps - 1:
            loads[4].wait()
            loads[8].wait()
            own = before_own[...] + before_around[inner, :] + dot(dq[...], wq[...], NT)
            own += dot(dk[inner, :], wk[...], NT) + dot(dv[inner, :], wv[...], NT)
            before_own[...] = own
            loads[11].wait()
        far_of(step).wait_recv()
        fold(others, more_got, half - 2 * count, count)
        if step:
            sent.append(far_of(step - 1))
            sent[-1].start()
        else:
            for r in range(1, mp):
                copy = remote(
                    others.at[pl.ds(0, block), pl.ds((r - 1) * columns, columns)],
                    shards.at[r],
                    z_send.at[r],
                    z_recv.at[r],
                    (d, lax.rem(z - r + mp, mp)),
                )
                copy.start()
                sent.append(copy)
        near.wait_recv()
        fold(keep, got, at_near, count)
        at_near += count

    for i in range(12, 18):
        loads[i].wait()
    for comes, wait, *_ in copies:
        pl.when(comes)(wait)
    for _, _, place, at, reach in copies:
        span = slice(place, place + reach)
        before_own[span, :] = before_own[span, :] + halo_in[at : at + reach, :].astype(F32)
    hat, factor = norm_parts(stream[...])
    upstream = before_own[...]
    add = lambda v: jnp.sum(v, axis=0, keepdims=True)
    back = grad_mid[...] + norm_back(upstream, hat, factor, narrow[0:1, :])
    grad_tokens[...] = back.astype(BF16)
    table[0:1, :] = add(upstream * hat)
    table[1:2, :] = add(upstream)
    table[2:6, :] = sums[0:4, :]
    mine = pl.ds(pl.multiple_of(z * extent, extent), extent)
    table[6:7, mine] = add(dq[...].astype(F32))
    table[7:8, mine] = add(dv[...].astype(F32))
    for r in range(1, mp):
        place = pl.ds(pl.multiple_of(lax.rem(z - r + mp, mp) * extent, extent), extent)
        table[6:8, place] = bias[0:2, (r - 1) * extent : r * extent]
    each = dp // (width // 128)
    hidden = broad.shape[1]
    lines = hidden // dp // 128
    per = hidden // mp // 128
    sheets[...] = jnp.zeros_like(sheets)
    for i in range(dp):
        c = i // each
        sheets[i, 0:8, :] = table[:, c * 128 : (c + 1) * 128]
        for n in range(lines):
            shard, at = (i * lines + n) // per, (i * lines + n) % per
            start = (lax.rem(z - shard + mp, mp) * per + at) * 128
            sheets[i, 8 + n : 9 + n, :] = broad[0:1, pl.ds(pl.multiple_of(start, 128), 128)]
    along_dp = lambda step: (lax.rem(d + step, dp), z)
    along_mp = lambda step: (d, lax.rem(z + step, mp))
    out = peers_start(sheets, second, send_two, recv_two, along_dp, d, dp, True)
    peers_finish(out, second, recv_two, d, dp)
    middle[0] = jnp.sum(second[...], axis=0)
    out = peers_start(middle, first, send_one, recv_one, along_mp, z, mp, False)
    for copy in loads[18:]:
        copy.wait()
    full = loaded[18][...]
    for item in loaded[19:]:
        full = full + item[...].astype(F32)
    tile = min(512, full.shape[1] // 2)
    for n in range(full.shape[1] // tile // 2):
        span = slice(n * tile, (n + 1) * tile)
        grad_expand[:, span] = full[:, 2 * n * tile : (2 * n + 1) * tile]
        grad_reduce[span, :] = full[:, (2 * n + 1) * tile : (2 * n + 2) * tile].T

    full = keep[:block, :].astype(F32)
    for r in range(1, mp):
        pltpu.make_async_copy(shards.at[r], shards.at[r], z_recv.at[r]).wait()
        full += shards[r].astype(F32)
    for n, item in enumerate(totals):
        part = full[:, n * extent : (n + 1) * extent]
        item[...] = part if n < 3 else part.T
    peers_finish(out, first, recv_one, z, mp)
    vectors[...] = jnp.sum(first[...], axis=0)
    for copy in sent:
        copy.wait_send()
    for when, wait in waits:
        pl.when(when)(wait)


def finish(arrays, upper, plane, mp, hops, margin):
    dp = plane.size
    rows, extent = arrays[0].shape
    width = arrays[4].shape[0]
    block, half, columns = width // dp, width // 2, 4 * extent
    hidden = arrays[18].shape[1] // 2
    vmem, anywhere = pl.BlockSpec(memory_space=pltpu.VMEM), pl.BlockSpec(memory_space=pl.ANY)
    dma = pltpu.SemaphoreType.DMA
    left = sum(hops)
    return pl.pallas_call(
        functools.partial(finish_kernel, plane, mp, hops, margin),
        out_shape=[
            jax.ShapeDtypeStruct((rows, width), BF16),
            *[jax.ShapeDtypeStruct((block, extent), F32)] * 3,
            jax.ShapeDtypeStruct((extent, block), F32),
            jax.ShapeDtypeStruct((block, hidden), F32),
            jax.ShapeDtypeStruct((hidden, block), F32),
            jax.ShapeDtypeStruct((16, 128), F32),
        ],
        in_specs=[anywhere] * (len(arrays) + 1),
        out_specs=[vmem] * 8,
        scratch_shapes=[pltpu.VMEM(item.shape, item.dtype) for item in arrays]
        + [
            pltpu.VMEM((2 * left, width), BF16),
            pltpu.VMEM((2 * left, width), BF16),
            pltpu.VMEM((half, columns), BF16),
            pltpu.VMEM((half, columns), BF16),
            pltpu.VMEM((2 * half, columns), BF16),
            pltpu.VMEM((half, (mp - 1) * columns), BF16),
            pltpu.VMEM((mp, block, columns), BF16),
            pltpu.VMEM((8, width), F32),
            pltpu.VMEM((dp, 16, 128), F32),
            pltpu.VMEM((1, 16, 128), F32),
            pltpu.VMEM((mp, 16, 128), F32),
            pltpu.VMEM((dp, 16, 128), F32),
            dma((len(arrays),)),
            dma((2 * len(hops),)),
            dma((2 * len(hops),)),
            dma((2,)),
            dma((plane.steps,)),
            dma((plane.steps,)),
            dma((plane.steps,)),
            dma((plane.steps,)),
            dma((mp,)),
            dma((mp,)),
            dma((mp,)),
            dma((mp,)),
            dma((dp,)),
            dma((dp,)),
        ],
        compiler_params=pltpu.CompilerParams(
            collective_id=2, has_side_effects=True, vmem_limit_bytes=60 * MIB
        ),
        cost_estimate=pl.CostEstimate(flops=5 * 10**10, bytes_accessed=0, transcendentals=0),
        name="finish",
    )(*arrays, upper)


def local(
    tokens,
    kept_index,
    lengths,
    first_gain,
    first_shift,
    query_weight,
    key_weight,
    value_weight,
    query_bias,
    value_bias,
    output_weight,
    output_bias,
    second_gain,
    second_shift,
    expand_weight,
    expand_bias,
    reduce_weight,
    reduce_bias,
    cotangent,
):
    dp, mp = lax.axis_size("dp"), lax.axis_size("mp")
    d, z = lax.axis_index("dp"), lax.axis_index("mp")
    plane = Plane(dp)
    rows, width = tokens.shape
    group_rows = rows * mp
    block = width // dp
    full_hidden = expand_weight.shape[1] * mp
    meta = jnp.concatenate([z[None], plane.order(d)]).astype(jnp.int32)

    singles = (
        first_gain,
        first_shift,
        output_bias,
        second_gain,
        second_shift,
        reduce_bias,
        query_bias,
        value_bias,
    )
    single, wide = first_gain.shape[0], expand_bias.shape[0]
    me = d * mp + z
    lane = jnp.arange(128, dtype=jnp.int32)
    lines = full_hidden // dp // 128

    def placed(stack):
        count = 128 // stack.shape[1]
        return jnp.where(lane // stack.shape[1] == me % count, jnp.tile(stack, (1, count)), 0.0)

    line = placed(expand_bias[None].astype(F32))
    at_line = (jnp.arange(8, dtype=jnp.int32) == me * wide // 128 % lines)[:, None]
    sheet = jnp.concatenate(
        [placed(jnp.stack(singles).astype(F32)), jnp.where(at_line, line, 0.0)], axis=0
    )
    scal = jnp.concatenate([z[None], lengths[0]]).astype(jnp.int32)
    reach, hops, left = LONGEST - 1, [], 0
    while reach > 0:
        extent = min(rows, -(-reach // 16) * 16)
        hops.append(extent)
        left, reach = left + extent, reach - extent
    margin = -(-left // 128) * 128
    while (2 * margin + rows) % TILE:
        margin += 128

    begun = begin(
        sheet[None],
        tokens,
        kept_index[None],
        jnp.asarray(position_lines(width)),
        (query_weight, key_weight, value_weight, output_weight, expand_weight, reduce_weight),
        plane,
        mp,
        hops,
        margin,
    )
    narrow, broad, stream, around, normed_one, second = begun[:6]
    buffers = begun[6:]
    shares = {1: shifted(second, 1, mp)}
    around_t = turned_rows(around, meta, block)
    projections = (query_weight, key_weight, value_weight)
    pairs = width // (2 * HEAD_SIZE) // mp
    own = project(normed_one, around, projections, narrow, meta, block, mp, True)
    tied = after(narrow, shares[1], *own)
    rest = project(normed_one, around, buffers, tied, meta, block, mp, False)
    heads = [own, rest]
    for r in range(2, mp):
        shares[r] = shifted(after(second, shares[1]), r, mp)
    early = spread_chips(shares[1], plane)
    far, late = (), []
    for r in range(1, mp):
        part = ((r - 1) * pairs, pairs, (mp - 1) * pairs)
        if r == 1:
            far = attention_forward(after(scal, early[-1]), mp, *heads[1], part, far)
            early = join(early, 0)
            early = (early, lax.ppermute(early, "dp", plane.pairs(plane.steps - 1)))
            near = attention_forward(after(scal, *far), mp, *heads[0], (0, pairs, pairs))
        else:
            tied = after(scal, *far, *near, shares[r])
            far = attention_forward(tied, mp, *heads[1], part, far)
            late.extend(spread_chips(shares[r], plane))
    attended, lses = [near[0], far[0]], [near[1], far[1]]

    results = middle(
        (stream, *attended, cotangent, narrow, broad),
        (output_weight, expand_weight, reduce_weight),
        buffers,
        (*early, *late),
        plane,
        mp,
        full_hidden,
    )
    sums_mid, grad_bias, own_two, ready = results[:4]
    activations, grad_middle, branch_t, grad_near, grad_far, kept, upper = results[4:11]
    moved_one = [
        lax.ppermute(ready[r // 2 - 1], "mp", [(j, (j - r) % mp) for j in range(mp)])
        for r in range(2, mp, 2)
    ]
    sums_two = Scatter(kept, upper, list(range(1, mp, 2)), plane, mp)

    grads_far = ()
    for r in range(1, mp):
        part = ((r - 1) * pairs, pairs, (mp - 1) * pairs)
        tied = after(scal, *grads_far, sums_two.got) if r == mp - 1 else after(scal, *grads_far)
        grads_far = attention_backward(
            tied,
            mp,
            *heads[1],
            grad_far,
            attended[1],
            lses[1],
            part,
            tuple(grads_far),
        )
    while sums_two.step > 0:
        sums_two.next()
    partial = tail(
        around_t,
        branch_t,
        grads_far,
        attended[1],
        buffers,
        (sums_two.keep, sums_two.got),
        own_two,
        moved_one,
        plane,
        mp,
        margin,
    )
    breadth = own_two.shape[1]
    moved_two = [
        lax.ppermute(
            partial[6][:, i * breadth : (i + 1) * breadth],
            "mp",
            [(j, (j - r) % mp) for j in range(mp)],
        )
        for i, r in enumerate(range(3, mp, 2))
    ]
    grads_near = attention_backward(
        after(scal, partial[0]),
        mp,
        *heads[0],
        grad_near,
        attended[0],
        lses[0],
        (0, pairs, pairs),
    )

    grad_tokens, grad_query, grad_key, grad_value, grad_out, grad_expand, grad_reduce, summed = finish(
        (
            *grads_near,
            attended[0],
            *projections,
            partial[1],
            partial[0],
            around_t,
            branch_t,
            partial[2],
            stream,
            grad_middle,
            narrow,
            sums_mid,
            partial[4],
            grad_bias,
            partial[5],
            *moved_two,
        ),
        partial[3],
        plane,
        mp,
        hops,
        margin,
    )

    taken = lambda stack, extent: lax.dynamic_slice_in_dim(
        stack, me % (128 // extent) * extent, extent, 1
    )
    small = taken(summed[:8], single)
    broad_row = lax.dynamic_slice_in_dim(summed[8:], me * wide // 128 % lines, 1, 0)
    return (
        activations,
        grad_tokens,
        grad_query,
        grad_key,
        grad_value,
        grad_out,
        grad_expand,
        grad_reduce,
        small[0],
        small[1],
        small[6],
        small[7],
        small[2],
        small[3],
        small[4],
        taken(broad_row, wide)[0],
        small[5],
    )


def solution(mesh):
    vector = P(("dp", "mp"))
    tall = P(("dp", "mp"), None)
    in_specs = (
        tall,
        vector,
        P("dp", None),
        vector,
        vector,
        P(None, "mp"),
        P(None, "mp"),
        P(None, "mp"),
        vector,
        vector,
        P("mp", None),
        vector,
        vector,
        vector,
        P(None, "mp"),
        vector,
        P("mp", None),
        vector,
        tall,
    )
    out_specs = (
        tall,
        tall,
        P("dp", "mp"),
        P("dp", "mp"),
        P("dp", "mp"),
        P("mp", "dp"),
        P("dp", "mp"),
        P("mp", "dp"),
    ) + (vector,) * 9
    return jax.shard_map(local, mesh=mesh, in_specs=in_specs, out_specs=out_specs, check_vma=False)
```

```python
import functools
import math

import jax
import jax.numpy as jnp
import numpy as np
from jax import lax
from jax.experimental import pallas as pl
from jax.experimental.pallas import tpu as pltpu
from jax.sharding import PartitionSpec as P

HEAD_SIZE = 64
LONGEST = 549
EPSILON = 1e-06
TILE = 256
PAIR = 2 * HEAD_SIZE
PAIRS = 2
MIB = 1024 * 1024
F32 = jnp.float32
BF16 = jnp.bfloat16

NN = (((1,), (0,)), ((), ()))
NT = (((1,), (1,)), ((), ()))
TN = (((0,), (0,)), ((), ()))


def dot(left, right, dims=NN):
    return lax.dot_general(left, right, dims, preferred_element_type=F32)


def position_lines(extent):
    quarter = extent // 4
    spatial = (extent - quarter) // 2
    table = np.zeros((128, extent), np.float32)
    at, first = 0, 0
    for count, part in ((8, quarter), (14, spatial), (14, spatial)):
        half = part // 2
        inverse = np.exp(np.arange(half, dtype=np.float32) * np.float32(-math.log(10000.0) / half))
        angles = np.arange(count, dtype=np.float32)[:, None] * inverse[None, :]
        table[first : first + count, at : at + half] = np.sin(angles)
        table[first : first + count, at + half : at + part] = np.cos(angles)
        at, first = at + part, first + count
    return table


def norm_parts(values):
    center = values - jnp.mean(values, axis=-1, keepdims=True)
    spread = jnp.mean(center * center, axis=-1, keepdims=True)
    factor = lax.rsqrt(spread + EPSILON)
    return center * factor, factor


def norm_back(upstream, hat, factor, gain):
    scaled = upstream * gain
    first = jnp.mean(scaled, axis=-1, keepdims=True)
    second = jnp.mean(scaled * hat, axis=-1, keepdims=True)
    return factor * (scaled - first - hat * second)


def clip_label(places, scal, clips, rows, mp):
    label, end = jnp.zeros_like(places), 0
    for c in range(clips):
        end = end + scal[1 + c]
        label = label + (places >= end).astype(jnp.int32)
    return jnp.where((places >= 0) & (places < rows * mp), label, -1)


def tile_range(first, last, base, scal, clips):
    start, end, stop = 0, 0, 0
    for c in range(clips):
        length = scal[1 + c]
        stop = jnp.where(end <= last, end + length, stop)
        end = end + length
        start = jnp.where(end <= first, end, start)
    return lax.div(start - base, TILE), lax.div(stop - base + TILE - 1, TILE)


def forward_kernel(layout, scal, q_ref, k_ref, v_ref, o_ref, lse_ref, s_ref, lq_ref, lk_ref):
    clips, mp = layout
    rows, window = q_ref.shape[0], k_ref.shape[0]
    base = scal[0] * rows - (window - rows) // 2

    @pl.when(pl.program_id(0) == 0)
    def _():
        own = scal[0] * rows + lax.broadcasted_iota(jnp.int32, lq_ref.shape, 1)
        lq_ref[...] = clip_label(own, scal, clips, rows, mp)
        around = base + lax.broadcasted_iota(jnp.int32, lk_ref.shape, 0)
        lk_ref[...] = clip_label(around, scal, clips, rows, mp)

    row = lax.broadcasted_iota(jnp.int32, (2 * HEAD_SIZE, TILE), 0)
    beside = lambda pair: jnp.concatenate(pair, axis=1)
    groups = lambda array: array.reshape(TILE // 8, 8, 2 * TILE)
    pairs = q_ref.shape[1] // PAIR
    for block in range(rows // TILE):
        first = scal[0] * rows + block * TILE
        low, high = tile_range(first, first + TILE - 1, base, scal, clips)
        span = slice(block * TILE, (block + 1) * TILE)
        query_th = []
        for g in range(pairs):
            query_t = q_ref[span, g * PAIR : (g + 1) * PAIR].T
            zero = jnp.zeros_like(query_t)
            query_th.append(
                beside(
                    [
                        jnp.where(row < HEAD_SIZE, query_t, zero),
                        jnp.where(row < HEAD_SIZE, zero, query_t),
                    ]
                )
            )
        label = lq_ref[0:1, span]
        label = beside([label, label])

        def scores(t, carry):
            at = pl.multiple_of(t * TILE, TILE)
            same = beside([lk_ref[pl.ds(at, TILE), :]] * 4) == label
            out = []
            for g in range(pairs):
                key = k_ref[pl.ds(at, TILE), g * PAIR : (g + 1) * PAIR]
                s = jnp.where(same, dot(key, query_th[g]), -1e30)
                s_ref[g, pl.ds(at, TILE), :] = s
                out.append(jnp.maximum(carry[g], jnp.max(groups(s), axis=0)))
            return tuple(out)

        least = jnp.full((8, 2 * TILE), -1e30, F32)
        peaks = lax.fori_loop(low, high, scores, (least,) * pairs)
        peaks = [jnp.max(item, axis=0, keepdims=True) for item in peaks]

        def blend(t, carry):
            at = pl.multiple_of(t * TILE, TILE)
            out = []
            for g in range(pairs):
                total, *accs = carry[g]
                p = jnp.exp(s_ref[g, pl.ds(at, TILE), :] - peaks[g])
                weights = p.astype(BF16)
                value_t = v_ref[pl.ds(at, TILE), g * PAIR : (g + 1) * PAIR].T
                total = total + jnp.sum(groups(p), axis=0)
                parts = [
                    accs[h]
                    + dot(
                        value_t[h * HEAD_SIZE : (h + 1) * HEAD_SIZE],
                        weights[:, h * TILE : (h + 1) * TILE],
                    )
                    for h in range(2)
                ]
                out.append((total, *parts))
            return tuple(out)

        zero = jnp.zeros((HEAD_SIZE, TILE), F32)
        start = (jnp.zeros((8, 2 * TILE), F32), zero, zero)
        done = lax.fori_loop(low, high, blend, (start,) * pairs)
        for g in range(pairs):
            total, *accs = done[g]
            total = jnp.sum(total, axis=0, keepdims=True)
            lse = peaks[g] + jnp.log(total)
            for h in range(2):
                columns = slice(h * TILE, (h + 1) * TILE)
                lse_ref[g, h : h + 1, span] = lse[:, columns]
                accs[h] = accs[h] / total[:, columns]
            o_ref[span, g * PAIR : (g + 1) * PAIR] = jnp.concatenate(accs, axis=0).T.astype(BF16)


def backward_kernel(
    layout,
    scal,
    q_ref,
    k_ref,
    v_ref,
    do_ref,
    o_ref,
    lse_ref,
    dq_ref,
    dk_ref,
    dv_ref,
    dk_acc,
    dv_acc,
    lq_ref,
    lk_ref,
):
    clips, mp = layout
    rows, window = q_ref.shape[0], k_ref.shape[0]
    base = scal[0] * rows - (window - rows) // 2

    @pl.when(pl.program_id(0) == 0)
    def _():
        own = scal[0] * rows + lax.broadcasted_iota(jnp.int32, lq_ref.shape, 1)
        lq_ref[...] = clip_label(own, scal, clips, rows, mp)
        around = base + lax.broadcasted_iota(jnp.int32, lk_ref.shape, 0)
        lk_ref[...] = clip_label(around, scal, clips, rows, mp)

    lane = lax.broadcasted_iota(jnp.int32, (TILE, 2 * HEAD_SIZE), 1)
    row = lax.broadcasted_iota(jnp.int32, (2 * HEAD_SIZE, TILE), 0)
    dk_acc[...] = jnp.zeros_like(dk_acc)
    dv_acc[...] = jnp.zeros_like(dv_acc)

    def halves(array, where):
        zero = jnp.zeros_like(array)
        return [jnp.where(where < HEAD_SIZE, array, zero), jnp.where(where < HEAD_SIZE, zero, array)]

    beside = lambda pair: jnp.concatenate(pair, axis=1)
    pairs = q_ref.shape[1] // PAIR
    for block in range(rows // TILE):
        first = scal[0] * rows + block * TILE
        low, high = tile_range(first, first + TILE - 1, base, scal, clips)
        span = slice(block * TILE, (block + 1) * TILE)
        label = lq_ref[0:1, span]
        label = beside([label, label])
        fixed = []
        for g in range(pairs):
            own = slice(g * PAIR, (g + 1) * PAIR)
            query, grad = q_ref[span, own], do_ref[span, own]
            query_t, grad_t = query.T, grad.T
            product = grad_t.astype(F32) * o_ref[span, own].T.astype(F32)
            delta = beside(
                [
                    jnp.sum(product[h * HEAD_SIZE : (h + 1) * HEAD_SIZE], axis=0, keepdims=True)
                    for h in range(2)
                ]
            )
            lse = beside([lse_ref[g, h : h + 1, span] for h in range(2)])
            query_h = jnp.concatenate(halves(query, lane), axis=0)
            grad_h = jnp.concatenate(halves(grad, lane), axis=0)
            query_th, grad_th = beside(halves(query_t, row)), beside(halves(grad_t, row))
            fixed.append((own, delta, lse, query_h, grad_h, query_th, grad_th))

        def step(t, carry):
            at = pl.multiple_of(t * TILE, TILE)
            same = beside([lk_ref[pl.ds(at, TILE), :]] * 4) == label
            out = []
            for g in range(pairs):
                own, delta, lse, query_h, grad_h, query_th, grad_th = fixed[g]
                key, value = k_ref[pl.ds(at, TILE), own], v_ref[pl.ds(at, TILE), own]
                key_t = key.T
                p = jnp.where(same, jnp.exp(dot(key, query_th) - lse), 0.0)
                ds = (p * (dot(value, grad_th) - delta)).astype(BF16)
                dv_acc[pl.ds(at, TILE), own] += dot(p.astype(BF16), grad_h)
                dk_acc[pl.ds(at, TILE), own] += dot(ds, query_h)
                out.extend(
                    carry[2 * g + h]
                    + dot(
                        key_t[h * HEAD_SIZE : (h + 1) * HEAD_SIZE], ds[:, h * TILE : (h + 1) * TILE]
                    )
                    for h in range(2)
                )
            return tuple(out)

        zero = jnp.zeros((HEAD_SIZE, TILE), F32)
        parts = lax.fori_loop(low, high, step, (zero,) * (2 * pairs))
        for g in range(pairs):
            total = jnp.concatenate(parts[2 * g : 2 * g + 2], axis=0) * (1.0 / math.sqrt(HEAD_SIZE))
            dq_ref[span, fixed[g][0]] = total.T.astype(BF16)
    dk_ref[...] = dk_acc[...].astype(BF16)
    dv_ref[...] = dv_acc[...].astype(BF16)


def attention_call(kernel, name, scal, columns, others, outs, scratch, part, before, work):
    first, count, total = part
    each = min(PAIRS, count)
    pair, first, count = each * PAIR, first // each, count // each
    anywhere = pl.BlockSpec(memory_space=pl.ANY)
    column = lambda item: pl.BlockSpec((item.shape[0], pair), lambda p, b: (0, first + p))
    result = pl.pallas_call(
        kernel,
        grid_spec=pltpu.PrefetchScalarGridSpec(
            num_scalar_prefetch=1,
            grid=(count,),
            in_specs=[column(item) for item in columns]
            + [
                pl.BlockSpec((each,) + item.shape[1:], lambda p, b: (first + p, 0, 0))
                if item.ndim == 3
                else pl.BlockSpec(item.shape, lambda p, b: (0, 0))
                for item in others
            ]
            + [anywhere] * len(before),
            out_specs=[
                pl.BlockSpec((each,) + shape[1:], lambda p, b: (first + p, 0, 0))
                if len(shape) == 3
                else pl.BlockSpec((shape[0], pair), lambda p, b: (0, first + p))
                for shape, _ in outs
            ],
            scratch_shapes=scratch,
        ),
        out_shape=[jax.ShapeDtypeStruct(shape, kind) for shape, kind in outs],
        input_output_aliases={
            1 + len(columns) + len(others) + i: i for i in range(len(before))
        },
        compiler_params=pltpu.CompilerParams(vmem_limit_bytes=32 * MIB),
        cost_estimate=pl.CostEstimate(flops=count * each * work, bytes_accessed=0, transcendentals=0),
        name=name,
    )(scal, *columns, *others, *before)
    return result


def attention_forward(scal, mp, queries, keys, values, part, before=()):
    rows, width = queries.shape
    window = keys.shape[0]

    def kernel(*refs):
        forward_kernel((scal.shape[0] - 1, mp), *refs[:4], *refs[4 + len(before) :])

    return attention_call(
        kernel,
        "attention_forward",
        scal,
        (queries, keys, values),
        (),
        [((rows, width), BF16), ((part[2], 2, rows), F32)],
        [
            pltpu.VMEM((min(PAIRS, part[1]), window, 2 * TILE), F32),
            pltpu.VMEM((8, rows), jnp.int32),
            pltpu.VMEM((window, 128), jnp.int32),
        ],
        part,
        before,
        5 * 10**9,
    )


def attention_backward(scal, mp, queries, keys, values, grads, attended, lse, part, before=()):
    rows, width = queries.shape
    window = keys.shape[0]

    def kernel(*refs):
        backward_kernel((scal.shape[0] - 1, mp), *refs[:7], *refs[7 + len(before) :])

    return attention_call(
        kernel,
        "attention_backward",
        scal,
        (queries, keys, values, grads, attended),
        (lse,),
        [((rows, width), BF16), ((window, width), BF16), ((window, width), BF16)],
        [pltpu.VMEM((window, min(PAIRS, part[1]) * PAIR), F32)] * 2
        + [pltpu.VMEM((8, rows), jnp.int32), pltpu.VMEM((window, 128), jnp.int32)],
        part,
        before,
        6 * 10**9,
    )


def assemble(target, buffers, meta, block, first=0):
    each = buffers[0].shape[0] // block
    span = slice(first, first + buffers[0].shape[1])
    for i in range(len(buffers) * each):
        at = pl.multiple_of(meta[1 + i] * block, block)
        source = buffers[i // each]
        target[pl.ds(at, block), span] = source[i % each * block : (i % each + 1) * block, :]


def turn(target, source, meta, block, lead):
    lead[...] = source.T
    for i in range(target.shape[0] // block):
        at = pl.multiple_of(meta[1 + i] * block, block)
        target[i * block : (i + 1) * block, :] = lead[pl.ds(at, block), :]


def fixed(shape):
    return pl.BlockSpec(shape, lambda *_: (0,) * len(shape), pipeline_mode=pl.Buffered(1))


def call(kernel, name, grid, meta, ins, outs, scratch, vmem, flops, moved=0):
    return pl.pallas_call(
        kernel,
        grid_spec=pltpu.PrefetchScalarGridSpec(
            num_scalar_prefetch=1,
            grid=grid,
            in_specs=[spec for _, spec in ins],
            out_specs=[spec for _, _, spec in outs],
            scratch_shapes=scratch,
        ),
        out_shape=[jax.ShapeDtypeStruct(shape, kind) for shape, kind, _ in outs],
        compiler_params=pltpu.CompilerParams(vmem_limit_bytes=vmem * MIB),
        cost_estimate=pl.CostEstimate(flops=flops, bytes_accessed=moved, transcendentals=0),
        name=name,
    )(meta, *[array for array, _ in ins])


def turn_kernel(block, meta, source, target, lead):
    turn(target, source[...], meta, block, lead)


def turned_rows(source, meta, block):
    rows, width = source.shape
    return call(
        functools.partial(turn_kernel, block),
        "turn",
        (1,),
        meta,
        [(source, fixed(source.shape))],
        [((width, rows), BF16, fixed((width, rows)))],
        [pltpu.VMEM((width, rows), BF16)],
        24,
        4 * 10**9,
    )[0]


def project_kernel(block, scale, own, meta, x, around, bias, *refs):
    weights, (q, k, v), scratch = refs[:-6], refs[-6:-3], refs[-3:]
    if own:
        scratch = weights
    else:
        for w in range(3):
            assemble(scratch[w], weights[4 * w : 4 * w + 4], meta, block)
    q[...] = (dot(x[...], scratch[0][...]) + bias[6:7, :]).astype(BF16) * jnp.asarray(scale, BF16)
    k[...] = dot(around[...], scratch[1][...]).astype(BF16)
    v[...] = (dot(around[...], scratch[2][...]) + bias[7:8, :]).astype(BF16)


def gathered_specs(buffers, kinds, extent, stride):
    return [
        (item, pl.BlockSpec((item.shape[0], extent), lambda i, m, kind=kind: (0, i * stride + kind)))
        for kind in kinds
        for item in buffers
    ]


def project(x, around, weights, narrow, meta, block, mp, own):
    rows, width = x.shape
    window = around.shape[0]
    extent = width // mp
    first, count = (0, 1) if own else (1, mp - 1)
    column = lambda n: pl.BlockSpec((n, extent), lambda i, m: (0, i))
    turned = lambda i, m: (0, lax.rem(m[0] - first - i + mp, mp))
    return call(
        functools.partial(project_kernel, block, 1.0 / math.sqrt(HEAD_SIZE), own),
        "project",
        (count,),
        meta,
        [
            (x, fixed(x.shape)),
            (around, fixed(around.shape)),
            (narrow, pl.BlockSpec((8, extent), turned)),
        ]
        + (
            [(w, fixed(w.shape)) for w in weights]
            if own
            else gathered_specs(weights, (0, 1, 2), extent, 4)
        ),
        [
            ((rows, count * extent), BF16, column(rows)),
            ((window, count * extent), BF16, column(window)),
            ((window, count * extent), BF16, column(window)),
        ],
        [pltpu.VMEM((width, extent), BF16)] * 3,
        40,
        count * 4 * 10**9,
    )


def join(parts, axis):
    return jnp.concatenate(parts, axis=axis)


class Plane:
    def __init__(self, size):
        self.size = size
        bits = list(range(1, size.bit_length() - 1))
        turn = len(bits) // 2
        self.orders = [bits, bits[turn:] + bits[:turn]]
        held = []
        for order in self.orders:
            masks = [0]
            for bit in order:
                masks = masks + [m ^ (1 << bit) for m in masks]
            held.append(masks)
        self.masks = [held[c] + [1 ^ m for m in held[1 - c]] for c in range(2)]
        self.steps = len(bits)

    def pairs(self, step):
        return [(i, i ^ (1 << self.orders[i % 2][step])) for i in range(self.size)]

    def siblings(self):
        return [(i, i ^ 1) for i in range(self.size)]

    def order(self, d):
        return jnp.bitwise_xor(jnp.array(self.masks, jnp.int32)[d % 2], d)


def shifted(payload, r, mp):
    return lax.ppermute(payload, "mp", [(i, (i + r) % mp) for i in range(mp)])


def spread_chips(held, plane):
    for step in range(plane.steps - 2):
        held = join([held, lax.ppermute(held, "dp", plane.pairs(step))], 0)
    return held, lax.ppermute(held, "dp", plane.pairs(plane.steps - 2))


def added(left, right):
    return (left.astype(F32) + right.astype(F32)).astype(BF16)


def folded(keep, got):
    half = keep.shape[0] // 2
    return added(keep[:half], got[:half]), added(keep[half:], got[half:])


def after(value, *others):
    return lax.optimization_barrier((value,) + others)[0]


class Scatter:
    def __init__(self, keep, upper, shifts, plane, mp):
        self.keep, self.shifts, self.plane, self.mp = keep, shifts, plane, mp
        self.step = plane.steps - 1
        self.got = lax.ppermute(upper, "dp", plane.pairs(self.step))

    def next(self):
        self.step -= 1
        self.keep, upper = folded(self.keep, self.got)
        self.got = lax.ppermute(upper, "dp", self.plane.pairs(self.step))
        return self


MESH = pl.DeviceIdType.MESH


def flipped(d, bit):
    return d + (1 - 2 * lax.rem(lax.div(d, 1 << bit), 2)) * (1 << bit)


def greet(d, z, dp, mp):
    barrier = pltpu.get_barrier_semaphore()
    for step in range(1, dp):
        there = (lax.rem(d + step, dp), z)
        pl.semaphore_signal(barrier, inc=1, device_id=there, device_id_type=MESH)
    for step in range(1, mp):
        there = (d, lax.rem(z + step, mp))
        pl.semaphore_signal(barrier, inc=1, device_id=there, device_id_type=MESH)


def gather_peers(dp, mp):
    pl.semaphore_wait(pltpu.get_barrier_semaphore(), dp + mp - 2)


def meet(d, z, dp, mp):
    greet(d, z, dp, mp)
    gather_peers(dp, mp)


def remote(source, target, send_sem, recv_sem, device):
    return pltpu.make_async_remote_copy(
        src_ref=source,
        dst_ref=target,
        send_sem=send_sem,
        recv_sem=recv_sem,
        device_id=device,
        device_id_type=MESH,
    )


def peers_start(source, slots, send_sem, recv_sem, along, me, extent, each):
    copies = []
    for step in range(1, extent):
        place = lax.rem(me + step, extent)
        copies.append(
            remote(
                source.at[place if each else 0],
                slots.at[me],
                send_sem.at[step],
                recv_sem.at[me],
                along(step),
            )
        )
        copies[-1].start()
    slots[me] = source[me if each else 0]
    return copies


def peers_finish(copies, slots, recv_sem, me, extent):
    for step in range(1, extent):
        copies[step - 1].wait_send()
        sender = lax.rem(me + step, extent)
        pltpu.make_async_copy(slots.at[sender], slots.at[sender], recv_sem.at[sender]).wait()


def begin_kernel(plane, mp, hops, margin, *refs):
    (sheet, tokens, index, table), shards_in, refs = refs[:4], refs[4:10], refs[10:]
    (narrow, broad, stream, around, normed_out, second_out), buffers = refs[:6], refs[6:10]
    (middle, first, second, normed, zeros, payload, out_in, out_t), refs = refs[10:18], refs[18:]
    (reduce_in, reduce_t, take), refs = refs[:3], refs[3:]
    send_one, recv_one, send_two, recv_two, refs = *refs[:4], refs[4:]
    z_send, z_recv, chip_send, chip_recv, core_send, core_recv, halo_send, halo_recv, local = refs
    dp = plane.size
    d, z = lax.axis_index("dp"), lax.axis_index("mp")
    core = lax.rem(d, 2)
    rows, width = tokens.shape
    block, columns = payload.shape
    along_dp = lambda step: (lax.rem(d + step, dp), z)
    along_mp = lambda step: (d, lax.rem(z + step, mp))

    query, key, value, output, expand, reduce = shards_in
    extent, hidden_extent = query.shape[1], expand.shape[1]
    mine = pl.ds(pl.multiple_of(d * block, block), block)
    line = pl.ds(pl.multiple_of(lax.div(d * block, 128) * 128, 128), 128)
    taken = [
        pltpu.make_async_copy(
            source.at[mine, :], payload.at[:, pl.ds(w * extent, extent)], take.at[w]
        )
        for w, source in enumerate((query, key, value))
    ]
    taken.append(pltpu.make_async_copy(output.at[:, line], out_in, take.at[3]))
    taken.append(pltpu.make_async_copy(reduce.at[:, line], reduce_in, take.at[4]))
    taken.append(
        pltpu.make_async_copy(
            expand.at[mine, :], second_out.at[:, pl.ds(0, hidden_extent)], take.at[5]
        )
    )
    for copy in taken:
        copy.start()
    zeros[...] = jnp.zeros_like(zeros)
    meet(d, z, dp, mp)
    vectors = peers_start(sheet, first, send_one, recv_one, along_mp, z, mp, False)
    for copy in taken[:4]:
        copy.wait()
    out_t[...] = out_in[...].T
    within = pl.ds(pl.multiple_of(lax.rem(d * block, 128), block), block)
    payload[:, 3 * extent :] = out_t[within, :]

    each = dp // 4

    def place(j, r, other=False):
        return buffers[j // each + (2 if other else 0)].at[
            pl.ds(j % each * block, block), pl.ds((r - 1) * columns, columns)
        ]

    def passed_on(way, r):
        before = r - 1 if way == 0 else (r + 1) % mp
        source = place(0, before) if before else payload
        return remote(
            source, place(0, r), z_send.at[way, r], z_recv.at[r], (d, z + 1 if way == 0 else z - 1)
        )

    last, least = z + 1 < mp, z > 0
    line_sends = [(last & (z >= r - 1), passed_on(0, r).wait_send) for r in range(1, mp)]
    line_sends += [(least & (z <= r), passed_on(1, r).wait_send) for r in range(1, mp)]
    pl.when(last)(passed_on(0, 1).start)
    pl.when(least)(passed_on(1, mp - 1).start)

    kept = index[...]
    coarse = lax.div(kept, 14)
    frame = lax.div(kept, 196)
    across = coarse - frame * 14
    line = kept - coarse * 14
    count = lax.broadcasted_iota(jnp.int32, (table.shape[0], rows), 0)
    hot = ((count == frame) | (count == across + 8) | (count == line + 22)).astype(F32)
    hidden = tokens[...].astype(F32) + lax.dot_general(
        hot, table[...], TN, precision=lax.Precision.HIGHEST, preferred_element_type=F32
    )
    stream[...] = hidden

    peers_finish(vectors, first, recv_one, z, mp)
    middle[0] = jnp.sum(first[...], axis=0)
    vectors = peers_start(middle, second, send_two, recv_two, along_dp, d, dp, False)
    hat, _ = norm_parts(hidden)
    peers_finish(vectors, second, recv_two, d, dp)
    share = dp // (width // 128)
    for c in range(width // 128):
        narrow[:, c * 128 : (c + 1) * 128] = jnp.sum(
            second[c * share : (c + 1) * share, 0:8, :], axis=0
        )
    lines = broad.shape[1] // 128
    per = lines // dp
    for c in range(lines):
        row = second[c // per, 8 + c % per : 9 + c % per, :]
        broad[:, c * 128 : (c + 1) * 128] = jnp.broadcast_to(row, (8, 128))
    normed[...] = (hat * narrow[0:1, :] + narrow[1:2, :]).astype(BF16)
    taken[4].wait()
    reduce_t[...] = reduce_in[...].T
    shares = (
        pltpu.make_async_copy(
            reduce_t.at[within, :],
            second_out.at[:, pl.ds(hidden_extent, hidden_extent)],
            take.at[6],
        ),
        pltpu.make_async_copy(normed, normed_out, take.at[7]),
    )
    for copy in shares:
        copy.start()

    sent = []

    def arrived(j, r):
        pltpu.make_async_copy(place(j, r), place(j, r), z_recv.at[r]).wait()

    def copies_of(j, r):
        copies = []
        for step in range(plane.steps):
            if j < 1 << step:
                there = (1 - core) * flipped(d, plane.orders[0][step]) + core * flipped(
                    d, plane.orders[1][step]
                )
                to = (1 << step) + j
                copies.append(
                    remote(
                        place(j, r),
                        place(to, r),
                        chip_send.at[r, to],
                        chip_recv.at[r, to],
                        (there, z),
                    )
                )
        copies.append(
            remote(
                place(j, r),
                place(j, r, True),
                core_send.at[r, j],
                core_recv.at[r, j],
                (flipped(d, 0), z),
            )
        )
        return copies

    def forward(j, r):
        for copy in copies_of(j, r):
            copy.start()

    def handle(h):

        @pl.when(z >= h)
        def _():
            arrived(0, h)
            if h + 1 < mp:
                pl.when(last)(passed_on(0, h + 1).start)
            forward(0, h)

        @pl.when(z + h < mp)
        def _():
            arrived(0, mp - h)
            if mp - h > 1:
                pl.when(least)(passed_on(1, mp - h - 1).start)
            forward(0, mp - h)

    for h in range(1, mp - 1):
        handle(h)

    waits, at_left, at_right = [], margin, margin + rows
    inside = pltpu.make_async_copy(
        normed, around.at[pl.ds(margin, rows), :], local.at[0]
    )
    inside.start()
    waits.append((None, inside.wait))
    for hop, extent in enumerate(hops, 1):
        left = around.at[pl.ds(at_left - extent, extent), :]
        right = around.at[pl.ds(at_right, extent), :]
        sides = (
            (left, normed.at[pl.ds(rows - extent, extent), :], z + hop, z - hop, 2 * hop - 2),
            (right, normed.at[pl.ds(0, extent), :], z - hop, z + hop, 2 * hop - 1),
        )
        for target, source, there, back, n in sides:
            goes = (there >= 0) & (there < mp)
            comes = (back >= 0) & (back < mp)
            copy = remote(source, target, halo_send.at[n], halo_recv.at[n], (d, there))
            blank = pltpu.make_async_copy(zeros.at[pl.ds(0, extent), :], target, local.at[1 + n])
            pl.when(goes)(copy.start)
            pl.when(jnp.logical_not(comes))(blank.start)
            waits.append((goes, copy.wait_send))
            waits.append((comes, copy.wait_recv))
            waits.append((jnp.logical_not(comes), blank.wait))
        at_left, at_right = at_left - extent, at_right + extent
    if at_left:
        for n, at in enumerate((0, at_right)):
            blank = pltpu.make_async_copy(
                zeros.at[pl.ds(0, at_left), :],
                around.at[pl.ds(at, at_left), :],
                local.at[1 + 2 * len(hops) + n],
            )
            blank.start()
            waits.append((None, blank.wait))

    for h in range(mp - 1, mp):
        handle(h)
    for r in range(1, mp):
        sent.extend(copies_of(0, r))
    for j in range(1, 1 << plane.steps):
        for r in range(1, mp):
            pltpu.make_async_copy(place(j, r), place(j, r), chip_recv.at[r, j]).wait()
            forward(j, r)
            sent.extend(copies_of(j, r))
    for j in range(1 << plane.steps):
        for r in range(1, mp):
            pltpu.make_async_copy(place(j, r, True), place(j, r, True), core_recv.at[r, j]).wait()
    for copy in sent:
        copy.wait_send()
    for when, wait in line_sends:
        pl.when(when)(wait)
    taken[5].wait()
    for copy in shares:
        copy.wait()
    for when, wait in waits:
        wait() if when is None else pl.when(when)(wait)


def begin(sheet, tokens, index, table, shards, plane, mp, hops, margin):
    dp = plane.size
    rows, width = tokens.shape
    extent, hidden = shards[0].shape[1], shards[4].shape[1]
    block, columns, full_hidden = width // dp, 4 * extent, hidden * mp
    vmem, anywhere = pl.BlockSpec(memory_space=pltpu.VMEM), pl.BlockSpec(memory_space=pl.ANY)
    window = 2 * margin + rows
    dma = pltpu.SemaphoreType.DMA
    blocks = dp // 2
    return pl.pallas_call(
        functools.partial(begin_kernel, plane, mp, hops, margin),
        out_shape=[
            jax.ShapeDtypeStruct((8, width), F32),
            jax.ShapeDtypeStruct((8, full_hidden), F32),
            jax.ShapeDtypeStruct((rows, width), F32),
            jax.ShapeDtypeStruct((window, width), BF16),
            jax.ShapeDtypeStruct((rows, width), BF16),
            jax.ShapeDtypeStruct((block, 2 * hidden), BF16),
        ]
        + [jax.ShapeDtypeStruct((width // 4, (mp - 1) * columns), BF16)] * 4,
        in_specs=[vmem] * 4 + [anywhere] * 6,
        out_specs=[vmem] * 3 + [anywhere] * 7,
        scratch_shapes=[
            pltpu.VMEM((1, 16, 128), F32),
            pltpu.VMEM((mp, 16, 128), F32),
            pltpu.VMEM((dp, 16, 128), F32),
            pltpu.VMEM((rows, width), BF16),
            pltpu.VMEM((rows, width), BF16),
            pltpu.VMEM((block, columns), BF16),
            pltpu.VMEM((extent, 128), BF16),
            pltpu.VMEM((128, extent), BF16),
            pltpu.VMEM((hidden, 128), BF16),
            pltpu.VMEM((128, hidden), BF16),
            dma((8,)),
            dma((mp,)),
            dma((mp,)),
            dma((dp,)),
            dma((dp,)),
            dma((2, mp)),
            dma((mp,)),
            dma((mp, blocks)),
            dma((mp, blocks)),
            dma((mp, blocks)),
            dma((mp, blocks)),
            dma((2 * len(hops),)),
            dma((2 * len(hops),)),
            dma((3 + 2 * len(hops),)),
        ],
        compiler_params=pltpu.CompilerParams(
            collective_id=1, has_side_effects=True, vmem_limit_bytes=60 * MIB
        ),
        cost_estimate=pl.CostEstimate(flops=4 * 10**10, bytes_accessed=0, transcendentals=0),
        name="begin",
    )(sheet, tokens, index, table, *shards)


def xored(d, mask):
    for bit in range(mask.bit_length()):
        if mask >> bit & 1:
            d = flipped(d, bit)
    return d


def middle_kernel(plane, mp, tile, *refs):
    (stream_in, near_in, far_in, g_in, narrow_in, broad_in), refs = refs[:6], refs[6:]
    own_o, own_e, own_r, out_parts, refs = *refs[:3], refs[3:7], refs[7:]
    (early_a, early_b), late_a, refs = refs[:2], refs[2 : 2 * mp - 2], refs[2 * mp - 2 :]
    (sums, db, own_total, moved, act, grad_mid, branch_t, grad_near, grad_far), refs = refs[:9], refs[9:]
    (keep_out, upper_out, early_o, late_b, late_c, late_d), refs = refs[:6], refs[6:]
    (mid, near, far, g, narrow, broad, o_temp, weight_o, weights, r_temp), refs = refs[:10], refs[10:]
    (x, x_t, g_t, lead, out_acc, dx_acc, keep, send, got, more), refs = refs[:10], refs[10:]
    load, weight_sem, own_sem, core_send, core_recv, chip_send, chip_recv, refs = *refs[:7], refs[7:]
    sum_send, sum_recv, near_send, near_recv, store = refs
    dp, steps = plane.size, plane.steps
    d, z = lax.axis_index("dp"), lax.axis_index("mp")
    core = lax.rem(d, 2)
    rows, width = x.shape
    block, half, quarter = width // dp, width // 2, width // 4
    extent = own_e.shape[1]
    per = extent // tile
    tiles = mp * per
    wide = 2 * extent
    full = mp // 2
    orders = [
        (1 - core) * xored(d, plane.masks[0][i]) + core * xored(d, plane.masks[1][i])
        for i in range(dp)
    ]
    sibling = (flipped(d, 0), z)

    def partner(step):
        there = (1 - core) * flipped(d, plane.orders[0][step]) + core * flipped(
            d, plane.orders[1][step]
        )
        return there, z

    def home(i):
        return pl.ds(pl.multiple_of(orders[i] * block, block), block)

    def turned(target, source):
        lead[...] = source.T
        for i in range(dp):
            target[i * block : (i + 1) * block, :] = lead[home(i), :]

    loads = [
        pltpu.make_async_copy(source, target, load.at[i])
        for i, (source, target) in enumerate(
            (
                (stream_in, mid),
                (near_in, near),
                (far_in, far),
                (g_in, g),
                (narrow_in, narrow),
                (broad_in, broad),
                (own_o, o_temp),
            )
        )
    ]
    each = dp // 4
    part_o = own_o.shape[0]
    for i in range(dp):
        for r in range(1, mp):
            pltpu.make_async_copy(
                out_parts[i // each].at[
                    pl.ds(i % each * block, block), pl.ds((4 * r - 1) * part_o, part_o)
                ],
                weight_o.at[home(i), pl.ds(r * part_o, part_o)],
                load.at[7],
            ).start()
    rest_o = weight_o.at[:, pl.ds(part_o, width - part_o)]
    for copy in loads:
        copy.start()

    def fetch(i):
        slot, r, t = i % 2, i // per, i % per
        if r == 0:
            return [
                pltpu.make_async_copy(
                    own_e.at[:, pl.ds(t * tile, tile)], weights.at[slot, 0], own_sem.at[0]
                ),
                pltpu.make_async_copy(own_r.at[pl.ds(t * tile, tile), :], r_temp, own_sem.at[1]),
            ]
        if r == 1:
            parts = (early_a, early_b) + tuple(
                early_o.at[pl.ds(n * quarter, quarter), :] for n in range(2)
            )
            first = 0
        else:
            parts, first = (None, late_b, late_c, late_d), (r - 2) * wide

        def piece(n, kind):
            column = kind * extent + t * tile
            if r > 1 and n < each:
                few = each // 2
                return late_a[2 * (r - 2) + n // few].at[
                    pl.ds(n % few * block, block), pl.ds(column, tile)
                ]
            return parts[n // each].at[pl.ds(n % each * block, block), pl.ds(first + column, tile)]

        return [
            pltpu.make_async_copy(
                piece(n, kind),
                weights.at[slot, kind, home(n), :],
                weight_sem.at[slot],
            )
            for kind in range(2)
            for n in range(dp)
        ]

    for copy in fetch(0):
        copy.start()
    meet(d, z, dp, mp)

    def late(buffer, r):
        return buffer.at[:, pl.ds((r - 2) * wide, wide)]

    sent = []
    swaps, hops = {}, {}
    for n, part in enumerate((early_a, early_b)):
        swaps[1, n] = remote(
            part,
            early_o.at[pl.ds(n * quarter, quarter), :],
            core_send.at[1, n],
            core_recv.at[1, n],
            sibling,
        )
    for r in range(2, mp):
        for n in range(2):
            part = late_a[2 * (r - 2) + n]
            span = pl.ds(n * quarter // 2, quarter // 2)
            columns = pl.ds((r - 2) * wide, wide)
            hops[r, n] = remote(
                part,
                late_b.at[span, columns],
                chip_send.at[r, n],
                chip_recv.at[r, n],
                partner(steps - 1),
            )
            swaps[r, n] = remote(
                part, late_c.at[span, columns], core_send.at[r, n], core_recv.at[r, n], sibling
            )
        swaps[r, 2] = remote(
            late(late_b, r), late(late_d, r), core_send.at[r, 2], core_recv.at[r, 2], sibling
        )
    swaps[1, 0].start()
    swaps[1, 1].start()
    for r in range(2, mp):
        for n in range(2):
            hops[r, n].start()
        for n in range(2):
            swaps[r, n].start()

    for i in range(7):
        loads[i].wait()
    pltpu.make_async_copy(rest_o, rest_o, load.at[7]).wait()
    weight_o[:, :part_o] = o_temp[...].T
    cut = near.shape[1]
    mixed = dot(near[...], weight_o[:, :cut], NT) + dot(far[...], weight_o[:, cut:], NT)
    mid[...] = mid[...] + mixed + narrow[2:3, :]
    hat, _ = norm_parts(mid[...])
    x[...] = (hat * narrow[3:4, :] + narrow[4:5, :]).astype(BF16)
    turned(x_t, x[...])
    turned(g_t, g[...])
    out_acc[...] = jnp.zeros_like(out_acc)
    dx_acc[...] = jnp.zeros_like(dx_acc)

    def swap_of(c):
        return remote(
            send.at[c % 2], got.at[c], near_send.at[c], near_recv.at[c], sibling
        )

    def rows_of(step):
        count = half >> (steps - step)
        return count, half - 2 * count

    def sum_of(c, step):
        count, at = rows_of(step)
        return remote(
            keep.at[c, pl.ds(count, count), :],
            more.at[c // 2, pl.ds(at, count), :],
            sum_send.at[c // 2, step],
            sum_recv.at[c // 2, step],
            partner(step),
        )

    def outs_of(c):
        span = pl.ds(c // 2 * wide, wide)
        return [
            pltpu.make_async_copy(
                keep.at[c, pl.ds(n * quarter, quarter), :], target.at[:, span], store.at[c, n]
            )
            for n, target in enumerate((keep_out, upper_out))
        ]

    def core_done(c):
        swap_of(c).wait_recv()
        keep[c] = added(keep[c], got[c])
        if c % 2 == 0:
            sum_of(c, steps - 1).start()
        else:
            for copy in outs_of(c):
                copy.start()

    def chips_done(c, step):
        sum_of(c, step).wait_recv()
        count, at = rows_of(step)
        keep[c, :count, :] = added(keep[c, :count, :], more[c // 2, pl.ds(at, count), :])
        if step:
            sum_of(c, step - 1).start()

    events = {}
    for r in range(2, mp):

        def passed(r=r):
            hops[r, 0].wait_recv()
            hops[r, 1].wait_recv()
            swaps[r, 2].start()

        events.setdefault((r - 1) * per, []).append(passed)
    for r in range(1, mp):

        def arrived(r=r):
            for n in range(2 if r == 1 else 3):
                swaps[r, n].wait_recv()

        events.setdefault(r * per - 1, []).append(arrived)
    for i in range(1, tiles):

        def ahead(i=i):
            for copy in fetch(i):
                copy.start()

        if i >= per:
            events.setdefault(i - 1, []).append(ahead)
    for c in range(mp - 1):
        events.setdefault((c + 2) * per - 1, []).append(functools.partial(core_done, c))
    events.setdefault(tiles - per, []).append(functools.partial(chips_done, 0, steps - 1))

    def body(i, carry):
        slot, c, t = lax.rem(i, 2), lax.div(i, per), lax.rem(i, per)

        @pl.when(c == 0)
        def _():
            pltpu.make_async_copy(weights.at[0, 0], weights.at[0, 0], own_sem.at[0]).wait()
            pltpu.make_async_copy(r_temp, r_temp, own_sem.at[1]).wait()
            weights[slot, 1] = r_temp[...].T

        @pl.when(c > 0)
        def _():
            pltpu.make_async_copy(weights.at[slot], weights.at[slot], weight_sem.at[slot]).wait()

        for n in range(1, per):

            @pl.when(i == n - 1)
            def _():
                for copy in fetch(n):
                    copy.start()

        for n, actions in events.items():

            @pl.when(i == n)
            def _():
                for action in actions:
                    action()

        @pl.when((t == 0) & (c >= 2))
        def _():
            remote(
                send.at[lax.rem(c, 2)], got.at[c], near_send.at[c - 2], near_recv.at[c], sibling
            ).wait_send()

        at = pl.multiple_of(lax.rem(z - c + mp, mp) * extent + t * tile, tile)
        bias = broad[0:1, pl.ds(at, tile)]
        out = lax.rem(c, 2)
        hiddens, grads = [], []
        few = tile // 2
        for part in range(2):
            span = slice(part * few, (part + 1) * few)
            pre = dot(x[...], weights[slot, 0, :, span]) + bias[:, span]
            cumulative = 0.5 * (1.0 + lax.erf(pre * 0.7071067811865476))
            hidden = (pre * cumulative).astype(BF16)
            slope = cumulative + pre * jnp.exp(-0.5 * pre * pre) * (1.0 / math.sqrt(2.0 * math.pi))
            grad_pre = (dot(g[...], weights[slot, 1, :, span]) * slope).astype(BF16)
            line = jnp.sum(grad_pre.astype(F32), axis=0, keepdims=True)
            db[:, pl.ds(pl.multiple_of(i * tile + part * few, few), few)] = jnp.broadcast_to(
                line, (8, few)
            )
            first = pl.ds(pl.multiple_of(2 * t * tile + part * few, few), few)
            second = pl.ds(pl.multiple_of((2 * t + 1) * tile + part * few, few), few)
            send[out, :, first] = dot(x_t[half:, :], grad_pre).astype(BF16)
            send[out, :, second] = dot(g_t[half:, :], hidden).astype(BF16)
            keep[c, :, first] = dot(x_t[:half, :], grad_pre).astype(BF16)
            keep[c, :, second] = dot(g_t[:half, :], hidden).astype(BF16)
            hiddens.append(hidden)
            grads.append(grad_pre)
        hidden, grad_pre = jnp.concatenate(hiddens, axis=1), jnp.concatenate(grads, axis=1)
        weight_e, weight_r = weights[slot, 0], weights[slot, 1]

        @pl.when(t == per - 1)
        def _():
            remote(send.at[out], got.at[c], near_send.at[c], near_recv.at[c], sibling).start()

        out_acc[...] += dot(hidden, weight_r, NT)
        dx_acc[...] += dot(grad_pre, weight_e, NT)
        return carry

    lax.fori_loop(0, tiles, body, 0)

    value, grad, dy = mid[...], g[...].astype(F32), dx_acc[...]
    x[...] = (value + out_acc[...] + narrow[5:6, :]).astype(BF16)
    hat, factor = norm_parts(value)
    back = grad + norm_back(dy, hat, factor, narrow[3:4, :])
    add = lambda v: jnp.sum(v, axis=0, keepdims=True)
    zero = jnp.zeros((4, width), F32)
    sums[...] = jnp.concatenate([add(back), add(dy * hat), add(dy), add(grad), zero], axis=0)
    mid[...] = back
    rounded = back.astype(BF16)
    turned(x_t, rounded)
    near[...] = dot(rounded, weight_o[:, :cut]).astype(BF16)
    far[...] = dot(rounded, weight_o[:, cut:]).astype(BF16)
    results = [
        pltpu.make_async_copy(source, target, load.at[i])
        for i, (source, target) in enumerate(
            ((x, act), (mid, grad_mid), (x_t, branch_t), (near, grad_near), (far, grad_far))
        )
    ]
    for copy in results:
        copy.start()

    core_done(mp - 1)
    for c in range(2, mp, 2):
        chips_done(c, steps - 1)
    for step in reversed(range(steps - 1)):
        for c in range(0, mp, 2):
            chips_done(c, step)
    own_total[...] = keep[0, :block, :].astype(F32)
    for c in range(2, mp, 2):
        moved[c // 2 - 1] = keep[c, :block, :]
    for c in range(max(0, mp - 2), mp):
        swap_of(c).wait_send()
    for c in range(0, mp, 2):
        for step in range(steps):
            sum_of(c, step).wait_send()
    for c in range(1, mp, 2):
        for copy in outs_of(c):
            copy.wait()
    for copy in list(hops.values()) + list(swaps.values()):
        copy.wait_send()
    for copy in results:
        copy.wait()


def middle(arrays, weights, buffers, parts, plane, mp, hidden):
    dp = plane.size
    rows, width = arrays[0].shape
    extent = hidden // mp
    tile = min(512, extent)
    wide, half, quarter, full = 2 * extent, width // 2, width // 4, mp // 2
    vmem, anywhere = pl.BlockSpec(memory_space=pltpu.VMEM), pl.BlockSpec(memory_space=pl.ANY)
    dma = pltpu.SemaphoreType.DMA
    shape = jax.ShapeDtypeStruct
    near = arrays[1].shape[1]
    late = (quarter, (mp - 2) * wide)
    return pl.pallas_call(
        functools.partial(middle_kernel, plane, mp, tile),
        out_shape=[
            shape((8, width), F32),
            shape((8, hidden), F32),
            shape((width // dp, wide), F32),
            shape((max(full - 1, 1), width // dp, wide), BF16),
            shape((rows, width), BF16),
            shape((rows, width), F32),
            shape((width, rows), BF16),
            shape((rows, near), BF16),
            shape((rows, width - near), BF16),
            shape((quarter, (mp - full) * wide), BF16),
            shape((quarter, (mp - full) * wide), BF16),
            shape((half, wide), BF16),
            shape(late, BF16),
            shape(late, BF16),
            shape(late, BF16),
        ],
        in_specs=[anywhere] * (len(arrays) + len(weights) + len(buffers) + len(parts)),
        out_specs=[vmem] * 4 + [anywhere] * 11,
        scratch_shapes=[
            pltpu.VMEM((rows, width), F32),
            pltpu.VMEM(arrays[1].shape, BF16),
            pltpu.VMEM(arrays[2].shape, BF16),
            pltpu.VMEM((rows, width), BF16),
            pltpu.VMEM((8, width), F32),
            pltpu.VMEM((8, hidden), F32),
            pltpu.VMEM(weights[0].shape, BF16),
            pltpu.VMEM((width, width), BF16),
            pltpu.VMEM((2, 2, width, tile), BF16),
            pltpu.VMEM((tile, width), BF16),
            pltpu.VMEM((rows, width), BF16),
            pltpu.VMEM((width, rows), BF16),
            pltpu.VMEM((width, rows), BF16),
            pltpu.VMEM((width, rows), BF16),
            pltpu.VMEM((rows, width), F32),
            pltpu.VMEM((rows, width), F32),
            pltpu.VMEM((mp, half, wide), BF16),
            pltpu.VMEM((2, half, wide), BF16),
            pltpu.VMEM((mp, half, wide), BF16),
            pltpu.VMEM((full, half, wide), BF16),
            dma((8,)),
            dma((2,)),
            dma((2,)),
            dma((mp, 3)),
            dma((mp, 3)),
            dma((mp, 2)),
            dma((mp, 2)),
            dma((full, plane.steps)),
            dma((full, plane.steps)),
            dma((mp,)),
            dma((mp,)),
            dma((mp, 2)),
        ],
        compiler_params=pltpu.CompilerParams(
            collective_id=3, has_side_effects=True, vmem_limit_bytes=60 * MIB
        ),
        cost_estimate=pl.CostEstimate(flops=6 * 10**10, bytes_accessed=0, transcendentals=0),
        name="middle",
    )(*arrays, *weights, *buffers, *parts)


def orders_of(plane, d, core):
    return [
        (1 - core) * xored(d, plane.masks[0][i]) + core * xored(d, plane.masks[1][i])
        for i in range(plane.size)
    ]


def tail_kernel(plane, mp, margin, *refs):
    (around_t, branch_t, dq, dk, dv, att), got, refs = refs[:6], refs[6:18], refs[18:]
    (kept, came, own_two), even, refs = refs[:3], refs[3 : 2 + mp // 2], refs[2 + mp // 2 :]
    (own_out, around_out, lower, upper, bias, total_out, rest_out), refs = refs[:7], refs[7:]
    weights, (payload, shards, keep, send, arrived), refs = refs[:3], refs[3:8], refs[8:]
    z_send, z_recv, core_send, core_recv = refs
    dp = plane.size
    d, z = lax.axis_index("dp"), lax.axis_index("mp")
    step, last = pl.program_id(0), mp - 2
    rows, extent = dq.shape
    width = around_t.shape[0]
    half, quarter, block = width // 2, width // 4, width // dp
    wide = own_two.shape[1]
    sibling = (flipped(d, 0), z)

    def sum_of():
        return remote(
            payload, shards, z_send.at[0], z_recv.at[0], (d, lax.rem(z - 1 + mp, mp))
        )

    @pl.when(step == 0)
    def _():
        greet(d, z, dp, mp)
        payload[...] = added(kept[:, :wide], came[:, :wide])
        rest_out[...] = added(kept[:, wide:], came[:, wide:])

    orders = orders_of(plane, d, lax.rem(d, 2))
    each = dp // 4
    for w in range(3):
        for i in range(dp):
            source = got[4 * w + i // each]
            at = pl.multiple_of(orders[i] * block, block)
            weights[w][pl.ds(at, block), :] = source[i % each * block : (i % each + 1) * block, :]

    middle, everything = slice(margin, margin + rows), slice(None)
    for low, target in ((half, send), (0, keep)):
        for at, (left, span, right) in enumerate(
            (
                (around_t, middle, dq),
                (around_t, everything, dk),
                (around_t, everything, dv),
                (branch_t, everything, att),
            )
        ):
            target[step, :, at * extent : (at + 1) * extent] = dot(
                left[low : low + half, span], right[...]
            ).astype(BF16)
        if low:

            @pl.when(step == 0)
            def _():
                gather_peers(dp, mp)
                sum_of().start()

            remote(
                send.at[step], arrived.at[step], core_send.at[step], core_recv.at[step], sibling
            ).start()
    add = lambda v: jnp.sum(v[...].astype(F32), axis=0, keepdims=True)
    bias[...] = jnp.concatenate([add(dq), add(dv), jnp.zeros((6, extent), F32)], axis=0)
    back = dot(dk[...], weights[1][...], NT) + dot(dv[...], weights[2][...], NT)
    more = dot(dq[...], weights[0][...], NT)

    @pl.when(step == 0)
    def _():
        around_out[...] = back
        own_out[...] = more

    @pl.when(step > 0)
    def _():
        around_out[...] += back
        own_out[...] += more

    def fold(n):
        swap = remote(send.at[n], arrived.at[n], core_send.at[n], core_recv.at[n], sibling)
        swap.wait_recv()
        span = slice(n * 4 * extent, (n + 1) * 4 * extent)
        lower[:, span] = added(keep[n, :quarter, :], arrived[n, :quarter, :])
        upper[:, span] = added(keep[n, quarter:, :], arrived[n, quarter:, :])

    for n in range(last):
        pl.when(step == n + 1)(functools.partial(fold, n))

    @pl.when(step == last)
    def _():
        fold(last)
        total = own_two[...]
        for item in even:
            total = total + item[...].astype(F32)
        sum_of().wait_recv()
        total_out[...] = total + shards[...].astype(F32)
        sum_of().wait_send()
        for n in range(mp - 1):
            remote(
                send.at[n], arrived.at[n], core_send.at[n], core_recv.at[n], sibling
            ).wait_send()


def tail(around_t, branch_t, grads, att, weights, sums, own_two, even, plane, mp, margin):
    dq, dk, dv = grads
    rows, width = dq.shape[0], around_t.shape[0]
    window = around_t.shape[1]
    extent = width // mp
    half, quarter, block = width // 2, width // 4, width // plane.size
    count, wide = mp - 1, own_two.shape[1]
    column = lambda item: pl.BlockSpec((item.shape[0], extent), lambda i: (0, i))
    whole = lambda shape: pl.BlockSpec(
        shape, lambda i: (0,) * len(shape), pipeline_mode=pl.Buffered(1)
    )
    pieces = [
        pl.BlockSpec((item.shape[0], extent), lambda i, kind=kind: (0, i * 4 + kind))
        for kind in range(3)
        for item in weights
    ]
    outs = [
        ((rows, width), F32),
        ((window, width), F32),
        ((quarter, 4 * count * extent), BF16),
        ((quarter, 4 * count * extent), BF16),
        ((8, count * extent), F32),
        ((block, wide), F32),
        ((block, (mp // 2 - 1) * wide), BF16),
    ]
    specs = [whole(shape) for shape, _ in outs]
    specs[4] = pl.BlockSpec((8, extent), lambda i: (0, i))
    stack = pltpu.VMEM((count, half, 4 * extent), BF16)
    dma = pltpu.SemaphoreType.DMA
    constant = (*sums, own_two, *even)
    return pl.pallas_call(
        functools.partial(tail_kernel, plane, mp, margin),
        grid=(count,),
        in_specs=[whole(around_t.shape), whole(branch_t.shape)]
        + [column(item) for item in (dq, dk, dv, att)]
        + pieces
        + [whole(item.shape) for item in constant],
        out_specs=specs,
        out_shape=[jax.ShapeDtypeStruct(shape, kind) for shape, kind in outs],
        scratch_shapes=[pltpu.VMEM((width, extent), BF16)] * 3
        + [
            pltpu.VMEM((block, wide), BF16),
            pltpu.VMEM((block, wide), BF16),
            stack,
            stack,
            stack,
            dma((1,)),
            dma((1,)),
            dma((count,)),
            dma((count,)),
        ],
        compiler_params=pltpu.CompilerParams(
            collective_id=4, has_side_effects=True, vmem_limit_bytes=60 * MIB
        ),
        cost_estimate=pl.CostEstimate(flops=24 * 10**9, bytes_accessed=0, transcendentals=0),
        name="tail",
    )(around_t, branch_t, dq, dk, dv, att, *(list(weights) * 3), *constant)


def finish_kernel(plane, mp, hops, margin, *refs):
    inputs = 18 + mp // 2
    hbm, refs = refs[:inputs], refs[inputs:]
    upper, refs = refs[0], refs[1:]
    (grad_tokens, *totals, grad_expand, grad_reduce, vectors), refs = refs[:8], refs[8:]
    loaded, refs = refs[:inputs], refs[inputs:]
    (halo_out, halo_in, keep, send, got, more_got, shards, table, sheets), refs = refs[:9], refs[9:]
    (middle, first, second), refs = refs[:3], refs[3:]
    load_sem, halo_send, halo_recv, core_sem, near_send, near_recv, far_send, far_recv = refs[:8]
    z_send, z_recv, send_one, recv_one, send_two, recv_two = refs[8:]
    (dq, dk, dv, att, wq, wk, wv, before_around, before_own) = loaded[:9]
    (around_t, branch_t, others, stream, grad_mid, narrow, sums, bias, broad) = loaded[9:18]
    dp = plane.size
    d, z = lax.axis_index("dp"), lax.axis_index("mp")
    core = lax.rem(d, 2)
    rows, extent = dq.shape
    half = keep.shape[0]
    block = totals[0].shape[0]
    columns = 4 * extent

    loads = [
        pltpu.make_async_copy(source, target, load_sem.at[i])
        for i, (source, target) in enumerate(zip(hbm, loaded))
    ]
    for copy in loads:
        copy.start()
    width = wq.shape[0]
    halo_in[...] = jnp.zeros_like(halo_in)
    meet(d, z, dp, mp)

    def partner(step):
        there = (1 - core) * flipped(d, plane.orders[0][step]) + core * flipped(
            d, plane.orders[1][step]
        )
        return there, z

    def fold(target, source, at, count):
        target[:count, :] = added(target[:count, :], source[pl.ds(at, count), :])

    def far_of(step):
        count = half >> (plane.steps - step)
        first = step == plane.steps - 1
        return remote(
            upper if first else others.at[pl.ds(count, count), :],
            more_got.at[pl.ds(half - 2 * count, count), :],
            far_send.at[step],
            far_recv.at[step],
            partner(step),
        )

    sent = [far_of(plane.steps - 1)]
    sent[0].start()

    for i in (1, 2, 5, 6, 7):
        loads[i].wait()
    waits, at_left, at_right, at = [], margin, margin + rows, 0
    copies = []
    for hop, reach in enumerate(hops, 1):
        sides = (
            (at_left - reach, z - hop, z + hop, 2 * hop - 2, rows - reach),
            (at_right, z + hop, z - hop, 2 * hop - 1, 0),
        )
        for start, there, back, n, place in sides:
            span = slice(start, start + reach)
            here = pl.ds(at, reach)
            part = dot(dk[span, :], wk[...], NT) + dot(dv[span, :], wv[...], NT)
            halo_out[here, :] = (before_around[span, :] + part).astype(BF16)
            goes = (there >= 0) & (there < mp)
            comes = (back >= 0) & (back < mp)
            copy = remote(
                halo_out.at[here, :],
                halo_in.at[here, :],
                halo_send.at[n],
                halo_recv.at[n],
                (d, there),
            )
            pl.when(goes)(copy.start)
            waits.append((goes, copy.wait_send))
            copies.append((comes, copy.wait_recv, place, at, reach))
            at += reach
        at_left, at_right = at_left - reach, at_right + reach

    for i in (0, 3, 9, 10):
        loads[i].wait()
    inner, everything = slice(margin, margin + rows), slice(None)

    def weight_grads(target, low):
        for n, (source, span, right) in enumerate(
            (
                (around_t, inner, dq),
                (around_t, everything, dk),
                (around_t, everything, dv),
                (branch_t, everything, att),
            )
        ):
            target[:, n * extent : (n + 1) * extent] = dot(
                source[low : low + half, span], right[...]
            ).astype(BF16)

    weight_grads(send, half)
    swap = remote(send, got.at[pl.ds(0, half), :], core_sem.at[0], core_sem.at[1], (flipped(d, 0), z))
    swap.start()
    sent.append(swap)
    weight_grads(keep, 0)

    swap.wait_recv()
    fold(keep, got, 0, half)
    count, at_near = half, half
    for step in reversed(range(plane.steps)):
        count //= 2
        near = remote(
            keep.at[pl.ds(count, count), :],
            got.at[pl.ds(at_near, count), :],
            near_send.at[step],
            near_recv.at[step],
            partner(step),
        )
        near.start()
        sent.append(near)
        if step == plane.steps - 1:
            loads[4].wait()
            loads[8].wait()
            own = before_own[...] + before_around[inner, :] + dot(dq[...], wq[...], NT)
            own += dot(dk[inner, :], wk[...], NT) + dot(dv[inner, :], wv[...], NT)
            before_own[...] = own
            loads[11].wait()
        far_of(step).wait_recv()
        fold(others, more_got, half - 2 * count, count)
        if step:
            sent.append(far_of(step - 1))
            sent[-1].start()
        else:
            for r in range(1, mp):
                copy = remote(
                    others.at[pl.ds(0, block), pl.ds((r - 1) * columns, columns)],
                    shards.at[r],
                    z_send.at[r],
                    z_recv.at[r],
                    (d, lax.rem(z - r + mp, mp)),
                )
                copy.start()
                sent.append(copy)
        near.wait_recv()
        fold(keep, got, at_near, count)
        at_near += count

    for i in range(12, 18):
        loads[i].wait()
    for comes, wait, *_ in copies:
        pl.when(comes)(wait)
    for _, _, place, at, reach in copies:
        span = slice(place, place + reach)
        before_own[span, :] = before_own[span, :] + halo_in[at : at + reach, :].astype(F32)
    hat, factor = norm_parts(stream[...])
    upstream = before_own[...]
    add = lambda v: jnp.sum(v, axis=0, keepdims=True)
    back = grad_mid[...] + norm_back(upstream, hat, factor, narrow[0:1, :])
    grad_tokens[...] = back.astype(BF16)
    table[0:1, :] = add(upstream * hat)
    table[1:2, :] = add(upstream)
    table[2:6, :] = sums[0:4, :]
    mine = pl.ds(pl.multiple_of(z * extent, extent), extent)
    table[6:7, mine] = add(dq[...].astype(F32))
    table[7:8, mine] = add(dv[...].astype(F32))
    for r in range(1, mp):
        place = pl.ds(pl.multiple_of(lax.rem(z - r + mp, mp) * extent, extent), extent)
        table[6:8, place] = bias[0:2, (r - 1) * extent : r * extent]
    each = dp // (width // 128)
    hidden = broad.shape[1]
    lines = hidden // dp // 128
    per = hidden // mp // 128
    sheets[...] = jnp.zeros_like(sheets)
    for i in range(dp):
        c = i // each
        sheets[i, 0:8, :] = table[:, c * 128 : (c + 1) * 128]
        for n in range(lines):
            shard, at = (i * lines + n) // per, (i * lines + n) % per
            start = (lax.rem(z - shard + mp, mp) * per + at) * 128
            sheets[i, 8 + n : 9 + n, :] = broad[0:1, pl.ds(pl.multiple_of(start, 128), 128)]
    along_dp = lambda step: (lax.rem(d + step, dp), z)
    along_mp = lambda step: (d, lax.rem(z + step, mp))
    out = peers_start(sheets, second, send_two, recv_two, along_dp, d, dp, True)
    peers_finish(out, second, recv_two, d, dp)
    middle[0] = jnp.sum(second[...], axis=0)
    out = peers_start(middle, first, send_one, recv_one, along_mp, z, mp, False)
    for copy in loads[18:]:
        copy.wait()
    full = loaded[18][...]
    for item in loaded[19:]:
        full = full + item[...].astype(F32)
    tile = min(512, full.shape[1] // 2)
    for n in range(full.shape[1] // tile // 2):
        span = slice(n * tile, (n + 1) * tile)
        grad_expand[:, span] = full[:, 2 * n * tile : (2 * n + 1) * tile]
        grad_reduce[span, :] = full[:, (2 * n + 1) * tile : (2 * n + 2) * tile].T

    full = keep[:block, :].astype(F32)
    for r in range(1, mp):
        pltpu.make_async_copy(shards.at[r], shards.at[r], z_recv.at[r]).wait()
        full += shards[r].astype(F32)
    for n, item in enumerate(totals):
        part = full[:, n * extent : (n + 1) * extent]
        item[...] = part if n < 3 else part.T
    peers_finish(out, first, recv_one, z, mp)
    vectors[...] = jnp.sum(first[...], axis=0)
    for copy in sent:
        copy.wait_send()
    for when, wait in waits:
        pl.when(when)(wait)


def finish(arrays, upper, plane, mp, hops, margin):
    dp = plane.size
    rows, extent = arrays[0].shape
    width = arrays[4].shape[0]
    block, half, columns = width // dp, width // 2, 4 * extent
    hidden = arrays[18].shape[1] // 2
    vmem, anywhere = pl.BlockSpec(memory_space=pltpu.VMEM), pl.BlockSpec(memory_space=pl.ANY)
    dma = pltpu.SemaphoreType.DMA
    left = sum(hops)
    return pl.pallas_call(
        functools.partial(finish_kernel, plane, mp, hops, margin),
        out_shape=[
            jax.ShapeDtypeStruct((rows, width), BF16),
            *[jax.ShapeDtypeStruct((block, extent), F32)] * 3,
            jax.ShapeDtypeStruct((extent, block), F32),
            jax.ShapeDtypeStruct((block, hidden), F32),
            jax.ShapeDtypeStruct((hidden, block), F32),
            jax.ShapeDtypeStruct((16, 128), F32),
        ],
        in_specs=[anywhere] * (len(arrays) + 1),
        out_specs=[vmem] * 8,
        scratch_shapes=[pltpu.VMEM(item.shape, item.dtype) for item in arrays]
        + [
            pltpu.VMEM((2 * left, width), BF16),
            pltpu.VMEM((2 * left, width), BF16),
            pltpu.VMEM((half, columns), BF16),
            pltpu.VMEM((half, columns), BF16),
            pltpu.VMEM((2 * half, columns), BF16),
            pltpu.VMEM((half, (mp - 1) * columns), BF16),
            pltpu.VMEM((mp, block, columns), BF16),
            pltpu.VMEM((8, width), F32),
            pltpu.VMEM((dp, 16, 128), F32),
            pltpu.VMEM((1, 16, 128), F32),
            pltpu.VMEM((mp, 16, 128), F32),
            pltpu.VMEM((dp, 16, 128), F32),
            dma((len(arrays),)),
            dma((2 * len(hops),)),
            dma((2 * len(hops),)),
            dma((2,)),
            dma((plane.steps,)),
            dma((plane.steps,)),
            dma((plane.steps,)),
            dma((plane.steps,)),
            dma((mp,)),
            dma((mp,)),
            dma((mp,)),
            dma((mp,)),
            dma((dp,)),
            dma((dp,)),
        ],
        compiler_params=pltpu.CompilerParams(
            collective_id=2, has_side_effects=True, vmem_limit_bytes=60 * MIB
        ),
        cost_estimate=pl.CostEstimate(flops=5 * 10**10, bytes_accessed=0, transcendentals=0),
        name="finish",
    )(*arrays, upper)


def local(
    tokens,
    kept_index,
    lengths,
    first_gain,
    first_shift,
    query_weight,
    key_weight,
    value_weight,
    query_bias,
    value_bias,
    output_weight,
    output_bias,
    second_gain,
    second_shift,
    expand_weight,
    expand_bias,
    reduce_weight,
    reduce_bias,
    cotangent,
):
    dp, mp = lax.axis_size("dp"), lax.axis_size("mp")
    d, z = lax.axis_index("dp"), lax.axis_index("mp")
    plane = Plane(dp)
    rows, width = tokens.shape
    group_rows = rows * mp
    block = width // dp
    full_hidden = expand_weight.shape[1] * mp
    meta = jnp.concatenate([z[None], plane.order(d)]).astype(jnp.int32)

    singles = (
        first_gain,
        first_shift,
        output_bias,
        second_gain,
        second_shift,
        reduce_bias,
        query_bias,
        value_bias,
    )
    single, wide = first_gain.shape[0], expand_bias.shape[0]
    me = d * mp + z
    lane = jnp.arange(128, dtype=jnp.int32)
    lines = full_hidden // dp // 128

    def placed(stack):
        count = 128 // stack.shape[1]
        return jnp.where(lane // stack.shape[1] == me % count, jnp.tile(stack, (1, count)), 0.0)

    line = placed(expand_bias[None].astype(F32))
    at_line = (jnp.arange(8, dtype=jnp.int32) == me * wide // 128 % lines)[:, None]
    sheet = jnp.concatenate(
        [placed(jnp.stack(singles).astype(F32)), jnp.where(at_line, line, 0.0)], axis=0
    )
    scal = jnp.concatenate([z[None], lengths[0]]).astype(jnp.int32)
    reach, hops, left = LONGEST - 1, [], 0
    while reach > 0:
        extent = min(rows, -(-reach // 16) * 16)
        hops.append(extent)
        left, reach = left + extent, reach - extent
    margin = -(-left // 128) * 128
    while (2 * margin + rows) % TILE:
        margin += 128

    begun = begin(
        sheet[None],
        tokens,
        kept_index[None],
        jnp.asarray(position_lines(width)),
        (query_weight, key_weight, value_weight, output_weight, expand_weight, reduce_weight),
        plane,
        mp,
        hops,
        margin,
    )
    narrow, broad, stream, around, normed_one, second = begun[:6]
    buffers = begun[6:]
    shares = {1: shifted(second, 1, mp)}
    around_t = turned_rows(around, meta, block)
    projections = (query_weight, key_weight, value_weight)
    pairs = width // (2 * HEAD_SIZE) // mp
    own = project(normed_one, around, projections, narrow, meta, block, mp, True)
    tied = after(narrow, shares[1], *own)
    rest = project(normed_one, around, buffers, tied, meta, block, mp, False)
    heads = [own, rest]
    for r in range(2, mp):
        shares[r] = shifted(after(second, shares[1]), r, mp)
    early = spread_chips(shares[1], plane)
    far, late = (), []
    for r in range(1, mp):
        part = ((r - 1) * pairs, pairs, (mp - 1) * pairs)
        if r == 1:
            far = attention_forward(after(scal, early[-1]), mp, *heads[1], part, far)
            early = join(early, 0)
            early = (early, lax.ppermute(early, "dp", plane.pairs(plane.steps - 1)))
            near = attention_forward(after(scal, *far), mp, *heads[0], (0, pairs, pairs))
        else:
            tied = after(scal, *far, *near, shares[r])
            far = attention_forward(tied, mp, *heads[1], part, far)
            late.extend(spread_chips(shares[r], plane))
    attended, lses = [near[0], far[0]], [near[1], far[1]]

    results = middle(
        (stream, *attended, cotangent, narrow, broad),
        (output_weight, expand_weight, reduce_weight),
        buffers,
        (*early, *late),
        plane,
        mp,
        full_hidden,
    )
    sums_mid, grad_bias, own_two, ready = results[:4]
    activations, grad_middle, branch_t, grad_near, grad_far, kept, upper = results[4:11]
    moved_one = [
        lax.ppermute(ready[r // 2 - 1], "mp", [(j, (j - r) % mp) for j in range(mp)])
        for r in range(2, mp, 2)
    ]
    sums_two = Scatter(kept, upper, list(range(1, mp, 2)), plane, mp)

    grads_far = ()
    for r in range(1, mp):
        part = ((r - 1) * pairs, pairs, (mp - 1) * pairs)
        tied = after(scal, *grads_far, sums_two.got) if r == mp - 1 else after(scal, *grads_far)
        grads_far = attention_backward(
            tied,
            mp,
            *heads[1],
            grad_far,
            attended[1],
            lses[1],
            part,
            tuple(grads_far),
        )
    while sums_two.step > 0:
        sums_two.next()
    partial = tail(
        around_t,
        branch_t,
        grads_far,
        attended[1],
        buffers,
        (sums_two.keep, sums_two.got),
        own_two,
        moved_one,
        plane,
        mp,
        margin,
    )
    breadth = own_two.shape[1]
    moved_two = [
        lax.ppermute(
            partial[6][:, i * breadth : (i + 1) * breadth],
            "mp",
            [(j, (j - r) % mp) for j in range(mp)],
        )
        for i, r in enumerate(range(3, mp, 2))
    ]
    grads_near = attention_backward(
        after(scal, partial[0]),
        mp,
        *heads[0],
        grad_near,
        attended[0],
        lses[0],
        (0, pairs, pairs),
    )

    grad_tokens, grad_query, grad_key, grad_value, grad_out, grad_expand, grad_reduce, summed = finish(
        (
            *grads_near,
            attended[0],
            *projections,
            partial[1],
            partial[0],
            around_t,
            branch_t,
            partial[2],
            stream,
            grad_middle,
            narrow,
            sums_mid,
            partial[4],
            grad_bias,
            partial[5],
            *moved_two,
        ),
        partial[3],
        plane,
        mp,
        hops,
        margin,
    )

    taken = lambda stack, extent: lax.dynamic_slice_in_dim(
        stack, me % (128 // extent) * extent, extent, 1
    )
    small = taken(summed[:8], single)
    broad_row = lax.dynamic_slice_in_dim(summed[8:], me * wide // 128 % lines, 1, 0)
    return (
        activations,
        grad_tokens,
        grad_query,
        grad_key,
        grad_value,
        grad_out,
        grad_expand,
        grad_reduce,
        small[0],
        small[1],
        small[6],
        small[7],
        small[2],
        small[3],
        small[4],
        taken(broad_row, wide)[0],
        small[5],
    )


def solution(mesh):
    vector = P(("dp", "mp"))
    tall = P(("dp", "mp"), None)
    in_specs = (
        tall,
        vector,
        P("dp", None),
        vector,
        vector,
        P(None, "mp"),
        P(None, "mp"),
        P(None, "mp"),
        vector,
        vector,
        P("mp", None),
        vector,
        vector,
        vector,
        P(None, "mp"),
        vector,
        P("mp", None),
        vector,
        tall,
    )
    out_specs = (
        tall,
        tall,
        P("dp", "mp"),
        P("dp", "mp"),
        P("dp", "mp"),
        P("mp", "dp"),
        P("dp", "mp"),
        P("mp", "dp"),
    ) + (vector,) * 9
    return jax.shard_map(local, mesh=mesh, in_specs=in_specs, out_specs=out_specs, check_vma=False)
```
